32 devices in a mesh: group: 4 (over y, x), expert: 4 (over z), dp: 2 (over core).
Axes of the slice: x: 2, y: 2, z: 4, core: 2. Of those that a mesh axis runs over, the one named last changes fastest.
Arguments:
- patches: bfloat16 [32768, 16], P(('group', 'expert', 'dp')), may hold values from -6 to 6
- target_noise: float32 [32768, 16], P(('group', 'expert', 'dp')), may hold values from -12 to 12
- timesteps: int32 [128], P(('group', 'expert', 'dp')), may hold values from 0 to 999
- labels: int32 [128], P(('group', 'expert', 'dp')), may hold values from 0 to 1000
- routes: int32 [2, 32768, 2], P(None, ('group', 'expert', 'dp')), may hold values from 0 to 3, all different within a row; in each aligned block of 1024 rows (0 to 1023, 1024 to 2047, ..., all dimensions but the last counted through in order) at most 1024 rows name the same one
- route_gates: float32 [2, 32768, 2], P(None, ('group', 'expert', 'dp')), may hold values from 0.3 to 1
- stem_weights: float32 [2441, 384], P(None, ('expert', 'dp')), may hold values from -3 to 3
- layer_in: float32 [2, 384, 6912], P(None, None, ('expert', 'dp')), may hold values from -2 to 2
- layer_out: float32 [2, 3072, 384], P(None, ('expert', 'dp')), may hold values from -0.15625 to 0.15625
- experts: float32 [2, 4, 2, 384, 1536], P(None, 'expert', None, None, 'dp'), may hold values from -0.21875 to 0.21875
- stem_first: float32 [4, 2441, 384], P('group', None, ('expert', 'dp')), may hold values from -16 to 16
- layer_in_first: float32 [4, 2, 384, 6912], P('group', None, None, ('expert', 'dp')), may hold values from -4 to 4
- layer_out_first: float32 [4, 2, 3072, 384], P('group', None, ('expert', 'dp')), may hold values from -4 to 4
- experts_first: float32 [4, 2, 4, 2, 384, 1536], P('group', None, 'expert', None, None, 'dp'), may hold values from -4 to 4
- stem_second: float32 [4, 2441, 384], P('group', None, ('expert', 'dp')), may hold values from 38.5024 to 155.648
- layer_in_second: float32 [4, 2, 384, 6912], P('group', None, None, ('expert', 'dp')), may hold values from 4.34176 to 17.2032
- layer_out_second: float32 [4, 2, 3072, 384], P('group', None, ('expert', 'dp')), may hold values from 4.34176 to 17.2032
- experts_second: float32 [4, 2, 4, 2, 384, 1536], P('group', None, 'expert', None, None, 'dp'), may hold values from 2.17088 to 8.6016
- stem_moment: float32 [2441, 384], P(None, ('expert', 'dp')), may hold values from -0.15625 to 0.15625
- layer_in_moment: float32 [2, 384, 6912], P(None, None, ('expert', 'dp')), may hold values from -0.15625 to 0.15625
- layer_out_moment: float32 [2, 3072, 384], P(None, ('expert', 'dp')), may hold values from -0.15625 to 0.15625
- experts_moment: float32 [2, 4, 2, 384, 1536], P(None, 'expert', None, None, 'dp'), may hold values from -0.15625 to 0.15625
Outputs:
- loss_sum: float32 [], replicated
- stem_new: float32 [2441, 384], P(None, ('expert', 'dp'))
- layer_in_new: float32 [2, 384, 6912], P(None, None, ('expert', 'dp'))
- layer_out_new: float32 [2, 3072, 384], P(None, ('expert', 'dp'))
- experts_new: float32 [2, 4, 2, 384, 1536], P(None, 'expert', None, None, 'dp')
- stem_half: bfloat16 [2441, 384], P(None, ('expert', 'dp'))
- layer_in_half: bfloat16 [2, 384, 6912], P(None, None, ('expert', 'dp'))
- layer_out_half: bfloat16 [2, 3072, 384], P(None, ('expert', 'dp'))
- experts_half: bfloat16 [2, 4, 2, 384, 1536], P(None, 'expert', None, None, 'dp')
- stem_first_new: float32 [4, 2441, 384], P('group', None, ('expert', 'dp'))
- layer_in_first_new: float32 [4, 2, 384, 6912], P('group', None, None, ('expert', 'dp'))
- layer_out_first_new: float32 [4, 2, 3072, 384], P('group', None, ('expert', 'dp'))
- experts_first_new: float32 [4, 2, 4, 2, 384, 1536], P('group', None, 'expert', None, None, 'dp')
- stem_second_new: float32 [4, 2441, 384], P('group', None, ('expert', 'dp'))
- layer_in_second_new: float32 [4, 2, 384, 6912], P('group', None, None, ('expert', 'dp'))
- layer_out_second_new: float32 [4, 2, 3072, 384], P('group', None, ('expert', 'dp'))
- experts_second_new: float32 [4, 2, 4, 2, 384, 1536], P('group', None, 'expert', None, None, 'dp')
- stem_moment_new: float32 [2441, 384], P(None, ('expert', 'dp'))
- layer_in_moment_new: float32 [2, 384, 6912], P(None, None, ('expert', 'dp'))
- layer_out_moment_new: float32 [2, 3072, 384], P(None, ('expert', 'dp'))
- experts_moment_new: float32 [2, 4, 2, 384, 1536], P(None, 'expert', None, None, 'dp')
The draws below stay inside these ranges and needn't reach their ends.
Inputs may be any that keep to these rules, and one draw needn't show every extreme that they name: `routes`: within the rows of one device in each layer, no expert is named more than 1024 times; some expert is named exactly 1024 times.
All inputs are finite; a program needn't handle non-finite values.
Results may differ from the reference program's by a relative error of at most 0.015.
The reference program's roundings to bfloat16 on the way count: a program that leaves them out, or rounds other values in their place, can miss the bound.
Values may be sent and summed in bfloat16 or wider, within the bound.
A program may use at most 448 MiB of HBM per device.

```python
import math
import jax
import jax.numpy as jnp
import numpy as np
from jax import lax

D = 384
HEADS = 6
FF = 1536
IMG = 32
FREQ = 256
CLASSES = 1000
LAYERS = 2
STEP = 10
PATCH_DIM = 16
PATCHES = 256
TOK_DEV = 1024
TOKENS = 32768
ITEMS = 128
GROUP_TOK = 8192
EXPERTS = 4
CAP = 1024
SROWS = 2441
COLS = 6912
N_GROUP = 4
N_EXPERT = 4
N_DP = 2


def draw_target_noise(key, part):
    key = jax.random.fold_in(key, 11)
    row_ids = jnp.arange(TOKENS, dtype=jnp.int32)
    device_id = row_ids // TOK_DEV
    in_group = N_EXPERT * N_DP
    group_pos = (device_id // in_group).astype(jnp.float32) / max(N_GROUP - 1, 1)
    expert_pos = (device_id // N_DP % N_EXPERT).astype(jnp.float32) / max(N_EXPERT - 1, 1)
    core_pos = (device_id % N_DP).astype(jnp.float32) / max(N_DP - 1, 1)
    position = group_pos + expert_pos + core_pos
    base = jnp.clip(jax.random.normal(key, (TOKENS, PATCH_DIM), jnp.float32), -4.0, 4.0)
    scale_row = 0.5 * jnp.exp(0.55 * position)
    return base * scale_row[:, None]


def draw_stem_weights(key, part):
    key = jax.random.fold_in(key, 12)
    row_count = 2 * PATCH_DIM + FREQ + 3 * D + CLASSES + 1
    base = jnp.clip(jax.random.normal(key, (row_count, D), jnp.float32), -4.0, 4.0)
    row_ids = jnp.arange(row_count, dtype=jnp.int32)
    end_patch = PATCH_DIM
    end_time = end_patch + FREQ
    end_second = end_time + D
    end_table = end_second + CLASSES + 1
    end_ada = end_table + 2 * D
    scale_row = jnp.where(row_ids < end_patch, PATCH_DIM ** (-0.5), jnp.where(row_ids < end_time, 1.4 * FREQ ** (-0.5), jnp.where(row_ids < end_second, 1.5 * D ** (-0.5), jnp.where(row_ids < end_table, 0.1, jnp.where(row_ids < end_ada, D ** (-0.5), D ** (-0.5))))))
    return base * scale_row[:, None]


def draw_layer_in(key, part):
    key = jax.random.fold_in(key, 13)
    col_count = 10 * D + 2 * FF
    base = jnp.clip(jax.random.normal(key, (LAYERS, D, col_count), jnp.float32), -4.0, 4.0)
    col_ids = jnp.arange(col_count, dtype=jnp.int32)
    scale_col = jnp.where((col_ids >= 3 * D) & (col_ids < 4 * D), 0.5 * PATCHES ** 0.5 * D ** (-0.5), D ** (-0.5))
    return base * scale_col[None, None, :]


def with_ends(values, stream_key, smallest, largest):
    shape = values.shape
    index_at = [jax.random.randint(jax.random.fold_in(stream_key, axis), (), 0, shape[axis]) for axis in range(len(shape))]
    values = values.at[tuple(index_at)].set(smallest)
    longest = shape.index(max(shape))
    index_at[longest] = (index_at[longest] + 1) % shape[longest]
    return values.at[tuple(index_at)].set(largest)


def steps_of(stream_key, shape, pieces, low, high):
    def one(axis_at, parts):
        draws = jax.random.uniform(jax.random.fold_in(jax.random.fold_in(stream_key, 6), axis_at), (parts,), jnp.float32, low / len(pieces), high / len(pieces))
        return jnp.repeat(jnp.exp(draws), shape[axis_at] // parts).reshape((-1,) + (1,) * (len(shape) - axis_at - 1))

    level = one(*pieces[0])
    for cut in pieces[1:]:
        level = level * one(*cut)
    return level


def shared_out(own_key, own, number, rows, amount, top, limit, skew):
    ranking = jax.random.permutation(own_key, amount)
    crowded, ordinary = load_shares(amount, rows * top, limit, skew, True), load_shares(amount, rows * top, limit, skew, False)
    places = jnp.arange(amount)

    def named(tallies, rotation):
        used = int((tallies > 0).sum())
        fixed = max(1, used // 4)
        shifted = fixed + (places - fixed + rotation * (used - fixed)) % max(1, amount - fixed)
        return jnp.zeros((amount,), jnp.int32).at[ranking[jnp.where(places < fixed, places, shifted)]].set(jnp.asarray(tallies, jnp.int32))

    tallies = jnp.where(number % 4 == 0, named(crowded, number // 4), named(ordinary, number - number // 4 - 1))
    mixed = jax.random.permutation(jax.random.fold_in(own, 3), amount)
    source_of, receiver = mixed[0:amount // 2 * 2:2], mixed[1:amount // 2 * 2:2]
    room = jnp.minimum(tallies[source_of] - 1, limit - tallies[receiver]) // 2
    room = jnp.where((source_of == ranking[0]) | (receiver == ranking[0]) | (tallies[receiver] == 0), 0, jnp.maximum(room, 0))
    shifted = jax.random.randint(jax.random.fold_in(own, 4), (amount // 2,), 0, 1 << 20) % (room + 1)
    tallies = tallies.at[source_of].add(-shifted).at[receiver].add(shifted)
    items = jnp.searchsorted(jnp.cumsum(tallies), jnp.arange(rows * top), side="right").astype(jnp.int32)
    table = items.reshape(top, rows).T
    table = table[jax.random.permutation(jax.random.fold_in(own, 1), rows)]
    rotation = jax.random.randint(jax.random.fold_in(own, 2), (rows, 1), 0, top)
    return jnp.take_along_axis(table, (jnp.arange(top)[None, :] + rotation) % top, axis=1)


def load_shares(amount, total, most, lean, full):
    loads = [(1 << 20) // math.isqrt(grade ** lean) + 1 for grade in range(1, amount + 1)]
    largest = most if full else min(most, max(-(-total // amount), total * loads[0] // sum(loads)))
    least = 1 if total - largest >= amount - 1 else 0
    given, surplus = [largest] + [least] * (amount - 1), total - largest - least * (amount - 1)
    while surplus > 0:
        free = [i for i in range(1, amount) if given[i] < largest] or [i for i in range(1, amount) if given[i] < most]
        pool, budget = sum([loads[i] for i in free]), surplus
        for i in free:
            more = min(most - given[i], max(1, budget * loads[i] // pool), surplus)
            given[i] = given[i] + more
            surplus = surplus - more
    return np.array(given)


def scatter_about(rng, shape, width, bound, cuts=(), kind=jnp.bfloat16):
    values = width * jax.random.normal(rng, shape, jnp.float32)
    if cuts:
        values = values * steps_of(rng, shape, cuts, -0.22, 0.18)
    return jnp.clip(values, -bound, bound).astype(kind)


def setup_inputs(seed: int = 0) -> dict:
    key_list = jax.random.split(jax.random.key(seed), 23)
    patches = scatter_about(key_list[0], (TOKENS, PATCH_DIM), 1.0, 6.0, ((0, 32),))
    target_noise = draw_target_noise(jax.random.fold_in(key_list[22], 71), 0)
    timesteps = with_ends(jax.random.randint(key_list[2], (ITEMS,), 0, 1000), jax.random.fold_in(key_list[2], 1), 0, 999).astype(jnp.int32)
    labels = with_ends(jax.random.randint(key_list[3], (ITEMS,), 0, CLASSES + 1), jax.random.fold_in(key_list[3], 1), 0, CLASSES).astype(jnp.int32)
    routes_keys = jax.random.split(jax.random.fold_in(key_list[4], 1), LAYERS * TOKENS // TOK_DEV)
    routes_turns = jax.random.permutation(jax.random.fold_in(key_list[4], 3), LAYERS * TOKENS // TOK_DEV)
    routes = jax.vmap(lambda own, number: shared_out(jax.random.fold_in(key_list[4], 2), own, number, TOK_DEV, EXPERTS, 2, CAP, 1))(routes_keys, routes_turns).reshape((LAYERS, TOKENS, 2))
    route_gates = jnp.clip(0.3 + 0.7 * jax.random.uniform(key_list[5], (LAYERS, TOKENS, 2), jnp.float32) ** steps_of(key_list[5], (LAYERS, TOKENS, 2), ((1, 32),), -0.2, 0.2), 0.3, 1.0)
    stem_weights = draw_stem_weights(jax.random.fold_in(key_list[22], 71), 0)
    layer_in = draw_layer_in(jax.random.fold_in(key_list[22], 71), 0)
    layer_out = scatter_about(key_list[8], (LAYERS, 2 * FF, D), FF ** -0.5, 0.15625, ((1, 8),), jnp.float32)
    experts = scatter_about(key_list[9], (LAYERS, EXPERTS, 2, D, FF), (2 * D) ** -0.5, 0.21875, ((1, 4), (4, 2)), jnp.float32)
    stem_first = scatter_about(key_list[10], (N_GROUP, SROWS, D), (0.033 * GROUP_TOK ** 0.5), 16.0, ((0, 4), (2, 8)), jnp.float32)
    layer_in_first = scatter_about(key_list[11], (N_GROUP, LAYERS, D, COLS), (0.011 * GROUP_TOK ** 0.5), 4.0, ((0, 4), (3, 8)), jnp.float32)
    layer_out_first = scatter_about(key_list[12], (N_GROUP, LAYERS, 2 * FF, D), (0.011 * GROUP_TOK ** 0.5), 4.0, ((0, 4), (2, 8)), jnp.float32)
    experts_first = scatter_about(key_list[13], (N_GROUP, LAYERS, EXPERTS, 2, D, FF), (0.011 * (2 * GROUP_TOK // EXPERTS) ** 0.5), 4.0, ((0, 4), (2, 4), (5, 2)), jnp.float32)
    stem_second = jnp.clip(jnp.exp(math.log(155.648) - 1.3968765 * jax.random.uniform(key_list[14], (N_GROUP, SROWS, D), jnp.float32) ** steps_of(key_list[14], (N_GROUP, SROWS, D), ((0, 4), (2, 8)), -0.2, 0.2)), 38.5024, 155.648)
    layer_in_second = jnp.clip(jnp.exp(math.log(17.2032) - 1.3768155 * jax.random.uniform(key_list[15], (N_GROUP, LAYERS, D, COLS), jnp.float32) ** steps_of(key_list[15], (N_GROUP, LAYERS, D, COLS), ((0, 4), (3, 8)), -0.2, 0.2)), 4.34176, 17.2032)
    layer_out_second = jnp.clip(jnp.exp(math.log(17.2032) - 1.3768155 * jax.random.uniform(key_list[16], (N_GROUP, LAYERS, 2 * FF, D), jnp.float32) ** steps_of(key_list[16], (N_GROUP, LAYERS, 2 * FF, D), ((0, 4), (2, 8)), -0.2, 0.2)), 4.34176, 17.2032)
    experts_second = jnp.clip(jnp.exp(math.log(8.6016) - 1.3768155 * jax.random.uniform(key_list[17], (N_GROUP, LAYERS, EXPERTS, 2, D, FF), jnp.float32) ** steps_of(key_list[17], (N_GROUP, LAYERS, EXPERTS, 2, D, FF), ((0, 4), (2, 4), (5, 2)), -0.2, 0.2)), 2.17088, 8.6016)
    stem_moment = scatter_about(key_list[18], (SROWS, D), 0.01, 0.15625, ((1, 8),), jnp.float32)
    layer_in_moment = scatter_about(key_list[19], (LAYERS, D, COLS), 0.01, 0.15625, ((2, 8),), jnp.float32)
    layer_out_moment = scatter_about(key_list[20], (LAYERS, 2 * FF, D), 0.01, 0.15625, ((1, 8),), jnp.float32)
    experts_moment = scatter_about(key_list[21], (LAYERS, EXPERTS, 2, D, FF), 0.01, 0.15625, ((1, 4), (4, 2)), jnp.float32)
    return {"patches": patches, "target_noise": target_noise, "timesteps": timesteps, "labels": labels, "routes": routes, "route_gates": route_gates, "stem_weights": stem_weights, "layer_in": layer_in, "layer_out": layer_out, "experts": experts, "stem_first": stem_first, "layer_in_first": layer_in_first, "layer_out_first": layer_out_first, "experts_first": experts_first, "stem_second": stem_second, "layer_in_second": layer_in_second, "layer_out_second": layer_out_second, "experts_second": experts_second, "stem_moment": stem_moment, "layer_in_moment": layer_in_moment, "layer_out_moment": layer_out_moment, "experts_moment": experts_moment}


highest = lax.Precision.HIGHEST
beta_one = 0.9
beta_two = 0.95
eps_adam = 1e-08
inner_rate = 0.03
weight_decay = 0.05
outer_rate = 0.7
outer_mom = 0.9
ln_eps = 1e-06

@jax.custom_vjp
def low(v):
    return lax.optimization_barrier(v.astype(jnp.bfloat16)).astype(jnp.float32)

@jax.custom_vjp
def low_back(v):
    return v

def low_keep(v):
    return (low(v), None)

def low_pass(kept, grad):
    return (grad,)

def back_keep(v):
    return (v, None)

def back_low(kept, grad):
    return (low(grad),)
low.defvjp(low_keep, low_pass)
low_back.defvjp(back_keep, back_low)

def norm_mod(values, shift_in, scale_in):
    centre = values - lax.optimization_barrier(jnp.mean(values, axis=-1, keepdims=True))
    spread = lax.optimization_barrier(jnp.mean(centre * centre, axis=-1, keepdims=True))
    return centre * lax.rsqrt(spread + ln_eps) * (1.0 + scale_in) + shift_in

def positions_table():
    grid_side = IMG // 2
    quarter = D // 4
    omegas = 1.0 / 10000.0 ** (jnp.arange(quarter, dtype=jnp.float32) / quarter)
    index_all = jnp.arange(PATCHES, dtype=jnp.int32)
    row_angle = (index_all // grid_side).astype(jnp.float32)[:, None] * omegas[None, :]
    col_angle = (index_all % grid_side).astype(jnp.float32)[:, None] * omegas[None, :]
    return jnp.concatenate([jnp.sin(row_angle), jnp.cos(row_angle), jnp.sin(col_angle), jnp.cos(col_angle)], axis=1)

def time_features(step_ids):
    half_freq = FREQ // 2
    frequency = jnp.exp(-jnp.log(10000.0) * jnp.arange(half_freq, dtype=jnp.float32) / half_freq)
    angles = step_ids.astype(jnp.float32)[:, None] * frequency[None, :]
    return jnp.concatenate([jnp.cos(angles), jnp.sin(angles)], axis=1)

def label_table(label_ids):
    return (label_ids[:, None] == jnp.arange(CLASSES + 1, dtype=jnp.int32)[None, :]).astype(jnp.float32)

def split_stem(stem_all):
    end_patch = PATCH_DIM
    end_time = end_patch + FREQ
    end_second = end_time + D
    end_table = end_second + CLASSES + 1
    end_ada = end_table + 2 * D
    return (stem_all[:end_patch], stem_all[end_patch:end_time], stem_all[end_time:end_second], stem_all[end_second:end_table], stem_all[end_table:end_ada], stem_all[end_ada:])

def attend_item(operands):
    queries, keys_in, values_in = operands
    scores = low_back(jnp.einsum('qhd,khd->hqk', queries, keys_in, precision=highest) * (D // HEADS) ** (-0.5))
    attn_probs = low(jax.nn.softmax(scores, axis=-1))
    return jnp.einsum('hqk,khd->qhd', attn_probs, values_in, precision=highest)

def expert_apply(operands):
    rows_e, weights_e = operands
    inner_pre = low_back(jnp.dot(rows_e, weights_e[0], precision=highest))
    active = low(jax.nn.gelu(inner_pre, approximate=True))
    return low(low_back(jnp.dot(active, weights_e[1].T, precision=highest)))

def routed_part(normed_two, route_ids, gate_vals, expert_set):
    group_cap = N_EXPERT * N_DP * CAP
    flat_ids = route_ids.reshape(-1)
    one_hot_ids = (flat_ids[:, None] == jnp.arange(EXPERTS, dtype=jnp.int32)[None, :]).astype(jnp.int32)
    rank_in = lax.optimization_barrier(jnp.sum((jnp.cumsum(one_hot_ids, axis=0) - one_hot_ids) * one_hot_ids, axis=1))
    slot_index = (flat_ids * group_cap + rank_in).astype(jnp.int32).reshape(-1, 2)
    buffer = jnp.zeros((EXPERTS * group_cap, D), jnp.float32)
    for route_k in range(2):
        buffer = buffer.at[slot_index[:, route_k]].add(low_back(normed_two))
    result = lax.map(jax.checkpoint(expert_apply), (buffer.reshape(EXPERTS, group_cap, D), expert_set))
    result = result.reshape(EXPERTS * group_cap, D)
    total_out = gate_vals[:, 0:1] * result[slot_index[:, 0]]
    return total_out + gate_vals[:, 1:2] * result[slot_index[:, 1]]

def layer_apply(tokens, cond_act, lin, lout, expert_set, route_ids, gate_vals):
    item_count = cond_act.shape[0]
    mods = jnp.dot(cond_act, lin[:, 4 * D:10 * D], precision=highest).reshape(item_count, 6, 1, D)
    shaped = tokens.reshape(item_count, PATCHES, D)
    normed = low(norm_mod(shaped, mods[:, 0], mods[:, 1]).reshape(-1, D))
    qkv = low(low_back(jnp.dot(normed, lin[:, :3 * D], precision=highest)))
    qkv = qkv.reshape(item_count, PATCHES, 3, HEADS, D // HEADS)
    attended = lax.map(jax.checkpoint(attend_item), (qkv[:, :, 0], qkv[:, :, 1], qkv[:, :, 2]))
    attended = low(low_back(attended.reshape(-1, D)))
    branch = low_back(jnp.dot(attended, lin[:, 3 * D:4 * D], precision=highest))
    middle = shaped + mods[:, 2] * branch.reshape(item_count, PATCHES, D)
    normed_two = low(norm_mod(middle, mods[:, 3], mods[:, 4]).reshape(-1, D))
    inner_pre = low_back(jnp.dot(normed_two, lin[:, 10 * D:], precision=highest))
    active = low(jax.nn.gelu(inner_pre, approximate=True))
    shared = low_back(jnp.dot(active, lout, precision=highest))
    mixed_out = shared + routed_part(normed_two, route_ids, gate_vals, expert_set)
    return (middle + mods[:, 5] * mixed_out.reshape(item_count, PATCHES, D)).reshape(-1, D)

def group_loss(stem_weights, layer_in, layer_out, experts, patches, target_noise, timesteps, labels, routes, route_gates):
    stem_weights = low(stem_weights)
    layer_in = low(layer_in)
    layer_out = low(layer_out)
    experts = low(experts)
    patch_w, time_one, time_two, table_w, final_ada, final_out = split_stem(stem_weights)
    hidden_time = jax.nn.silu(jnp.dot(time_features(timesteps), time_one, precision=highest))
    cond_act = jax.nn.silu(jnp.dot(hidden_time, time_two, precision=highest) + jnp.dot(label_table(labels), table_w, precision=highest))
    item_count = timesteps.shape[0]
    tokens = low_back(jnp.dot(patches, patch_w, precision=highest))
    tokens = (tokens.reshape(item_count, PATCHES, D) + positions_table()[None]).reshape(-1, D)
    for layer_idx in range(LAYERS):
        tokens = layer_apply(tokens, cond_act, layer_in[layer_idx], layer_out[layer_idx], experts[layer_idx], routes[layer_idx], route_gates[layer_idx])
    final_mods = jnp.dot(cond_act, final_ada.T, precision=highest).reshape(item_count, 2, 1, D)
    final_normed = low(norm_mod(tokens.reshape(item_count, PATCHES, D), final_mods[:, 0], final_mods[:, 1]).reshape(-1, D))
    predicted = low_back(jnp.dot(final_normed, final_out.T, precision=highest))
    residual_err = predicted - target_noise
    return jnp.sum(residual_err * residual_err)

def adam_step(weight_in, gradient, first_in, second_in):
    first_new = beta_one * first_in + (1.0 - beta_one) * gradient
    second_new = beta_two * second_in + (1.0 - beta_two) * gradient * gradient
    first_hat = first_new / (1.0 - beta_one ** STEP)
    second_hat = second_new / (1.0 - beta_two ** STEP)
    stepped = weight_in - inner_rate * (first_hat / (jnp.sqrt(second_hat) + eps_adam) + weight_decay * weight_in)
    return (weight_in - stepped, first_new, second_new)

def reference(patches, target_noise, timesteps, labels, routes, route_gates, stem_weights, layer_in, layer_out, experts, stem_first, layer_in_first, layer_out_first, experts_first, stem_second, layer_in_second, layer_out_second, experts_second, stem_moment, layer_in_moment, layer_out_moment, experts_moment):
    weights_all = (stem_weights, layer_in, layer_out, experts)
    firsts = (stem_first, layer_in_first, layer_out_first, experts_first)
    seconds = (stem_second, layer_in_second, layer_out_second, experts_second)
    moments = (stem_moment, layer_in_moment, layer_out_moment, experts_moment)
    group_tokens = TOKENS // N_GROUP
    group_items = group_tokens // PATCHES
    patches_f = patches.astype(jnp.float32)
    loss_total = jnp.zeros((), jnp.float32)
    delta_sum = [jnp.zeros_like(weight_in) for weight_in in weights_all]
    first_lists = [[], [], [], []]
    second_lists = [[], [], [], []]
    for group_idx in range(N_GROUP):
        tok_lo = group_idx * group_tokens
        item_lo = group_idx * group_items
        group_data = (patches_f[tok_lo:tok_lo + group_tokens], target_noise[tok_lo:tok_lo + group_tokens], timesteps[item_lo:item_lo + group_items], labels[item_lo:item_lo + group_items], routes[:, tok_lo:tok_lo + group_tokens], route_gates[:, tok_lo:tok_lo + group_tokens])

        def loss_of(stem_arg, lin_arg, lout_arg, expert_arg):
            return group_loss(stem_arg, lin_arg, lout_arg, expert_arg, *group_data)
        loss_value, pullback = jax.vjp(loss_of, *weights_all)
        gradients = pullback(jnp.ones((), jnp.float32))
        loss_total = loss_total + loss_value
        for array_idx in range(4):
            delta, first_new, second_new = adam_step(weights_all[array_idx], gradients[array_idx], firsts[array_idx][group_idx], seconds[array_idx][group_idx])
            delta_sum[array_idx] = delta_sum[array_idx] + delta
            first_lists[array_idx].append(first_new)
            second_lists[array_idx].append(second_new)
    new_weights = []
    new_moments = []
    for array_idx in range(4):
        mean_delta = delta_sum[array_idx] / N_GROUP
        moment_new = outer_mom * moments[array_idx] + mean_delta
        new_weights.append(weights_all[array_idx] - outer_rate * (mean_delta + outer_mom * moment_new))
        new_moments.append(moment_new)
    half_copies = [weight_new.astype(jnp.bfloat16) for weight_new in new_weights]
    first_out = [jnp.stack(entry) for entry in first_lists]
    second_out = [jnp.stack(entry) for entry in second_lists]
    return (loss_total, new_weights[0], new_weights[1], new_weights[2], new_weights[3], half_copies[0], half_copies[1], half_copies[2], half_copies[3], first_out[0], first_out[1], first_out[2], first_out[3], second_out[0], second_out[1], second_out[2], second_out[3], new_moments[0], new_moments[1], new_moments[2], new_moments[3])
```

```python
import functools

import jax
import jax.numpy as jnp
from jax import lax
from jax.experimental import pallas as pl
from jax.experimental.pallas import tpu as pltpu
from jax.sharding import PartitionSpec as P

D = 384
HEADS = 6
IMG = 32
FREQ = 256
CLASSES = 1000
LAYERS = 2
STEP = 10
PATCH_DIM = 16
PATCHES = 256


highest = lax.Precision.HIGHEST
beta_one = 0.9
beta_two = 0.95
eps_adam = 1e-08
inner_rate = 0.03
weight_decay = 0.05
outer_rate = 0.7
outer_mom = 0.9
ln_eps = 1e-06


def to_half(values):
    return values.astype(jnp.bfloat16)


def product(left_in, right_in):
    return jnp.dot(left_in, right_in, preferred_element_type=jnp.float32)


def product_tn(left_in, right_in):
    return lax.dot_general(
        left_in, right_in, (((0,), (0,)), ((), ())), preferred_element_type=jnp.float32
    )


def product_nt(left_in, right_in):
    return lax.dot_general(
        left_in, right_in, (((1,), (1,)), ((), ())), preferred_element_type=jnp.float32
    )


def gelu_tanh(values):
    return jax.nn.gelu(values, approximate=True)


def gelu_back(values, gradient):
    _, pull = jax.vjp(gelu_tanh, values)
    return pull(gradient)[0]


def norm_mod(values, shift_in, scale_in):
    centre = values - jnp.mean(values, axis=-1, keepdims=True)
    spread = jnp.mean(centre * centre, axis=-1, keepdims=True)
    return centre * lax.rsqrt(spread + ln_eps) * (1.0 + scale_in) + shift_in


def positions_table():
    grid_side = IMG // 2
    quarter = D // 4
    omegas = 1.0 / 10000.0 ** (jnp.arange(quarter, dtype=jnp.float32) / quarter)
    index_all = jnp.arange(PATCHES, dtype=jnp.int32)
    row_angle = (index_all // grid_side).astype(jnp.float32)[:, None] * omegas[None, :]
    col_angle = (index_all % grid_side).astype(jnp.float32)[:, None] * omegas[None, :]
    return jnp.concatenate(
        [jnp.sin(row_angle), jnp.cos(row_angle), jnp.sin(col_angle), jnp.cos(col_angle)], axis=1
    )


def time_features(step_ids):
    half_freq = FREQ // 2
    frequency = jnp.exp(-jnp.log(10000.0) * jnp.arange(half_freq, dtype=jnp.float32) / half_freq)
    angles = step_ids.astype(jnp.float32)[:, None] * frequency[None, :]
    return jnp.concatenate([jnp.cos(angles), jnp.sin(angles)], axis=1)


def label_table(label_ids):
    return (label_ids[:, None] == jnp.arange(CLASSES + 1, dtype=jnp.int32)[None, :]).astype(
        jnp.float32
    )


def split_stem(stem_all):
    end_patch = PATCH_DIM
    end_time = end_patch + FREQ
    end_second = end_time + D
    end_table = end_second + CLASSES + 1
    end_ada = end_table + 2 * D
    return (
        stem_all[:end_patch],
        stem_all[end_patch:end_time],
        stem_all[end_time:end_second],
        stem_all[end_second:end_table],
        stem_all[end_table:end_ada],
        stem_all[end_ada:],
    )


def slot_places(route_ids, expert_count, capacity):
    flat_ids = route_ids.reshape(-1)
    one_hot_ids = (flat_ids[:, None] == jnp.arange(expert_count, dtype=jnp.int32)[None, :]).astype(
        jnp.int32
    )
    rank_in = jnp.sum((jnp.cumsum(one_hot_ids, axis=0) - one_hot_ids) * one_hot_ids, axis=1)
    return flat_ids * capacity + rank_in


def expert_major(received, local_count):
    sources = received.shape[0] // local_count
    shaped = received.reshape(sources, local_count, received.shape[1], received.shape[2])
    return jnp.swapaxes(shaped, 0, 1).reshape(local_count, -1, received.shape[2])


def source_major(rows_in, sources):
    local_count = rows_in.shape[0]
    shaped = rows_in.reshape(local_count, sources, -1, rows_in.shape[2])
    return jnp.swapaxes(shaped, 0, 1).reshape(sources * local_count, -1, rows_in.shape[2])


def attention_split(qkv, item_count):
    head_dim = qkv.shape[1] // (3 * HEADS)
    shaped = qkv.reshape(item_count, -1, 3, HEADS, head_dim)
    return (shaped[:, :, 0], shaped[:, :, 1], shaped[:, :, 2], head_dim ** (-0.5))


def attention_forward(qkv, item_count):
    queries, keys_in, values_in, scale_att = attention_split(qkv, item_count)
    scores = (
        jnp.einsum("bqhd,bkhd->bhqk", queries, keys_in, preferred_element_type=jnp.float32)
        * scale_att
    )
    row_max = jnp.max(scores, axis=-1, keepdims=True)
    log_sums = row_max + jnp.log(jnp.sum(jnp.exp(scores - row_max), axis=-1, keepdims=True))
    attn_probs = to_half(jnp.exp(scores - log_sums))
    attended = jnp.einsum(
        "bhqk,bkhd->bqhd", attn_probs, values_in, preferred_element_type=jnp.float32
    )
    return (to_half(attended.reshape(qkv.shape[0], -1)), log_sums)


def attention_backward(qkv, log_sums, grad_attended, item_count):
    queries, keys_in, values_in, scale_att = attention_split(qkv, item_count)
    scores = (
        jnp.einsum("bqhd,bkhd->bhqk", queries, keys_in, preferred_element_type=jnp.float32)
        * scale_att
    )
    probs_full = jnp.exp(scores - log_sums)
    grad_out = grad_attended.reshape(queries.shape)
    grad_values = jnp.einsum(
        "bhqk,bqhd->bkhd", to_half(probs_full), grad_out, preferred_element_type=jnp.float32
    )
    grad_probs = jnp.einsum(
        "bqhd,bkhd->bhqk", grad_out, values_in, preferred_element_type=jnp.float32
    )
    grad_scores = probs_full * (
        grad_probs - jnp.sum(probs_full * grad_probs, axis=-1, keepdims=True)
    )
    grad_half = to_half(grad_scores)
    grad_queries = (
        jnp.einsum("bhqk,bkhd->bqhd", grad_half, keys_in, preferred_element_type=jnp.float32)
        * scale_att
    )
    grad_keys = (
        jnp.einsum("bhqk,bqhd->bkhd", grad_half, queries, preferred_element_type=jnp.float32)
        * scale_att
    )
    stacked = jnp.stack([grad_queries, grad_keys, grad_values], axis=2)
    return to_half(stacked.reshape(qkv.shape[0], -1))


def layer_forward(tokens, cond_act, lin, lout, expert_w, route_ids, gate_vals):
    item_count = cond_act.shape[0]
    model_width = tokens.shape[1]
    local_count = expert_w.shape[0]
    expert_count = lax.axis_size("expert") * local_count
    capacity = 4 * tokens.shape[0] // expert_count
    mods = jnp.dot(
        cond_act, lin[:, 4 * model_width : 10 * model_width].astype(jnp.float32), precision=highest
    )
    mods = mods.reshape(item_count, 6, 1, model_width)
    shaped = tokens.reshape(item_count, -1, model_width)
    normed = to_half(norm_mod(shaped, mods[:, 0], mods[:, 1]).reshape(-1, model_width))
    qkv = to_half(product(normed, lin[:, : 3 * model_width]))
    attended, log_sums = attention_forward(qkv, item_count)
    branch = product(attended, lin[:, 3 * model_width : 4 * model_width])
    middle = shaped + mods[:, 2] * branch.reshape(item_count, -1, model_width)
    normed_two = to_half(norm_mod(middle, mods[:, 3], mods[:, 4]).reshape(-1, model_width))
    inner_pre = product(normed_two, lin[:, 10 * model_width :])
    active = to_half(gelu_tanh(inner_pre))
    shared = product(active, lout)
    slot_index = slot_places(route_ids, expert_count, capacity)
    send_rows = jnp.zeros((expert_count * capacity, model_width), jnp.bfloat16)
    send_rows = send_rows.at[slot_index].set(jnp.repeat(normed_two, 2, axis=0))
    received = lax.all_to_all(
        send_rows.reshape(expert_count, capacity, model_width),
        "expert",
        split_axis=0,
        concat_axis=0,
        tiled=True,
    )
    rows_exp = expert_major(received, local_count)
    inner_exp = jnp.einsum(
        "erd,edf->erf", rows_exp, expert_w[:, 0], preferred_element_type=jnp.float32
    )
    active_exp = to_half(gelu_tanh(inner_exp))
    out_exp = to_half(
        jnp.einsum("erf,edf->erd", active_exp, expert_w[:, 1], preferred_element_type=jnp.float32)
    )
    returned = lax.all_to_all(
        source_major(out_exp, lax.axis_size("expert")),
        "expert",
        split_axis=0,
        concat_axis=0,
        tiled=True,
    )
    picked = (
        returned.reshape(-1, model_width)[slot_index]
        .astype(jnp.float32)
        .reshape(-1, 2, model_width)
    )
    mixed_out = shared + jnp.sum(gate_vals[:, :, None] * picked, axis=1)
    result = middle + mods[:, 5] * mixed_out.reshape(item_count, -1, model_width)
    saved = (
        tokens,
        mods,
        normed,
        qkv,
        attended,
        log_sums,
        branch,
        middle,
        normed_two,
        inner_pre,
        active,
        mixed_out,
        slot_index,
        rows_exp,
        inner_exp,
        active_exp,
    )
    return (result.reshape(-1, model_width), saved)


def layer_backward(grad_tokens, saved, cond_act, lin, lout, expert_w, gate_vals):
    (
        tokens,
        mods,
        normed,
        qkv,
        attended,
        log_sums,
        branch,
        middle,
        normed_two,
        inner_pre,
        active,
        mixed_out,
        slot_index,
        rows_exp,
        inner_exp,
        active_exp,
    ) = saved
    item_count = cond_act.shape[0]
    model_width = tokens.shape[1]
    local_count = expert_w.shape[0]
    expert_count = lax.axis_size("expert") * local_count
    capacity = 4 * tokens.shape[0] // expert_count
    grad_shaped = grad_tokens.reshape(item_count, -1, model_width)
    grad_gate_two = jnp.sum(
        grad_shaped * mixed_out.reshape(item_count, -1, model_width), axis=1, keepdims=True
    )
    grad_mixed = (mods[:, 5] * grad_shaped).reshape(-1, model_width)
    grad_shared = to_half(grad_mixed)
    grad_lout = product_tn(active, grad_shared)
    grad_inner = to_half(gelu_back(inner_pre, product_nt(grad_shared, lout)))
    grad_w_up = product_tn(normed_two, grad_inner)
    grad_normed_two = product_nt(grad_inner, lin[:, 10 * model_width :])
    routed_grad = to_half(gate_vals[:, :, None] * grad_mixed[:, None, :]).reshape(-1, model_width)
    send_grad = (
        jnp.zeros((expert_count * capacity, model_width), jnp.bfloat16)
        .at[slot_index]
        .set(routed_grad)
    )
    received = lax.all_to_all(
        send_grad.reshape(expert_count, capacity, model_width),
        "expert",
        split_axis=0,
        concat_axis=0,
        tiled=True,
    )
    grad_rows = expert_major(received, local_count)
    grad_down_exp = jnp.einsum(
        "erd,erf->edf", grad_rows, active_exp, preferred_element_type=jnp.float32
    )
    grad_active_exp = jnp.einsum(
        "erd,edf->erf", grad_rows, expert_w[:, 1], preferred_element_type=jnp.float32
    )
    grad_inner_exp = to_half(gelu_back(inner_exp, grad_active_exp))
    grad_up_exp = jnp.einsum(
        "erd,erf->edf", rows_exp, grad_inner_exp, preferred_element_type=jnp.float32
    )
    grad_rows_in = to_half(
        jnp.einsum(
            "erf,edf->erd", grad_inner_exp, expert_w[:, 0], preferred_element_type=jnp.float32
        )
    )
    back_rows = lax.all_to_all(
        source_major(grad_rows_in, lax.axis_size("expert")),
        "expert",
        split_axis=0,
        concat_axis=0,
        tiled=True,
    )
    picked = (
        back_rows.reshape(-1, model_width)[slot_index]
        .astype(jnp.float32)
        .reshape(-1, 2, model_width)
    )
    grad_normed_two = grad_normed_two + jnp.sum(picked, axis=1)
    _, second_back = jax.vjp(norm_mod, middle, mods[:, 3], mods[:, 4])
    grad_middle, grad_shift_two, grad_scale_two = second_back(
        grad_normed_two.reshape(item_count, -1, model_width)
    )
    grad_middle = grad_middle + grad_shaped
    grad_gate_one = jnp.sum(
        grad_middle * branch.reshape(item_count, -1, model_width), axis=1, keepdims=True
    )
    grad_branch = to_half((mods[:, 2] * grad_middle).reshape(-1, model_width))
    grad_w_out = product_tn(attended, grad_branch)
    grad_attended = to_half(product_nt(grad_branch, lin[:, 3 * model_width : 4 * model_width]))
    grad_qkv = attention_backward(qkv, log_sums, grad_attended, item_count)
    grad_w_qkv = product_tn(normed, grad_qkv)
    grad_normed = product_nt(grad_qkv, lin[:, : 3 * model_width])
    _, first_back = jax.vjp(
        norm_mod, tokens.reshape(item_count, -1, model_width), mods[:, 0], mods[:, 1]
    )
    grad_input, grad_shift_one, grad_scale_one = first_back(
        grad_normed.reshape(item_count, -1, model_width)
    )
    grad_input = grad_input + grad_middle
    grad_mods = jnp.stack(
        [
            grad_shift_one,
            grad_scale_one,
            grad_gate_one,
            grad_shift_two,
            grad_scale_two,
            grad_gate_two,
        ],
        axis=1,
    )
    grad_mods = grad_mods.reshape(item_count, 6 * model_width)
    grad_ada = jnp.dot(cond_act.T, grad_mods, precision=highest)
    grad_cond = jnp.dot(
        grad_mods,
        lin[:, 4 * model_width : 10 * model_width].astype(jnp.float32).T,
        precision=highest,
    )
    grad_lin = jnp.concatenate([grad_w_qkv, grad_w_out, grad_ada, grad_w_up], axis=1)
    grad_expert = jnp.stack([grad_up_exp, grad_down_exp], axis=1)
    return (grad_input.reshape(-1, model_width), grad_cond, grad_lin, grad_lout, grad_expert)


def adam_step(weight_in, gradient, first_in, second_in):
    first_new = beta_one * first_in + (1.0 - beta_one) * gradient
    second_new = beta_two * second_in + (1.0 - beta_two) * gradient * gradient
    first_hat = first_new / (1.0 - beta_one**STEP)
    second_hat = second_new / (1.0 - beta_two**STEP)
    stepped = weight_in - inner_rate * (
        first_hat / (jnp.sqrt(second_hat) + eps_adam) + weight_decay * weight_in
    )
    return (weight_in - stepped, first_new, second_new)


def per_device(
    patches,
    target_noise,
    timesteps,
    labels,
    routes,
    route_gates,
    stem_weights,
    layer_in,
    layer_out,
    experts,
    stem_first,
    layer_in_first,
    layer_out_first,
    experts_first,
    stem_second,
    layer_in_second,
    layer_out_second,
    experts_second,
    stem_moment,
    layer_in_moment,
    layer_out_moment,
    experts_moment,
):
    stem_all, lin_all, lout_all = (
        lax.all_gather(to_half(stem_weights), ("expert", "dp"), axis=1, tiled=True),
        lax.all_gather(to_half(layer_in), ("expert", "dp"), axis=2, tiled=True),
        lax.all_gather(to_half(layer_out), ("expert", "dp"), axis=1, tiled=True),
    )
    expert_all = lax.all_gather(to_half(experts), "dp", axis=4, tiled=True)
    model_width = stem_all.shape[1]
    item_count = timesteps.shape[0]
    patch_w, time_one, time_two, table_w, final_ada, final_out = split_stem(stem_all)
    features = time_features(timesteps)
    hot_labels = label_table(labels)

    def condition(first_w, second_w, table_in):
        hidden_time = jax.nn.silu(jnp.dot(features, first_w, precision=highest))
        return jax.nn.silu(
            jnp.dot(hidden_time, second_w, precision=highest)
            + jnp.dot(hot_labels, table_in, precision=highest)
        )

    cond_act, cond_back = jax.vjp(
        condition,
        time_one.astype(jnp.float32),
        time_two.astype(jnp.float32),
        table_w.astype(jnp.float32),
    )
    tokens = product(patches, patch_w)
    tokens = (tokens.reshape(item_count, -1, model_width) + positions_table()[None]).reshape(
        -1, model_width
    )
    saved_all = []
    for layer_idx in range(LAYERS):
        tokens, saved = layer_forward(
            tokens,
            cond_act,
            lin_all[layer_idx],
            lout_all[layer_idx],
            expert_all[layer_idx],
            routes[layer_idx],
            route_gates[layer_idx],
        )
        saved_all.append(saved)
    final_ada_f = final_ada.astype(jnp.float32)
    final_mods = jnp.dot(cond_act, final_ada_f.T, precision=highest).reshape(
        item_count, 2, 1, model_width
    )
    final_pre, final_back = jax.vjp(
        norm_mod, tokens.reshape(item_count, -1, model_width), final_mods[:, 0], final_mods[:, 1]
    )
    final_normed = to_half(final_pre.reshape(-1, model_width))
    predicted = product_nt(final_normed, final_out)
    residual_err = predicted - target_noise
    loss_total = lax.psum(jnp.sum(residual_err * residual_err), ("group", "expert", "dp"))
    grad_pred = to_half(2.0 * residual_err)
    grad_final_out = product_tn(grad_pred, final_normed)
    grad_final_normed = product(grad_pred, final_out)
    grad_tokens, grad_fshift, grad_fscale = final_back(
        grad_final_normed.reshape(item_count, -1, model_width)
    )
    grad_tokens = grad_tokens.reshape(-1, model_width)
    grad_final_mods = jnp.concatenate([grad_fshift, grad_fscale], axis=1).reshape(
        item_count, 2 * model_width
    )
    grad_final_ada = jnp.dot(grad_final_mods.T, cond_act, precision=highest)
    grad_cond = jnp.dot(grad_final_mods, final_ada_f, precision=highest)
    lin_grads = []
    lout_grads = []
    expert_grads = []
    for layer_idx in reversed(range(LAYERS)):
        grad_tokens, grad_cond_layer, grad_lin, grad_lout, grad_expert = layer_backward(
            grad_tokens,
            saved_all[layer_idx],
            cond_act,
            lin_all[layer_idx],
            lout_all[layer_idx],
            expert_all[layer_idx],
            route_gates[layer_idx],
        )
        grad_cond = grad_cond + grad_cond_layer
        lin_grads.append(grad_lin)
        lout_grads.append(grad_lout)
        expert_grads.append(grad_expert)
    lin_stack = jnp.stack(lin_grads[::-1])
    lout_stack = jnp.stack(lout_grads[::-1])
    expert_stack = jnp.stack(expert_grads[::-1])
    grad_patch = product_tn(patches, to_half(grad_tokens))
    grad_time_one, grad_time_two, grad_table = cond_back(grad_cond)
    grad_stem = jnp.concatenate(
        [grad_patch, grad_time_one, grad_time_two, grad_table, grad_final_ada, grad_final_out],
        axis=0,
    )
    stem_sum, lin_sum, lout_sum = (
        lax.psum_scatter(grad_stem, ("expert", "dp"), scatter_dimension=1, tiled=True),
        lax.psum_scatter(lin_stack, ("expert", "dp"), scatter_dimension=2, tiled=True),
        lax.psum_scatter(lout_stack, ("expert", "dp"), scatter_dimension=1, tiled=True),
    )
    expert_sum = lax.psum_scatter(
        expert_stack.astype(jnp.bfloat16), "dp", scatter_dimension=4, tiled=True
    ).astype(jnp.float32)
    weights_all = (stem_weights, layer_in, layer_out, experts)
    gradients = (stem_sum, lin_sum, lout_sum, expert_sum)
    firsts = (stem_first, layer_in_first, layer_out_first, experts_first)
    seconds = (stem_second, layer_in_second, layer_out_second, experts_second)
    moments = (stem_moment, layer_in_moment, layer_out_moment, experts_moment)
    stepped = [
        adam_step(
            weights_all[array_idx],
            gradients[array_idx],
            firsts[array_idx][0],
            seconds[array_idx][0],
        )
        for array_idx in range(4)
    ]
    delta_all = (
        lax.psum(stepped[0][0].astype(jnp.bfloat16), "group").astype(jnp.float32),
        lax.psum(stepped[1][0].astype(jnp.bfloat16), "group").astype(jnp.float32),
        lax.psum(stepped[2][0].astype(jnp.bfloat16), "group").astype(jnp.float32),
        lax.psum(stepped[3][0].astype(jnp.bfloat16), "group").astype(jnp.float32),
    )
    group_count = lax.axis_size("group")
    new_weights = []
    new_moments = []
    for array_idx in range(4):
        mean_delta = delta_all[array_idx] / group_count
        moment_new = outer_mom * moments[array_idx] + mean_delta
        new_weights.append(
            weights_all[array_idx] - outer_rate * (mean_delta + outer_mom * moment_new)
        )
        new_moments.append(moment_new)
    return (
        loss_total,
        new_weights[0],
        new_weights[1],
        new_weights[2],
        new_weights[3],
        to_half(new_weights[0]),
        to_half(new_weights[1]),
        to_half(new_weights[2]),
        to_half(new_weights[3]),
        stepped[0][1][None],
        stepped[1][1][None],
        stepped[2][1][None],
        stepped[3][1][None],
        stepped[0][2][None],
        stepped[1][2][None],
        stepped[2][2][None],
        stepped[3][2][None],
        new_moments[0],
        new_moments[1],
        new_moments[2],
        new_moments[3],
    )


bf16 = jnp.bfloat16
f32 = jnp.float32
MIB = 1024 * 1024
CHUNK = 768
STEM_SIZES = (PATCH_DIM, FREQ, D, CLASSES + 1, 2 * D, PATCH_DIM)
STEM_PADDED = tuple(-(-size // 128) * 128 for size in STEM_SIZES)
STEM_AT = tuple(sum(STEM_PADDED[:place]) for place in range(len(STEM_PADDED)))
STEM_LANES = sum(STEM_PADDED)


def dot_nn(left_in, right_in):
    return lax.dot_general(left_in, right_in, (((1,), (0,)), ((), ())), preferred_element_type=f32)


def dot_nt(left_in, right_in):
    return lax.dot_general(left_in, right_in, (((1,), (1,)), ((), ())), preferred_element_type=f32)


def dot_tn(left_in, right_in):
    return lax.dot_general(left_in, right_in, (((0,), (0,)), ((), ())), preferred_element_type=f32)


def three_parts(rows):
    high = rows.astype(bf16).astype(f32)
    rest = rows - high
    mid = rest.astype(bf16).astype(f32)
    low = rest - mid
    return jnp.concatenate([high, mid, low, jnp.zeros_like(low)], axis=0).astype(bf16)


def three_sum(stacked):
    return stacked[0:8] + stacked[8:16] + stacked[16:24]


def full_nt(rows, weight):
    return three_sum(dot_nt(three_parts(rows), weight))


def full_nn(rows, weight):
    return three_sum(dot_nn(three_parts(rows), weight))


def silu_slope(values):
    gate = 1.0 / (1.0 + jnp.exp(-values))
    return gate * (1.0 + values * (1.0 - gate))


def silu_of(values):
    return values / (1.0 + jnp.exp(-values))


def stem_piece(stem_ref, place):
    return stem_ref[:, STEM_AT[place] : STEM_AT[place] + STEM_PADDED[place]]


def cond_kernel(feat_ref, hot_ref, stem_ref, ada_a, ada_b, cond_ref, hid_ref, one_ref, two_ref, mods_ref, fin_ref):
    pre_one = full_nt(feat_ref[...], stem_piece(stem_ref, 1))
    hidden = silu_of(pre_one)
    pre_two = full_nt(hidden, stem_piece(stem_ref, 2)) + dot_nt(hot_ref[...], stem_piece(stem_ref, 3))[0:8]
    cond = silu_of(pre_two)
    one_ref[...] = pre_one
    two_ref[...] = pre_two
    hid_ref[...] = hidden
    cond_ref[...] = cond
    parts = three_parts(cond)
    for place in range(6):
        rows = pl.ds(place * D, D)
        mods_ref[0, :, rows] = three_sum(dot_nt(parts, ada_a[rows, :]))
        mods_ref[1, :, rows] = three_sum(dot_nt(parts, ada_b[rows, :]))
    fin_ref[...] = three_sum(dot_nn(parts, stem_piece(stem_ref, 4)))


def cond_back_kernel(gm_a, gm_b, gf_ref, one_ref, two_ref, stem_ref, ada_a, ada_b, done_ref, dtwo_ref):
    grad_cond = full_nt(gf_ref[...], stem_piece(stem_ref, 4))
    grad_cond = grad_cond + full_nn(gm_a[...], ada_a[...]) + full_nn(gm_b[...], ada_b[...])
    dtwo = grad_cond * silu_slope(two_ref[...])
    dtwo_ref[...] = dtwo
    dhid = full_nn(dtwo, stem_piece(stem_ref, 2))
    done_ref[...] = dhid * silu_slope(one_ref[...])


def norm_parts(values):
    centre = values - jnp.mean(values, axis=-1, keepdims=True)
    spread = jnp.mean(centre * centre, axis=-1, keepdims=True)
    root = lax.rsqrt(spread + ln_eps)
    return centre * root, root


def norm_back(values, scale_in, gradient):
    unit, root = norm_parts(values)
    grad_unit = gradient * (1.0 + scale_in)
    inner = jnp.mean(grad_unit * unit, axis=-1, keepdims=True)
    grad_in = root * (grad_unit - jnp.mean(grad_unit, axis=-1, keepdims=True) - unit * inner)
    return (
        grad_in,
        jnp.sum(gradient, axis=0, keepdims=True),
        jnp.sum(gradient * unit, axis=0, keepdims=True),
    )


def mod_row(mods_ref, item, place):
    return mods_ref[pl.ds(item, 1), place * D : (place + 1) * D]


def head_masks():
    lane = lax.broadcasted_iota(jnp.int32, (1, 128), 1)
    return lane, [(lane // 64 == half).astype(f32).astype(bf16) for half in range(2)]


def attn_fwd_kernel(x_ref, mods_ref, w_ref, normed_ref, qkv_ref, att_ref, branch_ref, mid_ref, n2_ref):
    item = pl.program_id(0)
    tokens = x_ref[...]
    unit, _ = norm_parts(tokens)
    normed = (unit * (1.0 + mod_row(mods_ref, item, 1)) + mod_row(mods_ref, item, 0)).astype(bf16)
    normed_ref[...] = normed
    qkv_ref[...] = dot_nt(normed, w_ref[0 : 3 * D, :]).astype(bf16)
    lane, masks = head_masks()
    for pair in range(HEADS // 2):
        at = pair * 128
        queries = qkv_ref[:, at : at + 128]
        keys = qkv_ref[:, D + at : D + at + 128]
        vals = qkv_ref[:, 2 * D + at : 2 * D + at + 128]
        outs = []
        for half in range(2):
            scores = dot_nt(queries * masks[half], keys) * 0.125
            powers = jnp.exp(scores - jnp.max(scores, axis=-1, keepdims=True))
            probs = (powers * (1.0 / jnp.sum(powers, axis=-1, keepdims=True))).astype(bf16)
            outs.append(dot_nn(probs, vals))
        att_ref[:, at : at + 128] = jnp.where(lane < 64, outs[0], outs[1]).astype(bf16)
    branch = dot_nt(att_ref[...], w_ref[3 * D : 4 * D, :])
    branch_ref[...] = branch
    middle = tokens + mod_row(mods_ref, item, 2) * branch
    mid_ref[...] = middle
    unit, _ = norm_parts(middle)
    n2_ref[...] = (unit * (1.0 + mod_row(mods_ref, item, 4)) + mod_row(mods_ref, item, 3)).astype(bf16)


def attn_bwd_kernel(
    gn2_ref, g_ref, mid_ref, x_ref, normed_ref, qkv_ref, att_ref, branch_ref, mods_ref, gg_ref, w_ref,
    gx_ref, gmods_ref, dw_ref, dqkv, acc,
):
    item = pl.program_id(0)

    @pl.when(item == 0)
    def _():
        acc[...] = jnp.zeros_like(acc)
        gmods_ref[...] = jnp.zeros_like(gmods_ref)

    grad_mid, dshift, dscale = norm_back(mid_ref[...], mod_row(mods_ref, item, 4), gn2_ref[...])
    grad_mid = grad_mid + g_ref[...]
    dgate = jnp.sum(grad_mid * branch_ref[...], axis=0, keepdims=True)
    gmods_ref[pl.ds(item, 1), 2 * D : 3 * D] = dgate
    gmods_ref[pl.ds(item, 1), 3 * D : 4 * D] = dshift
    gmods_ref[pl.ds(item, 1), 4 * D : 5 * D] = dscale
    gmods_ref[pl.ds(item, 1), 5 * D : 6 * D] = gg_ref[pl.ds(item, 1), :]
    grad_branch = (mod_row(mods_ref, item, 2) * grad_mid).astype(bf16)
    acc[3 * D : 4 * D, :] += dot_tn(grad_branch, att_ref[...])
    grad_att = dot_nn(grad_branch, w_ref[3 * D : 4 * D, :]).astype(bf16)
    lane, masks = head_masks()
    for pair in range(HEADS // 2):
        at = pair * 128
        queries = qkv_ref[:, at : at + 128]
        keys = qkv_ref[:, D + at : D + at + 128]
        vals = qkv_ref[:, 2 * D + at : 2 * D + at + 128]
        grad_out = grad_att[:, at : at + 128]
        parts = []
        for half in range(2):
            scores = dot_nt(queries * masks[half], keys) * 0.125
            powers = jnp.exp(scores - jnp.max(scores, axis=-1, keepdims=True))
            probs = powers * (1.0 / jnp.sum(powers, axis=-1, keepdims=True))
            grad_vals = dot_tn(probs.astype(bf16), grad_out)
            grad_probs = dot_nt(grad_out * masks[half], vals)
            inner = jnp.sum(probs * grad_probs, axis=-1, keepdims=True)
            grad_scores = (probs * (grad_probs - inner)).astype(bf16)
            parts.append((dot_nn(grad_scores, keys) * 0.125, dot_tn(grad_scores, queries) * 0.125, grad_vals))
        for place in range(3):
            dqkv[:, place * D + at : place * D + at + 128] = jnp.where(
                lane < 64, parts[0][place], parts[1][place]
            ).astype(bf16)
    acc[0 : 3 * D, :] += dot_tn(dqkv[...], normed_ref[...])
    grad_normed = dot_nn(dqkv[...], w_ref[0 : 3 * D, :])
    grad_in, dshift, dscale = norm_back(x_ref[...], mod_row(mods_ref, item, 1), grad_normed)
    gx_ref[...] = grad_in + grad_mid
    gmods_ref[pl.ds(item, 1), 0:D] = dshift
    gmods_ref[pl.ds(item, 1), D : 2 * D] = dscale

    @pl.when(item == pl.num_programs(0) - 1)
    def _():
        dw_ref[...] = acc[...].astype(bf16)


def gelu_both(values):
    outer = 0.7978845608028654
    cubic = outer * 0.044715
    square = values * values
    angle = jnp.tanh(values * (square * cubic + outer))
    half = 0.5 * values
    active = half * angle + half
    slope = half * (square * (3.0 * cubic) + outer) * (1.0 - angle * angle) + (0.5 * angle + 0.5)
    return active.astype(bf16), slope.astype(bf16)


def gate_column(g4_ref, rows, expert):
    gates = g4_ref[rows, :]
    lane = lax.broadcasted_iota(jnp.int32, gates.shape, 1)
    return jnp.sum(jnp.where(lane == expert, gates, 0.0), axis=1, keepdims=True)


def ffn_fwd_kernel(shared_steps, halves, n2_ref, mid_ref, mods_ref, g4_ref, up_ref, dn_ref, ex_ref, act_ref, dg_ref, mixed_ref, x_ref, acc, racc):
    step = pl.program_id(0)
    items = n2_ref.shape[0] // PATCHES

    @pl.when(step < shared_steps)
    def _():
        for item in range(items):
            rows = pl.ds(item * PATCHES, PATCHES)
            active, slope = gelu_both(dot_nt(n2_ref[rows, :], up_ref[...]))
            act_ref[0, rows, :] = active
            dg_ref[0, rows, :] = slope
            part = dot_nn(active, dn_ref[...])

            @pl.when(step == 0)
            def _():
                acc[rows, :] = part

            @pl.when(step > 0)
            def _():
                acc[rows, :] += part

    @pl.when(step >= shared_steps)
    def _():
        expert, half = (step - shared_steps) // halves, (step - shared_steps) % halves
        for item in range(items):
            rows = pl.ds(item * PATCHES, PATCHES)
            active, slope = gelu_both(dot_nn(n2_ref[rows, :], ex_ref[0, 0]))
            act_ref[0, rows, :] = active
            dg_ref[0, rows, :] = slope
            part = dot_nt(active, ex_ref[0, 1])

            @pl.when(half == 0)
            def _():
                racc[rows, :] = part

            @pl.when(half > 0)
            def _():
                routed = (racc[rows, :] + part).astype(bf16).astype(f32)
                acc[rows, :] += gate_column(g4_ref, rows, expert) * routed

    @pl.when(step == pl.num_programs(0) - 1)
    def _():
        mixed_ref[...] = acc[...]
        for item in range(items):
            rows = pl.ds(item * PATCHES, PATCHES)
            x_ref[rows, :] = mid_ref[rows, :] + mod_row(mods_ref, item, 5) * acc[rows, :]


def ffn_bwd_kernel(
    shared_steps, halves, g_ref, n2_ref, mods_ref, g4_ref, mixed_ref, act_ref, dg_ref, up_ref, dn_ref, ex_ref,
    dup_ref, ddn_ref, dex_ref, gn2_ref, gg_ref, gmix, gs, gst, n2t, din, acc, racc,
):
    step = pl.program_id(0)
    items = n2_ref.shape[0] // PATCHES

    @pl.when(step == 0)
    def _():
        gg_ref[...] = jnp.zeros_like(gg_ref)
        for item in range(items):
            rows = pl.ds(item * PATCHES, PATCHES)
            grad = g_ref[rows, :]
            gg_ref[pl.ds(item, 1), :] = jnp.sum(grad * mixed_ref[rows, :], axis=0, keepdims=True)
            grad = mod_row(mods_ref, item, 5) * grad
            gmix[rows, :] = grad
            gs[rows, :] = grad.astype(bf16)
            gst[:, rows] = grad.astype(bf16).T
            n2t[:, rows] = n2_ref[rows, :].T
        acc[...] = jnp.zeros_like(acc)

    @pl.when(step < shared_steps)
    def _():
        for item in range(items):
            rows = pl.ds(item * PATCHES, PATCHES)
            inner = (dot_nt(gs[rows, :], dn_ref[...]) * dg_ref[0, rows, :].astype(f32)).astype(bf16)
            din[rows, :] = inner
            acc[rows, :] += dot_nn(inner, up_ref[...])
        dup_ref[...] = dot_nn(n2t[...], din[...]).astype(bf16).T
        ddn_ref[...] = dot_nn(gst[...], act_ref[0]).astype(bf16).T

    @pl.when(step >= shared_steps)
    def _():
        expert, half = (step - shared_steps) // halves, (step - shared_steps) % halves

        @pl.when(half == 0)
        def _():
            for item in range(items):
                rows = pl.ds(item * PATCHES, PATCHES)
                grad = (gate_column(g4_ref, rows, expert) * gmix[rows, :]).astype(bf16)
                gs[rows, :] = grad
                gst[:, rows] = grad.T

        for item in range(items):
            rows = pl.ds(item * PATCHES, PATCHES)
            inner = (dot_nn(gs[rows, :], ex_ref[0, 1]) * dg_ref[0, rows, :].astype(f32)).astype(bf16)
            din[rows, :] = inner
            part = dot_nt(inner, ex_ref[0, 0])

            @pl.when(half == 0)
            def _():
                racc[rows, :] = part

            @pl.when(half > 0)
            def _():
                acc[rows, :] += (racc[rows, :] + part).astype(bf16).astype(f32)

        dex_ref[0, 0] = dot_nn(n2t[...], din[...]).astype(bf16)
        dex_ref[0, 1] = dot_nn(gst[...], act_ref[0]).astype(bf16)

    @pl.when(step == pl.num_programs(0) - 1)
    def _():
        gn2_ref[...] = acc[...]


def final_kernel(x_ref, mods_ref, fo_ref, tgt_ref, gx_ref, gfm_ref, dfo_ref, loss_ref):
    item = pl.program_id(0)

    @pl.when(item == 0)
    def _():
        gfm_ref[...] = jnp.zeros_like(gfm_ref)
        dfo_ref[...] = jnp.zeros_like(dfo_ref)
        loss_ref[...] = jnp.zeros_like(loss_ref)

    tokens = x_ref[...]
    unit, _ = norm_parts(tokens)
    scale = mod_row(mods_ref, item, 1)
    normed = (unit * (1.0 + scale) + mod_row(mods_ref, item, 0)).astype(bf16)
    err = dot_nt(fo_ref[...], normed) - tgt_ref[...]
    loss_ref[...] += jnp.sum(err * err, axis=1, keepdims=True)
    grad_pred = (2.0 * err).astype(bf16)
    dfo_ref[...] += dot_nn(grad_pred, normed)
    grad_in, dshift, dscale = norm_back(tokens, scale, dot_tn(grad_pred, fo_ref[...]))
    gx_ref[...] = grad_in
    gfm_ref[pl.ds(item, 1), 0:D] = dshift
    gfm_ref[pl.ds(item, 1), D : 2 * D] = dscale


def params(limit):
    return pltpu.CompilerParams(vmem_limit_bytes=limit * MIB)


def whole(shape):
    return pl.BlockSpec(shape, lambda step: (0,) * len(shape))


def rows_of(width):
    return pl.BlockSpec((PATCHES, width), lambda step: (step, 0))


def shape_of(shape, kind):
    return jax.ShapeDtypeStruct(shape, kind)


def cond_forward(feat, hot, stem_t, lin_a, lin_b):
    ada = pl.BlockSpec((6 * D, D), lambda: (0, 0))
    shapes = [(8, D)] * 4 + [(LAYERS, 8, 6 * D), (8, 2 * D)]
    ada_at = [lax.slice_in_dim(lin, 4 * D, 10 * D, axis=0) for lin in (lin_a, lin_b)]
    del ada
    return pl.pallas_call(
        cond_kernel,
        out_shape=[shape_of(shape, f32) for shape in shapes],
        compiler_params=params(40),
        name="cond_forward",
    )(feat, hot, stem_t, *ada_at), ada_at


def cond_backward(gm_a, gm_b, gfm, pre_one, pre_two, stem_t, ada_at):
    return pl.pallas_call(
        cond_back_kernel,
        out_shape=[shape_of((8, D), f32)] * 2,
        compiler_params=params(40),
        name="cond_backward",
    )(gm_a, gm_b, gfm, pre_one, pre_two, stem_t, *ada_at)


def attn_forward(tokens, mods, lin):
    count = tokens.shape[0]
    return pl.pallas_call(
        attn_fwd_kernel,
        grid=(count // PATCHES,),
        in_specs=[rows_of(D), whole(mods.shape), whole((4 * D, D))],
        out_specs=[rows_of(D), rows_of(3 * D), rows_of(D), rows_of(D), rows_of(D), rows_of(D)],
        out_shape=[
            shape_of((count, D), bf16),
            shape_of((count, 3 * D), bf16),
            shape_of((count, D), bf16),
            shape_of((count, D), f32),
            shape_of((count, D), f32),
            shape_of((count, D), bf16),
        ],
        compiler_params=params(40),
        name="attention_forward",
    )(tokens, mods, lin)


def attn_backward(gn2, grad, middle, tokens, normed, qkv, attended, branch, mods, grad_gate, lin):
    count = tokens.shape[0]
    return pl.pallas_call(
        attn_bwd_kernel,
        grid=(count // PATCHES,),
        in_specs=[rows_of(D)] * 5
        + [rows_of(3 * D), rows_of(D), rows_of(D), whole(mods.shape), whole(grad_gate.shape), whole((4 * D, D))],
        out_specs=[rows_of(D), whole((8, 6 * D)), whole((4 * D, D))],
        out_shape=[shape_of((count, D), f32), shape_of((8, 6 * D), f32), shape_of((4 * D, D), bf16)],
        scratch_shapes=[pltpu.VMEM((PATCHES, 3 * D), bf16), pltpu.VMEM((4 * D, D), f32)],
        compiler_params=params(50),
        name="attention_backward",
    )(gn2, grad, middle, tokens, normed, qkv, attended, branch, mods, grad_gate, lin)


def weight_specs(shared_steps, lin_rows):
    up_at = lin_rows // CHUNK - shared_steps
    return [
        pl.BlockSpec((CHUNK, D), lambda step: (up_at + jnp.minimum(step, shared_steps - 1), 0)),
        pl.BlockSpec((CHUNK, D), lambda step: (jnp.minimum(step, shared_steps - 1), 0)),
        pl.BlockSpec((1, 2, D, CHUNK), lambda step: (jnp.maximum(step - shared_steps, 0), 0, 0, 0)),
    ]


def ffn_forward(n2, middle, mods, g4, lin, lout, experts_w, halves):
    count = n2.shape[0]
    shared_steps = lout.shape[0] // CHUNK
    steps = shared_steps + experts_w.shape[0]
    wide = pl.BlockSpec((1, count, CHUNK), lambda step: (step, 0, 0))
    return pl.pallas_call(
        functools.partial(ffn_fwd_kernel, shared_steps, halves),
        grid=(steps,),
        in_specs=[whole(n2.shape), whole(middle.shape), whole(mods.shape), whole(g4.shape)]
        + weight_specs(shared_steps, lin.shape[0]),
        out_specs=[wide, wide, whole((count, D)), whole((count, D))],
        out_shape=[
            shape_of((steps, count, CHUNK), bf16),
            shape_of((steps, count, CHUNK), bf16),
            shape_of((count, D), f32),
            shape_of((count, D), f32),
        ],
        scratch_shapes=[pltpu.VMEM((count, D), f32)] * 2,
        compiler_params=params(56),
        name="ffn_forward",
    )(n2, middle, mods, g4, lin, lout, experts_w)


def ffn_backward(grad, n2, mods, g4, mixed, active, slope, lin, lout, experts_w, halves):
    count = n2.shape[0]
    shared_steps = lout.shape[0] // CHUNK
    steps = shared_steps + experts_w.shape[0]
    wide = pl.BlockSpec((1, count, CHUNK), lambda step: (step, 0, 0))
    specs = weight_specs(shared_steps, lin.shape[0])
    return pl.pallas_call(
        functools.partial(ffn_bwd_kernel, shared_steps, halves),
        grid=(steps,),
        in_specs=[whole(grad.shape), whole(n2.shape), whole(mods.shape), whole(g4.shape), whole(mixed.shape), wide, wide]
        + specs,
        out_specs=[specs[1], specs[1], specs[2], whole((count, D)), whole((8, D))],
        out_shape=[
            shape_of(lout.shape, bf16),
            shape_of(lout.shape, bf16),
            shape_of(experts_w.shape, bf16),
            shape_of((count, D), f32),
            shape_of((8, D), f32),
        ],
        scratch_shapes=[
            pltpu.VMEM((count, D), f32),
            pltpu.VMEM((count, D), bf16),
            pltpu.VMEM((D, count), bf16),
            pltpu.VMEM((D, count), bf16),
            pltpu.VMEM((count, CHUNK), bf16),
            pltpu.VMEM((count, D), f32),
            pltpu.VMEM((count, D), f32),
        ],
        compiler_params=params(60),
        name="ffn_backward",
    )(grad, n2, mods, g4, mixed, active, slope, lin, lout, experts_w)


def final_step(tokens, mods, fo_rows, target_t):
    count = tokens.shape[0]
    return pl.pallas_call(
        final_kernel,
        grid=(count // PATCHES,),
        in_specs=[
            rows_of(D),
            whole(mods.shape),
            whole(fo_rows.shape),
            pl.BlockSpec((PATCH_DIM, PATCHES), lambda step: (0, step)),
        ],
        out_specs=[rows_of(D), whole((8, 2 * D)), whole((PATCH_DIM, D)), whole((PATCH_DIM, 1))],
        out_shape=[
            shape_of((count, D), f32),
            shape_of((8, 2 * D), f32),
            shape_of((PATCH_DIM, D), f32),
            shape_of((PATCH_DIM, 1), f32),
        ],
        compiler_params=params(40),
        name="final_step",
    )(tokens, mods, fo_rows, target_t)


def pad_rows(values):
    return jnp.pad(values, ((0, 8 - values.shape[0]), (0, 0)))


def stem_lanes(stem_t):
    pieces, at = [], 0
    for size, padded in zip(STEM_SIZES, STEM_PADDED):
        pieces.append(jnp.pad(stem_t[:, at : at + size], ((0, 0), (0, padded - size))))
        at = at + size
    return jnp.concatenate(pieces, axis=1)


SHARD = ("expert", "dp")


def few_experts(
    patches,
    target_noise,
    timesteps,
    labels,
    routes,
    route_gates,
    stem_weights,
    layer_in,
    layer_out,
    experts,
    stem_first,
    layer_in_first,
    layer_out_first,
    experts_first,
    stem_second,
    layer_in_second,
    layer_out_second,
    experts_second,
    stem_moment,
    layer_in_moment,
    layer_out_moment,
    experts_moment,
):
    count = patches.shape[0]
    items = timesteps.shape[0]
    halves = lax.axis_size("dp")
    sharers = lax.axis_size("expert") * halves
    expert_count = lax.axis_size("expert") * experts.shape[1]
    place = lax.axis_index("expert") * halves + lax.axis_index("dp")

    stem_t = stem_weights.T
    lin_t = jnp.swapaxes(layer_in, 1, 2)
    stem_all = lax.all_gather(stem_lanes(to_half(stem_t)), SHARD, axis=0, tiled=True)
    lin_all, lout_all, expert_all = [], [], []
    for layer in range(LAYERS):
        lin_all.append(lax.all_gather(to_half(lin_t[layer]), SHARD, axis=0, tiled=True))
        lout_all.append(lax.all_gather(to_half(layer_out[layer]), SHARD, axis=0, tiled=True))
        expert_all.append(lax.all_gather(to_half(experts[layer]), SHARD, axis=0, tiled=True))

    feat = time_features(timesteps)
    hot = label_table(labels)
    hot_pad = jnp.pad(hot, ((0, 32 - items), (0, STEM_PADDED[3] - hot.shape[1]))).astype(bf16)
    (cond, hidden, pre_one, pre_two, mods, fin_mods), ada_at = cond_forward(
        pad_rows(feat), hot_pad, stem_all, lin_all[0], lin_all[1]
    )
    tokens = product_nt(patches, stem_all[:, :PATCH_DIM])
    tokens = (tokens.reshape(items, -1, D) + positions_table()[None]).reshape(-1, D)
    expert_ids = jnp.arange(expert_count, dtype=jnp.int32)
    saved = []
    for layer in range(LAYERS):
        g4 = jnp.sum(
            jnp.where(routes[layer][:, :, None] == expert_ids, route_gates[layer][:, :, None], 0.0), axis=1
        )
        normed, qkv, attended, branch, middle, n2 = attn_forward(tokens, mods[layer], lin_all[layer])
        active, slope, mixed, result = ffn_forward(
            n2, middle, mods[layer], g4, lin_all[layer], lout_all[layer], expert_all[layer], halves
        )
        saved.append((tokens, g4, normed, qkv, attended, branch, middle, n2, active, slope, mixed))
        tokens = result
    fo_rows = stem_all[:, STEM_AT[5] : STEM_AT[5] + PATCH_DIM].T
    grad, grad_fin, grad_out_w, loss_rows = final_step(tokens, fin_mods, fo_rows, target_noise.T)
    loss_total = lax.psum(jnp.sum(loss_rows), ("group", "expert", "dp"))

    grad_mods = [None] * LAYERS
    lin_sum, lout_sum, expert_sum = [None] * LAYERS, [None] * LAYERS, [None] * LAYERS
    for layer in reversed(range(LAYERS)):
        tokens, g4, normed, qkv, attended, branch, middle, n2, active, slope, mixed = saved[layer]
        dup, ddn, dex, gn2, grad_gate = ffn_backward(
            grad, n2, mods[layer], g4, mixed, active, slope, lin_all[layer], lout_all[layer], expert_all[layer], halves
        )
        grad, grad_mods[layer], dqkvo = attn_backward(
            gn2, grad, middle, tokens, normed, qkv, attended, branch, mods[layer], grad_gate, lin_all[layer]
        )
        expert_sum[layer] = lax.psum_scatter(dex, SHARD, scatter_dimension=0, tiled=True)
        lout_sum[layer] = lax.psum_scatter(ddn, SHARD, scatter_dimension=0, tiled=True)
        dlin = jnp.concatenate([dqkvo, jnp.zeros((6 * D, D), bf16), dup], axis=0)
        lin_sum[layer] = lax.psum_scatter(dlin, SHARD, scatter_dimension=0, tiled=True)
    grad_patch = product_tn(patches, to_half(grad))
    dpre_one, dpre_two = cond_backward(grad_mods[0], grad_mods[1], grad_fin, pre_one, pre_two, stem_all, ada_at)

    factors = jnp.concatenate(
        [cond[:items], hidden[:items], dpre_one[:items], dpre_two[:items], grad_fin[:items], grad_mods[0][:items], grad_mods[1][:items], feat],
        axis=1,
    )
    width = factors.shape[1]
    packed = jnp.concatenate([factors.reshape(-1), grad_patch.reshape(-1), grad_out_w.reshape(-1)])
    gathered = lax.all_gather(packed, SHARD, axis=0, tiled=False)
    ends = gathered[:, items * width :].reshape(sharers, 2, PATCH_DIM, D).sum(axis=0)
    factors = gathered[:, : items * width].reshape(sharers * items, width)
    hot_all = label_table(lax.all_gather(labels, SHARD, axis=0, tiled=True))
    cond_f, hidden_f, done_f, dtwo_f, fin_f, gm_a, gm_b, feat_f = jnp.split(
        factors, [D, 2 * D, 3 * D, 4 * D, 6 * D, 12 * D, 18 * D], axis=1
    )
    stem_cols = stem_weights.shape[1]
    lin_cols = layer_in.shape[2]

    def own(values):
        return lax.dynamic_slice_in_dim(values, place * stem_cols, stem_cols, axis=1)

    def outer(left_in, right_in):
        return lax.dot_general(left_in, right_in, (((0,), (0,)), ((), ())), precision=highest)

    stem_grad = jnp.concatenate(
        [
            own(ends[0]).T,
            outer(own(done_f), feat_f),
            outer(own(dtwo_f), hidden_f),
            outer(own(dtwo_f), hot_all),
            outer(own(cond_f), fin_f),
            own(ends[1]).T,
        ],
        axis=1,
    )
    lin_grads = []
    for layer, gm in ((0, gm_a), (1, gm_b)):
        spread = jnp.pad(gm, ((0, 0), (4 * D, lin_cols * sharers - 10 * D)))
        window = lax.dynamic_slice_in_dim(spread, place * lin_cols, lin_cols, axis=1)
        lin_grads.append(lin_sum[layer].astype(f32) + outer(window, cond_f))
    lin_grad = jnp.stack(lin_grads)
    lout_grad = jnp.stack(lout_sum).astype(f32)
    expert_grad = jnp.stack(expert_sum).astype(f32)

    weights_all = (stem_t, lin_t, layer_out, experts)
    gradients = (stem_grad, lin_grad, lout_grad, expert_grad)
    firsts = (stem_first[0].T, jnp.swapaxes(layer_in_first[0], 1, 2), layer_out_first[0], experts_first[0])
    seconds = (stem_second[0].T, jnp.swapaxes(layer_in_second[0], 1, 2), layer_out_second[0], experts_second[0])
    moments = (stem_moment.T, jnp.swapaxes(layer_in_moment, 1, 2), layer_out_moment, experts_moment)
    group_count = lax.axis_size("group")
    new_weights, halves_out, first_out, second_out, new_moments = [], [], [], [], []
    for at in range(4):
        delta, first_new, second_new = adam_step(weights_all[at], gradients[at], firsts[at], seconds[at])
        mean_delta = lax.psum(to_half(delta), "group").astype(f32) / group_count
        moment_new = outer_mom * moments[at] + mean_delta
        new_weight = weights_all[at] - outer_rate * (mean_delta + outer_mom * moment_new)
        results = [new_weight, to_half(new_weight), first_new, second_new, moment_new]
        if at == 0:
            results = [value.T for value in results]
        if at == 1:
            results = [jnp.swapaxes(value, 1, 2) for value in results]
        new_weights.append(results[0])
        halves_out.append(results[1])
        first_out.append(results[2][None])
        second_out.append(results[3][None])
        new_moments.append(results[4])
    return (loss_total, *new_weights, *halves_out, *first_out, *second_out, *new_moments)


def solution(mesh):
    placed = (
        P(("group", "expert", "dp"), None),
        P(("group", "expert", "dp"), None),
        P(("group", "expert", "dp")),
        P(("group", "expert", "dp")),
        P(None, ("group", "expert", "dp"), None),
        P(None, ("group", "expert", "dp"), None),
        P(None, ("expert", "dp")),
        P(None, None, ("expert", "dp")),
        P(None, ("expert", "dp"), None),
        P(None, "expert", None, None, "dp"),
        P("group", None, ("expert", "dp")),
        P("group", None, None, ("expert", "dp")),
        P("group", None, ("expert", "dp"), None),
        P("group", None, "expert", None, None, "dp"),
        P("group", None, ("expert", "dp")),
        P("group", None, None, ("expert", "dp")),
        P("group", None, ("expert", "dp"), None),
        P("group", None, "expert", None, None, "dp"),
        P(None, ("expert", "dp")),
        P(None, None, ("expert", "dp")),
        P(None, ("expert", "dp"), None),
        P(None, "expert", None, None, "dp"),
    )
    step = few_experts if mesh.shape["expert"] <= 4 else per_device
    return jax.shard_map(
        step,
        mesh=mesh,
        in_specs=placed,
        out_specs=(
            P(),
            P(None, ("expert", "dp")),
            P(None, None, ("expert", "dp")),
            P(None, ("expert", "dp"), None),
            P(None, "expert", None, None, "dp"),
            P(None, ("expert", "dp")),
            P(None, None, ("expert", "dp")),
            P(None, ("expert", "dp"), None),
            P(None, "expert", None, None, "dp"),
            P("group", None, ("expert", "dp")),
            P("group", None, None, ("expert", "dp")),
            P("group", None, ("expert", "dp"), None),
            P("group", None, "expert", None, None, "dp"),
            P("group", None, ("expert", "dp")),
            P("group", None, None, ("expert", "dp")),
            P("group", None, ("expert", "dp"), None),
            P("group", None, "expert", None, None, "dp"),
            P(None, ("expert", "dp")),
            P(None, None, ("expert", "dp")),
            P(None, ("expert", "dp"), None),
            P(None, "expert", None, None, "dp"),
        ),
        check_vma=False,
    )
```

```python
import functools

import jax
import jax.numpy as jnp
from jax import lax
from jax.experimental import pallas as pl
from jax.experimental.pallas import tpu as pltpu
from jax.sharding import PartitionSpec as P

D = 384
HEADS = 6
IMG = 32
FREQ = 256
CLASSES = 1000
LAYERS = 2
STEP = 10
PATCH_DIM = 16
PATCHES = 256


highest = lax.Precision.HIGHEST
beta_one = 0.9
beta_two = 0.95
eps_adam = 1e-08
inner_rate = 0.03
weight_decay = 0.05
outer_rate = 0.7
outer_mom = 0.9
ln_eps = 1e-06


def to_half(values):
    return values.astype(jnp.bfloat16)


def product(left_in, right_in):
    return jnp.dot(left_in, right_in, preferred_element_type=jnp.float32)


def product_tn(left_in, right_in):
    return lax.dot_general(
        left_in, right_in, (((0,), (0,)), ((), ())), preferred_element_type=jnp.float32
    )


def product_nt(left_in, right_in):
    return lax.dot_general(
        left_in, right_in, (((1,), (1,)), ((), ())), preferred_element_type=jnp.float32
    )


def gelu_tanh(values):
    return jax.nn.gelu(values, approximate=True)


def gelu_back(values, gradient):
    _, pull = jax.vjp(gelu_tanh, values)
    return pull(gradient)[0]


def norm_mod(values, shift_in, scale_in):
    centre = values - jnp.mean(values, axis=-1, keepdims=True)
    spread = jnp.mean(centre * centre, axis=-1, keepdims=True)
    return centre * lax.rsqrt(spread + ln_eps) * (1.0 + scale_in) + shift_in


def positions_table():
    grid_side = IMG // 2
    quarter = D // 4
    omegas = 1.0 / 10000.0 ** (jnp.arange(quarter, dtype=jnp.float32) / quarter)
    index_all = jnp.arange(PATCHES, dtype=jnp.int32)
    row_angle = (index_all // grid_side).astype(jnp.float32)[:, None] * omegas[None, :]
    col_angle = (index_all % grid_side).astype(jnp.float32)[:, None] * omegas[None, :]
    return jnp.concatenate(
        [jnp.sin(row_angle), jnp.cos(row_angle), jnp.sin(col_angle), jnp.cos(col_angle)], axis=1
    )


def time_features(step_ids):
    half_freq = FREQ // 2
    frequency = jnp.exp(-jnp.log(10000.0) * jnp.arange(half_freq, dtype=jnp.float32) / half_freq)
    angles = step_ids.astype(jnp.float32)[:, None] * frequency[None, :]
    return jnp.concatenate([jnp.cos(angles), jnp.sin(angles)], axis=1)


def label_table(label_ids):
    return (label_ids[:, None] == jnp.arange(CLASSES + 1, dtype=jnp.int32)[None, :]).astype(
        jnp.float32
    )


def split_stem(stem_all):
    end_patch = PATCH_DIM
    end_time = end_patch + FREQ
    end_second = end_time + D
    end_table = end_second + CLASSES + 1
    end_ada = end_table + 2 * D
    return (
        stem_all[:end_patch],
        stem_all[end_patch:end_time],
        stem_all[end_time:end_second],
        stem_all[end_second:end_table],
        stem_all[end_table:end_ada],
        stem_all[end_ada:],
    )


def slot_places(route_ids, expert_count, capacity):
    flat_ids = route_ids.reshape(-1)
    one_hot_ids = (flat_ids[:, None] == jnp.arange(expert_count, dtype=jnp.int32)[None, :]).astype(
        jnp.int32
    )
    rank_in = jnp.sum((jnp.cumsum(one_hot_ids, axis=0) - one_hot_ids) * one_hot_ids, axis=1)
    return flat_ids * capacity + rank_in


def expert_major(received, local_count):
    sources = received.shape[0] // local_count
    shaped = received.reshape(sources, local_count, received.shape[1], received.shape[2])
    return jnp.swapaxes(shaped, 0, 1).reshape(local_count, -1, received.shape[2])


def source_major(rows_in, sources):
    local_count = rows_in.shape[0]
    shaped = rows_in.reshape(local_count, sources, -1, rows_in.shape[2])
    return jnp.swapaxes(shaped, 0, 1).reshape(sources * local_count, -1, rows_in.shape[2])


def attention_split(qkv, item_count):
    head_dim = qkv.shape[1] // (3 * HEADS)
    shaped = qkv.reshape(item_count, -1, 3, HEADS, head_dim)
    return (shaped[:, :, 0], shaped[:, :, 1], shaped[:, :, 2], head_dim ** (-0.5))


def attention_forward(qkv, item_count):
    queries, keys_in, values_in, scale_att = attention_split(qkv, item_count)
    scores = (
        jnp.einsum("bqhd,bkhd->bhqk", queries, keys_in, preferred_element_type=jnp.float32)
        * scale_att
    )
    row_max = jnp.max(scores, axis=-1, keepdims=True)
    log_sums = row_max + jnp.log(jnp.sum(jnp.exp(scores - row_max), axis=-1, keepdims=True))
    attn_probs = to_half(jnp.exp(scores - log_sums))
    attended = jnp.einsum(
        "bhqk,bkhd->bqhd", attn_probs, values_in, preferred_element_type=jnp.float32
    )
    return (to_half(attended.reshape(qkv.shape[0], -1)), log_sums)


def attention_backward(qkv, log_sums, grad_attended, item_count):
    queries, keys_in, values_in, scale_att = attention_split(qkv, item_count)
    scores = (
        jnp.einsum("bqhd,bkhd->bhqk", queries, keys_in, preferred_element_type=jnp.float32)
        * scale_att
    )
    probs_full = jnp.exp(scores - log_sums)
    grad_out = grad_attended.reshape(queries.shape)
    grad_values = jnp.einsum(
        "bhqk,bqhd->bkhd", to_half(probs_full), grad_out, preferred_element_type=jnp.float32
    )
    grad_probs = jnp.einsum(
        "bqhd,bkhd->bhqk", grad_out, values_in, preferred_element_type=jnp.float32
    )
    grad_scores = probs_full * (
        grad_probs - jnp.sum(probs_full * grad_probs, axis=-1, keepdims=True)
    )
    grad_half = to_half(grad_scores)
    grad_queries = (
        jnp.einsum("bhqk,bkhd->bqhd", grad_half, keys_in, preferred_element_type=jnp.float32)
        * scale_att
    )
    grad_keys = (
        jnp.einsum("bhqk,bqhd->bkhd", grad_half, queries, preferred_element_type=jnp.float32)
        * scale_att
    )
    stacked = jnp.stack([grad_queries, grad_keys, grad_values], axis=2)
    return to_half(stacked.reshape(qkv.shape[0], -1))


def layer_forward(tokens, cond_act, lin, lout, expert_w, route_ids, gate_vals):
    item_count = cond_act.shape[0]
    model_width = tokens.shape[1]
    local_count = expert_w.shape[0]
    expert_count = lax.axis_size("expert") * local_count
    capacity = 4 * tokens.shape[0] // expert_count
    mods = jnp.dot(
        cond_act, lin[:, 4 * model_width : 10 * model_width].astype(jnp.float32), precision=highest
    )
    mods = mods.reshape(item_count, 6, 1, model_width)
    shaped = tokens.reshape(item_count, -1, model_width)
    normed = to_half(norm_mod(shaped, mods[:, 0], mods[:, 1]).reshape(-1, model_width))
    qkv = to_half(product(normed, lin[:, : 3 * model_width]))
    attended, log_sums = attention_forward(qkv, item_count)
    branch = product(attended, lin[:, 3 * model_width : 4 * model_width])
    middle = shaped + mods[:, 2] * branch.reshape(item_count, -1, model_width)
    normed_two = to_half(norm_mod(middle, mods[:, 3], mods[:, 4]).reshape(-1, model_width))
    inner_pre = product(normed_two, lin[:, 10 * model_width :])
    active = to_half(gelu_tanh(inner_pre))
    shared = product(active, lout)
    slot_index = slot_places(route_ids, expert_count, capacity)
    send_rows = jnp.zeros((expert_count * capacity, model_width), jnp.bfloat16)
    send_rows = send_rows.at[slot_index].set(jnp.repeat(normed_two, 2, axis=0))
    received = lax.all_to_all(
        send_rows.reshape(expert_count, capacity, model_width),
        "expert",
        split_axis=0,
        concat_axis=0,
        tiled=True,
    )
    rows_exp = expert_major(received, local_count)
    inner_exp = jnp.einsum(
        "erd,edf->erf", rows_exp, expert_w[:, 0], preferred_element_type=jnp.float32
    )
    active_exp = to_half(gelu_tanh(inner_exp))
    out_exp = to_half(
        jnp.einsum("erf,edf->erd", active_exp, expert_w[:, 1], preferred_element_type=jnp.float32)
    )
    returned = lax.all_to_all(
        source_major(out_exp, lax.axis_size("expert")),
        "expert",
        split_axis=0,
        concat_axis=0,
        tiled=True,
    )
    picked = (
        returned.reshape(-1, model_width)[slot_index]
        .astype(jnp.float32)
        .reshape(-1, 2, model_width)
    )
    mixed_out = shared + jnp.sum(gate_vals[:, :, None] * picked, axis=1)
    result = middle + mods[:, 5] * mixed_out.reshape(item_count, -1, model_width)
    saved = (
        tokens,
        mods,
        normed,
        qkv,
        attended,
        log_sums,
        branch,
        middle,
        normed_two,
        inner_pre,
        active,
        mixed_out,
        slot_index,
        rows_exp,
        inner_exp,
        active_exp,
    )
    return (result.reshape(-1, model_width), saved)


def layer_backward(grad_tokens, saved, cond_act, lin, lout, expert_w, gate_vals):
    (
        tokens,
        mods,
        normed,
        qkv,
        attended,
        log_sums,
        branch,
        middle,
        normed_two,
        inner_pre,
        active,
        mixed_out,
        slot_index,
        rows_exp,
        inner_exp,
        active_exp,
    ) = saved
    item_count = cond_act.shape[0]
    model_width = tokens.shape[1]
    local_count = expert_w.shape[0]
    expert_count = lax.axis_size("expert") * local_count
    capacity = 4 * tokens.shape[0] // expert_count
    grad_shaped = grad_tokens.reshape(item_count, -1, model_width)
    grad_gate_two = jnp.sum(
        grad_shaped * mixed_out.reshape(item_count, -1, model_width), axis=1, keepdims=True
    )
    grad_mixed = (mods[:, 5] * grad_shaped).reshape(-1, model_width)
    grad_shared = to_half(grad_mixed)
    grad_lout = product_tn(active, grad_shared)
    grad_inner = to_half(gelu_back(inner_pre, product_nt(grad_shared, lout)))
    grad_w_up = product_tn(normed_two, grad_inner)
    grad_normed_two = product_nt(grad_inner, lin[:, 10 * model_width :])
    routed_grad = to_half(gate_vals[:, :, None] * grad_mixed[:, None, :]).reshape(-1, model_width)
    send_grad = (
        jnp.zeros((expert_count * capacity, model_width), jnp.bfloat16)
        .at[slot_index]
        .set(routed_grad)
    )
    received = lax.all_to_all(
        send_grad.reshape(expert_count, capacity, model_width),
        "expert",
        split_axis=0,
        concat_axis=0,
        tiled=True,
    )
    grad_rows = expert_major(received, local_count)
    grad_down_exp = jnp.einsum(
        "erd,erf->edf", grad_rows, active_exp, preferred_element_type=jnp.float32
    )
    grad_active_exp = jnp.einsum(
        "erd,edf->erf", grad_rows, expert_w[:, 1], preferred_element_type=jnp.float32
    )
    grad_inner_exp = to_half(gelu_back(inner_exp, grad_active_exp))
    grad_up_exp = jnp.einsum(
        "erd,erf->edf", rows_exp, grad_inner_exp, preferred_element_type=jnp.float32
    )
    grad_rows_in = to_half(
        jnp.einsum(
            "erf,edf->erd", grad_inner_exp, expert_w[:, 0], preferred_element_type=jnp.float32
        )
    )
    back_rows = lax.all_to_all(
        source_major(grad_rows_in, lax.axis_size("expert")),
        "expert",
        split_axis=0,
        concat_axis=0,
        tiled=True,
    )
    picked = (
        back_rows.reshape(-1, model_width)[slot_index]
        .astype(jnp.float32)
        .reshape(-1, 2, model_width)
    )
    grad_normed_two = grad_normed_two + jnp.sum(picked, axis=1)
    _, second_back = jax.vjp(norm_mod, middle, mods[:, 3], mods[:, 4])
    grad_middle, grad_shift_two, grad_scale_two = second_back(
        grad_normed_two.reshape(item_count, -1, model_width)
    )
    grad_middle = grad_middle + grad_shaped
    grad_gate_one = jnp.sum(
        grad_middle * branch.reshape(item_count, -1, model_width), axis=1, keepdims=True
    )
    grad_branch = to_half((mods[:, 2] * grad_middle).reshape(-1, model_width))
    grad_w_out = product_tn(attended, grad_branch)
    grad_attended = to_half(product_nt(grad_branch, lin[:, 3 * model_width : 4 * model_width]))
    grad_qkv = attention_backward(qkv, log_sums, grad_attended, item_count)
    grad_w_qkv = product_tn(normed, grad_qkv)
    grad_normed = product_nt(grad_qkv, lin[:, : 3 * model_width])
    _, first_back = jax.vjp(
        norm_mod, tokens.reshape(item_count, -1, model_width), mods[:, 0], mods[:, 1]
    )
    grad_input, grad_shift_one, grad_scale_one = first_back(
        grad_normed.reshape(item_count, -1, model_width)
    )
    grad_input = grad_input + grad_middle
    grad_mods = jnp.stack(
        [
            grad_shift_one,
            grad_scale_one,
            grad_gate_one,
            grad_shift_two,
            grad_scale_two,
            grad_gate_two,
        ],
        axis=1,
    )
    grad_mods = grad_mods.reshape(item_count, 6 * model_width)
    grad_ada = jnp.dot(cond_act.T, grad_mods, precision=highest)
    grad_cond = jnp.dot(
        grad_mods,
        lin[:, 4 * model_width : 10 * model_width].astype(jnp.float32).T,
        precision=highest,
    )
    grad_lin = jnp.concatenate([grad_w_qkv, grad_w_out, grad_ada, grad_w_up], axis=1)
    grad_expert = jnp.stack([grad_up_exp, grad_down_exp], axis=1)
    return (grad_input.reshape(-1, model_width), grad_cond, grad_lin, grad_lout, grad_expert)


def adam_step(weight_in, gradient, first_in, second_in):
    first_new = beta_one * first_in + (1.0 - beta_one) * gradient
    second_new = beta_two * second_in + (1.0 - beta_two) * gradient * gradient
    first_hat = first_new / (1.0 - beta_one**STEP)
    second_hat = second_new / (1.0 - beta_two**STEP)
    stepped = weight_in - inner_rate * (
        first_hat / (jnp.sqrt(second_hat) + eps_adam) + weight_decay * weight_in
    )
    return (weight_in - stepped, first_new, second_new)


def per_device(
    patches,
    target_noise,
    timesteps,
    labels,
    routes,
    route_gates,
    stem_weights,
    layer_in,
    layer_out,
    experts,
    stem_first,
    layer_in_first,
    layer_out_first,
    experts_first,
    stem_second,
    layer_in_second,
    layer_out_second,
    experts_second,
    stem_moment,
    layer_in_moment,
    layer_out_moment,
    experts_moment,
):
    stem_all, lin_all, lout_all = (
        lax.all_gather(to_half(stem_weights), ("expert", "dp"), axis=1, tiled=True),
        lax.all_gather(to_half(layer_in), ("expert", "dp"), axis=2, tiled=True),
        lax.all_gather(to_half(layer_out), ("expert", "dp"), axis=1, tiled=True),
    )
    expert_all = lax.all_gather(to_half(experts), "dp", axis=4, tiled=True)
    model_width = stem_all.shape[1]
    item_count = timesteps.shape[0]
    patch_w, time_one, time_two, table_w, final_ada, final_out = split_stem(stem_all)
    features = time_features(timesteps)
    hot_labels = label_table(labels)

    def condition(first_w, second_w, table_in):
        hidden_time = jax.nn.silu(jnp.dot(features, first_w, precision=highest))
        return jax.nn.silu(
            jnp.dot(hidden_time, second_w, precision=highest)
            + jnp.dot(hot_labels, table_in, precision=highest)
        )

    cond_act, cond_back = jax.vjp(
        condition,
        time_one.astype(jnp.float32),
        time_two.astype(jnp.float32),
        table_w.astype(jnp.float32),
    )
    tokens = product(patches, patch_w)
    tokens = (tokens.reshape(item_count, -1, model_width) + positions_table()[None]).reshape(
        -1, model_width
    )
    saved_all = []
    for layer_idx in range(LAYERS):
        tokens, saved = layer_forward(
            tokens,
            cond_act,
            lin_all[layer_idx],
            lout_all[layer_idx],
            expert_all[layer_idx],
            routes[layer_idx],
            route_gates[layer_idx],
        )
        saved_all.append(saved)
    final_ada_f = final_ada.astype(jnp.float32)
    final_mods = jnp.dot(cond_act, final_ada_f.T, precision=highest).reshape(
        item_count, 2, 1, model_width
    )
    final_pre, final_back = jax.vjp(
        norm_mod, tokens.reshape(item_count, -1, model_width), final_mods[:, 0], final_mods[:, 1]
    )
    final_normed = to_half(final_pre.reshape(-1, model_width))
    predicted = product_nt(final_normed, final_out)
    residual_err = predicted - target_noise
    loss_total = lax.psum(jnp.sum(residual_err * residual_err), ("group", "expert", "dp"))
    grad_pred = to_half(2.0 * residual_err)
    grad_final_out = product_tn(grad_pred, final_normed)
    grad_final_normed = product(grad_pred, final_out)
    grad_tokens, grad_fshift, grad_fscale = final_back(
        grad_final_normed.reshape(item_count, -1, model_width)
    )
    grad_tokens = grad_tokens.reshape(-1, model_width)
    grad_final_mods = jnp.concatenate([grad_fshift, grad_fscale], axis=1).reshape(
        item_count, 2 * model_width
    )
    grad_final_ada = jnp.dot(grad_final_mods.T, cond_act, precision=highest)
    grad_cond = jnp.dot(grad_final_mods, final_ada_f, precision=highest)
    lin_grads = []
    lout_grads = []
    expert_grads = []
    for layer_idx in reversed(range(LAYERS)):
        grad_tokens, grad_cond_layer, grad_lin, grad_lout, grad_expert = layer_backward(
            grad_tokens,
            saved_all[layer_idx],
            cond_act,
            lin_all[layer_idx],
            lout_all[layer_idx],
            expert_all[layer_idx],
            route_gates[layer_idx],
        )
        grad_cond = grad_cond + grad_cond_layer
        lin_grads.append(grad_lin)
        lout_grads.append(grad_lout)
        expert_grads.append(grad_expert)
    lin_stack = jnp.stack(lin_grads[::-1])
    lout_stack = jnp.stack(lout_grads[::-1])
    expert_stack = jnp.stack(expert_grads[::-1])
    grad_patch = product_tn(patches, to_half(grad_tokens))
    grad_time_one, grad_time_two, grad_table = cond_back(grad_cond)
    grad_stem = jnp.concatenate(
        [grad_patch, grad_time_one, grad_time_two, grad_table, grad_final_ada, grad_final_out],
        axis=0,
    )
    stem_sum, lin_sum, lout_sum = (
        lax.psum_scatter(grad_stem, ("expert", "dp"), scatter_dimension=1, tiled=True),
        lax.psum_scatter(lin_stack, ("expert", "dp"), scatter_dimension=2, tiled=True),
        lax.psum_scatter(lout_stack, ("expert", "dp"), scatter_dimension=1, tiled=True),
    )
    expert_sum = lax.psum_scatter(
        expert_stack.astype(jnp.bfloat16), "dp", scatter_dimension=4, tiled=True
    ).astype(jnp.float32)
    weights_all = (stem_weights, layer_in, layer_out, experts)
    gradients = (stem_sum, lin_sum, lout_sum, expert_sum)
    firsts = (stem_first, layer_in_first, layer_out_first, experts_first)
    seconds = (stem_second, layer_in_second, layer_out_second, experts_second)
    moments = (stem_moment, layer_in_moment, layer_out_moment, experts_moment)
    stepped = [
        adam_step(
            weights_all[array_idx],
            gradients[array_idx],
            firsts[array_idx][0],
            seconds[array_idx][0],
        )
        for array_idx in range(4)
    ]
    delta_all = (
        lax.psum(stepped[0][0].astype(jnp.bfloat16), "group").astype(jnp.float32),
        lax.psum(stepped[1][0].astype(jnp.bfloat16), "group").astype(jnp.float32),
        lax.psum(stepped[2][0].astype(jnp.bfloat16), "group").astype(jnp.float32),
        lax.psum(stepped[3][0].astype(jnp.bfloat16), "group").astype(jnp.float32),
    )
    group_count = lax.axis_size("group")
    new_weights = []
    new_moments = []
    for array_idx in range(4):
        mean_delta = delta_all[array_idx] / group_count
        moment_new = outer_mom * moments[array_idx] + mean_delta
        new_weights.append(
            weights_all[array_idx] - outer_rate * (mean_delta + outer_mom * moment_new)
        )
        new_moments.append(moment_new)
    return (
        loss_total,
        new_weights[0],
        new_weights[1],
        new_weights[2],
        new_weights[3],
        to_half(new_weights[0]),
        to_half(new_weights[1]),
        to_half(new_weights[2]),
        to_half(new_weights[3]),
        stepped[0][1][None],
        stepped[1][1][None],
        stepped[2][1][None],
        stepped[3][1][None],
        stepped[0][2][None],
        stepped[1][2][None],
        stepped[2][2][None],
        stepped[3][2][None],
        new_moments[0],
        new_moments[1],
        new_moments[2],
        new_moments[3],
    )


bf16 = jnp.bfloat16
f32 = jnp.float32
MIB = 1024 * 1024
CHUNK = 768
STEM_SIZES = (PATCH_DIM, FREQ, D, CLASSES + 1, 2 * D, PATCH_DIM)
STEM_PADDED = tuple(-(-size // 128) * 128 for size in STEM_SIZES)
STEM_AT = tuple(sum(STEM_PADDED[:place]) for place in range(len(STEM_PADDED)))
STEM_LANES = sum(STEM_PADDED)


def dot_nn(left_in, right_in):
    return lax.dot_general(left_in, right_in, (((1,), (0,)), ((), ())), preferred_element_type=f32)


def dot_nt(left_in, right_in):
    return lax.dot_general(left_in, right_in, (((1,), (1,)), ((), ())), preferred_element_type=f32)


def dot_tn(left_in, right_in):
    return lax.dot_general(left_in, right_in, (((0,), (0,)), ((), ())), preferred_element_type=f32)


def three_parts(rows):
    high = rows.astype(bf16).astype(f32)
    rest = rows - high
    mid = rest.astype(bf16).astype(f32)
    low = rest - mid
    return jnp.concatenate([high, mid, low, jnp.zeros_like(low)], axis=0).astype(bf16)


def three_sum(stacked):
    return stacked[0:8] + stacked[8:16] + stacked[16:24]


def full_nt(rows, weight):
    return three_sum(dot_nt(three_parts(rows), weight))


def full_nn(rows, weight):
    return three_sum(dot_nn(three_parts(rows), weight))


def silu_slope(values):
    gate = 1.0 / (1.0 + jnp.exp(-values))
    return gate * (1.0 + values * (1.0 - gate))


def silu_of(values):
    return values / (1.0 + jnp.exp(-values))


def stem_piece(stem_ref, place):
    return stem_ref[:, STEM_AT[place] : STEM_AT[place] + STEM_PADDED[place]]


def cond_kernel(feat_ref, hot_ref, stem_ref, ada_a, ada_b, cond_ref, hid_ref, one_ref, two_ref, mods_ref, fin_ref):
    pre_one = full_nt(feat_ref[...], stem_piece(stem_ref, 1))
    hidden = silu_of(pre_one)
    pre_two = full_nt(hidden, stem_piece(stem_ref, 2)) + dot_nt(hot_ref[...], stem_piece(stem_ref, 3))[0:8]
    cond = silu_of(pre_two)
    one_ref[...] = pre_one
    two_ref[...] = pre_two
    hid_ref[...] = hidden
    cond_ref[...] = cond
    parts = three_parts(cond)
    for place in range(6):
        rows = pl.ds(place * D, D)
        mods_ref[0, :, rows] = three_sum(dot_nt(parts, ada_a[rows, :]))
        mods_ref[1, :, rows] = three_sum(dot_nt(parts, ada_b[rows, :]))
    fin_ref[...] = three_sum(dot_nn(parts, stem_piece(stem_ref, 4)))


def cond_back_kernel(gm_a, gm_b, gf_ref, one_ref, two_ref, stem_ref, ada_a, ada_b, done_ref, dtwo_ref):
    grad_cond = full_nt(gf_ref[...], stem_piece(stem_ref, 4))
    grad_cond = grad_cond + full_nn(gm_a[...], ada_a[...]) + full_nn(gm_b[...], ada_b[...])
    dtwo = grad_cond * silu_slope(two_ref[...])
    dtwo_ref[...] = dtwo
    dhid = full_nn(dtwo, stem_piece(stem_ref, 2))
    done_ref[...] = dhid * silu_slope(one_ref[...])


def norm_parts(values):
    centre = values - jnp.mean(values, axis=-1, keepdims=True)
    spread = jnp.mean(centre * centre, axis=-1, keepdims=True)
    root = lax.rsqrt(spread + ln_eps)
    return centre * root, root


def norm_back(values, scale_in, gradient):
    unit, root = norm_parts(values)
    grad_unit = gradient * (1.0 + scale_in)
    inner = jnp.mean(grad_unit * unit, axis=-1, keepdims=True)
    grad_in = root * (grad_unit - jnp.mean(grad_unit, axis=-1, keepdims=True) - unit * inner)
    return (
        grad_in,
        jnp.sum(gradient, axis=0, keepdims=True),
        jnp.sum(gradient * unit, axis=0, keepdims=True),
    )


def mod_row(mods_ref, item, place):
    return mods_ref[pl.ds(item, 1), place * D : (place + 1) * D]


def head_masks():
    lane = lax.broadcasted_iota(jnp.int32, (1, 128), 1)
    return lane, [(lane // 64 == half).astype(f32).astype(bf16) for half in range(2)]


def attn_fwd_kernel(x_ref, mods_ref, w_ref, normed_ref, qkv_ref, att_ref, branch_ref, mid_ref, n2_ref):
    item = pl.program_id(0)
    tokens = x_ref[...]
    unit, _ = norm_parts(tokens)
    normed = (unit * (1.0 + mod_row(mods_ref, item, 1)) + mod_row(mods_ref, item, 0)).astype(bf16)
    normed_ref[...] = normed
    qkv_ref[...] = dot_nt(normed, w_ref[0 : 3 * D, :]).astype(bf16)
    lane, masks = head_masks()
    for pair in range(HEADS // 2):
        at = pair * 128
        queries = qkv_ref[:, at : at + 128]
        keys = qkv_ref[:, D + at : D + at + 128]
        vals = qkv_ref[:, 2 * D + at : 2 * D + at + 128]
        outs = []
        for half in range(2):
            scores = dot_nt(queries * masks[half], keys) * 0.125
            powers = jnp.exp(scores - jnp.max(scores, axis=-1, keepdims=True))
            probs = (powers * (1.0 / jnp.sum(powers, axis=-1, keepdims=True))).astype(bf16)
            outs.append(dot_nn(probs, vals))
        att_ref[:, at : at + 128] = jnp.where(lane < 64, outs[0], outs[1]).astype(bf16)
    branch = dot_nt(att_ref[...], w_ref[3 * D : 4 * D, :])
    branch_ref[...] = branch
    middle = tokens + mod_row(mods_ref, item, 2) * branch
    mid_ref[...] = middle
    unit, _ = norm_parts(middle)
    n2_ref[...] = (unit * (1.0 + mod_row(mods_ref, item, 4)) + mod_row(mods_ref, item, 3)).astype(bf16)


def attn_bwd_kernel(
    gn2_ref, g_ref, mid_ref, x_ref, normed_ref, qkv_ref, att_ref, branch_ref, mods_ref, gg_ref, w_ref,
    gx_ref, gmods_ref, dw_ref, dqkv, acc,
):
    item = pl.program_id(0)

    @pl.when(item == 0)
    def _():
        acc[...] = jnp.zeros_like(acc)
        gmods_ref[...] = jnp.zeros_like(gmods_ref)

    grad_mid, dshift, dscale = norm_back(mid_ref[...], mod_row(mods_ref, item, 4), gn2_ref[...])
    grad_mid = grad_mid + g_ref[...]
    dgate = jnp.sum(grad_mid * branch_ref[...], axis=0, keepdims=True)
    gmods_ref[pl.ds(item, 1), 2 * D : 3 * D] = dgate
    gmods_ref[pl.ds(item, 1), 3 * D : 4 * D] = dshift
    gmods_ref[pl.ds(item, 1), 4 * D : 5 * D] = dscale
    gmods_ref[pl.ds(item, 1), 5 * D : 6 * D] = gg_ref[pl.ds(item, 1), :]
    grad_branch = (mod_row(mods_ref, item, 2) * grad_mid).astype(bf16)
    acc[3 * D : 4 * D, :] += dot_tn(grad_branch, att_ref[...])
    grad_att = dot_nn(grad_branch, w_ref[3 * D : 4 * D, :]).astype(bf16)
    lane, masks = head_masks()
    for pair in range(HEADS // 2):
        at = pair * 128
        queries = qkv_ref[:, at : at + 128]
        keys = qkv_ref[:, D + at : D + at + 128]
        vals = qkv_ref[:, 2 * D + at : 2 * D + at + 128]
        grad_out = grad_att[:, at : at + 128]
        parts = []
        for half in range(2):
            scores = dot_nt(queries * masks[half], keys) * 0.125
            powers = jnp.exp(scores - jnp.max(scores, axis=-1, keepdims=True))
            probs = powers * (1.0 / jnp.sum(powers, axis=-1, keepdims=True))
            grad_vals = dot_tn(probs.astype(bf16), grad_out)
            grad_probs = dot_nt(grad_out * masks[half], vals)
            inner = jnp.sum(probs * grad_probs, axis=-1, keepdims=True)
            grad_scores = (probs * (grad_probs - inner)).astype(bf16)
            parts.append((dot_nn(grad_scores, keys) * 0.125, dot_tn(grad_scores, queries) * 0.125, grad_vals))
        for place in range(3):
            dqkv[:, place * D + at : place * D + at + 128] = jnp.where(
                lane < 64, parts[0][place], parts[1][place]
            ).astype(bf16)
    acc[0 : 3 * D, :] += dot_tn(dqkv[...], normed_ref[...])
    grad_normed = dot_nn(dqkv[...], w_ref[0 : 3 * D, :])
    grad_in, dshift, dscale = norm_back(x_ref[...], mod_row(mods_ref, item, 1), grad_normed)
    gx_ref[...] = grad_in + grad_mid
    gmods_ref[pl.ds(item, 1), 0:D] = dshift
    gmods_ref[pl.ds(item, 1), D : 2 * D] = dscale

    @pl.when(item == pl.num_programs(0) - 1)
    def _():
        dw_ref[0 : 4 * D, :] = acc[...].astype(bf16)
        dw_ref[4 * D :, :] = jnp.zeros_like(dw_ref[4 * D :, :])


def gelu_both(values):
    outer = 0.7978845608028654
    cubic = outer * 0.044715
    square = values * values
    angle = jnp.tanh(values * (square * cubic + outer))
    half = 0.5 * values
    active = half * angle + half
    slope = half * (square * (3.0 * cubic) + outer) * (1.0 - angle * angle) + (0.5 * angle + 0.5)
    return active.astype(bf16), slope.astype(bf16)


def gate_column(g4_ref, rows, expert):
    gates = g4_ref[rows, :]
    lane = lax.broadcasted_iota(jnp.int32, gates.shape, 1)
    return jnp.sum(jnp.where(lane == expert, gates, 0.0), axis=1, keepdims=True)


def ffn_fwd_kernel(shared_steps, halves, n2_ref, mid_ref, mods_ref, g4_ref, up_ref, dn_ref, ex_ref, act_ref, dg_ref, mixed_ref, x_ref, acc, racc):
    step = pl.program_id(0)
    items = n2_ref.shape[0] // PATCHES

    @pl.when(step < shared_steps)
    def _():
        for item in range(items):
            rows = pl.ds(item * PATCHES, PATCHES)
            active, slope = gelu_both(dot_nt(n2_ref[rows, :], up_ref[...]))
            act_ref[0, rows, :] = active
            dg_ref[0, rows, :] = slope
            part = dot_nn(active, dn_ref[...])

            @pl.when(step == 0)
            def _():
                acc[rows, :] = part

            @pl.when(step > 0)
            def _():
                acc[rows, :] += part

    @pl.when(step >= shared_steps)
    def _():
        expert, half = (step - shared_steps) // halves, (step - shared_steps) % halves
        for item in range(items):
            rows = pl.ds(item * PATCHES, PATCHES)
            active, slope = gelu_both(dot_nn(n2_ref[rows, :], ex_ref[0, 0]))
            act_ref[0, rows, :] = active
            dg_ref[0, rows, :] = slope
            part = dot_nt(active, ex_ref[0, 1])

            @pl.when(half == 0)
            def _():
                racc[rows, :] = part

            @pl.when(half > 0)
            def _():
                routed = (racc[rows, :] + part).astype(bf16).astype(f32)
                acc[rows, :] += gate_column(g4_ref, rows, expert) * routed

    @pl.when(step == pl.num_programs(0) - 1)
    def _():
        mixed_ref[...] = acc[...]
        for item in range(items):
            rows = pl.ds(item * PATCHES, PATCHES)
            x_ref[rows, :] = mid_ref[rows, :] + mod_row(mods_ref, item, 5) * acc[rows, :]


def ffn_bwd_kernel(
    shared_steps, halves, g_ref, n2_ref, mods_ref, g4_ref, mixed_ref, act_ref, dg_ref, up_ref, dn_ref, ex_ref,
    dup_ref, ddn_ref, dex_ref, gn2_ref, gg_ref, gmix, gs, gst, n2t, din, acc, racc,
):
    step = pl.program_id(0)
    items = n2_ref.shape[0] // PATCHES

    @pl.when(step == 0)
    def _():
        gg_ref[...] = jnp.zeros_like(gg_ref)
        dup_ref[0:D, :] = jnp.zeros((D, D), bf16)
        for item in range(items):
            rows = pl.ds(item * PATCHES, PATCHES)
            grad = g_ref[rows, :]
            gg_ref[pl.ds(item, 1), :] = jnp.sum(grad * mixed_ref[rows, :], axis=0, keepdims=True)
            grad = mod_row(mods_ref, item, 5) * grad
            gmix[rows, :] = grad
            gs[rows, :] = grad.astype(bf16)
            gst[:, rows] = grad.astype(bf16).T
            n2t[:, rows] = n2_ref[rows, :].T
        acc[...] = jnp.zeros_like(acc)

    @pl.when(step < shared_steps)
    def _():
        for item in range(items):
            rows = pl.ds(item * PATCHES, PATCHES)
            inner = (dot_nt(gs[rows, :], dn_ref[...]) * dg_ref[0, rows, :].astype(f32)).astype(bf16)
            din[rows, :] = inner
            acc[rows, :] += dot_nn(inner, up_ref[...])
        at = dup_ref.shape[0] - shared_steps * CHUNK + step * CHUNK
        dup_ref[pl.ds(pl.multiple_of(at, D), CHUNK), :] = dot_nn(n2t[...], din[...]).astype(bf16).T
        ddn_ref[...] = dot_nn(gst[...], act_ref[0]).astype(bf16).T

    @pl.when(step >= shared_steps)
    def _():
        expert, half = (step - shared_steps) // halves, (step - shared_steps) % halves

        @pl.when(half == 0)
        def _():
            for item in range(items):
                rows = pl.ds(item * PATCHES, PATCHES)
                grad = (gate_column(g4_ref, rows, expert) * gmix[rows, :]).astype(bf16)
                gs[rows, :] = grad
                gst[:, rows] = grad.T

        for item in range(items):
            rows = pl.ds(item * PATCHES, PATCHES)
            inner = (dot_nn(gs[rows, :], ex_ref[0, 1]) * dg_ref[0, rows, :].astype(f32)).astype(bf16)
            din[rows, :] = inner
            part = dot_nt(inner, ex_ref[0, 0])

            @pl.when(half == 0)
            def _():
                racc[rows, :] = part

            @pl.when(half > 0)
            def _():
                acc[rows, :] += (racc[rows, :] + part).astype(bf16).astype(f32)

        dex_ref[0, 0] = dot_nn(n2t[...], din[...]).astype(bf16)
        dex_ref[0, 1] = dot_nn(gst[...], act_ref[0]).astype(bf16)

    @pl.when(step == pl.num_programs(0) - 1)
    def _():
        gn2_ref[...] = acc[...]


def final_kernel(x_ref, mods_ref, fo_ref, tgt_ref, gx_ref, gfm_ref, dfo_ref, loss_ref):
    item = pl.program_id(0)

    @pl.when(item == 0)
    def _():
        gfm_ref[...] = jnp.zeros_like(gfm_ref)
        dfo_ref[...] = jnp.zeros_like(dfo_ref)
        loss_ref[...] = jnp.zeros_like(loss_ref)

    tokens = x_ref[...]
    unit, _ = norm_parts(tokens)
    scale = mod_row(mods_ref, item, 1)
    normed = (unit * (1.0 + scale) + mod_row(mods_ref, item, 0)).astype(bf16)
    err = dot_nt(fo_ref[...], normed) - tgt_ref[...]
    loss_ref[...] += jnp.sum(err * err, axis=1, keepdims=True)
    grad_pred = (2.0 * err).astype(bf16)
    dfo_ref[...] += dot_nn(grad_pred, normed)
    grad_in, dshift, dscale = norm_back(tokens, scale, dot_tn(grad_pred, fo_ref[...]))
    gx_ref[...] = grad_in
    gfm_ref[pl.ds(item, 1), 0:D] = dshift
    gfm_ref[pl.ds(item, 1), D : 2 * D] = dscale


def params(limit):
    return pltpu.CompilerParams(vmem_limit_bytes=limit * MIB)


def cost(multiplies, moved):
    return pl.CostEstimate(flops=2 * multiplies, bytes_accessed=moved, transcendentals=0)


def whole(shape):
    return pl.BlockSpec(shape, lambda step: (0,) * len(shape))


def rows_of(width):
    return pl.BlockSpec((PATCHES, width), lambda step: (step, 0))


def shape_of(shape, kind):
    return jax.ShapeDtypeStruct(shape, kind)


def cond_forward(feat, hot, stem_t, lin_a, lin_b):
    ada = pl.BlockSpec((6 * D, D), lambda: (0, 0))
    shapes = [(8, D)] * 4 + [(LAYERS, 8, 6 * D), (8, 2 * D)]
    ada_at = [lax.slice_in_dim(lin, 4 * D, 10 * D, axis=0) for lin in (lin_a, lin_b)]
    del ada
    return pl.pallas_call(
        cond_kernel,
        out_shape=[shape_of(shape, f32) for shape in shapes],
        compiler_params=params(40),
        name="cond_forward",
    )(feat, hot, stem_t, *ada_at), ada_at


def cond_backward(gm_a, gm_b, gfm, pre_one, pre_two, stem_t, ada_at):
    return pl.pallas_call(
        cond_back_kernel,
        out_shape=[shape_of((8, D), f32)] * 2,
        compiler_params=params(40),
        name="cond_backward",
    )(gm_a, gm_b, gfm, pre_one, pre_two, stem_t, *ada_at)


def attn_forward(tokens, mods, lin):
    count = tokens.shape[0]
    return pl.pallas_call(
        attn_fwd_kernel,
        grid=(count // PATCHES,),
        in_specs=[rows_of(D), whole(mods.shape), whole((4 * D, D))],
        out_specs=[rows_of(D), rows_of(3 * D), rows_of(D), rows_of(D), rows_of(D), rows_of(D)],
        out_shape=[
            shape_of((count, D), bf16),
            shape_of((count, 3 * D), bf16),
            shape_of((count, D), bf16),
            shape_of((count, D), f32),
            shape_of((count, D), f32),
            shape_of((count, D), bf16),
        ],
        compiler_params=params(40),
        cost_estimate=cost(count * D * 4 * D * 9, 16 * count * D),
        name="attention_forward",
    )(tokens, mods, lin)


def attn_backward(gn2, grad, middle, tokens, normed, qkv, attended, branch, mods, grad_gate, lin, out_rows):
    count = tokens.shape[0]
    return pl.pallas_call(
        attn_bwd_kernel,
        grid=(count // PATCHES,),
        in_specs=[rows_of(D)] * 5
        + [rows_of(3 * D), rows_of(D), rows_of(D), whole(mods.shape), whole(grad_gate.shape), whole((4 * D, D))],
        out_specs=[rows_of(D), whole((8, 6 * D)), whole((out_rows, D))],
        out_shape=[shape_of((count, D), f32), shape_of((8, 6 * D), f32), shape_of((out_rows, D), bf16)],
        scratch_shapes=[pltpu.VMEM((PATCHES, 3 * D), bf16), pltpu.VMEM((4 * D, D), f32)],
        compiler_params=params(50),
        cost_estimate=cost(count * D * 4 * D * 22, 16 * count * D),
        name="attention_backward",
    )(gn2, grad, middle, tokens, normed, qkv, attended, branch, mods, grad_gate, lin)


def weight_specs(shared_steps, lin_rows):
    up_at = lin_rows // CHUNK - shared_steps
    return [
        pl.BlockSpec((CHUNK, D), lambda step: (up_at + jnp.minimum(step, shared_steps - 1), 0)),
        pl.BlockSpec((CHUNK, D), lambda step: (jnp.minimum(step, shared_steps - 1), 0)),
        pl.BlockSpec((1, 2, D, CHUNK), lambda step: (jnp.maximum(step - shared_steps, 0), 0, 0, 0)),
    ]


def ffn_forward(n2, middle, mods, g4, lin, lout, experts_w, halves):
    count = n2.shape[0]
    shared_steps = lout.shape[0] // CHUNK
    steps = shared_steps + experts_w.shape[0]
    wide = pl.BlockSpec((1, count, CHUNK), lambda step: (step, 0, 0))
    return pl.pallas_call(
        functools.partial(ffn_fwd_kernel, shared_steps, halves),
        grid=(steps,),
        in_specs=[whole(n2.shape), whole(middle.shape), whole(mods.shape), whole(g4.shape)]
        + weight_specs(shared_steps, lin.shape[0]),
        out_specs=[wide, wide, whole((count, D)), whole((count, D))],
        out_shape=[
            shape_of((steps, count, CHUNK), bf16),
            shape_of((steps, count, CHUNK), bf16),
            shape_of((count, D), f32),
            shape_of((count, D), f32),
        ],
        scratch_shapes=[pltpu.VMEM((count, D), f32)] * 2,
        compiler_params=params(56),
        cost_estimate=cost(4 * steps * count * D * CHUNK * 2, 8 * steps * count * CHUNK),
        name="ffn_forward",
    )(n2, middle, mods, g4, lin, lout, experts_w)


def ffn_backward(grad, n2, mods, g4, mixed, active, slope, lin, lout, experts_w, halves):
    count = n2.shape[0]
    shared_steps = lout.shape[0] // CHUNK
    steps = shared_steps + experts_w.shape[0]
    wide = pl.BlockSpec((1, count, CHUNK), lambda step: (step, 0, 0))
    specs = weight_specs(shared_steps, lin.shape[0])
    return pl.pallas_call(
        functools.partial(ffn_bwd_kernel, shared_steps, halves),
        grid=(steps,),
        in_specs=[whole(grad.shape), whole(n2.shape), whole(mods.shape), whole(g4.shape), whole(mixed.shape), wide, wide]
        + specs,
        out_specs=[whole((lout.shape[0] + D, D)), specs[1], specs[2], whole((count, D)), whole((8, D))],
        out_shape=[
            shape_of((lout.shape[0] + D, D), bf16),
            shape_of(lout.shape, bf16),
            shape_of(experts_w.shape, bf16),
            shape_of((count, D), f32),
            shape_of((8, D), f32),
        ],
        scratch_shapes=[
            pltpu.VMEM((count, D), f32),
            pltpu.VMEM((count, D), bf16),
            pltpu.VMEM((D, count), bf16),
            pltpu.VMEM((D, count), bf16),
            pltpu.VMEM((count, CHUNK), bf16),
            pltpu.VMEM((count, D), f32),
            pltpu.VMEM((count, D), f32),
        ],
        compiler_params=params(60),
        cost_estimate=cost(4 * steps * count * D * CHUNK * 4 // 2, 8 * steps * count * CHUNK),
        name="ffn_backward",
    )(grad, n2, mods, g4, mixed, active, slope, lin, lout, experts_w)


def final_step(tokens, mods, fo_rows, target_t):
    count = tokens.shape[0]
    return pl.pallas_call(
        final_kernel,
        grid=(count // PATCHES,),
        in_specs=[
            rows_of(D),
            whole(mods.shape),
            whole(fo_rows.shape),
            pl.BlockSpec((PATCH_DIM, PATCHES), lambda step: (0, step)),
        ],
        out_specs=[rows_of(D), whole((8, 2 * D)), whole((PATCH_DIM, D)), whole((PATCH_DIM, 1))],
        out_shape=[
            shape_of((count, D), f32),
            shape_of((8, 2 * D), f32),
            shape_of((PATCH_DIM, D), f32),
            shape_of((PATCH_DIM, 1), f32),
        ],
        compiler_params=params(40),
        name="final_step",
    )(tokens, mods, fo_rows, target_t)


def pad_rows(values):
    return jnp.pad(values, ((0, 8 - values.shape[0]), (0, 0)))


def stem_lanes(stem_t):
    pieces, at = [], 0
    for size, padded in zip(STEM_SIZES, STEM_PADDED):
        pieces.append(jnp.pad(stem_t[:, at : at + size], ((0, 0), (0, padded - size))))
        at = at + size
    return jnp.concatenate(pieces, axis=1)


MESH_ID = pl.DeviceIdType.MESH
TILE = 48


def plane_partners():
    group = lax.axis_index("group")
    return {"group": group + 1 - 2 * lax.rem(group, 2)}, {"group": lax.rem(group + 2, 4)}


def greet(partners, line_at, line_size):
    barrier = pltpu.get_barrier_semaphore()
    for partner in partners:
        pl.semaphore_signal(barrier, inc=1, device_id=partner, device_id_type=MESH_ID)

    @pl.when(line_at > 0)
    def _():
        pl.semaphore_signal(barrier, inc=1, device_id={"expert": line_at - 1}, device_id_type=MESH_ID)

    @pl.when(line_at < line_size - 1)
    def _():
        pl.semaphore_signal(barrier, inc=1, device_id={"expert": line_at + 1}, device_id_type=MESH_ID)

    ends = jnp.where(line_at == 0, 1, 0) + jnp.where(line_at == line_size - 1, 1, 0)
    pl.semaphore_wait(barrier, len(partners) + 2 - ends)


def row_tiles(rows, body):
    def step(index, carry):
        body(pl.ds(pl.multiple_of(index * TILE, TILE), TILE))
        return carry

    lax.fori_loop(0, rows // TILE, step, 0)


def adam_delta(weight, gradient, first, second):
    return adam_step(weight, gradient, first, second)[0]


def reduce_units():
    units = []
    for matrix in range(2):
        for half in range(2):
            units.append((0, matrix, half * D // 2, D // 2, CHUNK, ()))
    for half in range(2):
        units.append((1, 0, half * 432, 432, D, (1,)))
    units.append((2, 0, 0, D, D, ()))
    return units


def reduce_kernel(
    layer, dex, dqkvo, dup, ddn, extra, ex_w, ex_f, ex_s, li_w, li_f, li_s, lo_w, lo_f, lo_s,
    g_ex, g_li, g_lo, m_ex, m_li, m_lo, *scratch,
):
    units = reduce_units()
    number = len(units)
    banks = [scratch[at * number : (at + 1) * number] for at in range(9)]
    chip, local, came, delta, swapped, swapped_two, weight, first, second = banks
    extra_buf = scratch[9 * number]
    core_send, core_recv, line_send, line_recv, load_sem, plane_send, plane_recv, out_sem = scratch[9 * number + 1 :]
    at = lax.axis_index("expert")
    core = lax.axis_index("dp")
    sibling = {"dp": 1 - core}
    side_x, side_y = plane_partners()
    greet([sibling, side_x, side_y], at, 4)

    def pieces(unit, which):
        kind, matrix, row, rows, _, _ = units[unit]
        if kind == 0:
            return [(dex.at[:, which, matrix, pl.ds(row, rows)], slice(0, 4))]
        if kind == 2:
            return [(ddn.at[:, which, pl.ds(row, rows)], slice(0, 4))]
        return [
            (dqkvo.at[which, pl.ds(row, rows)], 0),
            (dup.at[0, which, pl.ds(row, rows)], 2),
            (dup.at[1, which, pl.ds(row, rows)], 3),
        ]

    def dest(bank, unit, where):
        return bank[unit].at[pl.ds(0, 4)] if isinstance(where, slice) else bank[unit].at[where]

    given, loads = [], []
    for unit in range(number):
        given.append([])
        for place, (source, where) in enumerate(pieces(unit, 1 - core)):
            copy = pltpu.make_async_remote_copy(
                source, dest(chip, unit, where), core_send.at[unit, place], core_recv.at[unit, place],
                device_id=sibling, device_id_type=MESH_ID,
            )
            copy.start()
            given[unit].append(copy)
        loads.append([])
        for place, (source, where) in enumerate(pieces(unit, core)):
            copy = pltpu.make_async_copy(source, dest(local, unit, where), load_sem.at[unit, place])
            copy.start()
            loads[unit].append(copy)
    state_loads = []
    for unit, (kind, matrix, row, rows, _, _) in enumerate(units):
        if kind == 0:
            sources = [ex_w.at[layer, 0, matrix], ex_f.at[0, layer, 0, matrix], ex_s.at[0, layer, 0, matrix]]
        elif kind == 1:
            sources = [li_w.at[layer], li_f.at[layer], li_s.at[layer]]
        else:
            sources = [lo_w.at[layer], lo_f.at[0, layer], lo_s.at[0, layer]]
        state_loads.append([])
        for place, (source, bank) in enumerate(zip(sources, (weight, first, second))):
            copy = pltpu.make_async_copy(source.at[pl.ds(row, rows)], bank[unit], load_sem.at[unit, 3 + place])
            copy.start()
            state_loads[unit].append(copy)
    extra_load = pltpu.make_async_copy(extra, extra_buf, load_sem.at[number, 0])
    extra_load.start()

    def line_copy(unit, owner, step, place):
        slot = 4 if step == -1 and owner == place - 1 else owner
        return pltpu.make_async_remote_copy(
            chip[unit].at[owner], came[unit].at[slot], line_send.at[unit, owner], line_recv.at[unit, slot],
            device_id={"expert": at + step}, device_id_type=MESH_ID,
        )

    def arrived(unit, slot):
        pltpu.make_async_remote_copy(
            came[unit].at[slot], came[unit].at[slot], line_send.at[unit, 0], line_recv.at[unit, slot],
            device_id=sibling, device_id_type=MESH_ID,
        ).wait_recv()

    routes_of = {0: [(3, 1), (2, 1), (1, 1)], 1: [(3, 1), (2, 1), (0, -1)], 2: [(0, -1), (1, -1), (3, 1)], 3: [(0, -1), (1, -1), (2, -1)]}
    finals = {0: [4], 1: [1, 4], 2: [2, 4], 3: [3]}

    for unit, (kind, matrix, row, rows, _, absent) in enumerate(units):
        for copy in given[unit]:
            copy.wait_recv()
        for copy in loads[unit]:
            copy.wait()
        for owner in range(4):
            if owner in absent:
                chip[unit][owner] = jnp.zeros(chip[unit].shape[1:], bf16)
                continue

            def add(tile, owner=owner, unit=unit):
                total = chip[unit][owner, tile, :].astype(f32) + local[unit][owner, tile, :].astype(f32)
                chip[unit][owner, tile, :] = total.astype(bf16)

            row_tiles(rows, add)
        for end in (0, 3):

            @pl.when(at == end)
            def _(unit=unit, end=end, absent=absent):
                for owner, step in routes_of[end]:
                    if owner not in absent:
                        line_copy(unit, owner, step, end).start()
                came[unit][0 if end == 0 else 4] = jnp.zeros(chip[unit].shape[1:], bf16)

        for owner in absent:

            @pl.when(at == owner)
            def _(unit=unit, owner=owner):
                came[unit][owner] = jnp.zeros(chip[unit].shape[1:], bf16)
                came[unit][4] = jnp.zeros(chip[unit].shape[1:], bf16)

    def forward(unit):
        rows, absent = units[unit][3], units[unit][5]
        for middle in (1, 2):

            @pl.when(at == middle)
            def _(middle=middle):
                for owner, step in routes_of[middle]:
                    if owner in absent:
                        continue
                    arrived(unit, owner)

                    def add(tile, owner=owner):
                        total = chip[unit][owner, tile, :].astype(f32) + came[unit][owner, tile, :].astype(f32)
                        chip[unit][owner, tile, :] = total.astype(bf16)

                    row_tiles(rows, add)
                    line_copy(unit, owner, step, middle).start()

    def plane_copies(unit, second_step):
        rows = units[unit][3]
        middle = rows // 32 * 16
        sides = (side_y, side_x) if second_step else (side_x, side_y)
        landing = swapped_two if second_step else swapped
        copies = []
        for half, (begin, size) in enumerate(((0, middle), (middle, rows - middle))):
            part = pl.ds(begin, size)
            copies.append(
                pltpu.make_async_remote_copy(
                    delta[unit].at[part], landing[unit].at[part], plane_send.at[unit, 2 * second_step + half],
                    plane_recv.at[unit, 2 * second_step + half], device_id=sides[half], device_id_type=MESH_ID,
                )
            )
        return copies

    def out_copy(unit, means):
        kind, matrix, row, rows, _, _ = units[unit]
        target = ((g_ex.at[matrix], g_li, g_lo), (m_ex.at[matrix], m_li, m_lo))[means][kind]
        source = first[unit] if means else weight[unit]
        return pltpu.make_async_copy(source, target.at[pl.ds(row, rows)], out_sem.at[unit, means])

    firsts, seconds = {}, {}

    def finish(unit):
        kind, matrix, row, rows, _, absent = units[unit]
        for place in range(4):

            @pl.when(at == place)
            def _(place=place):
                if place not in absent:
                    for slot in finals[place]:
                        arrived(unit, slot)

        for copy in state_loads[unit]:
            copy.wait()
        if kind == 1 and row == 0:
            extra_load.wait()

        def body(tile):
            grad = chip[unit][at, tile, :].astype(f32) + came[unit][at, tile, :].astype(f32)
            grad = grad + came[unit][4, tile, :].astype(f32)
            if kind == 1:
                grad = grad + extra_buf[pl.ds(row + tile.start, TILE), :]
            change = adam_delta(weight[unit][tile, :], grad, first[unit][tile, :], second[unit][tile, :])
            delta[unit][tile, :] = change.astype(bf16)
            weight[unit][tile, :] = grad

        row_tiles(rows, body)
        out_copy(unit, 0).start()
        firsts[unit] = plane_copies(unit, 0)
        for copy in firsts[unit]:
            copy.start()

    def exchange(unit):
        for copy in firsts[unit]:
            copy.wait()

        def body(tile):
            total = delta[unit][tile, :].astype(f32) + swapped[unit][tile, :].astype(f32)
            delta[unit][tile, :] = total.astype(bf16)

        row_tiles(units[unit][3], body)
        seconds[unit] = plane_copies(unit, 1)
        for copy in seconds[unit]:
            copy.start()

    def close(unit):
        for copy in seconds[unit]:
            copy.wait_recv()

        def body(tile):
            first[unit][tile, :] = delta[unit][tile, :].astype(f32) + swapped_two[unit][tile, :].astype(f32)

        row_tiles(units[unit][3], body)
        out_copy(unit, 1).start()

    for turn in range(number + 3):
        for lag, action in enumerate((forward, finish, exchange, close)):
            if 0 <= turn - lag < number:
                action(turn - lag)

    for unit in range(number):
        for copy in given[unit]:
            copy.wait_send()
        for copy in seconds[unit]:
            copy.wait_send()
        out_copy(unit, 0).wait()
        out_copy(unit, 1).wait()
        for place in range(4):

            @pl.when(at == place)
            def _(place=place, unit=unit):
                for owner, step in routes_of[place]:
                    if owner not in units[unit][5]:
                        line_copy(unit, owner, step, place).wait_send()


def reduce_layer(layer, dex, dqkvo, dup, ddn, extra, states):
    units = reduce_units()
    scratch = []
    for lead, kind in (((4,), bf16), ((4,), bf16), ((5,), bf16), ((), bf16), ((), bf16), ((), bf16), ((), f32), ((), f32), ((), f32)):
        scratch += [pltpu.VMEM(lead + (unit[3], unit[4]), kind) for unit in units]
    number = len(units)
    scratch.append(pltpu.VMEM(extra.shape, f32))
    dma = pltpu.SemaphoreType.DMA
    scratch += [dma((number, 3)), dma((number, 3)), dma((number, 4)), dma((number, 5)), dma((number + 1, 6))]
    scratch += [dma((number, 4)), dma((number, 4)), dma((number, 2))]
    anywhere = pl.BlockSpec(memory_space=pl.ANY)
    shapes = [(2, D, CHUNK), extra.shape, (D, D)] * 2
    return pl.pallas_call(
        functools.partial(reduce_kernel, layer),
        out_shape=[shape_of(shape, f32) for shape in shapes],
        in_specs=[anywhere] * (5 + len(states)),
        out_specs=[anywhere] * 6,
        scratch_shapes=scratch,
        compiler_params=pltpu.CompilerParams(
            vmem_limit_bytes=62 * MIB, collective_id=1 + layer, has_side_effects=True
        ),
        name="reduce_layer",
    )(dex, dqkvo, dup, ddn, extra, *states)


def plane_sum(delta):
    middle = delta.shape[0] // 2
    swaps = [[(i, i ^ bit) for i in range(4)] for bit in (1, 2)]
    totals = []
    for half, order in ((delta[:middle], (0, 1)), (delta[middle:], (1, 0))):
        for axis in order:
            half = to_half(half.astype(f32) + lax.ppermute(half, "group", swaps[axis]).astype(f32))
        totals.append(half.astype(f32))
    return jnp.concatenate(totals, axis=0)


SHARD = ("expert", "dp")


def few_experts(
    patches,
    target_noise,
    timesteps,
    labels,
    routes,
    route_gates,
    stem_weights,
    layer_in,
    layer_out,
    experts,
    stem_first,
    layer_in_first,
    layer_out_first,
    experts_first,
    stem_second,
    layer_in_second,
    layer_out_second,
    experts_second,
    stem_moment,
    layer_in_moment,
    layer_out_moment,
    experts_moment,
):
    count = patches.shape[0]
    items = timesteps.shape[0]
    halves = lax.axis_size("dp")
    sharers = lax.axis_size("expert") * halves
    expert_count = lax.axis_size("expert") * experts.shape[1]
    place = lax.axis_index("expert") * halves + lax.axis_index("dp")

    stem_t = stem_weights.T
    lin_t = jnp.swapaxes(layer_in, 1, 2)
    stem_all = lax.all_gather(stem_lanes(to_half(stem_t)), SHARD, axis=0, tiled=True)
    lin_all, lout_all, expert_all = [], [], []
    for layer in range(LAYERS):
        lin_all.append(lax.all_gather(to_half(lin_t[layer]), SHARD, axis=0, tiled=True))
        lout_all.append(lax.all_gather(to_half(layer_out[layer]), SHARD, axis=0, tiled=True))
        expert_all.append(lax.all_gather(to_half(experts[layer]), SHARD, axis=0, tiled=True))

    feat = time_features(timesteps)
    hot = label_table(labels)
    hot_pad = jnp.pad(hot, ((0, 32 - items), (0, STEM_PADDED[3] - hot.shape[1]))).astype(bf16)
    (cond, hidden, pre_one, pre_two, mods, fin_mods), ada_at = cond_forward(
        pad_rows(feat), hot_pad, stem_all, lin_all[0], lin_all[1]
    )
    tokens = product_nt(patches, stem_all[:, :PATCH_DIM])
    tokens = (tokens.reshape(items, -1, D) + positions_table()[None]).reshape(-1, D)
    expert_ids = jnp.arange(expert_count, dtype=jnp.int32)
    saved = []
    for layer in range(LAYERS):
        g4 = jnp.sum(
            jnp.where(routes[layer][:, :, None] == expert_ids, route_gates[layer][:, :, None], 0.0), axis=1
        )
        normed, qkv, attended, branch, middle, n2 = attn_forward(tokens, mods[layer], lin_all[layer])
        active, slope, mixed, result = ffn_forward(
            n2, middle, mods[layer], g4, lin_all[layer], lout_all[layer], expert_all[layer], halves
        )
        saved.append((tokens, g4, normed, qkv, attended, branch, middle, n2, active, slope, mixed))
        tokens = result
    fo_rows = stem_all[:, STEM_AT[5] : STEM_AT[5] + PATCH_DIM].T
    grad, grad_fin, grad_out_w, loss_rows = final_step(tokens, fin_mods, fo_rows, target_noise.T)
    loss_total = lax.psum(jnp.sum(loss_rows), ("group", "expert", "dp"))

    stem_cols = stem_weights.shape[1]
    lin_cols = layer_in.shape[2]

    def outer(left_in, right_in):
        return lax.dot_general(left_in, right_in, (((0,), (0,)), ((), ())), precision=highest)

    def flip(values):
        return jnp.swapaxes(values, -1, -2)

    states = (experts, experts_first, experts_second, lin_t, flip(layer_in_first[0]), flip(layer_in_second[0]))
    states = states + (layer_out, layer_out_first, layer_out_second)
    grad_mods, reduced = [None] * LAYERS, [None] * LAYERS
    for layer in reversed(range(LAYERS)):
        tokens, g4, normed, qkv, attended, branch, middle, n2, active, slope, mixed = saved[layer]
        dup, ddn, dex, gn2, grad_gate = ffn_backward(
            grad, n2, mods[layer], g4, mixed, active, slope, lin_all[layer], lout_all[layer], expert_all[layer], halves
        )
        grad, grad_mods[layer], dqkvo = attn_backward(
            gn2, grad, middle, tokens, normed, qkv, attended, branch, mods[layer], grad_gate, lin_all[layer],
            halves * lin_cols,
        )
        factors = jnp.concatenate([cond[:items], grad_mods[layer][:items]], axis=1)
        factors = lax.all_gather(factors, SHARD, axis=0, tiled=True)
        spread = jnp.pad(factors[:, D:], ((0, 0), (4 * D, lin_cols * sharers - 10 * D)))
        window = lax.dynamic_slice_in_dim(spread, place * lin_cols, lin_cols, axis=1)
        reduced[layer] = reduce_layer(
            layer,
            dex.reshape((-1, halves) + dex.shape[1:]),
            dqkvo.reshape(halves, lin_cols, D),
            dup.reshape(-1, halves, lin_cols, D),
            ddn.reshape(-1, halves, layer_out.shape[1], D),
            outer(window, factors[:, :D]),
            states,
        )
    grad_patch = product_tn(patches, to_half(grad))
    dpre_one, dpre_two = cond_backward(grad_mods[0], grad_mods[1], grad_fin, pre_one, pre_two, stem_all, ada_at)

    factors = jnp.concatenate(
        [cond[:items], hidden[:items], dpre_one[:items], dpre_two[:items], grad_fin[:items], feat], axis=1
    )
    width = factors.shape[1]
    packed = jnp.concatenate([factors.reshape(-1), grad_patch.reshape(-1), grad_out_w.reshape(-1)])
    gathered = lax.all_gather(packed, SHARD, axis=0, tiled=False)
    ends = gathered[:, items * width :].reshape(sharers, 2, PATCH_DIM, D).sum(axis=0)
    factors = gathered[:, : items * width].reshape(sharers * items, width)
    hot_all = label_table(lax.all_gather(labels, SHARD, axis=0, tiled=True))
    cond_f, hidden_f, done_f, dtwo_f, fin_f, feat_f = jnp.split(factors, [D, 2 * D, 3 * D, 4 * D, 6 * D], axis=1)

    def own(values):
        return lax.dynamic_slice_in_dim(values, place * stem_cols, stem_cols, axis=1)

    stem_grad = jnp.concatenate(
        [
            own(ends[0]).T,
            outer(own(done_f), feat_f),
            outer(own(dtwo_f), hidden_f),
            outer(own(dtwo_f), hot_all),
            outer(own(cond_f), fin_f),
            own(ends[1]).T,
        ],
        axis=1,
    )
    group_count = lax.axis_size("group")

    def update(weight, gradient, first, second, moment, total):
        delta, first_new, second_new = adam_step(weight, gradient, first, second)
        if total is None:
            total = plane_sum(to_half(delta))
        mean_delta = total / group_count
        moment_new = outer_mom * moment + mean_delta
        new_weight = weight - outer_rate * (mean_delta + outer_mom * moment_new)
        return new_weight, to_half(new_weight), first_new[None], second_new[None], moment_new

    def update_layers(at, weight, first, second, moment):
        parts = [
            update(weight[layer], reduced[layer][at], first[layer], second[layer], moment[layer], reduced[layer][3 + at])
            for layer in range(LAYERS)
        ]
        return [jnp.stack([parts[0][out], parts[1][out]], axis=1 if out in (2, 3) else 0) for out in range(5)]

    stem_out = [flip(v) for v in update(stem_t, stem_grad, stem_first[0].T, stem_second[0].T, stem_moment.T, None)]
    lin_out = update_layers(1, lin_t, flip(layer_in_first[0]), flip(layer_in_second[0]), flip(layer_in_moment))
    lin_out = [flip(v) for v in lin_out]
    lout_out = update_layers(2, layer_out, layer_out_first[0], layer_out_second[0], layer_out_moment)
    pairs = [v.reshape((LAYERS,) + v.shape[-3:]) for v in (experts, experts_first, experts_second, experts_moment)]
    expert_out = update_layers(0, *pairs)
    likes = (experts, experts, experts_first, experts_second, experts)
    expert_out = [v.reshape(like.shape) for v, like in zip(expert_out, likes)]
    results = []
    for at in range(5):
        results += [stem_out[at], lin_out[at], lout_out[at], expert_out[at]]
    return (loss_total, *results)


def solution(mesh):
    placed = (
        P(("group", "expert", "dp"), None),
        P(("group", "expert", "dp"), None),
        P(("group", "expert", "dp")),
        P(("group", "expert", "dp")),
        P(None, ("group", "expert", "dp"), None),
        P(None, ("group", "expert", "dp"), None),
        P(None, ("expert", "dp")),
        P(None, None, ("expert", "dp")),
        P(None, ("expert", "dp"), None),
        P(None, "expert", None, None, "dp"),
        P("group", None, ("expert", "dp")),
        P("group", None, None, ("expert", "dp")),
        P("group", None, ("expert", "dp"), None),
        P("group", None, "expert", None, None, "dp"),
        P("group", None, ("expert", "dp")),
        P("group", None, None, ("expert", "dp")),
        P("group", None, ("expert", "dp"), None),
        P("group", None, "expert", None, None, "dp"),
        P(None, ("expert", "dp")),
        P(None, None, ("expert", "dp")),
        P(None, ("expert", "dp"), None),
        P(None, "expert", None, None, "dp"),
    )
    step = few_experts if mesh.shape["expert"] <= 4 else per_device
    return jax.shard_map(
        step,
        mesh=mesh,
        in_specs=placed,
        out_specs=(
            P(),
            P(None, ("expert", "dp")),
            P(None, None, ("expert", "dp")),
            P(None, ("expert", "dp"), None),
            P(None, "expert", None, None, "dp"),
            P(None, ("expert", "dp")),
            P(None, None, ("expert", "dp")),
            P(None, ("expert", "dp"), None),
            P(None, "expert", None, None, "dp"),
            P("group", None, ("expert", "dp")),
            P("group", None, None, ("expert", "dp")),
            P("group", None, ("expert", "dp"), None),
            P("group", None, "expert", None, None, "dp"),
            P("group", None, ("expert", "dp")),
            P("group", None, None, ("expert", "dp")),
            P("group", None, ("expert", "dp"), None),
            P("group", None, "expert", None, None, "dp"),
            P(None, ("expert", "dp")),
            P(None, None, ("expert", "dp")),
            P(None, ("expert", "dp"), None),
            P(None, "expert", None, None, "dp"),
        ),
        check_vma=False,
    )
```

```python
import functools

import jax
import jax.numpy as jnp
from jax import lax
from jax.experimental import pallas as pl
from jax.experimental.pallas import tpu as pltpu
from jax.sharding import PartitionSpec as P

GROUP, LINE, CORE = "group", "expert", "dp"
D = 384
HEADS = 6
IMG = 32
FREQ = 256
CLASSES = 1000
LAYERS = 2
STEP = 10
PATCH_DIM = 16
PATCHES = 256


highest = lax.Precision.HIGHEST
beta_one = 0.9
beta_two = 0.95
eps_adam = 1e-08
inner_rate = 0.03
weight_decay = 0.05
outer_rate = 0.7
outer_mom = 0.9
ln_eps = 1e-06


def to_half(values):
    return values.astype(jnp.bfloat16)


def product(left_in, right_in):
    return jnp.dot(left_in, right_in, preferred_element_type=jnp.float32)


def product_tn(left_in, right_in):
    return lax.dot_general(
        left_in, right_in, (((0,), (0,)), ((), ())), preferred_element_type=jnp.float32
    )


def product_nt(left_in, right_in):
    return lax.dot_general(
        left_in, right_in, (((1,), (1,)), ((), ())), preferred_element_type=jnp.float32
    )


def gelu_tanh(values):
    return jax.nn.gelu(values, approximate=True)


def gelu_back(values, gradient):
    _, pull = jax.vjp(gelu_tanh, values)
    return pull(gradient)[0]


def norm_mod(values, shift_in, scale_in):
    centre = values - jnp.mean(values, axis=-1, keepdims=True)
    spread = jnp.mean(centre * centre, axis=-1, keepdims=True)
    return centre * lax.rsqrt(spread + ln_eps) * (1.0 + scale_in) + shift_in


def positions_table():
    grid_side = IMG // 2
    quarter = D // 4
    omegas = 1.0 / 10000.0 ** (jnp.arange(quarter, dtype=jnp.float32) / quarter)
    index_all = jnp.arange(PATCHES, dtype=jnp.int32)
    row_angle = (index_all // grid_side).astype(jnp.float32)[:, None] * omegas[None, :]
    col_angle = (index_all % grid_side).astype(jnp.float32)[:, None] * omegas[None, :]
    return jnp.concatenate(
        [jnp.sin(row_angle), jnp.cos(row_angle), jnp.sin(col_angle), jnp.cos(col_angle)], axis=1
    )


def time_features(step_ids):
    half_freq = FREQ // 2
    frequency = jnp.exp(-jnp.log(10000.0) * jnp.arange(half_freq, dtype=jnp.float32) / half_freq)
    angles = step_ids.astype(jnp.float32)[:, None] * frequency[None, :]
    return jnp.concatenate([jnp.cos(angles), jnp.sin(angles)], axis=1)


def label_table(label_ids):
    return (label_ids[:, None] == jnp.arange(CLASSES + 1, dtype=jnp.int32)[None, :]).astype(
        jnp.float32
    )


def split_stem(stem_all):
    end_patch = PATCH_DIM
    end_time = end_patch + FREQ
    end_second = end_time + D
    end_table = end_second + CLASSES + 1
    end_ada = end_table + 2 * D
    return (
        stem_all[:end_patch],
        stem_all[end_patch:end_time],
        stem_all[end_time:end_second],
        stem_all[end_second:end_table],
        stem_all[end_table:end_ada],
        stem_all[end_ada:],
    )


def slot_places(route_ids, expert_count, capacity):
    flat_ids = route_ids.reshape(-1)
    one_hot_ids = (flat_ids[:, None] == jnp.arange(expert_count, dtype=jnp.int32)[None, :]).astype(
        jnp.int32
    )
    rank_in = jnp.sum((jnp.cumsum(one_hot_ids, axis=0) - one_hot_ids) * one_hot_ids, axis=1)
    return flat_ids * capacity + rank_in


def expert_major(received, local_count):
    sources = received.shape[0] // local_count
    shaped = received.reshape(sources, local_count, received.shape[1], received.shape[2])
    return jnp.swapaxes(shaped, 0, 1).reshape(local_count, -1, received.shape[2])


def source_major(rows_in, sources):
    local_count = rows_in.shape[0]
    shaped = rows_in.reshape(local_count, sources, -1, rows_in.shape[2])
    return jnp.swapaxes(shaped, 0, 1).reshape(sources * local_count, -1, rows_in.shape[2])


def attention_split(qkv, item_count):
    head_dim = qkv.shape[1] // (3 * HEADS)
    shaped = qkv.reshape(item_count, -1, 3, HEADS, head_dim)
    return (shaped[:, :, 0], shaped[:, :, 1], shaped[:, :, 2], head_dim ** (-0.5))


def attention_forward(qkv, item_count):
    queries, keys_in, values_in, scale_att = attention_split(qkv, item_count)
    scores = (
        jnp.einsum("bqhd,bkhd->bhqk", queries, keys_in, preferred_element_type=jnp.float32)
        * scale_att
    )
    row_max = jnp.max(scores, axis=-1, keepdims=True)
    log_sums = row_max + jnp.log(jnp.sum(jnp.exp(scores - row_max), axis=-1, keepdims=True))
    attn_probs = to_half(jnp.exp(scores - log_sums))
    attended = jnp.einsum(
        "bhqk,bkhd->bqhd", attn_probs, values_in, preferred_element_type=jnp.float32
    )
    return (to_half(attended.reshape(qkv.shape[0], -1)), log_sums)


def attention_backward(qkv, log_sums, grad_attended, item_count):
    queries, keys_in, values_in, scale_att = attention_split(qkv, item_count)
    scores = (
        jnp.einsum("bqhd,bkhd->bhqk", queries, keys_in, preferred_element_type=jnp.float32)
        * scale_att
    )
    probs_full = jnp.exp(scores - log_sums)
    grad_out = grad_attended.reshape(queries.shape)
    grad_values = jnp.einsum(
        "bhqk,bqhd->bkhd", to_half(probs_full), grad_out, preferred_element_type=jnp.float32
    )
    grad_probs = jnp.einsum(
        "bqhd,bkhd->bhqk", grad_out, values_in, preferred_element_type=jnp.float32
    )
    grad_scores = probs_full * (
        grad_probs - jnp.sum(probs_full * grad_probs, axis=-1, keepdims=True)
    )
    grad_half = to_half(grad_scores)
    grad_queries = (
        jnp.einsum("bhqk,bkhd->bqhd", grad_half, keys_in, preferred_element_type=jnp.float32)
        * scale_att
    )
    grad_keys = (
        jnp.einsum("bhqk,bqhd->bkhd", grad_half, queries, preferred_element_type=jnp.float32)
        * scale_att
    )
    stacked = jnp.stack([grad_queries, grad_keys, grad_values], axis=2)
    return to_half(stacked.reshape(qkv.shape[0], -1))


def layer_forward(tokens, cond_act, lin, lout, expert_w, route_ids, gate_vals):
    item_count = cond_act.shape[0]
    model_width = tokens.shape[1]
    local_count = expert_w.shape[0]
    expert_count = lax.axis_size(LINE) * local_count
    capacity = 4 * tokens.shape[0] // expert_count
    mods = jnp.dot(
        cond_act, lin[:, 4 * model_width : 10 * model_width].astype(jnp.float32), precision=highest
    )
    mods = mods.reshape(item_count, 6, 1, model_width)
    shaped = tokens.reshape(item_count, -1, model_width)
    normed = to_half(norm_mod(shaped, mods[:, 0], mods[:, 1]).reshape(-1, model_width))
    qkv = to_half(product(normed, lin[:, : 3 * model_width]))
    attended, log_sums = attention_forward(qkv, item_count)
    branch = product(attended, lin[:, 3 * model_width : 4 * model_width])
    middle = shaped + mods[:, 2] * branch.reshape(item_count, -1, model_width)
    normed_two = to_half(norm_mod(middle, mods[:, 3], mods[:, 4]).reshape(-1, model_width))
    inner_pre = product(normed_two, lin[:, 10 * model_width :])
    active = to_half(gelu_tanh(inner_pre))
    shared = product(active, lout)
    slot_index = slot_places(route_ids, expert_count, capacity)
    send_rows = jnp.zeros((expert_count * capacity, model_width), jnp.bfloat16)
    send_rows = send_rows.at[slot_index].set(jnp.repeat(normed_two, 2, axis=0))
    received = lax.all_to_all(
        send_rows.reshape(expert_count, capacity, model_width),
        LINE,
        split_axis=0,
        concat_axis=0,
        tiled=True,
    )
    rows_exp = expert_major(received, local_count)
    inner_exp = jnp.einsum(
        "erd,edf->erf", rows_exp, expert_w[:, 0], preferred_element_type=jnp.float32
    )
    active_exp = to_half(gelu_tanh(inner_exp))
    out_exp = to_half(
        jnp.einsum("erf,edf->erd", active_exp, expert_w[:, 1], preferred_element_type=jnp.float32)
    )
    returned = lax.all_to_all(
        source_major(out_exp, lax.axis_size(LINE)),
        LINE,
        split_axis=0,
        concat_axis=0,
        tiled=True,
    )
    picked = (
        returned.reshape(-1, model_width)[slot_index]
        .astype(jnp.float32)
        .reshape(-1, 2, model_width)
    )
    mixed_out = shared + jnp.sum(gate_vals[:, :, None] * picked, axis=1)
    result = middle + mods[:, 5] * mixed_out.reshape(item_count, -1, model_width)
    saved = (
        tokens,
        mods,
        normed,
        qkv,
        attended,
        log_sums,
        branch,
        middle,
        normed_two,
        inner_pre,
        active,
        mixed_out,
        slot_index,
        rows_exp,
        inner_exp,
        active_exp,
    )
    return (result.reshape(-1, model_width), saved)


def layer_backward(grad_tokens, saved, cond_act, lin, lout, expert_w, gate_vals):
    (
        tokens,
        mods,
        normed,
        qkv,
        attended,
        log_sums,
        branch,
        middle,
        normed_two,
        inner_pre,
        active,
        mixed_out,
        slot_index,
        rows_exp,
        inner_exp,
        active_exp,
    ) = saved
    item_count = cond_act.shape[0]
    model_width = tokens.shape[1]
    local_count = expert_w.shape[0]
    expert_count = lax.axis_size(LINE) * local_count
    capacity = 4 * tokens.shape[0] // expert_count
    grad_shaped = grad_tokens.reshape(item_count, -1, model_width)
    grad_gate_two = jnp.sum(
        grad_shaped * mixed_out.reshape(item_count, -1, model_width), axis=1, keepdims=True
    )
    grad_mixed = (mods[:, 5] * grad_shaped).reshape(-1, model_width)
    grad_shared = to_half(grad_mixed)
    grad_lout = product_tn(active, grad_shared)
    grad_inner = to_half(gelu_back(inner_pre, product_nt(grad_shared, lout)))
    grad_w_up = product_tn(normed_two, grad_inner)
    grad_normed_two = product_nt(grad_inner, lin[:, 10 * model_width :])
    routed_grad = to_half(gate_vals[:, :, None] * grad_mixed[:, None, :]).reshape(-1, model_width)
    send_grad = (
        jnp.zeros((expert_count * capacity, model_width), jnp.bfloat16)
        .at[slot_index]
        .set(routed_grad)
    )
    received = lax.all_to_all(
        send_grad.reshape(expert_count, capacity, model_width),
        LINE,
        split_axis=0,
        concat_axis=0,
        tiled=True,
    )
    grad_rows = expert_major(received, local_count)
    grad_down_exp = jnp.einsum(
        "erd,erf->edf", grad_rows, active_exp, preferred_element_type=jnp.float32
    )
    grad_active_exp = jnp.einsum(
        "erd,edf->erf", grad_rows, expert_w[:, 1], preferred_element_type=jnp.float32
    )
    grad_inner_exp = to_half(gelu_back(inner_exp, grad_active_exp))
    grad_up_exp = jnp.einsum(
        "erd,erf->edf", rows_exp, grad_inner_exp, preferred_element_type=jnp.float32
    )
    grad_rows_in = to_half(
        jnp.einsum(
            "erf,edf->erd", grad_inner_exp, expert_w[:, 0], preferred_element_type=jnp.float32
        )
    )
    back_rows = lax.all_to_all(
        source_major(grad_rows_in, lax.axis_size(LINE)),
        LINE,
        split_axis=0,
        concat_axis=0,
        tiled=True,
    )
    picked = (
        back_rows.reshape(-1, model_width)[slot_index]
        .astype(jnp.float32)
        .reshape(-1, 2, model_width)
    )
    grad_normed_two = grad_normed_two + jnp.sum(picked, axis=1)
    _, second_back = jax.vjp(norm_mod, middle, mods[:, 3], mods[:, 4])
    grad_middle, grad_shift_two, grad_scale_two = second_back(
        grad_normed_two.reshape(item_count, -1, model_width)
    )
    grad_middle = grad_middle + grad_shaped
    grad_gate_one = jnp.sum(
        grad_middle * branch.reshape(item_count, -1, model_width), axis=1, keepdims=True
    )
    grad_branch = to_half((mods[:, 2] * grad_middle).reshape(-1, model_width))
    grad_w_out = product_tn(attended, grad_branch)
    grad_attended = to_half(product_nt(grad_branch, lin[:, 3 * model_width : 4 * model_width]))
    grad_qkv = attention_backward(qkv, log_sums, grad_attended, item_count)
    grad_w_qkv = product_tn(normed, grad_qkv)
    grad_normed = product_nt(grad_qkv, lin[:, : 3 * model_width])
    _, first_back = jax.vjp(
        norm_mod, tokens.reshape(item_count, -1, model_width), mods[:, 0], mods[:, 1]
    )
    grad_input, grad_shift_one, grad_scale_one = first_back(
        grad_normed.reshape(item_count, -1, model_width)
    )
    grad_input = grad_input + grad_middle
    grad_mods = jnp.stack(
        [
            grad_shift_one,
            grad_scale_one,
            grad_gate_one,
            grad_shift_two,
            grad_scale_two,
            grad_gate_two,
        ],
        axis=1,
    )
    grad_mods = grad_mods.reshape(item_count, 6 * model_width)
    grad_ada = jnp.dot(cond_act.T, grad_mods, precision=highest)
    grad_cond = jnp.dot(
        grad_mods,
        lin[:, 4 * model_width : 10 * model_width].astype(jnp.float32).T,
        precision=highest,
    )
    grad_lin = jnp.concatenate([grad_w_qkv, grad_w_out, grad_ada, grad_w_up], axis=1)
    grad_expert = jnp.stack([grad_up_exp, grad_down_exp], axis=1)
    return (grad_input.reshape(-1, model_width), grad_cond, grad_lin, grad_lout, grad_expert)


def adam_step(weight_in, gradient, first_in, second_in):
    first_new = beta_one * first_in + (1.0 - beta_one) * gradient
    second_new = beta_two * second_in + (1.0 - beta_two) * gradient * gradient
    first_hat = first_new / (1.0 - beta_one**STEP)
    second_hat = second_new / (1.0 - beta_two**STEP)
    stepped = weight_in - inner_rate * (
        first_hat / (jnp.sqrt(second_hat) + eps_adam) + weight_decay * weight_in
    )
    return (weight_in - stepped, first_new, second_new)


def per_device(
    patches,
    target_noise,
    timesteps,
    labels,
    routes,
    route_gates,
    stem_weights,
    layer_in,
    layer_out,
    experts,
    stem_first,
    layer_in_first,
    layer_out_first,
    experts_first,
    stem_second,
    layer_in_second,
    layer_out_second,
    experts_second,
    stem_moment,
    layer_in_moment,
    layer_out_moment,
    experts_moment,
):
    stem_all, lin_all, lout_all = (
        lax.all_gather(to_half(stem_weights), (LINE, CORE), axis=1, tiled=True),
        lax.all_gather(to_half(layer_in), (LINE, CORE), axis=2, tiled=True),
        lax.all_gather(to_half(layer_out), (LINE, CORE), axis=1, tiled=True),
    )
    expert_all = lax.all_gather(to_half(experts), CORE, axis=4, tiled=True)
    model_width = stem_all.shape[1]
    item_count = timesteps.shape[0]
    patch_w, time_one, time_two, table_w, final_ada, final_out = split_stem(stem_all)
    features = time_features(timesteps)
    hot_labels = label_table(labels)

    def condition(first_w, second_w, table_in):
        hidden_time = jax.nn.silu(jnp.dot(features, first_w, precision=highest))
        return jax.nn.silu(
            jnp.dot(hidden_time, second_w, precision=highest)
            + jnp.dot(hot_labels, table_in, precision=highest)
        )

    cond_act, cond_back = jax.vjp(
        condition,
        time_one.astype(jnp.float32),
        time_two.astype(jnp.float32),
        table_w.astype(jnp.float32),
    )
    tokens = product(patches, patch_w)
    tokens = (tokens.reshape(item_count, -1, model_width) + positions_table()[None]).reshape(
        -1, model_width
    )
    saved_all = []
    for layer_idx in range(LAYERS):
        tokens, saved = layer_forward(
            tokens,
            cond_act,
            lin_all[layer_idx],
            lout_all[layer_idx],
            expert_all[layer_idx],
            routes[layer_idx],
            route_gates[layer_idx],
        )
        saved_all.append(saved)
    final_ada_f = final_ada.astype(jnp.float32)
    final_mods = jnp.dot(cond_act, final_ada_f.T, precision=highest).reshape(
        item_count, 2, 1, model_width
    )
    final_pre, final_back = jax.vjp(
        norm_mod, tokens.reshape(item_count, -1, model_width), final_mods[:, 0], final_mods[:, 1]
    )
    final_normed = to_half(final_pre.reshape(-1, model_width))
    predicted = product_nt(final_normed, final_out)
    residual_err = predicted - target_noise
    loss_total = lax.psum(jnp.sum(residual_err * residual_err), (GROUP, LINE, CORE))
    grad_pred = to_half(2.0 * residual_err)
    grad_final_out = product_tn(grad_pred, final_normed)
    grad_final_normed = product(grad_pred, final_out)
    grad_tokens, grad_fshift, grad_fscale = final_back(
        grad_final_normed.reshape(item_count, -1, model_width)
    )
    grad_tokens = grad_tokens.reshape(-1, model_width)
    grad_final_mods = jnp.concatenate([grad_fshift, grad_fscale], axis=1).reshape(
        item_count, 2 * model_width
    )
    grad_final_ada = jnp.dot(grad_final_mods.T, cond_act, precision=highest)
    grad_cond = jnp.dot(grad_final_mods, final_ada_f, precision=highest)
    lin_grads = []
    lout_grads = []
    expert_grads = []
    for layer_idx in reversed(range(LAYERS)):
        grad_tokens, grad_cond_layer, grad_lin, grad_lout, grad_expert = layer_backward(
            grad_tokens,
            saved_all[layer_idx],
            cond_act,
            lin_all[layer_idx],
            lout_all[layer_idx],
            expert_all[layer_idx],
            route_gates[layer_idx],
        )
        grad_cond = grad_cond + grad_cond_layer
        lin_grads.append(grad_lin)
        lout_grads.append(grad_lout)
        expert_grads.append(grad_expert)
    lin_stack = jnp.stack(lin_grads[::-1])
    lout_stack = jnp.stack(lout_grads[::-1])
    expert_stack = jnp.stack(expert_grads[::-1])
    grad_patch = product_tn(patches, to_half(grad_tokens))
    grad_time_one, grad_time_two, grad_table = cond_back(grad_cond)
    grad_stem = jnp.concatenate(
        [grad_patch, grad_time_one, grad_time_two, grad_table, grad_final_ada, grad_final_out],
        axis=0,
    )
    stem_sum, lin_sum, lout_sum = (
        lax.psum_scatter(grad_stem, (LINE, CORE), scatter_dimension=1, tiled=True),
        lax.psum_scatter(lin_stack, (LINE, CORE), scatter_dimension=2, tiled=True),
        lax.psum_scatter(lout_stack, (LINE, CORE), scatter_dimension=1, tiled=True),
    )
    expert_sum = lax.psum_scatter(
        expert_stack.astype(jnp.bfloat16), CORE, scatter_dimension=4, tiled=True
    ).astype(jnp.float32)
    weights_all = (stem_weights, layer_in, layer_out, experts)
    gradients = (stem_sum, lin_sum, lout_sum, expert_sum)
    firsts = (stem_first, layer_in_first, layer_out_first, experts_first)
    seconds = (stem_second, layer_in_second, layer_out_second, experts_second)
    moments = (stem_moment, layer_in_moment, layer_out_moment, experts_moment)
    stepped = [
        adam_step(
            weights_all[array_idx],
            gradients[array_idx],
            firsts[array_idx][0],
            seconds[array_idx][0],
        )
        for array_idx in range(4)
    ]
    delta_all = (
        lax.psum(stepped[0][0].astype(jnp.bfloat16), GROUP).astype(jnp.float32),
        lax.psum(stepped[1][0].astype(jnp.bfloat16), GROUP).astype(jnp.float32),
        lax.psum(stepped[2][0].astype(jnp.bfloat16), GROUP).astype(jnp.float32),
        lax.psum(stepped[3][0].astype(jnp.bfloat16), GROUP).astype(jnp.float32),
    )
    group_count = lax.axis_size(GROUP)
    new_weights = []
    new_moments = []
    for array_idx in range(4):
        mean_delta = delta_all[array_idx] / group_count
        moment_new = outer_mom * moments[array_idx] + mean_delta
        new_weights.append(
            weights_all[array_idx] - outer_rate * (mean_delta + outer_mom * moment_new)
        )
        new_moments.append(moment_new)
    return (
        loss_total,
        new_weights[0],
        new_weights[1],
        new_weights[2],
        new_weights[3],
        to_half(new_weights[0]),
        to_half(new_weights[1]),
        to_half(new_weights[2]),
        to_half(new_weights[3]),
        stepped[0][1][None],
        stepped[1][1][None],
        stepped[2][1][None],
        stepped[3][1][None],
        stepped[0][2][None],
        stepped[1][2][None],
        stepped[2][2][None],
        stepped[3][2][None],
        new_moments[0],
        new_moments[1],
        new_moments[2],
        new_moments[3],
    )


bf16 = jnp.bfloat16
f32 = jnp.float32
MIB = 1024 * 1024
CHUNK = 768
FWD_ROWS = 256
BWD_ROWS = 256
STEM_SIZES = (PATCH_DIM, FREQ, D, CLASSES + 1, 2 * D, PATCH_DIM)
STEM_PADDED = tuple(-(-size // 128) * 128 for size in STEM_SIZES)
STEM_AT = tuple(sum(STEM_PADDED[:place]) for place in range(len(STEM_PADDED)))
STEM_LANES = -(-sum(STEM_PADDED) // 1024) * 1024


def dot_nn(left_in, right_in):
    return lax.dot_general(left_in, right_in, (((1,), (0,)), ((), ())), preferred_element_type=f32)


def dot_nt(left_in, right_in):
    return lax.dot_general(left_in, right_in, (((1,), (1,)), ((), ())), preferred_element_type=f32)


def dot_tn(left_in, right_in):
    return lax.dot_general(left_in, right_in, (((0,), (0,)), ((), ())), preferred_element_type=f32)


def three_parts(rows):
    high = rows.astype(bf16).astype(f32)
    rest = rows - high
    mid = rest.astype(bf16).astype(f32)
    low = rest - mid
    return jnp.concatenate([high, mid, low, jnp.zeros_like(low)], axis=0).astype(bf16)


def three_sum(stacked):
    return stacked[0:8] + stacked[8:16] + stacked[16:24]


def full_nt(rows, weight):
    return three_sum(dot_nt(three_parts(rows), weight))


def full_nn(rows, weight):
    return three_sum(dot_nn(three_parts(rows), weight))


def silu_slope(values):
    gate = 1.0 / (1.0 + jnp.exp(-values))
    return gate * (1.0 + values * (1.0 - gate))


def silu_of(values):
    return values / (1.0 + jnp.exp(-values))


def stem_piece(stem_ref, place):
    return stem_ref[:, STEM_AT[place] : STEM_AT[place] + STEM_PADDED[place]]


def cond_kernel(feat_ref, hot_ref, stem_ref, ada_ref, cond_ref, hid_ref, one_ref, two_ref, mods_ref, fin_ref):
    @pl.when(pl.program_id(0) == 0)
    def _():
        pre_one = full_nt(feat_ref[...], stem_piece(stem_ref, 1))
        hidden = silu_of(pre_one)
        pre_two = full_nt(hidden, stem_piece(stem_ref, 2)) + dot_nt(hot_ref[...], stem_piece(stem_ref, 3))[0:8]
        cond = silu_of(pre_two)
        one_ref[...] = pre_one
        two_ref[...] = pre_two
        hid_ref[...] = hidden
        cond_ref[...] = cond
        fin_ref[...] = full_nn(cond, stem_piece(stem_ref, 4))

    for layer in range(LAYERS):
        mods_ref[layer] = full_nt(cond_ref[...], ada_ref[layer])


def cond_back_kernel(gm_a, gm_b, gf_ref, one_ref, two_ref, stem_ref, ada_ref, done_ref, dtwo_ref):
    @pl.when(pl.program_id(0) == 0)
    def _():
        dtwo_ref[...] = full_nt(gf_ref[...], stem_piece(stem_ref, 4))

    dtwo_ref[...] += full_nn(gm_a[...], ada_ref[0]) + full_nn(gm_b[...], ada_ref[1])

    @pl.when(pl.program_id(0) == pl.num_programs(0) - 1)
    def _():
        dtwo = dtwo_ref[...] * silu_slope(two_ref[...])
        dtwo_ref[...] = dtwo
        done_ref[...] = full_nn(dtwo, stem_piece(stem_ref, 2)) * silu_slope(one_ref[...])


def norm_parts(values):
    centre = values - jnp.mean(values, axis=-1, keepdims=True)
    spread = jnp.mean(centre * centre, axis=-1, keepdims=True)
    root = lax.rsqrt(spread + ln_eps)
    return centre * root, root


def norm_back(values, scale_in, gradient):
    unit, root = norm_parts(values)
    grad_unit = gradient * (1.0 + scale_in)
    inner = jnp.mean(grad_unit * unit, axis=-1, keepdims=True)
    grad_in = root * (grad_unit - jnp.mean(grad_unit, axis=-1, keepdims=True) - unit * inner)
    return (
        grad_in,
        jnp.sum(gradient, axis=0, keepdims=True),
        jnp.sum(gradient * unit, axis=0, keepdims=True),
    )


def mod_row(mods_ref, item, place):
    return mods_ref[pl.ds(item, 1), place * D : (place + 1) * D]


def head_masks():
    lane = lax.broadcasted_iota(jnp.int32, (1, 128), 1)
    return lane, [(lane // 64 == half).astype(f32).astype(bf16) for half in range(2)]


def attn_fwd_kernel(x_ref, mods_ref, w_ref, normed_ref, qkv_ref, att_ref, branch_ref, mid_ref, n2_ref):
    item = pl.program_id(0)
    tokens = x_ref[...]
    unit, _ = norm_parts(tokens)
    normed = (unit * (1.0 + mod_row(mods_ref, item, 1)) + mod_row(mods_ref, item, 0)).astype(bf16)
    normed_ref[...] = normed
    qkv_ref[...] = dot_nt(normed, w_ref[0 : 3 * D, :]).astype(bf16)
    lane, masks = head_masks()
    for pair in range(HEADS // 2):
        at = pair * 128
        queries = qkv_ref[:, at : at + 128]
        keys = qkv_ref[:, D + at : D + at + 128]
        vals = qkv_ref[:, 2 * D + at : 2 * D + at + 128]
        outs = []
        for half in range(2):
            scores = dot_nt(queries * masks[half], keys) * 0.125
            powers = jnp.exp(scores - jnp.max(scores, axis=-1, keepdims=True))
            probs = (powers * (1.0 / jnp.sum(powers, axis=-1, keepdims=True))).astype(bf16)
            outs.append(dot_nn(probs, vals))
        att_ref[:, at : at + 128] = jnp.where(lane < 64, outs[0], outs[1]).astype(bf16)
    branch = dot_nt(att_ref[...], w_ref[3 * D : 4 * D, :])
    branch_ref[...] = branch
    middle = tokens + mod_row(mods_ref, item, 2) * branch
    mid_ref[...] = middle
    unit, _ = norm_parts(middle)
    n2_ref[...] = (unit * (1.0 + mod_row(mods_ref, item, 4)) + mod_row(mods_ref, item, 3)).astype(bf16)


def attn_bwd_kernel(
    gn2_ref, g_ref, mid_ref, x_ref, normed_ref, qkv_ref, att_ref, branch_ref, mods_ref, gg_ref, w_ref,
    gx_ref, gmods_ref, dw_ref, dqkv, acc,
):
    item = pl.program_id(0)

    @pl.when(item == 0)
    def _():
        acc[...] = jnp.zeros_like(acc)
        gmods_ref[...] = jnp.zeros_like(gmods_ref)

    grad_mid, dshift, dscale = norm_back(mid_ref[...], mod_row(mods_ref, item, 4), gn2_ref[...])
    grad_mid = grad_mid + g_ref[...]
    dgate = jnp.sum(grad_mid * branch_ref[...], axis=0, keepdims=True)
    gmods_ref[pl.ds(item, 1), 2 * D : 3 * D] = dgate
    gmods_ref[pl.ds(item, 1), 3 * D : 4 * D] = dshift
    gmods_ref[pl.ds(item, 1), 4 * D : 5 * D] = dscale
    gmods_ref[pl.ds(item, 1), 5 * D : 6 * D] = gg_ref[pl.ds(item, 1), :]
    grad_branch = (mod_row(mods_ref, item, 2) * grad_mid).astype(bf16)
    acc[3 * D : 4 * D, :] += dot_tn(grad_branch, att_ref[...])
    grad_att = dot_nn(grad_branch, w_ref[3 * D : 4 * D, :]).astype(bf16)
    lane, masks = head_masks()
    for pair in range(HEADS // 2):
        at = pair * 128
        queries = qkv_ref[:, at : at + 128]
        keys = qkv_ref[:, D + at : D + at + 128]
        vals = qkv_ref[:, 2 * D + at : 2 * D + at + 128]
        grad_out = grad_att[:, at : at + 128]
        parts = []
        for half in range(2):
            scores = dot_nt(queries * masks[half], keys) * 0.125
            powers = jnp.exp(scores - jnp.max(scores, axis=-1, keepdims=True))
            probs = powers * (1.0 / jnp.sum(powers, axis=-1, keepdims=True))
            grad_vals = dot_tn(probs.astype(bf16), grad_out)
            grad_probs = dot_nt(grad_out * masks[half], vals)
            inner = jnp.sum(probs * grad_probs, axis=-1, keepdims=True)
            grad_scores = (probs * (grad_probs - inner)).astype(bf16)
            parts.append((dot_nn(grad_scores, keys) * 0.125, dot_tn(grad_scores, queries) * 0.125, grad_vals))
        for place in range(3):
            dqkv[:, place * D + at : place * D + at + 128] = jnp.where(
                lane < 64, parts[0][place], parts[1][place]
            ).astype(bf16)
    acc[0 : 3 * D, :] += dot_tn(dqkv[...], normed_ref[...])
    grad_normed = dot_nn(dqkv[...], w_ref[0 : 3 * D, :])
    grad_in, dshift, dscale = norm_back(x_ref[...], mod_row(mods_ref, item, 1), grad_normed)
    gx_ref[...] = grad_in + grad_mid
    gmods_ref[pl.ds(item, 1), 0:D] = dshift
    gmods_ref[pl.ds(item, 1), D : 2 * D] = dscale

    @pl.when(item == pl.num_programs(0) - 1)
    def _():
        dw_ref[0 : 4 * D, :] = acc[...].astype(bf16)
        dw_ref[4 * D :, :] = jnp.zeros_like(dw_ref[4 * D :, :])


def gelu_both(values):
    outer = 0.7978845608028654
    cubic = outer * 0.044715
    square = values * values
    angle = jnp.tanh(values * (square * cubic + outer))
    half = 0.5 * values
    above = 1.0 + angle
    slope = above * (half * (square * (3.0 * cubic) + outer) * (1.0 - angle) + 0.5)
    return (half * above).astype(bf16), slope.astype(bf16)


def gate_column(g4_ref, rows, expert):
    gates = g4_ref[rows, :]
    lane = lax.broadcasted_iota(jnp.int32, gates.shape, 1)
    return jnp.sum(jnp.where(lane == expert, gates, 0.0), axis=1, keepdims=True)


def ffn_fwd_kernel(shared_steps, halves, gathers, n2_ref, mid_ref, mods_ref, g4_ref, up_ref, dn_ref, ex_ref, *rest):
    step = pl.program_id(0)
    given, (act_ref, dg_ref, mixed_ref, x_ref) = rest[:gathers], rest[gathers : gathers + 4]
    taken, (acc, racc), sems = rest[gathers + 4 : 2 * gathers + 4], rest[2 * gathers + 4 : 2 * gathers + 6], rest[2 * gathers + 6 :]
    if gathers:
        gather_beside(step, pl.num_programs(0) - 1, given, taken, sems)
    items = n2_ref.shape[0] // PATCHES

    @pl.when(step == 0)
    def _():
        acc[...] = jnp.zeros_like(acc)
        racc[...] = jnp.zeros_like(racc)

    @pl.when(step < shared_steps)
    def _():
        for block in range(n2_ref.shape[0] // FWD_ROWS):
            rows = pl.ds(block * FWD_ROWS, FWD_ROWS)
            active, slope = gelu_both(dot_nt(n2_ref[rows, :], up_ref[...]))
            act_ref[0, rows, :] = active
            dg_ref[0, rows, :] = slope
            acc[rows, :] += dot_nn(active, dn_ref[...])

    @pl.when(step >= shared_steps)
    def _():
        for block in range(n2_ref.shape[0] // FWD_ROWS):
            rows = pl.ds(block * FWD_ROWS, FWD_ROWS)
            active, slope = gelu_both(dot_nn(n2_ref[rows, :], ex_ref[0, 0]))
            act_ref[0, rows, :] = active
            dg_ref[0, rows, :] = slope
            racc[rows, :] += dot_nt(active, ex_ref[0, 1])

    expert, half = (step - shared_steps) // halves, (step - shared_steps) % halves

    @pl.when((step >= shared_steps) & (half == halves - 1))
    def _():
        for item in range(items):
            rows = pl.ds(item * PATCHES, PATCHES)
            acc[rows, :] += gate_column(g4_ref, rows, expert) * racc[rows, :].astype(bf16).astype(f32)
            racc[rows, :] = jnp.zeros((PATCHES, D), f32)

    @pl.when(step == pl.num_programs(0) - 1)
    def _():
        mixed_ref[...] = acc[...]
        for item in range(items):
            rows = pl.ds(item * PATCHES, PATCHES)
            x_ref[rows, :] = mid_ref[rows, :] + mod_row(mods_ref, item, 5) * acc[rows, :]


def ffn_bwd_kernel(
    shared_steps, halves, g_ref, n2_ref, mods_ref, g4_ref, mixed_ref, act_ref, dg_ref, up_ref, dn_ref, ex_ref,
    dup_ref, ddn_ref, dex_ref, gn2_ref, gg_ref, gmix, gs, gst, n2t, din, acc, racc,
):
    step = pl.program_id(0)
    items = n2_ref.shape[0] // PATCHES

    @pl.when(step == 0)
    def _():
        gg_ref[...] = jnp.zeros_like(gg_ref)
        dup_ref[0:D, :] = jnp.zeros((D, D), bf16)
        for item in range(items):
            rows = pl.ds(item * PATCHES, PATCHES)
            grad = g_ref[rows, :]
            gg_ref[pl.ds(item, 1), :] = jnp.sum(grad * mixed_ref[rows, :], axis=0, keepdims=True)
            grad = mod_row(mods_ref, item, 5) * grad
            gmix[rows, :] = grad
            gs[rows, :] = grad.astype(bf16)
            gst[:, rows] = grad.astype(bf16).T
            n2t[:, rows] = n2_ref[rows, :].T
        acc[...] = jnp.zeros_like(acc)
        racc[...] = jnp.zeros_like(racc)

    @pl.when(step < shared_steps)
    def _():
        for block in range(n2_ref.shape[0] // BWD_ROWS):
            rows = pl.ds(block * BWD_ROWS, BWD_ROWS)
            inner = (dot_nt(gs[rows, :], dn_ref[...]) * dg_ref[0, rows, :].astype(f32)).astype(bf16)
            din[rows, :] = inner
            acc[rows, :] += dot_nn(inner, up_ref[...])
        at = dup_ref.shape[0] - shared_steps * CHUNK + step * CHUNK
        dup_ref[pl.ds(pl.multiple_of(at, D), CHUNK), :] = dot_nn(n2t[...], din[...]).astype(bf16).T
        ddn_ref[...] = dot_nn(gst[...], act_ref[0]).astype(bf16).T

    @pl.when(step >= shared_steps)
    def _():
        expert, half = (step - shared_steps) // halves, (step - shared_steps) % halves

        @pl.when(half == 0)
        def _():
            for item in range(items):
                rows = pl.ds(item * PATCHES, PATCHES)
                grad = (gate_column(g4_ref, rows, expert) * gmix[rows, :]).astype(bf16)
                gs[rows, :] = grad
                gst[:, rows] = grad.T

        for block in range(n2_ref.shape[0] // BWD_ROWS):
            rows = pl.ds(block * BWD_ROWS, BWD_ROWS)
            inner = (dot_nn(gs[rows, :], ex_ref[0, 1]) * dg_ref[0, rows, :].astype(f32)).astype(bf16)
            din[rows, :] = inner
            racc[rows, :] += dot_nt(inner, ex_ref[0, 0])

        dex_ref[0, 0] = dot_nn(n2t[...], din[...]).astype(bf16)
        dex_ref[0, 1] = dot_nn(gst[...], act_ref[0]).astype(bf16)

        @pl.when(half == halves - 1)
        def _():
            acc[...] += racc[...].astype(bf16).astype(f32)
            racc[...] = jnp.zeros_like(racc)

    @pl.when(step == pl.num_programs(0) - 1)
    def _():
        gn2_ref[...] = acc[...]


def final_kernel(x_ref, mods_ref, fo_ref, tgt_ref, gx_ref, gfm_ref, dfo_ref, loss_ref):
    item = pl.program_id(0)

    @pl.when(item == 0)
    def _():
        gfm_ref[...] = jnp.zeros_like(gfm_ref)
        dfo_ref[...] = jnp.zeros_like(dfo_ref)
        loss_ref[...] = jnp.zeros_like(loss_ref)

    tokens = x_ref[...]
    unit, _ = norm_parts(tokens)
    scale = mod_row(mods_ref, item, 1)
    normed = (unit * (1.0 + scale) + mod_row(mods_ref, item, 0)).astype(bf16)
    err = dot_nt(fo_ref[...], normed) - tgt_ref[...]
    loss_ref[...] += jnp.sum(err * err, axis=1, keepdims=True)
    grad_pred = (2.0 * err).astype(bf16)
    dfo_ref[...] += dot_nn(grad_pred, normed)
    grad_in, dshift, dscale = norm_back(tokens, scale, dot_tn(grad_pred, fo_ref[...]))
    gx_ref[...] = grad_in
    gfm_ref[pl.ds(item, 1), 0:D] = dshift
    gfm_ref[pl.ds(item, 1), D : 2 * D] = dscale


def params(limit):
    return pltpu.CompilerParams(vmem_limit_bytes=limit * MIB)


def cost(multiplies, moved):
    return pl.CostEstimate(flops=2 * multiplies, bytes_accessed=moved, transcendentals=0)


def whole(shape):
    return pl.BlockSpec(shape, lambda step: (0,) * len(shape))


def rows_of(width):
    return pl.BlockSpec((PATCHES, width), lambda step: (step, 0))


def shape_of(shape, kind):
    return jax.ShapeDtypeStruct(shape, kind)


ADA_STEPS = 6 * D // CHUNK
ADA_AT = 4 * D // CHUNK


def cond_forward(feat, hot, stem_t, lin):
    shapes = [(8, D)] * 4 + [(LAYERS, 8, 6 * D), (8, 2 * D)]
    return pl.pallas_call(
        cond_kernel,
        grid=(ADA_STEPS,),
        in_specs=[
            whole(feat.shape),
            whole(hot.shape),
            whole(stem_t.shape),
            pl.BlockSpec((LAYERS, CHUNK, D), lambda step: (0, ADA_AT + step, 0)),
        ],
        out_specs=[whole((8, D))] * 4 + [pl.BlockSpec((LAYERS, 8, CHUNK), lambda step: (0, 0, step)), whole((8, 2 * D))],
        out_shape=[shape_of(shape, f32) for shape in shapes],
        compiler_params=params(60),
        name="cond_forward",
    )(feat, hot, stem_t, lin)


def cond_backward(gm_a, gm_b, gfm, pre_one, pre_two, stem_t, lin):
    columns = pl.BlockSpec((8, CHUNK), lambda step: (0, step))
    return pl.pallas_call(
        cond_back_kernel,
        grid=(ADA_STEPS,),
        in_specs=[columns, columns, whole(gfm.shape), whole((8, D)), whole((8, D)), whole(stem_t.shape)]
        + [pl.BlockSpec((LAYERS, CHUNK, D), lambda step: (0, ADA_AT + step, 0))],
        out_specs=[whole((8, D))] * 2,
        out_shape=[shape_of((8, D), f32)] * 2,
        compiler_params=params(60),
        name="cond_backward",
    )(gm_a, gm_b, gfm, pre_one, pre_two, stem_t, lin)


def attn_forward(layer, tokens, mods, lin):
    count = tokens.shape[0]
    return pl.pallas_call(
        attn_fwd_kernel,
        grid=(count // PATCHES,),
        in_specs=[rows_of(D), whole(mods.shape), attn_weights(layer)],
        out_specs=[rows_of(D), rows_of(3 * D), rows_of(D), rows_of(D), rows_of(D), rows_of(D)],
        out_shape=[
            shape_of((count, D), bf16),
            shape_of((count, 3 * D), bf16),
            shape_of((count, D), bf16),
            shape_of((count, D), f32),
            shape_of((count, D), f32),
            shape_of((count, D), bf16),
        ],
        compiler_params=params(60),
        cost_estimate=cost(count * D * 4 * D * 9, 16 * count * D),
        name="attention_forward",
    )(tokens, mods, lin)


def attn_weights(layer):
    return pl.BlockSpec((None, 4 * D, D), lambda step: (layer, 0, 0))


def attn_backward(layer, gn2, grad, middle, tokens, normed, qkv, attended, branch, mods, grad_gate, lin, out_rows):
    count = tokens.shape[0]
    return pl.pallas_call(
        attn_bwd_kernel,
        grid=(count // PATCHES,),
        in_specs=[rows_of(D)] * 5
        + [rows_of(3 * D), rows_of(D), rows_of(D), whole(mods.shape), whole(grad_gate.shape), attn_weights(layer)],
        out_specs=[rows_of(D), whole((8, 6 * D)), whole((out_rows, D))],
        out_shape=[shape_of((count, D), f32), shape_of((8, 6 * D), f32), shape_of((out_rows, D), bf16)],
        scratch_shapes=[pltpu.VMEM((PATCHES, 3 * D), bf16), pltpu.VMEM((4 * D, D), f32)],
        compiler_params=params(60),
        cost_estimate=cost(count * D * 4 * D * 22, 16 * count * D),
        name="attention_backward",
    )(gn2, grad, middle, tokens, normed, qkv, attended, branch, mods, grad_gate, lin)


def weight_specs(layer, shared_steps, lin_rows):
    up_at = lin_rows // CHUNK - shared_steps
    return [
        pl.BlockSpec((None, CHUNK, D), lambda step: (layer, up_at + jnp.minimum(step, shared_steps - 1), 0)),
        pl.BlockSpec((CHUNK, D), lambda step: (jnp.minimum(step, shared_steps - 1), 0)),
        pl.BlockSpec((1, 2, D, CHUNK), lambda step: (jnp.maximum(step - shared_steps, 0), 0, 0, 0)),
    ]


def ffn_forward(layer, n2, middle, mods, g4, lin, lout, experts_w, halves, beside=()):
    count = n2.shape[0]
    shared_steps = lout.shape[0] // CHUNK
    steps = shared_steps + experts_w.shape[0]
    wide = pl.BlockSpec((1, count, CHUNK), lambda step: (step, 0, 0))
    anywhere = [pl.BlockSpec(memory_space=pl.ANY)] * len(beside)
    remote = pltpu.CompilerParams(vmem_limit_bytes=60 * MIB, collective_id=7, has_side_effects=True)
    return pl.pallas_call(
        functools.partial(ffn_fwd_kernel, shared_steps, halves, len(beside)),
        grid=(steps,),
        in_specs=[whole(n2.shape), whole(middle.shape), whole(mods.shape), whole(g4.shape)]
        + weight_specs(layer, shared_steps, lin.shape[1])
        + anywhere,
        out_specs=[wide, wide, whole((count, D)), whole((count, D))] + anywhere,
        out_shape=[
            shape_of((steps, count, CHUNK), bf16),
            shape_of((steps, count, CHUNK), bf16),
            shape_of((count, D), f32),
            shape_of((count, D), f32),
        ]
        + [shape_of((8,) + part.shape, bf16) for part in beside],
        scratch_shapes=[pltpu.VMEM((count, D), f32)] * 2 + (gather_semaphores(4) if beside else []),
        compiler_params=remote if beside else params(60),
        cost_estimate=cost(4 * steps * count * D * CHUNK * 2, 8 * steps * count * CHUNK),
        name="ffn_forward",
    )(n2, middle, mods, g4, lin, lout, experts_w, *beside)


def ffn_backward(layer, grad, n2, mods, g4, mixed, active, slope, lin, lout, experts_w, halves):
    count = n2.shape[0]
    shared_steps = lout.shape[0] // CHUNK
    steps = shared_steps + experts_w.shape[0]
    wide = pl.BlockSpec((1, count, CHUNK), lambda step: (step, 0, 0))
    specs = weight_specs(layer, shared_steps, lin.shape[1])
    return pl.pallas_call(
        functools.partial(ffn_bwd_kernel, shared_steps, halves),
        grid=(steps,),
        in_specs=[whole(grad.shape), whole(n2.shape), whole(mods.shape), whole(g4.shape), whole(mixed.shape), wide, wide]
        + specs,
        out_specs=[whole((lout.shape[0] + D, D)), specs[1], specs[2], whole((count, D)), whole((8, D))],
        out_shape=[
            shape_of((lout.shape[0] + D, D), bf16),
            shape_of(lout.shape, bf16),
            shape_of(experts_w.shape, bf16),
            shape_of((count, D), f32),
            shape_of((8, D), f32),
        ],
        scratch_shapes=[
            pltpu.VMEM((count, D), f32),
            pltpu.VMEM((count, D), bf16),
            pltpu.VMEM((D, count), bf16),
            pltpu.VMEM((D, count), bf16),
            pltpu.VMEM((count, CHUNK), bf16),
            pltpu.VMEM((count, D), f32),
            pltpu.VMEM((count, D), f32),
        ],
        compiler_params=params(60),
        cost_estimate=cost(4 * steps * count * D * CHUNK * 4 // 2, 8 * steps * count * CHUNK),
        name="ffn_backward",
    )(grad, n2, mods, g4, mixed, active, slope, lin, lout, experts_w)


def final_step(tokens, mods, fo_rows, target_t):
    count = tokens.shape[0]
    return pl.pallas_call(
        final_kernel,
        grid=(count // PATCHES,),
        in_specs=[
            rows_of(D),
            whole(mods.shape),
            whole(fo_rows.shape),
            pl.BlockSpec((PATCH_DIM, PATCHES), lambda step: (0, step)),
        ],
        out_specs=[rows_of(D), whole((8, 2 * D)), whole((PATCH_DIM, D)), whole((PATCH_DIM, 1))],
        out_shape=[
            shape_of((count, D), f32),
            shape_of((8, 2 * D), f32),
            shape_of((PATCH_DIM, D), f32),
            shape_of((PATCH_DIM, 1), f32),
        ],
        compiler_params=params(60),
        name="final_step",
    )(tokens, mods, fo_rows, target_t)


def update_kernel(groups, grad_a, grad_b, total_a, total_b, w_ref, f_ref, s_ref, m_ref, new_ref, half_ref, fn_ref, sn_ref, mn_ref):
    for layer, (grad_ref, total_ref) in enumerate(((grad_a, total_a), (grad_b, total_b))):

        @pl.when(pl.program_id(0) == layer)
        def _(grad_ref=grad_ref, total_ref=total_ref):
            gradient = grad_ref[...]
            fn_ref[0] = beta_one * f_ref[0] + (1.0 - beta_one) * gradient
            sn_ref[0] = beta_two * s_ref[0] + (1.0 - beta_two) * gradient * gradient
            mean_delta = total_ref[...] / groups
            moment_new = outer_mom * m_ref[0] + mean_delta
            weight = w_ref[0] - outer_rate * (mean_delta + outer_mom * moment_new)
            mn_ref[0] = moment_new
            new_ref[0] = weight
            half_ref[0] = weight.astype(bf16)


def update_arrays(tile, grads, totals, weight, first, second, moment):
    layers, rows, width = weight.shape
    tiles = rows // tile
    state = pl.BlockSpec((1, tile, width), lambda layer, step: (layer, step, 0))
    early = pl.BlockSpec((tile, width), lambda layer, step: (jnp.where(layer == 0, step, tiles - 1), 0))
    late = pl.BlockSpec((tile, width), lambda layer, step: (jnp.where(layer == 0, 0, step), 0))
    return pl.pallas_call(
        functools.partial(update_kernel, lax.axis_size(GROUP)),
        grid=(layers, tiles),
        in_specs=[early, late, early, late] + [state] * 4,
        out_specs=[state] * 5,
        out_shape=[shape_of(weight.shape, kind) for kind in (f32, bf16, f32, f32, f32)],
        compiler_params=params(60),
        name="update_arrays",
    )(*grads, *totals, weight, first, second, moment)


def pad_rows(values):
    return jnp.pad(values, ((0, 8 - values.shape[0]), (0, 0)))


def stem_lanes(stem_t):
    pieces, at = [], 0
    for size, padded in zip(STEM_SIZES, STEM_PADDED):
        pieces.append(jnp.pad(stem_t[:, at : at + size], ((0, 0), (0, padded - size))))
        at = at + size
    pieces.append(jnp.zeros((stem_t.shape[0], STEM_LANES - sum(STEM_PADDED)), stem_t.dtype))
    return jnp.concatenate(pieces, axis=1)


MESH_ID = pl.DeviceIdType.MESH
TILE = 48


def plane_partners():
    group = lax.axis_index(GROUP)
    return {GROUP: group + 1 - 2 * lax.rem(group, 2)}, {GROUP: lax.rem(group + 2, 4)}


def greet(partners, line_at, line_size):
    barrier = pltpu.get_barrier_semaphore()
    for partner in partners:
        pl.semaphore_signal(barrier, inc=1, device_id=partner, device_id_type=MESH_ID)

    @pl.when(line_at > 0)
    def _():
        pl.semaphore_signal(barrier, inc=1, device_id={LINE: line_at - 1}, device_id_type=MESH_ID)

    @pl.when(line_at < line_size - 1)
    def _():
        pl.semaphore_signal(barrier, inc=1, device_id={LINE: line_at + 1}, device_id_type=MESH_ID)

    ends = jnp.where(line_at == 0, 1, 0) + jnp.where(line_at == line_size - 1, 1, 0)
    pl.semaphore_wait(barrier, len(partners) + 2 - ends)


def row_tiles(rows, body):
    def step(index, carry):
        body(pl.ds(pl.multiple_of(index * TILE, TILE), TILE))
        return carry

    lax.fori_loop(0, rows // TILE, step, 0)


def adam_delta(weight, gradient, first, second):
    return adam_step(weight, gradient, first, second)[0]


def reduce_units():
    units = []
    for matrix in range(2):
        for half in range(2):
            units.append((0, matrix, half * D // 2, D // 2, CHUNK, ()))
    for half in range(2):
        units.append((1, 0, half * 432, 432, D, (1,)))
    units.append((2, 0, 0, D, D, ()))
    return units


def reduce_kernel(
    layer, with_stem, dex, dqkvo, dup, ddn, extra, ex_w, ex_f, ex_s, li_w, li_f, li_s, lo_w, lo_f, lo_s, *rest
):
    if with_stem:
        stem_in, *rest, stem_sem, stem_send, stem_recv, stem_a, stem_b, stem_c, stem_d = rest
        stem_out = rest.pop(6)
    g_ex, g_li, g_lo, m_ex, m_li, m_lo, *scratch = rest
    units = reduce_units()
    number = len(units)
    banks = [scratch[at * number : (at + 1) * number] for at in range(9)]
    chip, local, came, delta, swapped, swapped_two, weight, first, second = banks
    extra_buf = scratch[9 * number]
    core_send, core_recv, line_send, line_recv, load_sem, plane_send, plane_recv, out_sem = scratch[9 * number + 1 :]
    at = lax.axis_index(LINE)
    core = lax.axis_index(CORE)
    sibling = {CORE: 1 - core}
    side_x, side_y = plane_partners()
    greet([sibling, side_x, side_y], at, 4)

    def pieces(unit, which):
        kind, matrix, row, rows, _, _ = units[unit]
        if kind == 0:
            return [(dex.at[:, which, matrix, pl.ds(row, rows)], slice(0, 4))]
        if kind == 2:
            return [(ddn.at[:, which, pl.ds(row, rows)], slice(0, 4))]
        return [
            (dqkvo.at[which, pl.ds(row, rows)], 0),
            (dup.at[0, which, pl.ds(row, rows)], 2),
            (dup.at[1, which, pl.ds(row, rows)], 3),
        ]

    def dest(bank, unit, where):
        return bank[unit].at[pl.ds(0, 4)] if isinstance(where, slice) else bank[unit].at[where]

    if with_stem:
        load = pltpu.make_async_copy(stem_in, stem_a, stem_sem.at[0])
        load.start()
        load.wait()

    def stem_copies(second_step):
        landing, sides = ((stem_b, (side_x, side_y)), (stem_c, (side_y, side_x)))[second_step]
        return [
            pltpu.make_async_remote_copy(
                stem_a.at[pl.ds(begin, size)], landing.at[pl.ds(begin, size)], stem_send.at[2 * second_step + half],
                stem_recv.at[2 * second_step + half], device_id=sides[half], device_id_type=MESH_ID,
            )
            for half, (begin, size) in enumerate(((0, 16), (16, 32)))
        ]

    def stem_turn(turn):
        if not with_stem or turn > 2:
            return
        if turn == 0:
            for copy in stem_copies(0):
                copy.start()
        elif turn == 1:
            for copy in stem_copies(0):
                copy.wait()
            stem_a[...] = (stem_a[...].astype(f32) + stem_b[...].astype(f32)).astype(bf16)
            for copy in stem_copies(1):
                copy.start()
        else:
            for copy in stem_copies(1):
                copy.wait()
            stem_d[...] = stem_a[...].astype(f32) + stem_c[...].astype(f32)
            pltpu.make_async_copy(stem_d, stem_out, stem_sem.at[1]).start()

    given, loads = [], []
    for unit in range(number):
        given.append([])
        for place, (source, where) in enumerate(pieces(unit, 1 - core)):
            copy = pltpu.make_async_remote_copy(
                source, dest(chip, unit, where), core_send.at[unit, place], core_recv.at[unit, place],
                device_id=sibling, device_id_type=MESH_ID,
            )
            copy.start()
            given[unit].append(copy)
        loads.append([])
        for place, (source, where) in enumerate(pieces(unit, core)):
            copy = pltpu.make_async_copy(source, dest(local, unit, where), load_sem.at[unit, place])
            copy.start()
            loads[unit].append(copy)
    state_loads = []
    for unit, (kind, matrix, row, rows, _, _) in enumerate(units):
        if kind == 0:
            sources = [ex_w.at[layer, 0, matrix], ex_f.at[0, layer, 0, matrix], ex_s.at[0, layer, 0, matrix]]
        elif kind == 1:
            sources = [li_w.at[layer], li_f.at[layer], li_s.at[layer]]
        else:
            sources = [lo_w.at[layer], lo_f.at[0, layer], lo_s.at[0, layer]]
        state_loads.append([])
        for place, (source, bank) in enumerate(zip(sources, (weight, first, second))):
            copy = pltpu.make_async_copy(source.at[pl.ds(row, rows)], bank[unit], load_sem.at[unit, 3 + place])
            copy.start()
            state_loads[unit].append(copy)
    extra_load = pltpu.make_async_copy(extra, extra_buf, load_sem.at[number, 0])
    extra_load.start()

    def line_copy(unit, owner, step, place):
        slot = 4 if step == -1 and owner == place - 1 else owner
        return pltpu.make_async_remote_copy(
            chip[unit].at[owner], came[unit].at[slot], line_send.at[unit, owner], line_recv.at[unit, slot],
            device_id={LINE: at + step}, device_id_type=MESH_ID,
        )

    def arrived(unit, slot):
        pltpu.make_async_remote_copy(
            came[unit].at[slot], came[unit].at[slot], line_send.at[unit, 0], line_recv.at[unit, slot],
            device_id=sibling, device_id_type=MESH_ID,
        ).wait_recv()

    routes_of = {0: [(3, 1), (2, 1), (1, 1)], 1: [(3, 1), (2, 1), (0, -1)], 2: [(0, -1), (1, -1), (3, 1)], 3: [(0, -1), (1, -1), (2, -1)]}
    finals = {0: [4], 1: [1, 4], 2: [2, 4], 3: [3]}

    for unit, (kind, matrix, row, rows, _, absent) in enumerate(units):
        for copy in given[unit]:
            copy.wait_recv()
        for copy in loads[unit]:
            copy.wait()
        for owner in range(4):
            if owner in absent:
                chip[unit][owner] = jnp.zeros(chip[unit].shape[1:], bf16)
                continue

            def add(tile, owner=owner, unit=unit):
                total = chip[unit][owner, tile, :].astype(f32) + local[unit][owner, tile, :].astype(f32)
                chip[unit][owner, tile, :] = total.astype(bf16)

            row_tiles(rows, add)
        for end in (0, 3):

            @pl.when(at == end)
            def _(unit=unit, end=end, absent=absent):
                for owner, step in routes_of[end]:
                    if owner not in absent:
                        line_copy(unit, owner, step, end).start()
                came[unit][0 if end == 0 else 4] = jnp.zeros(chip[unit].shape[1:], bf16)

        for owner in absent:

            @pl.when(at == owner)
            def _(unit=unit, owner=owner):
                came[unit][owner] = jnp.zeros(chip[unit].shape[1:], bf16)
                came[unit][4] = jnp.zeros(chip[unit].shape[1:], bf16)

    def forward(unit):
        rows, absent = units[unit][3], units[unit][5]
        for middle in (1, 2):

            @pl.when(at == middle)
            def _(middle=middle):
                for owner, step in routes_of[middle]:
                    if owner in absent:
                        continue
                    arrived(unit, owner)

                    def add(tile, owner=owner):
                        total = chip[unit][owner, tile, :].astype(f32) + came[unit][owner, tile, :].astype(f32)
                        chip[unit][owner, tile, :] = total.astype(bf16)

                    row_tiles(rows, add)
                    line_copy(unit, owner, step, middle).start()

    def plane_copies(unit, second_step):
        rows = units[unit][3]
        middle = rows // 32 * 16
        sides = (side_y, side_x) if second_step else (side_x, side_y)
        landing = swapped_two if second_step else swapped
        copies = []
        for half, (begin, size) in enumerate(((0, middle), (middle, rows - middle))):
            part = pl.ds(begin, size)
            copies.append(
                pltpu.make_async_remote_copy(
                    delta[unit].at[part], landing[unit].at[part], plane_send.at[unit, 2 * second_step + half],
                    plane_recv.at[unit, 2 * second_step + half], device_id=sides[half], device_id_type=MESH_ID,
                )
            )
        return copies

    def out_copy(unit, means):
        kind, matrix, row, rows, _, _ = units[unit]
        target = ((g_ex.at[matrix], g_li, g_lo), (m_ex.at[matrix], m_li, m_lo))[means][kind]
        source = first[unit] if means else weight[unit]
        return pltpu.make_async_copy(source, target.at[pl.ds(row, rows)], out_sem.at[unit, means])

    firsts, seconds = {}, {}

    def finish(unit):
        kind, matrix, row, rows, _, absent = units[unit]
        for place in range(4):

            @pl.when(at == place)
            def _(place=place):
                if place not in absent:
                    for slot in finals[place]:
                        arrived(unit, slot)

        for copy in state_loads[unit]:
            copy.wait()
        if kind == 1 and row == 0:
            extra_load.wait()

        def body(tile):
            grad = chip[unit][at, tile, :].astype(f32) + came[unit][at, tile, :].astype(f32)
            grad = grad + came[unit][4, tile, :].astype(f32)
            if kind == 1:
                grad = grad + extra_buf[pl.ds(row + tile.start, TILE), :]
            change = adam_delta(weight[unit][tile, :], grad, first[unit][tile, :], second[unit][tile, :])
            delta[unit][tile, :] = change.astype(bf16)
            weight[unit][tile, :] = grad

        row_tiles(rows, body)
        out_copy(unit, 0).start()
        firsts[unit] = plane_copies(unit, 0)
        for copy in firsts[unit]:
            copy.start()

    def exchange(unit):
        for copy in firsts[unit]:
            copy.wait()

        def body(tile):
            total = delta[unit][tile, :].astype(f32) + swapped[unit][tile, :].astype(f32)
            delta[unit][tile, :] = total.astype(bf16)

        row_tiles(units[unit][3], body)
        seconds[unit] = plane_copies(unit, 1)
        for copy in seconds[unit]:
            copy.start()

    def close(unit):
        for copy in seconds[unit]:
            copy.wait_recv()

        def body(tile):
            first[unit][tile, :] = delta[unit][tile, :].astype(f32) + swapped_two[unit][tile, :].astype(f32)

        row_tiles(units[unit][3], body)
        out_copy(unit, 1).start()

    for turn in range(number + 3):
        stem_turn(turn)
        for lag, action in enumerate((forward, finish, exchange, close)):
            if 0 <= turn - lag < number:
                action(turn - lag)

    if with_stem:
        pltpu.make_async_copy(stem_d, stem_out, stem_sem.at[1]).wait()
    for unit in range(number):
        for copy in given[unit]:
            copy.wait_send()
        for copy in seconds[unit]:
            copy.wait_send()
        out_copy(unit, 0).wait()
        out_copy(unit, 1).wait()
        for place in range(4):

            @pl.when(at == place)
            def _(place=place, unit=unit):
                for owner, step in routes_of[place]:
                    if owner not in units[unit][5]:
                        line_copy(unit, owner, step, place).wait_send()


def reduce_layer(layer, dex, dqkvo, dup, ddn, extra, states, stem_delta=None):
    units = reduce_units()
    scratch = []
    for lead, kind in (((4,), bf16), ((4,), bf16), ((5,), bf16), ((), bf16), ((), bf16), ((), bf16), ((), f32), ((), f32), ((), f32)):
        scratch += [pltpu.VMEM(lead + (unit[3], unit[4]), kind) for unit in units]
    number = len(units)
    scratch.append(pltpu.VMEM(extra.shape, f32))
    dma = pltpu.SemaphoreType.DMA
    scratch += [dma((number, 3)), dma((number, 3)), dma((number, 4)), dma((number, 5)), dma((number + 1, 6))]
    scratch += [dma((number, 4)), dma((number, 4)), dma((number, 2))]
    anywhere = pl.BlockSpec(memory_space=pl.ANY)
    shapes = [(2, D, CHUNK), extra.shape, (D, D)] * 2
    stems = [] if stem_delta is None else [stem_delta]
    for delta in stems:
        shapes.append(delta.shape)
        scratch += [dma((2,)), dma((4,)), dma((4,))] + [pltpu.VMEM(delta.shape, bf16)] * 3
        scratch.append(pltpu.VMEM(delta.shape, f32))
    return pl.pallas_call(
        functools.partial(reduce_kernel, layer, bool(stems)),
        out_shape=[shape_of(shape, f32) for shape in shapes],
        in_specs=[anywhere] * (5 + len(states) + len(stems)),
        out_specs=[anywhere] * len(shapes),
        scratch_shapes=scratch,
        compiler_params=pltpu.CompilerParams(
            vmem_limit_bytes=62 * MIB, collective_id=1 + layer, has_side_effects=True
        ),
        name="reduce_layer",
    )(dex, dqkvo, dup, ddn, extra, *states, *stems)


def shard_part(kind, ref, quarter, half=None):
    if kind == "stem":
        begin, size = quarter * (STEM_LANES // 4), STEM_LANES // 4
        if half is not None:
            begin, size = begin + half * (size // 2), size // 2
        return ref.at[:, pl.ds(pl.multiple_of(begin, 128), size)]
    if kind == "lin":
        begin, size = lax.rem(quarter, 2) * 432, 432
        if half is not None:
            begin, size = begin + half * 208, (208, 224)[half]
        return ref.at[quarter // 2, pl.ds(pl.multiple_of(begin, 16), size)]
    begin, size = quarter * (D // 4), D // 4
    if half is not None:
        begin, size = begin + half * (size // 2), size // 2
    return ref.at[pl.ds(pl.multiple_of(begin, 16), size)]


class WeightGather:
    def __init__(self, kinds, sources, targets, sends, recvs, cores_send, cores_recv, own_sem):
        self.kinds, self.sources, self.targets = kinds, sources, targets
        self.sends, self.recvs = sends, recvs
        self.cores_send, self.cores_recv, self.own_sem = cores_send, cores_recv, own_sem
        self.at, self.core, self.group = lax.axis_index(LINE), lax.axis_index(CORE), lax.axis_index(GROUP)
        self.sibling = {CORE: 1 - self.core}
        self.side_x, self.side_y = plane_partners()
        self.group_x = self.group + 1 - 2 * lax.rem(self.group, 2)
        self.group_y = lax.rem(self.group + 2, 4)
        near = jnp.where(self.at == 3, 3, 1)
        far = jnp.where(self.at == 0, 3, jnp.where(self.at == 3, 1, 2))
        self.order = (near, 6 - near - far, far)

    def enter(self):
        greet([self.sibling, self.side_x, self.side_y], self.at, 4)

    def whole_part(self, unit, owner, core):
        target = self.targets[unit]
        if self.kinds[unit] == "lin":
            return target.at[:, owner * 2 + core]
        return target.at[owner * 2 + core]

    def copy(self, unit, source, target, slot, kind, device):
        return pltpu.make_async_remote_copy(
            source, target, self.sends.at[unit, slot, kind], self.recvs.at[unit, slot, kind],
            device_id=device, device_id_type=MESH_ID,
        )

    def line_copy(self, unit, owner, to_slot, send_slot, step, own):
        target = shard_part(self.kinds[unit], self.whole_part(unit, owner, self.core), self.group)
        source = shard_part(self.kinds[unit], self.sources[unit], self.group) if own else target
        return pltpu.make_async_remote_copy(
            source, target, self.sends.at[unit, send_slot, 0], self.recvs.at[unit, to_slot - 1, 0],
            device_id={LINE: self.at + step}, device_id_type=MESH_ID,
        )

    def owner_of(self, slot):
        return lax.rem(self.at + slot, 4)

    def part(self, unit, slot, quarter, half=None):
        return shard_part(self.kinds[unit], self.whole_part(unit, self.owner_of(slot), self.core), quarter, half)

    def core_copy(self, unit, slot, own=False):
        source = self.sources[unit] if own else self.whole_part(unit, self.owner_of(slot), self.core)
        return pltpu.make_async_remote_copy(
            source, self.whole_part(unit, self.owner_of(slot), self.core),
            self.cores_send.at[unit, slot], self.cores_recv.at[unit, slot],
            device_id=self.sibling, device_id_type=MESH_ID,
        )

    def own_copy(self, unit):
        return pltpu.make_async_copy(
            self.sources[unit], self.whole_part(unit, self.at, self.core), self.own_sem.at[unit]
        )

    def own_line(self, unit, act):
        for step, slot, send_slot, there in ((1, 3, 3, self.at < 3), (-1, 1, 4, self.at > 0)):

            @pl.when(there)
            def _(step=step, slot=slot, send_slot=send_slot):
                act(self.line_copy(unit, self.at, slot, send_slot, step, True))

    def begin(self, unit):
        self.own_line(unit, lambda copy: copy.start())
        self.core_copy(unit, 0, True).start()
        self.own_copy(unit).start()

    def forwards(self, unit, slot, act):
        left = self.at + slot >= 4
        for step, to_slot, there in ((1, slot - 1, left & (self.at < 3)), (-1, slot + 1, (self.at + slot < 4) & (self.at > 0))):

            @pl.when(there)
            def _(step=step, to_slot=to_slot):
                act(self.line_copy(unit, self.owner_of(slot), to_slot, slot - 1, step, False))

    def plane_copies(self, unit, slot):
        mine = self.part(unit, slot, self.group)
        return [self.copy(unit, mine, mine, slot - 1, 1, self.side_x), self.copy(unit, mine, mine, slot - 1, 2, self.side_y)]

    def plane_arrivals(self, unit, slot):
        parts = [self.part(unit, slot, self.group_x), self.part(unit, slot, self.group_y)]
        return [self.copy(unit, parts[0], parts[0], slot - 1, 1, self.side_x), self.copy(unit, parts[1], parts[1], slot - 1, 2, self.side_y)]

    def corner_copies(self, unit, slot):
        parts = [self.part(unit, slot, self.group_x, 0), self.part(unit, slot, self.group_y, 1)]
        return [self.copy(unit, parts[0], parts[0], slot - 1, 3, self.side_y), self.copy(unit, parts[1], parts[1], slot - 1, 4, self.side_x)]

    def corner_arrivals(self, unit, slot):
        corner = 3 - self.group
        parts = [self.part(unit, slot, corner, 0), self.part(unit, slot, corner, 1)]
        return [self.copy(unit, parts[0], parts[0], slot - 1, 3, self.side_y), self.copy(unit, parts[1], parts[1], slot - 1, 4, self.side_x)]

    def along_line(self, unit):
        for slot in self.order:
            mine = self.part(unit, slot, self.group)
            self.copy(unit, mine, mine, slot - 1, 0, self.sibling).wait_recv()
            self.forwards(unit, slot, lambda copy: copy.start())
            for copy in self.plane_copies(unit, slot):
                copy.start()

    def in_plane(self, unit):
        for slot in self.order:
            for copy in self.plane_arrivals(unit, slot):
                copy.wait_recv()
            for copy in self.corner_copies(unit, slot):
                copy.start()

    def to_sibling(self, unit):
        for slot in self.order:
            for copy in self.corner_arrivals(unit, slot):
                copy.wait_recv()
            self.core_copy(unit, slot).start()

    def end(self, unit):
        self.own_copy(unit).wait()
        self.own_line(unit, lambda copy: copy.wait_send())
        for slot in range(4):
            self.core_copy(unit, slot, slot == 0).wait_send()
            other = self.whole_part(unit, self.owner_of(slot), 1 - self.core)
            pltpu.make_async_remote_copy(
                other, other, self.cores_send.at[unit, slot], self.cores_recv.at[unit, slot],
                device_id=self.sibling, device_id_type=MESH_ID,
            ).wait_recv()
        for slot in (1, 2, 3):
            self.forwards(unit, slot, lambda copy: copy.wait_send())
            for copy in self.plane_copies(unit, slot) + self.corner_copies(unit, slot):
                copy.wait_send()


def gather_semaphores(number):
    dma = pltpu.SemaphoreType.DMA
    return [dma((number, 5, 5)), dma((number, 3, 5)), dma((number, 4)), dma((number, 4)), dma((number,))]


def gather_kernel(kinds, split, *refs):
    count = len(split)
    arrays_in, arrays_out, sems = refs[:count], refs[count : 2 * count], refs[2 * count :]
    sources, targets = [], []
    for given, target, parts in zip(arrays_in, arrays_out, split):
        for part in parts:
            sources.append(given if part is None else given.at[part])
            targets.append(target if part is None else target.at[(slice(None),) + part])
    work = WeightGather(kinds, sources, targets, *sems)
    work.enter()
    number = len(kinds)
    work.begin(0)
    work.begin(1)
    for turn in range(number + 2):
        for lag, action in enumerate((work.along_line, work.in_plane, work.to_sibling)):
            if 0 <= turn - lag < number:
                action(turn - lag)
            if lag == 0 and turn + 2 < number:
                work.begin(turn + 2)
    for unit in range(number):
        work.end(unit)


def gather_beside(step, last, given, taken, sems):
    parts = [(matrix, slice(None), pl.ds(begin, D)) for matrix in range(2) for begin in (0, D)]
    sources = [given[0].at[part] for part in parts]
    targets = [taken[0].at[(slice(None),) + part] for part in parts]
    work = WeightGather(["rows"] * 4, sources, targets, *sems)
    line, plane, pair = work.along_line, work.in_plane, work.to_sibling
    schedule = {
        0: [(work.begin, 0), (work.begin, 1)],
        2: [(line, 0), (work.begin, 2)],
        4: [(line, 1), (plane, 0), (work.begin, 3)],
        6: [(line, 2), (plane, 1), (pair, 0)],
        8: [(line, 3), (plane, 2), (pair, 1)],
        10: [(plane, 3), (pair, 2)],
        11: [(pair, 3)] + [(work.end, unit) for unit in range(4)],
    }
    for when, actions in schedule.items():

        @pl.when(step == (last if when == 11 else when))
        def _(when=when, actions=actions):
            if when == 0:
                work.enter()
            for action, unit in actions:
                action(unit)


def gather_weights(stem, lin, louts, experts_in):
    lanes = [pl.ds(begin, 128) for begin in range(0, D, 128)]
    every = slice(None)
    arrays = [stem, lin] + list(louts) + list(experts_in)
    kinds = ["stem"] + ["lin"] * len(lanes) + ["rows"] * (len(louts) + 4 * len(experts_in))
    split = [[None], [(every, every, part) for part in lanes]] + [[None]] * len(louts)
    split += [[(matrix, every, pl.ds(begin, D)) for matrix in range(2) for begin in (0, D)]] * len(experts_in)
    shapes = [(8,) + stem.shape, (lin.shape[0], 8) + lin.shape[1:]]
    shapes += [(8,) + part.shape for part in arrays[2:]]
    anywhere = pl.BlockSpec(memory_space=pl.ANY)
    return pl.pallas_call(
        functools.partial(gather_kernel, kinds, split),
        out_shape=[shape_of(shape, bf16) for shape in shapes],
        in_specs=[anywhere] * len(arrays),
        out_specs=[anywhere] * len(arrays),
        scratch_shapes=gather_semaphores(len(kinds)),
        compiler_params=pltpu.CompilerParams(collective_id=5, has_side_effects=True),
        name="gather_weights",
    )(*arrays)


def exchange_kernel(packed, loss, all_packed, total, from_x, from_y, losses, held, send, recv, core_send, core_recv, plane_send, plane_recv, own_sem):
    at, core = lax.axis_index(LINE), lax.axis_index(CORE)
    side_x, side_y = plane_partners()
    sibling = {CORE: 1 - core}
    barrier = pltpu.get_barrier_semaphore()
    others = [{LINE: lax.rem(at + step, 4)} for step in (1, 2, 3)]
    for partner in others + [sibling, side_x, side_y]:
        pl.semaphore_signal(barrier, inc=1, device_id=partner, device_id_type=MESH_ID)
    pl.semaphore_wait(barrier, 6)

    def slots(owner, which):
        return all_packed.at[owner * 2 + which], losses.at[owner * 2 + which]

    own = [pltpu.make_async_copy(source, target, own_sem.at[place]) for place, (source, target) in enumerate(zip((packed, loss), slots(at, core)))]
    for copy in own:
        copy.start()

    def line(step, place):
        source, target = ((packed, loss)[place], slots(at, core)[place])
        return pltpu.make_async_remote_copy(
            source, target, send.at[step - 1, place], recv.at[step - 1, place],
            device_id=others[step - 1], device_id_type=MESH_ID,
        )

    def across(step, place):
        owner = lax.rem(at + 4 - step, 4)
        source = (packed, loss)[place] if step == 0 else slots(owner, core)[place]
        return pltpu.make_async_remote_copy(
            source, slots(owner, core)[place], core_send.at[step, place], core_recv.at[step, place],
            device_id=sibling, device_id_type=MESH_ID,
        )

    def arrival(step, place, which, sem):
        here = slots(lax.rem(at + 4 - step, 4), which)[place]
        return pltpu.make_async_remote_copy(
            here, here, core_send.at[step, place], sem, device_id=sibling, device_id_type=MESH_ID
        )

    for place in (1, 0):
        for step in (2, 3, 1):
            line(step, place).start()
        across(0, place).start()
    for place in (1, 0):
        for step in (1, 3, 2):
            arrival(step, place, core, recv.at[step - 1, place]).wait_recv()
            across(step, place).start()
        for step in range(4):
            arrival(step, place, 1 - core, core_recv.at[step, place]).wait_recv()
        if place == 1:
            own[1].wait()
            held[...] = jnp.sum(losses[...], axis=0)
            first = pltpu.make_async_remote_copy(held, from_x, plane_send.at[0], plane_recv.at[0], device_id=side_x, device_id_type=MESH_ID)
            first.start()
    first.wait()
    held[...] += from_x[...]
    second = pltpu.make_async_remote_copy(held, from_y, plane_send.at[1], plane_recv.at[1], device_id=side_y, device_id_type=MESH_ID)
    second.start()
    second.wait()
    total[...] = held[...] + from_y[...]
    own[0].wait()
    for place in range(2):
        for step in (1, 2, 3):
            line(step, place).wait_send()
        for step in range(4):
            across(step, place).wait_send()


def exchange_small(packed, loss):
    dma = pltpu.SemaphoreType.DMA
    vmem = pl.BlockSpec(memory_space=pltpu.VMEM)
    return pl.pallas_call(
        exchange_kernel,
        out_shape=[shape_of((8,) + packed.shape, packed.dtype), shape_of(loss.shape, f32)],
        in_specs=[vmem, vmem],
        out_specs=[vmem, vmem],
        scratch_shapes=[pltpu.VMEM(loss.shape, f32)] * 2
        + [pltpu.VMEM((8,) + loss.shape, f32), pltpu.VMEM(loss.shape, f32)]
        + [dma((3, 2)), dma((3, 2)), dma((4, 2)), dma((4, 2)), dma((2,)), dma((2,)), dma((2,))],
        compiler_params=pltpu.CompilerParams(collective_id=6, has_side_effects=True, vmem_limit_bytes=16 * MIB),
        name="exchange_small",
    )(packed, loss)


def few_experts(
    patches,
    target_noise,
    timesteps,
    labels,
    routes,
    route_gates,
    stem_weights,
    layer_in,
    layer_out,
    experts,
    stem_first,
    layer_in_first,
    layer_out_first,
    experts_first,
    stem_second,
    layer_in_second,
    layer_out_second,
    experts_second,
    stem_moment,
    layer_in_moment,
    layer_out_moment,
    experts_moment,
):
    count = patches.shape[0]
    items = timesteps.shape[0]
    halves = lax.axis_size(CORE)
    sharers = lax.axis_size(LINE) * halves
    expert_count = lax.axis_size(LINE) * experts.shape[1]
    place = lax.axis_index(LINE) * halves + lax.axis_index(CORE)

    stem_t = stem_weights.T
    lin_t = jnp.swapaxes(layer_in, 1, 2)
    louts = [to_half(layer_out[layer]) for layer in range(LAYERS)]
    pairs = [to_half(experts[layer, 0]) for layer in range(LAYERS)]
    gathered = gather_weights(stem_lanes(to_half(stem_t)), to_half(lin_t), louts, pairs[:1])
    stem_all = gathered[0].reshape(D, STEM_LANES)
    lin_all = gathered[1].reshape(LAYERS, -1, D)
    lout_all = [gathered[2 + layer].reshape(-1, D) for layer in range(LAYERS)]
    expert_all = [gathered[2 + LAYERS]]

    feat = time_features(timesteps)
    hot = label_table(labels)
    hot_pad = jnp.pad(hot, ((0, 32 - items), (0, STEM_PADDED[3] - hot.shape[1]))).astype(bf16)
    cond, hidden, pre_one, pre_two, mods, fin_mods = cond_forward(pad_rows(feat), hot_pad, stem_all, lin_all)
    tokens = product_nt(patches, stem_all[:, :PATCH_DIM])
    tokens = (tokens.reshape(items, -1, D) + positions_table()[None]).reshape(-1, D)
    expert_ids = jnp.arange(expert_count, dtype=jnp.int32)
    saved = []
    for layer in range(LAYERS):
        g4 = jnp.sum(
            jnp.where(routes[layer][:, :, None] == expert_ids, route_gates[layer][:, :, None], 0.0), axis=1
        )
        normed, qkv, attended, branch, middle, n2 = attn_forward(layer, tokens, mods[layer], lin_all)
        beside = (pairs[layer + 1],) if layer + 1 < LAYERS else ()
        active, slope, mixed, result, *arrived = ffn_forward(
            layer, n2, middle, mods[layer], g4, lin_all, lout_all[layer], expert_all[layer], halves, beside
        )
        if beside:
            expert_all.append(arrived[0])
        saved.append((tokens, g4, normed, qkv, attended, branch, middle, n2, active, slope, mixed))
        tokens = result
    fo_rows = stem_all[:, STEM_AT[5] : STEM_AT[5] + PATCH_DIM].T
    grad, grad_fin, grad_out_w, loss_rows = final_step(tokens, fin_mods, fo_rows, target_noise.T)

    stem_cols = stem_weights.shape[1]
    lin_cols = layer_in.shape[2]

    def outer(left_in, right_in):
        return lax.dot_general(left_in, right_in, (((0,), (0,)), ((), ())), preferred_element_type=f32)

    def flip(values):
        return jnp.swapaxes(values, -1, -2)

    states = (experts, experts_first, experts_second, lin_t, flip(layer_in_first[0]), flip(layer_in_second[0]))
    states = states + (layer_out, layer_out_first, layer_out_second)
    grad_mods, reduced, outgoing = [None] * LAYERS, [None] * LAYERS, [None] * LAYERS
    for layer in reversed(range(LAYERS)):
        tokens, g4, normed, qkv, attended, branch, middle, n2, active, slope, mixed = saved[layer]
        dup, ddn, dex, gn2, grad_gate = ffn_backward(
            layer, grad, n2, mods[layer], g4, mixed, active, slope, lin_all, lout_all[layer], expert_all[layer], halves
        )
        grad, grad_mods[layer], dqkvo = attn_backward(
            layer, gn2, grad, middle, tokens, normed, qkv, attended, branch, mods[layer], grad_gate, lin_all,
            halves * lin_cols,
        )
        outgoing[layer] = (dex, dqkvo, dup, ddn)
    grad_patch = product_tn(patches, to_half(grad))
    dpre_one, dpre_two = cond_backward(grad_mods[0], grad_mods[1], grad_fin, pre_one, pre_two, stem_all, lin_all)

    names = jnp.stack([labels // 32, labels % 32], axis=1).astype(f32)
    factors = jnp.concatenate(
        [cond[:items], grad_mods[0][:items], grad_mods[1][:items], hidden[:items], dpre_one[:items], dpre_two[:items]]
        + [grad_fin[:items], feat, jnp.pad(names, ((0, 0), (0, 126)))],
        axis=1,
    ).astype(bf16)
    width = factors.shape[1]
    ends = jnp.concatenate([grad_patch, grad_out_w], axis=0).astype(bf16)
    packed = jnp.concatenate([factors.reshape(-1), ends.reshape(-1)])
    lanes = -(-packed.size // (16 * 128)) * 128
    packed = jnp.pad(packed, (0, 16 * lanes - packed.size)).reshape(16, lanes)
    loss = jnp.pad(loss_rows.reshape(1, PATCH_DIM), ((0, 7), (0, 128 - PATCH_DIM)))
    gathered, loss_all = exchange_small(packed, loss)
    loss_total = jnp.sum(loss_all)
    gathered = gathered.reshape(sharers, -1)
    factors = gathered[:, : items * width].reshape(sharers * items, width)
    ends = gathered[:, items * width : items * width + 2 * PATCH_DIM * D].reshape(sharers, 2, PATCH_DIM, D)
    ends = jnp.sum(ends.astype(f32), axis=0)
    cond_f, gm_a, gm_b, hidden_f, done_f, dtwo_f, fin_f, feat_f, names = jnp.split(
        factors, [D, 7 * D, 13 * D, 14 * D, 15 * D, 16 * D, 18 * D, 18 * D + FREQ], axis=1
    )
    hot_all = label_table((names[:, 0].astype(f32) * 32 + names[:, 1].astype(f32)).astype(jnp.int32)).astype(bf16)
    def own(values):
        return lax.dynamic_slice_in_dim(values, place * stem_cols, stem_cols, axis=1)

    stem_grad = jnp.concatenate(
        [
            own(ends[0]).T,
            outer(own(done_f), feat_f),
            outer(own(dtwo_f), hidden_f),
            outer(own(dtwo_f), hot_all),
            outer(own(cond_f), fin_f),
            own(ends[1]).T,
        ],
        axis=1,
    )
    stem_stepped = adam_step(stem_t, stem_grad, stem_first[0].T, stem_second[0].T)
    stem_delta = jnp.pad(to_half(stem_stepped[0]), ((0, 0), (0, -stem_t.shape[1] % 128)))
    for layer, gm in ((1, gm_b), (0, gm_a)):
        spread = jnp.pad(gm, ((0, 0), (4 * D, lin_cols * sharers - 10 * D)))
        window = lax.dynamic_slice_in_dim(spread, place * lin_cols, lin_cols, axis=1)
        dex, dqkvo, dup, ddn = outgoing[layer]
        reduced[layer] = reduce_layer(
            layer,
            dex.reshape((-1, halves) + dex.shape[1:]),
            dqkvo.reshape(halves, lin_cols, D),
            dup.reshape(-1, halves, lin_cols, D),
            ddn.reshape(-1, halves, layer_out.shape[1], D),
            outer(window, cond_f),
            states,
            stem_delta if layer == 1 else None,
        )
    stem_total = reduced[1][6]
    group_count = lax.axis_size(GROUP)

    mean_delta = stem_total[:, : stem_t.shape[1]] / group_count
    moment_new = outer_mom * stem_moment.T + mean_delta
    new_weight = stem_t - outer_rate * (mean_delta + outer_mom * moment_new)
    stem_out = [flip(v) for v in (new_weight, to_half(new_weight), stem_stepped[1][None], stem_stepped[2][None], moment_new)]

    def both(at, rows, tile, weight, first, second, moment):
        grads = [reduced[layer][at].reshape(rows, -1) for layer in range(LAYERS)]
        totals = [reduced[layer][3 + at].reshape(rows, -1) for layer in range(LAYERS)]
        shaped = [v.reshape(LAYERS, rows, -1) for v in (weight, first, second, moment)]
        return update_arrays(tile, grads, totals, *shaped)

    lin_out = both(1, lin_cols, 432, lin_t, flip(layer_in_first), flip(layer_in_second), flip(layer_in_moment))
    lin_out = [flip(v.reshape((1,) * (at in (2, 3)) + v.shape)) for at, v in enumerate(lin_out)]
    lout_rows = layer_out.shape[1]
    lout_out = both(2, lout_rows, lout_rows // 2, layer_out, layer_out_first, layer_out_second, layer_out_moment)
    lout_out = [v.reshape((1,) * (at in (2, 3)) + v.shape) for at, v in enumerate(lout_out)]
    expert_out = both(0, 2 * D, D // 2, experts, experts_first, experts_second, experts_moment)
    likes = (experts, experts, experts_first, experts_second, experts)
    expert_out = [v.reshape(like.shape) for v, like in zip(expert_out, likes)]
    results = []
    for at in range(5):
        results += [stem_out[at], lin_out[at], lout_out[at], expert_out[at]]
    return (loss_total, *results)


def solution(mesh):
    placed = (
        P((GROUP, LINE, CORE), None),
        P((GROUP, LINE, CORE), None),
        P((GROUP, LINE, CORE)),
        P((GROUP, LINE, CORE)),
        P(None, (GROUP, LINE, CORE), None),
        P(None, (GROUP, LINE, CORE), None),
        P(None, (LINE, CORE)),
        P(None, None, (LINE, CORE)),
        P(None, (LINE, CORE), None),
        P(None, LINE, None, None, CORE),
        P(GROUP, None, (LINE, CORE)),
        P(GROUP, None, None, (LINE, CORE)),
        P(GROUP, None, (LINE, CORE), None),
        P(GROUP, None, LINE, None, None, CORE),
        P(GROUP, None, (LINE, CORE)),
        P(GROUP, None, None, (LINE, CORE)),
        P(GROUP, None, (LINE, CORE), None),
        P(GROUP, None, LINE, None, None, CORE),
        P(None, (LINE, CORE)),
        P(None, None, (LINE, CORE)),
        P(None, (LINE, CORE), None),
        P(None, LINE, None, None, CORE),
    )
    step = few_experts if mesh.shape[LINE] <= 4 else per_device
    return jax.shard_map(
        step,
        mesh=mesh,
        in_specs=placed,
        out_specs=(
            P(),
            P(None, (LINE, CORE)),
            P(None, None, (LINE, CORE)),
            P(None, (LINE, CORE), None),
            P(None, LINE, None, None, CORE),
            P(None, (LINE, CORE)),
            P(None, None, (LINE, CORE)),
            P(None, (LINE, CORE), None),
            P(None, LINE, None, None, CORE),
            P(GROUP, None, (LINE, CORE)),
            P(GROUP, None, None, (LINE, CORE)),
            P(GROUP, None, (LINE, CORE), None),
            P(GROUP, None, LINE, None, None, CORE),
            P(GROUP, None, (LINE, CORE)),
            P(GROUP, None, None, (LINE, CORE)),
            P(GROUP, None, (LINE, CORE), None),
            P(GROUP, None, LINE, None, None, CORE),
            P(None, (LINE, CORE)),
            P(None, None, (LINE, CORE)),
            P(None, (LINE, CORE), None),
            P(None, LINE, None, None, CORE),
        ),
        check_vma=False,
    )
```

```python
import functools

import jax
import jax.numpy as jnp
from jax import lax
from jax.experimental import pallas as pl
from jax.experimental.pallas import tpu as pltpu
from jax.sharding import PartitionSpec as P

GROUP, LINE, CORE = "group", "expert", "dp"
D = 384
HEADS = 6
IMG = 32
FREQ = 256
CLASSES = 1000
LAYERS = 2
STEP = 10
PATCH_DIM = 16
PATCHES = 256


highest = lax.Precision.HIGHEST
beta_one = 0.9
beta_two = 0.95
eps_adam = 1e-08
inner_rate = 0.03
weight_decay = 0.05
outer_rate = 0.7
outer_mom = 0.9
ln_eps = 1e-06


def to_half(values):
    return values.astype(jnp.bfloat16)


def product(left_in, right_in):
    return jnp.dot(left_in, right_in, preferred_element_type=jnp.float32)


def product_tn(left_in, right_in):
    return lax.dot_general(
        left_in, right_in, (((0,), (0,)), ((), ())), preferred_element_type=jnp.float32
    )


def product_nt(left_in, right_in):
    return lax.dot_general(
        left_in, right_in, (((1,), (1,)), ((), ())), preferred_element_type=jnp.float32
    )


def gelu_tanh(values):
    return jax.nn.gelu(values, approximate=True)


def gelu_back(values, gradient):
    _, pull = jax.vjp(gelu_tanh, values)
    return pull(gradient)[0]


def norm_mod(values, shift_in, scale_in):
    centre = values - jnp.mean(values, axis=-1, keepdims=True)
    spread = jnp.mean(centre * centre, axis=-1, keepdims=True)
    return centre * lax.rsqrt(spread + ln_eps) * (1.0 + scale_in) + shift_in


def positions_table():
    grid_side = IMG // 2
    quarter = D // 4
    omegas = 1.0 / 10000.0 ** (jnp.arange(quarter, dtype=jnp.float32) / quarter)
    index_all = jnp.arange(PATCHES, dtype=jnp.int32)
    row_angle = (index_all // grid_side).astype(jnp.float32)[:, None] * omegas[None, :]
    col_angle = (index_all % grid_side).astype(jnp.float32)[:, None] * omegas[None, :]
    return jnp.concatenate(
        [jnp.sin(row_angle), jnp.cos(row_angle), jnp.sin(col_angle), jnp.cos(col_angle)], axis=1
    )


def time_features(step_ids):
    half_freq = FREQ // 2
    frequency = jnp.exp(-jnp.log(10000.0) * jnp.arange(half_freq, dtype=jnp.float32) / half_freq)
    angles = step_ids.astype(jnp.float32)[:, None] * frequency[None, :]
    return jnp.concatenate([jnp.cos(angles), jnp.sin(angles)], axis=1)


def label_table(label_ids):
    return (label_ids[:, None] == jnp.arange(CLASSES + 1, dtype=jnp.int32)[None, :]).astype(
        jnp.float32
    )


def split_stem(stem_all):
    end_patch = PATCH_DIM
    end_time = end_patch + FREQ
    end_second = end_time + D
    end_table = end_second + CLASSES + 1
    end_ada = end_table + 2 * D
    return (
        stem_all[:end_patch],
        stem_all[end_patch:end_time],
        stem_all[end_time:end_second],
        stem_all[end_second:end_table],
        stem_all[end_table:end_ada],
        stem_all[end_ada:],
    )


def slot_places(route_ids, expert_count, capacity):
    flat_ids = route_ids.reshape(-1)
    one_hot_ids = (flat_ids[:, None] == jnp.arange(expert_count, dtype=jnp.int32)[None, :]).astype(
        jnp.int32
    )
    rank_in = jnp.sum((jnp.cumsum(one_hot_ids, axis=0) - one_hot_ids) * one_hot_ids, axis=1)
    return flat_ids * capacity + rank_in


def expert_major(received, local_count):
    sources = received.shape[0] // local_count
    shaped = received.reshape(sources, local_count, received.shape[1], received.shape[2])
    return jnp.swapaxes(shaped, 0, 1).reshape(local_count, -1, received.shape[2])


def source_major(rows_in, sources):
    local_count = rows_in.shape[0]
    shaped = rows_in.reshape(local_count, sources, -1, rows_in.shape[2])
    return jnp.swapaxes(shaped, 0, 1).reshape(sources * local_count, -1, rows_in.shape[2])


def attention_split(qkv, item_count):
    head_dim = qkv.shape[1] // (3 * HEADS)
    shaped = qkv.reshape(item_count, -1, 3, HEADS, head_dim)
    return (shaped[:, :, 0], shaped[:, :, 1], shaped[:, :, 2], head_dim ** (-0.5))


def attention_forward(qkv, item_count):
    queries, keys_in, values_in, scale_att = attention_split(qkv, item_count)
    scores = (
        jnp.einsum("bqhd,bkhd->bhqk", queries, keys_in, preferred_element_type=jnp.float32)
        * scale_att
    )
    row_max = jnp.max(scores, axis=-1, keepdims=True)
    log_sums = row_max + jnp.log(jnp.sum(jnp.exp(scores - row_max), axis=-1, keepdims=True))
    attn_probs = to_half(jnp.exp(scores - log_sums))
    attended = jnp.einsum(
        "bhqk,bkhd->bqhd", attn_probs, values_in, preferred_element_type=jnp.float32
    )
    return (to_half(attended.reshape(qkv.shape[0], -1)), log_sums)


def attention_backward(qkv, log_sums, grad_attended, item_count):
    queries, keys_in, values_in, scale_att = attention_split(qkv, item_count)
    scores = (
        jnp.einsum("bqhd,bkhd->bhqk", queries, keys_in, preferred_element_type=jnp.float32)
        * scale_att
    )
    probs_full = jnp.exp(scores - log_sums)
    grad_out = grad_attended.reshape(queries.shape)
    grad_values = jnp.einsum(
        "bhqk,bqhd->bkhd", to_half(probs_full), grad_out, preferred_element_type=jnp.float32
    )
    grad_probs = jnp.einsum(
        "bqhd,bkhd->bhqk", grad_out, values_in, preferred_element_type=jnp.float32
    )
    grad_scores = probs_full * (
        grad_probs - jnp.sum(probs_full * grad_probs, axis=-1, keepdims=True)
    )
    grad_half = to_half(grad_scores)
    grad_queries = (
        jnp.einsum("bhqk,bkhd->bqhd", grad_half, keys_in, preferred_element_type=jnp.float32)
        * scale_att
    )
    grad_keys = (
        jnp.einsum("bhqk,bqhd->bkhd", grad_half, queries, preferred_element_type=jnp.float32)
        * scale_att
    )
    stacked = jnp.stack([grad_queries, grad_keys, grad_values], axis=2)
    return to_half(stacked.reshape(qkv.shape[0], -1))


def layer_forward(tokens, cond_act, lin, lout, expert_w, route_ids, gate_vals):
    item_count = cond_act.shape[0]
    model_width = tokens.shape[1]
    local_count = expert_w.shape[0]
    expert_count = lax.axis_size(LINE) * local_count
    capacity = 4 * tokens.shape[0] // expert_count
    mods = jnp.dot(
        cond_act, lin[:, 4 * model_width : 10 * model_width].astype(jnp.float32), precision=highest
    )
    mods = mods.reshape(item_count, 6, 1, model_width)
    shaped = tokens.reshape(item_count, -1, model_width)
    normed = to_half(norm_mod(shaped, mods[:, 0], mods[:, 1]).reshape(-1, model_width))
    qkv = to_half(product(normed, lin[:, : 3 * model_width]))
    attended, log_sums = attention_forward(qkv, item_count)
    branch = product(attended, lin[:, 3 * model_width : 4 * model_width])
    middle = shaped + mods[:, 2] * branch.reshape(item_count, -1, model_width)
    normed_two = to_half(norm_mod(middle, mods[:, 3], mods[:, 4]).reshape(-1, model_width))
    inner_pre = product(normed_two, lin[:, 10 * model_width :])
    active = to_half(gelu_tanh(inner_pre))
    shared = product(active, lout)
    slot_index = slot_places(route_ids, expert_count, capacity)
    send_rows = jnp.zeros((expert_count * capacity, model_width), jnp.bfloat16)
    send_rows = send_rows.at[slot_index].set(jnp.repeat(normed_two, 2, axis=0))
    received = lax.all_to_all(
        send_rows.reshape(expert_count, capacity, model_width),
        LINE,
        split_axis=0,
        concat_axis=0,
        tiled=True,
    )
    rows_exp = expert_major(received, local_count)
    inner_exp = jnp.einsum(
        "erd,edf->erf", rows_exp, expert_w[:, 0], preferred_element_type=jnp.float32
    )
    active_exp = to_half(gelu_tanh(inner_exp))
    out_exp = to_half(
        jnp.einsum("erf,edf->erd", active_exp, expert_w[:, 1], preferred_element_type=jnp.float32)
    )
    returned = lax.all_to_all(
        source_major(out_exp, lax.axis_size(LINE)),
        LINE,
        split_axis=0,
        concat_axis=0,
        tiled=True,
    )
    picked = (
        returned.reshape(-1, model_width)[slot_index]
        .astype(jnp.float32)
        .reshape(-1, 2, model_width)
    )
    mixed_out = shared + jnp.sum(gate_vals[:, :, None] * picked, axis=1)
    result = middle + mods[:, 5] * mixed_out.reshape(item_count, -1, model_width)
    saved = (
        tokens,
        mods,
        normed,
        qkv,
        attended,
        log_sums,
        branch,
        middle,
        normed_two,
        inner_pre,
        active,
        mixed_out,
        slot_index,
        rows_exp,
        inner_exp,
        active_exp,
    )
    return (result.reshape(-1, model_width), saved)


def layer_backward(grad_tokens, saved, cond_act, lin, lout, expert_w, gate_vals):
    (
        tokens,
        mods,
        normed,
        qkv,
        attended,
        log_sums,
        branch,
        middle,
        normed_two,
        inner_pre,
        active,
        mixed_out,
        slot_index,
        rows_exp,
        inner_exp,
        active_exp,
    ) = saved
    item_count = cond_act.shape[0]
    model_width = tokens.shape[1]
    local_count = expert_w.shape[0]
    expert_count = lax.axis_size(LINE) * local_count
    capacity = 4 * tokens.shape[0] // expert_count
    grad_shaped = grad_tokens.reshape(item_count, -1, model_width)
    grad_gate_two = jnp.sum(
        grad_shaped * mixed_out.reshape(item_count, -1, model_width), axis=1, keepdims=True
    )
    grad_mixed = (mods[:, 5] * grad_shaped).reshape(-1, model_width)
    grad_shared = to_half(grad_mixed)
    grad_lout = product_tn(active, grad_shared)
    grad_inner = to_half(gelu_back(inner_pre, product_nt(grad_shared, lout)))
    grad_w_up = product_tn(normed_two, grad_inner)
    grad_normed_two = product_nt(grad_inner, lin[:, 10 * model_width :])
    routed_grad = to_half(gate_vals[:, :, None] * grad_mixed[:, None, :]).reshape(-1, model_width)
    send_grad = (
        jnp.zeros((expert_count * capacity, model_width), jnp.bfloat16)
        .at[slot_index]
        .set(routed_grad)
    )
    received = lax.all_to_all(
        send_grad.reshape(expert_count, capacity, model_width),
        LINE,
        split_axis=0,
        concat_axis=0,
        tiled=True,
    )
    grad_rows = expert_major(received, local_count)
    grad_down_exp = jnp.einsum(
        "erd,erf->edf", grad_rows, active_exp, preferred_element_type=jnp.float32
    )
    grad_active_exp = jnp.einsum(
        "erd,edf->erf", grad_rows, expert_w[:, 1], preferred_element_type=jnp.float32
    )
    grad_inner_exp = to_half(gelu_back(inner_exp, grad_active_exp))
    grad_up_exp = jnp.einsum(
        "erd,erf->edf", rows_exp, grad_inner_exp, preferred_element_type=jnp.float32
    )
    grad_rows_in = to_half(
        jnp.einsum(
            "erf,edf->erd", grad_inner_exp, expert_w[:, 0], preferred_element_type=jnp.float32
        )
    )
    back_rows = lax.all_to_all(
        source_major(grad_rows_in, lax.axis_size(LINE)),
        LINE,
        split_axis=0,
        concat_axis=0,
        tiled=True,
    )
    picked = (
        back_rows.reshape(-1, model_width)[slot_index]
        .astype(jnp.float32)
        .reshape(-1, 2, model_width)
    )
    grad_normed_two = grad_normed_two + jnp.sum(picked, axis=1)
    _, second_back = jax.vjp(norm_mod, middle, mods[:, 3], mods[:, 4])
    grad_middle, grad_shift_two, grad_scale_two = second_back(
        grad_normed_two.reshape(item_count, -1, model_width)
    )
    grad_middle = grad_middle + grad_shaped
    grad_gate_one = jnp.sum(
        grad_middle * branch.reshape(item_count, -1, model_width), axis=1, keepdims=True
    )
    grad_branch = to_half((mods[:, 2] * grad_middle).reshape(-1, model_width))
    grad_w_out = product_tn(attended, grad_branch)
    grad_attended = to_half(product_nt(grad_branch, lin[:, 3 * model_width : 4 * model_width]))
    grad_qkv = attention_backward(qkv, log_sums, grad_attended, item_count)
    grad_w_qkv = product_tn(normed, grad_qkv)
    grad_normed = product_nt(grad_qkv, lin[:, : 3 * model_width])
    _, first_back = jax.vjp(
        norm_mod, tokens.reshape(item_count, -1, model_width), mods[:, 0], mods[:, 1]
    )
    grad_input, grad_shift_one, grad_scale_one = first_back(
        grad_normed.reshape(item_count, -1, model_width)
    )
    grad_input = grad_input + grad_middle
    grad_mods = jnp.stack(
        [
            grad_shift_one,
            grad_scale_one,
            grad_gate_one,
            grad_shift_two,
            grad_scale_two,
            grad_gate_two,
        ],
        axis=1,
    )
    grad_mods = grad_mods.reshape(item_count, 6 * model_width)
    grad_ada = jnp.dot(cond_act.T, grad_mods, precision=highest)
    grad_cond = jnp.dot(
        grad_mods,
        lin[:, 4 * model_width : 10 * model_width].astype(jnp.float32).T,
        precision=highest,
    )
    grad_lin = jnp.concatenate([grad_w_qkv, grad_w_out, grad_ada, grad_w_up], axis=1)
    grad_expert = jnp.stack([grad_up_exp, grad_down_exp], axis=1)
    return (grad_input.reshape(-1, model_width), grad_cond, grad_lin, grad_lout, grad_expert)


def adam_step(weight_in, gradient, first_in, second_in):
    first_new = beta_one * first_in + (1.0 - beta_one) * gradient
    second_new = beta_two * second_in + (1.0 - beta_two) * gradient * gradient
    first_hat = first_new / (1.0 - beta_one**STEP)
    second_hat = second_new / (1.0 - beta_two**STEP)
    stepped = weight_in - inner_rate * (
        first_hat / (jnp.sqrt(second_hat) + eps_adam) + weight_decay * weight_in
    )
    return (weight_in - stepped, first_new, second_new)


def per_device(
    patches,
    target_noise,
    timesteps,
    labels,
    routes,
    route_gates,
    stem_weights,
    layer_in,
    layer_out,
    experts,
    stem_first,
    layer_in_first,
    layer_out_first,
    experts_first,
    stem_second,
    layer_in_second,
    layer_out_second,
    experts_second,
    stem_moment,
    layer_in_moment,
    layer_out_moment,
    experts_moment,
):
    stem_all, lin_all, lout_all = (
        lax.all_gather(to_half(stem_weights), (LINE, CORE), axis=1, tiled=True),
        lax.all_gather(to_half(layer_in), (LINE, CORE), axis=2, tiled=True),
        lax.all_gather(to_half(layer_out), (LINE, CORE), axis=1, tiled=True),
    )
    expert_all = lax.all_gather(to_half(experts), CORE, axis=4, tiled=True)
    model_width = stem_all.shape[1]
    item_count = timesteps.shape[0]
    patch_w, time_one, time_two, table_w, final_ada, final_out = split_stem(stem_all)
    features = time_features(timesteps)
    hot_labels = label_table(labels)

    def condition(first_w, second_w, table_in):
        hidden_time = jax.nn.silu(jnp.dot(features, first_w, precision=highest))
        return jax.nn.silu(
            jnp.dot(hidden_time, second_w, precision=highest)
            + jnp.dot(hot_labels, table_in, precision=highest)
        )

    cond_act, cond_back = jax.vjp(
        condition,
        time_one.astype(jnp.float32),
        time_two.astype(jnp.float32),
        table_w.astype(jnp.float32),
    )
    tokens = product(patches, patch_w)
    tokens = (tokens.reshape(item_count, -1, model_width) + positions_table()[None]).reshape(
        -1, model_width
    )
    saved_all = []
    for layer_idx in range(LAYERS):
        tokens, saved = layer_forward(
            tokens,
            cond_act,
            lin_all[layer_idx],
            lout_all[layer_idx],
            expert_all[layer_idx],
            routes[layer_idx],
            route_gates[layer_idx],
        )
        saved_all.append(saved)
    final_ada_f = final_ada.astype(jnp.float32)
    final_mods = jnp.dot(cond_act, final_ada_f.T, precision=highest).reshape(
        item_count, 2, 1, model_width
    )
    final_pre, final_back = jax.vjp(
        norm_mod, tokens.reshape(item_count, -1, model_width), final_mods[:, 0], final_mods[:, 1]
    )
    final_normed = to_half(final_pre.reshape(-1, model_width))
    predicted = product_nt(final_normed, final_out)
    residual_err = predicted - target_noise
    loss_total = lax.psum(jnp.sum(residual_err * residual_err), (GROUP, LINE, CORE))
    grad_pred = to_half(2.0 * residual_err)
    grad_final_out = product_tn(grad_pred, final_normed)
    grad_final_normed = product(grad_pred, final_out)
    grad_tokens, grad_fshift, grad_fscale = final_back(
        grad_final_normed.reshape(item_count, -1, model_width)
    )
    grad_tokens = grad_tokens.reshape(-1, model_width)
    grad_final_mods = jnp.concatenate([grad_fshift, grad_fscale], axis=1).reshape(
        item_count, 2 * model_width
    )
    grad_final_ada = jnp.dot(grad_final_mods.T, cond_act, precision=highest)
    grad_cond = jnp.dot(grad_final_mods, final_ada_f, precision=highest)
    lin_grads = []
    lout_grads = []
    expert_grads = []
    for layer_idx in reversed(range(LAYERS)):
        grad_tokens, grad_cond_layer, grad_lin, grad_lout, grad_expert = layer_backward(
            grad_tokens,
            saved_all[layer_idx],
            cond_act,
            lin_all[layer_idx],
            lout_all[layer_idx],
            expert_all[layer_idx],
            route_gates[layer_idx],
        )
        grad_cond = grad_cond + grad_cond_layer
        lin_grads.append(grad_lin)
        lout_grads.append(grad_lout)
        expert_grads.append(grad_expert)
    lin_stack = jnp.stack(lin_grads[::-1])
    lout_stack = jnp.stack(lout_grads[::-1])
    expert_stack = jnp.stack(expert_grads[::-1])
    grad_patch = product_tn(patches, to_half(grad_tokens))
    grad_time_one, grad_time_two, grad_table = cond_back(grad_cond)
    grad_stem = jnp.concatenate(
        [grad_patch, grad_time_one, grad_time_two, grad_table, grad_final_ada, grad_final_out],
        axis=0,
    )
    stem_sum, lin_sum, lout_sum = (
        lax.psum_scatter(grad_stem, (LINE, CORE), scatter_dimension=1, tiled=True),
        lax.psum_scatter(lin_stack, (LINE, CORE), scatter_dimension=2, tiled=True),
        lax.psum_scatter(lout_stack, (LINE, CORE), scatter_dimension=1, tiled=True),
    )
    expert_sum = lax.psum_scatter(
        expert_stack.astype(jnp.bfloat16), CORE, scatter_dimension=4, tiled=True
    ).astype(jnp.float32)
    weights_all = (stem_weights, layer_in, layer_out, experts)
    gradients = (stem_sum, lin_sum, lout_sum, expert_sum)
    firsts = (stem_first, layer_in_first, layer_out_first, experts_first)
    seconds = (stem_second, layer_in_second, layer_out_second, experts_second)
    moments = (stem_moment, layer_in_moment, layer_out_moment, experts_moment)
    stepped = [
        adam_step(
            weights_all[array_idx],
            gradients[array_idx],
            firsts[array_idx][0],
            seconds[array_idx][0],
        )
        for array_idx in range(4)
    ]
    delta_all = (
        lax.psum(stepped[0][0].astype(jnp.bfloat16), GROUP).astype(jnp.float32),
        lax.psum(stepped[1][0].astype(jnp.bfloat16), GROUP).astype(jnp.float32),
        lax.psum(stepped[2][0].astype(jnp.bfloat16), GROUP).astype(jnp.float32),
        lax.psum(stepped[3][0].astype(jnp.bfloat16), GROUP).astype(jnp.float32),
    )
    group_count = lax.axis_size(GROUP)
    new_weights = []
    new_moments = []
    for array_idx in range(4):
        mean_delta = delta_all[array_idx] / group_count
        moment_new = outer_mom * moments[array_idx] + mean_delta
        new_weights.append(
            weights_all[array_idx] - outer_rate * (mean_delta + outer_mom * moment_new)
        )
        new_moments.append(moment_new)
    return (
        loss_total,
        new_weights[0],
        new_weights[1],
        new_weights[2],
        new_weights[3],
        to_half(new_weights[0]),
        to_half(new_weights[1]),
        to_half(new_weights[2]),
        to_half(new_weights[3]),
        stepped[0][1][None],
        stepped[1][1][None],
        stepped[2][1][None],
        stepped[3][1][None],
        stepped[0][2][None],
        stepped[1][2][None],
        stepped[2][2][None],
        stepped[3][2][None],
        new_moments[0],
        new_moments[1],
        new_moments[2],
        new_moments[3],
    )


bf16 = jnp.bfloat16
f32 = jnp.float32
MIB = 1024 * 1024
CHUNK = 768
FWD_ROWS = 256
BWD_ROWS = 256
STEM_SIZES = (PATCH_DIM, FREQ, D, CLASSES + 1, 2 * D, PATCH_DIM)
STEM_PADDED = tuple(-(-size // 128) * 128 for size in STEM_SIZES)
STEM_AT = tuple(sum(STEM_PADDED[:place]) for place in range(len(STEM_PADDED)))
STEM_LANES = -(-sum(STEM_PADDED) // 1024) * 1024


def dot_nn(left_in, right_in):
    return lax.dot_general(left_in, right_in, (((1,), (0,)), ((), ())), preferred_element_type=f32)


def dot_nt(left_in, right_in):
    return lax.dot_general(left_in, right_in, (((1,), (1,)), ((), ())), preferred_element_type=f32)


def dot_tn(left_in, right_in):
    return lax.dot_general(left_in, right_in, (((0,), (0,)), ((), ())), preferred_element_type=f32)


def three_parts(rows):
    high = rows.astype(bf16).astype(f32)
    rest = rows - high
    mid = rest.astype(bf16).astype(f32)
    low = rest - mid
    return jnp.concatenate([high, mid, low, jnp.zeros_like(low)], axis=0).astype(bf16)


def three_sum(stacked):
    return stacked[0:8] + stacked[8:16] + stacked[16:24]


def full_nt(rows, weight):
    return three_sum(dot_nt(three_parts(rows), weight))


def full_nn(rows, weight):
    return three_sum(dot_nn(three_parts(rows), weight))


def silu_slope(values):
    gate = 1.0 / (1.0 + jnp.exp(-values))
    return gate * (1.0 + values * (1.0 - gate))


def silu_of(values):
    return values / (1.0 + jnp.exp(-values))


def stem_piece(stem_ref, place):
    return stem_ref[:, STEM_AT[place] : STEM_AT[place] + STEM_PADDED[place]]


def cond_kernel(feat_ref, hot_ref, stem_ref, ada_ref, cond_ref, hid_ref, one_ref, two_ref, mods_ref, fin_ref):
    @pl.when(pl.program_id(0) == 0)
    def _():
        pre_one = full_nt(feat_ref[...], stem_piece(stem_ref, 1))
        hidden = silu_of(pre_one)
        pre_two = full_nt(hidden, stem_piece(stem_ref, 2)) + dot_nt(hot_ref[...], stem_piece(stem_ref, 3))[0:8]
        cond = silu_of(pre_two)
        one_ref[...] = pre_one
        two_ref[...] = pre_two
        hid_ref[...] = hidden
        cond_ref[...] = cond
        fin_ref[...] = full_nn(cond, stem_piece(stem_ref, 4))

    for layer in range(LAYERS):
        mods_ref[layer] = full_nt(cond_ref[...], ada_ref[layer])


def cond_back_kernel(gm_a, gm_b, gf_ref, one_ref, two_ref, stem_ref, ada_ref, done_ref, dtwo_ref):
    @pl.when(pl.program_id(0) == 0)
    def _():
        dtwo_ref[...] = full_nt(gf_ref[...], stem_piece(stem_ref, 4))

    dtwo_ref[...] += full_nn(gm_a[...], ada_ref[0]) + full_nn(gm_b[...], ada_ref[1])

    @pl.when(pl.program_id(0) == pl.num_programs(0) - 1)
    def _():
        dtwo = dtwo_ref[...] * silu_slope(two_ref[...])
        dtwo_ref[...] = dtwo
        done_ref[...] = full_nn(dtwo, stem_piece(stem_ref, 2)) * silu_slope(one_ref[...])


def norm_parts(values):
    centre = values - jnp.mean(values, axis=-1, keepdims=True)
    spread = jnp.mean(centre * centre, axis=-1, keepdims=True)
    root = lax.rsqrt(spread + ln_eps)
    return centre * root, root


def norm_back(values, scale_in, gradient):
    unit, root = norm_parts(values)
    grad_unit = gradient * (1.0 + scale_in)
    inner = jnp.mean(grad_unit * unit, axis=-1, keepdims=True)
    grad_in = root * (grad_unit - jnp.mean(grad_unit, axis=-1, keepdims=True) - unit * inner)
    return (
        grad_in,
        jnp.sum(gradient, axis=0, keepdims=True),
        jnp.sum(gradient * unit, axis=0, keepdims=True),
    )


def mod_row(mods_ref, item, place):
    return mods_ref[pl.ds(item, 1), place * D : (place + 1) * D]


def head_masks():
    lane = lax.broadcasted_iota(jnp.int32, (1, 128), 1)
    return lane, [(lane // 64 == half).astype(f32).astype(bf16) for half in range(2)]


def attn_fwd_kernel(x_ref, mods_ref, w_ref, normed_ref, qkv_ref, att_ref, branch_ref, mid_ref, n2_ref):
    item = pl.program_id(0)
    tokens = x_ref[...]
    unit, _ = norm_parts(tokens)
    normed = (unit * (1.0 + mod_row(mods_ref, item, 1)) + mod_row(mods_ref, item, 0)).astype(bf16)
    normed_ref[...] = normed
    qkv_ref[...] = dot_nt(normed, w_ref[0 : 3 * D, :]).astype(bf16)
    lane, masks = head_masks()
    for pair in range(HEADS // 2):
        at = pair * 128
        queries = qkv_ref[:, at : at + 128]
        keys = qkv_ref[:, D + at : D + at + 128]
        vals = qkv_ref[:, 2 * D + at : 2 * D + at + 128]
        outs = []
        for half in range(2):
            scores = dot_nt(queries * masks[half], keys) * 0.125
            powers = jnp.exp(scores - jnp.max(scores, axis=-1, keepdims=True))
            probs = (powers * (1.0 / jnp.sum(powers, axis=-1, keepdims=True))).astype(bf16)
            outs.append(dot_nn(probs, vals))
        att_ref[:, at : at + 128] = jnp.where(lane < 64, outs[0], outs[1]).astype(bf16)
    branch = dot_nt(att_ref[...], w_ref[3 * D : 4 * D, :])
    branch_ref[...] = branch
    middle = tokens + mod_row(mods_ref, item, 2) * branch
    mid_ref[...] = middle
    unit, _ = norm_parts(middle)
    n2_ref[...] = (unit * (1.0 + mod_row(mods_ref, item, 4)) + mod_row(mods_ref, item, 3)).astype(bf16)


def attn_bwd_kernel(
    gn2_ref, g_ref, mid_ref, x_ref, normed_ref, qkv_ref, att_ref, branch_ref, mods_ref, gg_ref, w_ref,
    gx_ref, gmods_ref, dw_ref, dqkv, acc,
):
    item = pl.program_id(0)

    @pl.when(item == 0)
    def _():
        acc[...] = jnp.zeros_like(acc)
        gmods_ref[...] = jnp.zeros_like(gmods_ref)

    grad_mid, dshift, dscale = norm_back(mid_ref[...], mod_row(mods_ref, item, 4), gn2_ref[...])
    grad_mid = grad_mid + g_ref[...]
    dgate = jnp.sum(grad_mid * branch_ref[...], axis=0, keepdims=True)
    gmods_ref[pl.ds(item, 1), 2 * D : 3 * D] = dgate
    gmods_ref[pl.ds(item, 1), 3 * D : 4 * D] = dshift
    gmods_ref[pl.ds(item, 1), 4 * D : 5 * D] = dscale
    gmods_ref[pl.ds(item, 1), 5 * D : 6 * D] = gg_ref[pl.ds(item, 1), :]
    grad_branch = (mod_row(mods_ref, item, 2) * grad_mid).astype(bf16)
    acc[3 * D : 4 * D, :] += dot_tn(grad_branch, att_ref[...])
    grad_att = dot_nn(grad_branch, w_ref[3 * D : 4 * D, :]).astype(bf16)
    lane, masks = head_masks()
    for pair in range(HEADS // 2):
        at = pair * 128
        queries = qkv_ref[:, at : at + 128]
        keys = qkv_ref[:, D + at : D + at + 128]
        vals = qkv_ref[:, 2 * D + at : 2 * D + at + 128]
        grad_out = grad_att[:, at : at + 128]
        parts = []
        for half in range(2):
            scores = dot_nt(queries * masks[half], keys) * 0.125
            powers = jnp.exp(scores - jnp.max(scores, axis=-1, keepdims=True))
            probs = powers * (1.0 / jnp.sum(powers, axis=-1, keepdims=True))
            grad_vals = dot_tn(probs.astype(bf16), grad_out)
            grad_probs = dot_nt(grad_out * masks[half], vals)
            inner = jnp.sum(probs * grad_probs, axis=-1, keepdims=True)
            grad_scores = (probs * (grad_probs - inner)).astype(bf16)
            parts.append((dot_nn(grad_scores, keys) * 0.125, dot_tn(grad_scores, queries) * 0.125, grad_vals))
        for place in range(3):
            dqkv[:, place * D + at : place * D + at + 128] = jnp.where(
                lane < 64, parts[0][place], parts[1][place]
            ).astype(bf16)
    acc[0 : 3 * D, :] += dot_tn(dqkv[...], normed_ref[...])
    grad_normed = dot_nn(dqkv[...], w_ref[0 : 3 * D, :])
    grad_in, dshift, dscale = norm_back(x_ref[...], mod_row(mods_ref, item, 1), grad_normed)
    gx_ref[...] = grad_in + grad_mid
    gmods_ref[pl.ds(item, 1), 0:D] = dshift
    gmods_ref[pl.ds(item, 1), D : 2 * D] = dscale

    @pl.when(item == pl.num_programs(0) - 1)
    def _():
        dw_ref[0 : 4 * D, :] = acc[...].astype(bf16)
        dw_ref[4 * D :, :] = jnp.zeros_like(dw_ref[4 * D :, :])


def gelu_both(values):
    outer = 0.7978845608028654
    cubic = outer * 0.044715
    square = values * values
    angle = jnp.tanh(values * (square * cubic + outer))
    half = 0.5 * values
    above = 1.0 + angle
    slope = above * (half * (square * (3.0 * cubic) + outer) * (1.0 - angle) + 0.5)
    return (half * above).astype(bf16), slope.astype(bf16)


def gate_column(g4_ref, rows, expert):
    gates = g4_ref[rows, :]
    lane = lax.broadcasted_iota(jnp.int32, gates.shape, 1)
    return jnp.sum(jnp.where(lane == expert, gates, 0.0), axis=1, keepdims=True)


def ffn_fwd_kernel(shared_steps, halves, gathers, n2_ref, mid_ref, mods_ref, g4_ref, up_ref, dn_ref, ex_ref, *rest):
    step = pl.program_id(0)
    given, (act_ref, dg_ref, mixed_ref, x_ref) = rest[:gathers], rest[gathers : gathers + 4]
    taken, (acc, racc), sems = rest[gathers + 4 : 2 * gathers + 4], rest[2 * gathers + 4 : 2 * gathers + 6], rest[2 * gathers + 6 :]
    if gathers:
        gather_beside(step, pl.num_programs(0) - 1, given, taken, sems)
    items = n2_ref.shape[0] // PATCHES

    @pl.when(step == 0)
    def _():
        acc[...] = jnp.zeros_like(acc)
        racc[...] = jnp.zeros_like(racc)

    @pl.when(step < shared_steps)
    def _():
        for block in range(n2_ref.shape[0] // FWD_ROWS):
            rows = pl.ds(block * FWD_ROWS, FWD_ROWS)
            active, slope = gelu_both(dot_nt(n2_ref[rows, :], up_ref[...]))
            act_ref[0, rows, :] = active
            dg_ref[0, rows, :] = slope
            acc[rows, :] += dot_nn(active, dn_ref[...])

    @pl.when(step >= shared_steps)
    def _():
        for block in range(n2_ref.shape[0] // FWD_ROWS):
            rows = pl.ds(block * FWD_ROWS, FWD_ROWS)
            active, slope = gelu_both(dot_nn(n2_ref[rows, :], ex_ref[0, 0]))
            act_ref[0, rows, :] = active
            dg_ref[0, rows, :] = slope
            racc[rows, :] += dot_nt(active, ex_ref[0, 1])

    expert, half = (step - shared_steps) // halves, (step - shared_steps) % halves

    @pl.when((step >= shared_steps) & (half == halves - 1))
    def _():
        for item in range(items):
            rows = pl.ds(item * PATCHES, PATCHES)
            acc[rows, :] += gate_column(g4_ref, rows, expert) * racc[rows, :].astype(bf16).astype(f32)
            racc[rows, :] = jnp.zeros((PATCHES, D), f32)

    @pl.when(step == pl.num_programs(0) - 1)
    def _():
        mixed_ref[...] = acc[...]
        for item in range(items):
            rows = pl.ds(item * PATCHES, PATCHES)
            x_ref[rows, :] = mid_ref[rows, :] + mod_row(mods_ref, item, 5) * acc[rows, :]


EARLY = 2
END_ROUTES = {0: [(3, 1), (2, 1), (1, 1)], 3: [(0, -1), (1, -1), (2, -1)]}


def early_slot(owner, step, place):
    return 4 if step == -1 and owner == place - 1 else owner


def early_beside(step, last, dex, chip_out, came_out, chip, local, core_send, core_recv, load_sem, line_send, line_recv, out_sem):
    at, core = lax.axis_index(LINE), lax.axis_index(CORE)
    units = reduce_units()[:EARLY]
    sibling = {CORE: 1 - core}

    def source(unit, which):
        _, matrix, row, rows, _, _ = units[unit]
        return dex.at[:, which, matrix, pl.ds(row, rows)]

    def given(unit):
        return pltpu.make_async_remote_copy(
            source(unit, 1 - core), chip.at[unit], core_send.at[unit], core_recv.at[unit],
            device_id=sibling, device_id_type=MESH_ID,
        )

    def loaded(unit):
        return pltpu.make_async_copy(source(unit, core), local.at[unit], load_sem.at[unit])

    def stored(unit):
        return pltpu.make_async_copy(chip.at[unit], chip_out.at[unit], out_sem.at[unit])

    def sent(unit, place, owner, direction):
        slot = early_slot(owner, direction, place)
        return pltpu.make_async_remote_copy(
            chip.at[unit, owner], came_out.at[unit, slot], line_send.at[unit, owner], line_recv.at[unit, slot],
            device_id={LINE: at + direction}, device_id_type=MESH_ID,
        )

    @pl.when(step == 0)
    def _():
        greet([sibling], at, 4)
        for unit in range(EARLY):
            given(unit).start()
            loaded(unit).start()

    for unit in range(EARLY):

        @pl.when(step == 1 + unit)
        def _(unit=unit):
            given(unit).wait_recv()
            loaded(unit).wait()
            for owner in range(4):

                def add(tile, owner=owner):
                    total = chip[unit, owner, tile, :].astype(f32) + local[unit, owner, tile, :].astype(f32)
                    chip[unit, owner, tile, :] = total.astype(bf16)

                row_tiles(units[unit][3], add)
            stored(unit).start()
            for place, routes in END_ROUTES.items():

                @pl.when(at == place)
                def _(place=place, routes=routes):
                    for owner, direction in routes:
                        sent(unit, place, owner, direction).start()

    @pl.when(step == last)
    def _():
        for unit in range(EARLY):
            given(unit).wait_send()
            stored(unit).wait()
            for place, routes in END_ROUTES.items():

                @pl.when(at == place)
                def _(unit=unit, place=place, routes=routes):
                    for owner, direction in routes:
                        sent(unit, place, owner, direction).wait_send()

                @pl.when(at == place + routes[0][1])
                def _(unit=unit, place=place, routes=routes):
                    for owner, direction in routes:
                        slot = early_slot(owner, direction, place)
                        pltpu.make_async_remote_copy(
                            came_out.at[unit, slot], came_out.at[unit, slot], line_send.at[unit, owner],
                            line_recv.at[unit, slot], device_id=sibling, device_id_type=MESH_ID,
                        ).wait_recv()


def ffn_bwd_kernel(
    shared_steps, halves, early, g_ref, n2_ref, mods_ref, g4_ref, mixed_ref, act_ref, dg_ref, up_ref, dn_ref, ex_ref, *rest
):
    step = pl.program_id(0)
    if early:
        other_dex, *rest = rest
        early_refs = [other_dex] + rest[5:7] + rest[14:]
        rest = rest[:5] + rest[7:14]
        early_beside(step, pl.num_programs(0) - 1, *early_refs)
    dup_ref, ddn_ref, dex_ref, gn2_ref, gg_ref, gmix, gs, gst, n2t, din, acc, racc = rest
    items = n2_ref.shape[0] // PATCHES

    @pl.when(step == 0)
    def _():
        gg_ref[...] = jnp.zeros_like(gg_ref)
        dup_ref[0:D, :] = jnp.zeros((D, D), bf16)
        for item in range(items):
            rows = pl.ds(item * PATCHES, PATCHES)
            grad = g_ref[rows, :]
            gg_ref[pl.ds(item, 1), :] = jnp.sum(grad * mixed_ref[rows, :], axis=0, keepdims=True)
            grad = mod_row(mods_ref, item, 5) * grad
            gmix[rows, :] = grad
            gs[rows, :] = grad.astype(bf16)
            gst[:, rows] = grad.astype(bf16).T
            n2t[:, rows] = n2_ref[rows, :].T
        acc[...] = jnp.zeros_like(acc)
        racc[...] = jnp.zeros_like(racc)

    @pl.when(step < shared_steps)
    def _():
        for block in range(n2_ref.shape[0] // BWD_ROWS):
            rows = pl.ds(block * BWD_ROWS, BWD_ROWS)
            inner = (dot_nt(gs[rows, :], dn_ref[...]) * dg_ref[0, rows, :].astype(f32)).astype(bf16)
            din[rows, :] = inner
            acc[rows, :] += dot_nn(inner, up_ref[...])
        at = dup_ref.shape[0] - shared_steps * CHUNK + step * CHUNK
        dup_ref[pl.ds(pl.multiple_of(at, D), CHUNK), :] = dot_nn(n2t[...], din[...]).astype(bf16).T
        ddn_ref[...] = dot_nn(gst[...], act_ref[0]).astype(bf16).T

    @pl.when(step >= shared_steps)
    def _():
        expert, half = (step - shared_steps) // halves, (step - shared_steps) % halves

        @pl.when(half == 0)
        def _():
            for item in range(items):
                rows = pl.ds(item * PATCHES, PATCHES)
                grad = (gate_column(g4_ref, rows, expert) * gmix[rows, :]).astype(bf16)
                gs[rows, :] = grad
                gst[:, rows] = grad.T

        for block in range(n2_ref.shape[0] // BWD_ROWS):
            rows = pl.ds(block * BWD_ROWS, BWD_ROWS)
            inner = (dot_nn(gs[rows, :], ex_ref[0, 1]) * dg_ref[0, rows, :].astype(f32)).astype(bf16)
            din[rows, :] = inner
            racc[rows, :] += dot_nt(inner, ex_ref[0, 0])

        dex_ref[0, 0] = dot_nn(n2t[...], din[...]).astype(bf16)
        dex_ref[0, 1] = dot_nn(gst[...], act_ref[0]).astype(bf16)

        @pl.when(half == halves - 1)
        def _():
            acc[...] += racc[...].astype(bf16).astype(f32)
            racc[...] = jnp.zeros_like(racc)

    @pl.when(step == pl.num_programs(0) - 1)
    def _():
        gn2_ref[...] = acc[...]


def final_kernel(x_ref, mods_ref, fo_ref, tgt_ref, gx_ref, gfm_ref, dfo_ref, loss_ref):
    item = pl.program_id(0)

    @pl.when(item == 0)
    def _():
        gfm_ref[...] = jnp.zeros_like(gfm_ref)
        dfo_ref[...] = jnp.zeros_like(dfo_ref)
        loss_ref[...] = jnp.zeros_like(loss_ref)

    tokens = x_ref[...]
    unit, _ = norm_parts(tokens)
    scale = mod_row(mods_ref, item, 1)
    normed = (unit * (1.0 + scale) + mod_row(mods_ref, item, 0)).astype(bf16)
    err = dot_nt(fo_ref[...], normed) - tgt_ref[...]
    loss_ref[...] += jnp.sum(err * err, axis=1, keepdims=True)
    grad_pred = (2.0 * err).astype(bf16)
    dfo_ref[...] += dot_nn(grad_pred, normed)
    grad_in, dshift, dscale = norm_back(tokens, scale, dot_tn(grad_pred, fo_ref[...]))
    gx_ref[...] = grad_in
    gfm_ref[pl.ds(item, 1), 0:D] = dshift
    gfm_ref[pl.ds(item, 1), D : 2 * D] = dscale


def params(limit):
    return pltpu.CompilerParams(vmem_limit_bytes=limit * MIB)


def cost(multiplies, moved):
    return pl.CostEstimate(flops=2 * multiplies, bytes_accessed=moved, transcendentals=0)


def whole(shape):
    return pl.BlockSpec(shape, lambda step: (0,) * len(shape))


def rows_of(width):
    return pl.BlockSpec((PATCHES, width), lambda step: (step, 0))


def shape_of(shape, kind):
    return jax.ShapeDtypeStruct(shape, kind)


ADA_STEPS = 6 * D // CHUNK
ADA_AT = 4 * D // CHUNK


def cond_forward(feat, hot, stem_t, lin):
    shapes = [(8, D)] * 4 + [(LAYERS, 8, 6 * D), (8, 2 * D)]
    return pl.pallas_call(
        cond_kernel,
        grid=(ADA_STEPS,),
        in_specs=[
            whole(feat.shape),
            whole(hot.shape),
            whole(stem_t.shape),
            pl.BlockSpec((LAYERS, CHUNK, D), lambda step: (0, ADA_AT + step, 0)),
        ],
        out_specs=[whole((8, D))] * 4 + [pl.BlockSpec((LAYERS, 8, CHUNK), lambda step: (0, 0, step)), whole((8, 2 * D))],
        out_shape=[shape_of(shape, f32) for shape in shapes],
        compiler_params=params(60),
        name="cond_forward",
    )(feat, hot, stem_t, lin)


def cond_backward(gm_a, gm_b, gfm, pre_one, pre_two, stem_t, lin):
    columns = pl.BlockSpec((8, CHUNK), lambda step: (0, step))
    return pl.pallas_call(
        cond_back_kernel,
        grid=(ADA_STEPS,),
        in_specs=[columns, columns, whole(gfm.shape), whole((8, D)), whole((8, D)), whole(stem_t.shape)]
        + [pl.BlockSpec((LAYERS, CHUNK, D), lambda step: (0, ADA_AT + step, 0))],
        out_specs=[whole((8, D))] * 2,
        out_shape=[shape_of((8, D), f32)] * 2,
        compiler_params=params(60),
        name="cond_backward",
    )(gm_a, gm_b, gfm, pre_one, pre_two, stem_t, lin)


def attn_forward(layer, tokens, mods, lin):
    count = tokens.shape[0]
    return pl.pallas_call(
        attn_fwd_kernel,
        grid=(count // PATCHES,),
        in_specs=[rows_of(D), whole(mods.shape), attn_weights(layer)],
        out_specs=[rows_of(D), rows_of(3 * D), rows_of(D), rows_of(D), rows_of(D), rows_of(D)],
        out_shape=[
            shape_of((count, D), bf16),
            shape_of((count, 3 * D), bf16),
            shape_of((count, D), bf16),
            shape_of((count, D), f32),
            shape_of((count, D), f32),
            shape_of((count, D), bf16),
        ],
        compiler_params=params(60),
        cost_estimate=cost(count * D * 4 * D * 9, 16 * count * D),
        name="attention_forward",
    )(tokens, mods, lin)


def attn_weights(layer):
    return pl.BlockSpec((None, 4 * D, D), lambda step: (layer, 0, 0))


def attn_backward(layer, gn2, grad, middle, tokens, normed, qkv, attended, branch, mods, grad_gate, lin, out_rows):
    count = tokens.shape[0]
    return pl.pallas_call(
        attn_bwd_kernel,
        grid=(count // PATCHES,),
        in_specs=[rows_of(D)] * 5
        + [rows_of(3 * D), rows_of(D), rows_of(D), whole(mods.shape), whole(grad_gate.shape), attn_weights(layer)],
        out_specs=[rows_of(D), whole((8, 6 * D)), whole((out_rows, D))],
        out_shape=[shape_of((count, D), f32), shape_of((8, 6 * D), f32), shape_of((out_rows, D), bf16)],
        scratch_shapes=[pltpu.VMEM((PATCHES, 3 * D), bf16), pltpu.VMEM((4 * D, D), f32)],
        compiler_params=params(60),
        cost_estimate=cost(count * D * 4 * D * 22, 16 * count * D),
        name="attention_backward",
    )(gn2, grad, middle, tokens, normed, qkv, attended, branch, mods, grad_gate, lin)


def weight_specs(layer, shared_steps, lin_rows):
    up_at = lin_rows // CHUNK - shared_steps
    return [
        pl.BlockSpec((None, CHUNK, D), lambda step: (layer, up_at + jnp.minimum(step, shared_steps - 1), 0)),
        pl.BlockSpec((CHUNK, D), lambda step: (jnp.minimum(step, shared_steps - 1), 0)),
        pl.BlockSpec((1, 2, D, CHUNK), lambda step: (jnp.maximum(step - shared_steps, 0), 0, 0, 0)),
    ]


def ffn_forward(layer, n2, middle, mods, g4, lin, lout, experts_w, halves, beside=()):
    count = n2.shape[0]
    shared_steps = lout.shape[0] // CHUNK
    steps = shared_steps + experts_w.shape[0]
    wide = pl.BlockSpec((1, count, CHUNK), lambda step: (step, 0, 0))
    anywhere = [pl.BlockSpec(memory_space=pl.ANY)] * len(beside)
    remote = pltpu.CompilerParams(vmem_limit_bytes=60 * MIB, collective_id=7, has_side_effects=True)
    return pl.pallas_call(
        functools.partial(ffn_fwd_kernel, shared_steps, halves, len(beside)),
        grid=(steps,),
        in_specs=[whole(n2.shape), whole(middle.shape), whole(mods.shape), whole(g4.shape)]
        + weight_specs(layer, shared_steps, lin.shape[1])
        + anywhere,
        out_specs=[wide, wide, whole((count, D)), whole((count, D))] + anywhere,
        out_shape=[
            shape_of((steps, count, CHUNK), bf16),
            shape_of((steps, count, CHUNK), bf16),
            shape_of((count, D), f32),
            shape_of((count, D), f32),
        ]
        + [shape_of((8,) + part.shape, bf16) for part in beside],
        scratch_shapes=[pltpu.VMEM((count, D), f32)] * 2 + (gather_semaphores(4) if beside else []),
        compiler_params=remote if beside else params(60),
        cost_estimate=cost(4 * steps * count * D * CHUNK * 2, 8 * steps * count * CHUNK),
        name="ffn_forward",
    )(n2, middle, mods, g4, lin, lout, experts_w, *beside)


def ffn_backward(layer, grad, n2, mods, g4, mixed, active, slope, lin, lout, experts_w, halves, early=()):
    count = n2.shape[0]
    shared_steps = lout.shape[0] // CHUNK
    steps = shared_steps + experts_w.shape[0]
    wide = pl.BlockSpec((1, count, CHUNK), lambda step: (step, 0, 0))
    specs = weight_specs(layer, shared_steps, lin.shape[1])
    anywhere = [pl.BlockSpec(memory_space=pl.ANY)] * len(early)
    remote = pltpu.CompilerParams(vmem_limit_bytes=62 * MIB, collective_id=8, has_side_effects=True)
    dma = pltpu.SemaphoreType.DMA
    early_scratch = [pltpu.VMEM((EARLY, 4, D // 2, CHUNK), bf16)] * 2
    early_scratch += [dma((EARLY,)), dma((EARLY,)), dma((EARLY,)), dma((EARLY, 4)), dma((EARLY, 5)), dma((EARLY,))]
    return pl.pallas_call(
        functools.partial(ffn_bwd_kernel, shared_steps, halves, len(early)),
        grid=(steps,),
        in_specs=[whole(grad.shape), whole(n2.shape), whole(mods.shape), whole(g4.shape), whole(mixed.shape), wide, wide]
        + specs
        + anywhere,
        out_specs=[whole((lout.shape[0] + D, D)), specs[1], specs[2], whole((count, D)), whole((8, D))] + anywhere * 2,
        out_shape=[
            shape_of((lout.shape[0] + D, D), bf16),
            shape_of(lout.shape, bf16),
            shape_of(experts_w.shape, bf16),
            shape_of((count, D), f32),
            shape_of((8, D), f32),
        ]
        + [shape_of((EARLY, lead, D // 2, CHUNK), bf16) for lead in (4, 5) if early],
        scratch_shapes=[
            pltpu.VMEM((count, D), f32),
            pltpu.VMEM((count, D), bf16),
            pltpu.VMEM((D, count), bf16),
            pltpu.VMEM((D, count), bf16),
            pltpu.VMEM((count, CHUNK), bf16),
            pltpu.VMEM((count, D), f32),
            pltpu.VMEM((count, D), f32),
        ]
        + (early_scratch if early else []),
        compiler_params=remote if early else params(60),
        cost_estimate=cost(4 * steps * count * D * CHUNK * 4 // 2, 8 * steps * count * CHUNK),
        name="ffn_backward",
    )(grad, n2, mods, g4, mixed, active, slope, lin, lout, experts_w, *early)


def final_step(tokens, mods, fo_rows, target_t):
    count = tokens.shape[0]
    return pl.pallas_call(
        final_kernel,
        grid=(count // PATCHES,),
        in_specs=[
            rows_of(D),
            whole(mods.shape),
            whole(fo_rows.shape),
            pl.BlockSpec((PATCH_DIM, PATCHES), lambda step: (0, step)),
        ],
        out_specs=[rows_of(D), whole((8, 2 * D)), whole((PATCH_DIM, D)), whole((PATCH_DIM, 1))],
        out_shape=[
            shape_of((count, D), f32),
            shape_of((8, 2 * D), f32),
            shape_of((PATCH_DIM, D), f32),
            shape_of((PATCH_DIM, 1), f32),
        ],
        compiler_params=params(60),
        name="final_step",
    )(tokens, mods, fo_rows, target_t)


def update_kernel(groups, grad_a, grad_b, total_a, total_b, w_ref, f_ref, s_ref, m_ref, new_ref, half_ref, fn_ref, sn_ref, mn_ref):
    for layer, (grad_ref, total_ref) in enumerate(((grad_a, total_a), (grad_b, total_b))):

        @pl.when(pl.program_id(0) == layer)
        def _(grad_ref=grad_ref, total_ref=total_ref):
            gradient = grad_ref[...]
            fn_ref[0] = beta_one * f_ref[0] + (1.0 - beta_one) * gradient
            sn_ref[0] = beta_two * s_ref[0] + (1.0 - beta_two) * gradient * gradient
            mean_delta = total_ref[...] / groups
            moment_new = outer_mom * m_ref[0] + mean_delta
            weight = w_ref[0] - outer_rate * (mean_delta + outer_mom * moment_new)
            mn_ref[0] = moment_new
            new_ref[0] = weight
            half_ref[0] = weight.astype(bf16)


def update_arrays(tile, grads, totals, weight, first, second, moment):
    layers, rows, width = weight.shape
    tiles = rows // tile
    state = pl.BlockSpec((1, tile, width), lambda layer, step: (layer, step, 0))
    early = pl.BlockSpec((tile, width), lambda layer, step: (jnp.where(layer == 0, step, tiles - 1), 0))
    late = pl.BlockSpec((tile, width), lambda layer, step: (jnp.where(layer == 0, 0, step), 0))
    return pl.pallas_call(
        functools.partial(update_kernel, lax.axis_size(GROUP)),
        grid=(layers, tiles),
        in_specs=[early, late, early, late] + [state] * 4,
        out_specs=[state] * 5,
        out_shape=[shape_of(weight.shape, kind) for kind in (f32, bf16, f32, f32, f32)],
        compiler_params=params(60),
        name="update_arrays",
    )(*grads, *totals, weight, first, second, moment)


def pad_rows(values):
    return jnp.pad(values, ((0, 8 - values.shape[0]), (0, 0)))


def stem_lanes(stem_t):
    pieces, at = [], 0
    for size, padded in zip(STEM_SIZES, STEM_PADDED):
        pieces.append(jnp.pad(stem_t[:, at : at + size], ((0, 0), (0, padded - size))))
        at = at + size
    pieces.append(jnp.zeros((stem_t.shape[0], STEM_LANES - sum(STEM_PADDED)), stem_t.dtype))
    return jnp.concatenate(pieces, axis=1)


MESH_ID = pl.DeviceIdType.MESH
TILE = 48


def plane_partners():
    group = lax.axis_index(GROUP)
    return {GROUP: group + 1 - 2 * lax.rem(group, 2)}, {GROUP: lax.rem(group + 2, 4)}


def greet(partners, line_at, line_size):
    barrier = pltpu.get_barrier_semaphore()
    for partner in partners:
        pl.semaphore_signal(barrier, inc=1, device_id=partner, device_id_type=MESH_ID)

    @pl.when(line_at > 0)
    def _():
        pl.semaphore_signal(barrier, inc=1, device_id={LINE: line_at - 1}, device_id_type=MESH_ID)

    @pl.when(line_at < line_size - 1)
    def _():
        pl.semaphore_signal(barrier, inc=1, device_id={LINE: line_at + 1}, device_id_type=MESH_ID)

    ends = jnp.where(line_at == 0, 1, 0) + jnp.where(line_at == line_size - 1, 1, 0)
    pl.semaphore_wait(barrier, len(partners) + 2 - ends)


def row_tiles(rows, body):
    def step(index, carry):
        body(pl.ds(pl.multiple_of(index * TILE, TILE), TILE))
        return carry

    lax.fori_loop(0, rows // TILE, step, 0)


def adam_delta(weight, gradient, first, second):
    return adam_step(weight, gradient, first, second)[0]


def reduce_units():
    units = []
    for matrix in range(2):
        for half in range(2):
            units.append((0, matrix, half * D // 2, D // 2, CHUNK, ()))
    for half in range(2):
        units.append((1, 0, half * 432, 432, D, (1,)))
    units.append((2, 0, 0, D, D, ()))
    return units


def reduce_kernel(
    layer, with_stem, dex, dqkvo, dup, ddn, extra, ex_w, ex_f, ex_s, li_w, li_f, li_s, lo_w, lo_f, lo_s, *rest
):
    early = EARLY if with_stem else 0
    if early:
        chip_in, came_in, *rest = rest
    if with_stem:
        stem_in, *rest, stem_sem, stem_send, stem_recv, stem_a, stem_b, stem_c, stem_d = rest
        stem_out = rest.pop(6)
    g_ex, g_li, g_lo, m_ex, m_li, m_lo, *scratch = rest
    units = reduce_units()
    number = len(units)
    banks = [scratch[at * number : (at + 1) * number] for at in range(9)]
    chip, local, came, delta, swapped, swapped_two, weight, first, second = banks
    extra_buf = scratch[9 * number]
    core_send, core_recv, line_send, line_recv, load_sem, plane_send, plane_recv, out_sem = scratch[9 * number + 1 :]
    at = lax.axis_index(LINE)
    core = lax.axis_index(CORE)
    sibling = {CORE: 1 - core}
    side_x, side_y = plane_partners()
    greet([sibling, side_x, side_y], at, 4)

    def pieces(unit, which):
        kind, matrix, row, rows, _, _ = units[unit]
        if kind == 0:
            return [(dex.at[:, which, matrix, pl.ds(row, rows)], slice(0, 4))]
        if kind == 2:
            return [(ddn.at[:, which, pl.ds(row, rows)], slice(0, 4))]
        return [
            (dqkvo.at[which, pl.ds(row, rows)], 0),
            (dup.at[0, which, pl.ds(row, rows)], 2),
            (dup.at[1, which, pl.ds(row, rows)], 3),
        ]

    def dest(bank, unit, where):
        return bank[unit].at[pl.ds(0, 4)] if isinstance(where, slice) else bank[unit].at[where]

    if with_stem:
        load = pltpu.make_async_copy(stem_in, stem_a, stem_sem.at[0])
        load.start()
        load.wait()

    def stem_copies(second_step):
        landing, sides = ((stem_b, (side_x, side_y)), (stem_c, (side_y, side_x)))[second_step]
        return [
            pltpu.make_async_remote_copy(
                stem_a.at[pl.ds(begin, size)], landing.at[pl.ds(begin, size)], stem_send.at[2 * second_step + half],
                stem_recv.at[2 * second_step + half], device_id=sides[half], device_id_type=MESH_ID,
            )
            for half, (begin, size) in enumerate(((0, 16), (16, 32)))
        ]

    def stem_turn(turn):
        if not with_stem or turn > 2:
            return
        if turn == 0:
            for copy in stem_copies(0):
                copy.start()
        elif turn == 1:
            for copy in stem_copies(0):
                copy.wait()
            stem_a[...] = (stem_a[...].astype(f32) + stem_b[...].astype(f32)).astype(bf16)
            for copy in stem_copies(1):
                copy.start()
        else:
            for copy in stem_copies(1):
                copy.wait()
            stem_d[...] = stem_a[...].astype(f32) + stem_c[...].astype(f32)
            pltpu.make_async_copy(stem_d, stem_out, stem_sem.at[1]).start()

    early_slots = {1: [3, 2, 1], 2: [0, 1, 4]}

    def early_load(unit, slot, index):
        sem = (load_sem.at[unit, 1], load_sem.at[unit, 2], load_sem.at[number, 1 + unit])[index]
        return pltpu.make_async_copy(came_in.at[unit, slot], came[unit].at[slot], sem)

    given, loads = [], []
    for unit in range(number):
        given.append([])
        loads.append([])
        if unit < early:
            copy = pltpu.make_async_copy(chip_in.at[unit], chip[unit], load_sem.at[unit, 0])
            copy.start()
            loads[unit].append(copy)
            for place, slots in early_slots.items():

                @pl.when(at == place)
                def _(unit=unit, slots=slots):
                    for index, slot in enumerate(slots):
                        early_load(unit, slot, index).start()

            continue
        for place, (source, where) in enumerate(pieces(unit, 1 - core)):
            copy = pltpu.make_async_remote_copy(
                source, dest(chip, unit, where), core_send.at[unit, place], core_recv.at[unit, place],
                device_id=sibling, device_id_type=MESH_ID,
            )
            copy.start()
            given[unit].append(copy)
        for place, (source, where) in enumerate(pieces(unit, core)):
            copy = pltpu.make_async_copy(source, dest(local, unit, where), load_sem.at[unit, place])
            copy.start()
            loads[unit].append(copy)
    state_loads = []
    for unit, (kind, matrix, row, rows, _, _) in enumerate(units):
        if kind == 0:
            sources = [ex_w.at[layer, 0, matrix], ex_f.at[0, layer, 0, matrix], ex_s.at[0, layer, 0, matrix]]
        elif kind == 1:
            sources = [li_w.at[layer], li_f.at[layer], li_s.at[layer]]
        else:
            sources = [lo_w.at[layer], lo_f.at[0, layer], lo_s.at[0, layer]]
        state_loads.append([])
        for place, (source, bank) in enumerate(zip(sources, (weight, first, second))):
            copy = pltpu.make_async_copy(source.at[pl.ds(row, rows)], bank[unit], load_sem.at[unit, 3 + place])
            copy.start()
            state_loads[unit].append(copy)
    extra_load = pltpu.make_async_copy(extra, extra_buf, load_sem.at[number, 0])
    extra_load.start()

    def line_copy(unit, owner, step, place):
        slot = 4 if step == -1 and owner == place - 1 else owner
        return pltpu.make_async_remote_copy(
            chip[unit].at[owner], came[unit].at[slot], line_send.at[unit, owner], line_recv.at[unit, slot],
            device_id={LINE: at + step}, device_id_type=MESH_ID,
        )

    def arrived(unit, slot, place):
        if unit < early and slot in early_slots.get(place, ()):
            early_load(unit, slot, early_slots[place].index(slot)).wait()
            return
        pltpu.make_async_remote_copy(
            came[unit].at[slot], came[unit].at[slot], line_send.at[unit, 0], line_recv.at[unit, slot],
            device_id=sibling, device_id_type=MESH_ID,
        ).wait_recv()

    routes_of = {0: [(3, 1), (2, 1), (1, 1)], 1: [(3, 1), (2, 1), (0, -1)], 2: [(0, -1), (1, -1), (3, 1)], 3: [(0, -1), (1, -1), (2, -1)]}
    finals = {0: [4], 1: [1, 4], 2: [2, 4], 3: [3]}

    def forward(unit):
        rows, absent = units[unit][3], units[unit][5]
        for middle in (1, 2):

            @pl.when(at == middle)
            def _(middle=middle):
                for owner, step in routes_of[middle]:
                    if owner in absent:
                        continue
                    arrived(unit, owner, middle)

                    def add(tile, owner=owner):
                        total = chip[unit][owner, tile, :].astype(f32) + came[unit][owner, tile, :].astype(f32)
                        chip[unit][owner, tile, :] = total.astype(bf16)

                    row_tiles(rows, add)
                    line_copy(unit, owner, step, middle).start()

    for unit, (kind, matrix, row, rows, _, absent) in enumerate(units):
        for copy in given[unit]:
            copy.wait_recv()
        for copy in loads[unit]:
            copy.wait()
        for owner in range(0 if unit < early else 4):
            if owner in absent:
                chip[unit][owner] = jnp.zeros(chip[unit].shape[1:], bf16)
                continue

            def add(tile, owner=owner, unit=unit):
                total = chip[unit][owner, tile, :].astype(f32) + local[unit][owner, tile, :].astype(f32)
                chip[unit][owner, tile, :] = total.astype(bf16)

            row_tiles(rows, add)
        for end in (0, 3):

            @pl.when(at == end)
            def _(unit=unit, end=end, absent=absent):
                for owner, step in routes_of[end]:
                    if owner not in absent and unit >= early:
                        line_copy(unit, owner, step, end).start()
                came[unit][0 if end == 0 else 4] = jnp.zeros(chip[unit].shape[1:], bf16)

        for owner in absent:

            @pl.when(at == owner)
            def _(unit=unit, owner=owner):
                came[unit][owner] = jnp.zeros(chip[unit].shape[1:], bf16)
                came[unit][4] = jnp.zeros(chip[unit].shape[1:], bf16)
        if unit < early:
            forward(unit)

    def plane_copies(unit, second_step):
        rows = units[unit][3]
        middle = rows // 32 * 16
        sides = (side_y, side_x) if second_step else (side_x, side_y)
        landing = swapped_two if second_step else swapped
        copies = []
        for half, (begin, size) in enumerate(((0, middle), (middle, rows - middle))):
            part = pl.ds(begin, size)
            copies.append(
                pltpu.make_async_remote_copy(
                    delta[unit].at[part], landing[unit].at[part], plane_send.at[unit, 2 * second_step + half],
                    plane_recv.at[unit, 2 * second_step + half], device_id=sides[half], device_id_type=MESH_ID,
                )
            )
        return copies

    def out_copy(unit, means):
        kind, matrix, row, rows, _, _ = units[unit]
        target = ((g_ex.at[matrix], g_li, g_lo), (m_ex.at[matrix], m_li, m_lo))[means][kind]
        source = first[unit] if means else weight[unit]
        return pltpu.make_async_copy(source, target.at[pl.ds(row, rows)], out_sem.at[unit, means])

    firsts, seconds = {}, {}

    def finish(unit):
        kind, matrix, row, rows, _, absent = units[unit]
        for place in range(4):

            @pl.when(at == place)
            def _(place=place):
                if place not in absent:
                    for slot in finals[place]:
                        arrived(unit, slot, place)

        for copy in state_loads[unit]:
            copy.wait()
        if kind == 1 and row == 0:
            extra_load.wait()

        def body(tile):
            grad = chip[unit][at, tile, :].astype(f32) + came[unit][at, tile, :].astype(f32)
            grad = grad + came[unit][4, tile, :].astype(f32)
            if kind == 1:
                grad = grad + extra_buf[pl.ds(row + tile.start, TILE), :]
            change = adam_delta(weight[unit][tile, :], grad, first[unit][tile, :], second[unit][tile, :])
            delta[unit][tile, :] = change.astype(bf16)
            weight[unit][tile, :] = grad

        row_tiles(rows, body)
        out_copy(unit, 0).start()
        firsts[unit] = plane_copies(unit, 0)
        for copy in firsts[unit]:
            copy.start()

    def exchange(unit):
        for copy in firsts[unit]:
            copy.wait()

        def body(tile):
            total = delta[unit][tile, :].astype(f32) + swapped[unit][tile, :].astype(f32)
            delta[unit][tile, :] = total.astype(bf16)

        row_tiles(units[unit][3], body)
        seconds[unit] = plane_copies(unit, 1)
        for copy in seconds[unit]:
            copy.start()

    def close(unit):
        for copy in seconds[unit]:
            copy.wait_recv()

        def body(tile):
            first[unit][tile, :] = delta[unit][tile, :].astype(f32) + swapped_two[unit][tile, :].astype(f32)

        row_tiles(units[unit][3], body)
        out_copy(unit, 1).start()

    for turn in range(number + 3):
        stem_turn(turn)
        for lag, action in enumerate((forward, finish, exchange, close)):
            if 0 <= turn - lag < number and (lag or turn >= early):
                action(turn - lag)

    if with_stem:
        pltpu.make_async_copy(stem_d, stem_out, stem_sem.at[1]).wait()
    for unit in range(number):
        for copy in given[unit]:
            copy.wait_send()
        for copy in seconds[unit]:
            copy.wait_send()
        out_copy(unit, 0).wait()
        out_copy(unit, 1).wait()
        for place in range(4):

            @pl.when(at == place)
            def _(place=place, unit=unit):
                for owner, step in routes_of[place]:
                    if owner not in units[unit][5] and (unit >= early or place in (1, 2)):
                        line_copy(unit, owner, step, place).wait_send()


def reduce_layer(layer, dex, dqkvo, dup, ddn, extra, states, stem_delta=None, begun=()):
    units = reduce_units()
    scratch = []
    for lead, kind in (((4,), bf16), ((4,), bf16), ((5,), bf16), ((), bf16), ((), bf16), ((), bf16), ((), f32), ((), f32), ((), f32)):
        scratch += [pltpu.VMEM(lead + (unit[3], unit[4]), kind) for unit in units]
    number = len(units)
    scratch.append(pltpu.VMEM(extra.shape, f32))
    dma = pltpu.SemaphoreType.DMA
    scratch += [dma((number, 3)), dma((number, 3)), dma((number, 4)), dma((number, 5)), dma((number + 1, 6))]
    scratch += [dma((number, 4)), dma((number, 4)), dma((number, 2))]
    anywhere = pl.BlockSpec(memory_space=pl.ANY)
    shapes = [(2, D, CHUNK), extra.shape, (D, D)] * 2
    stems = [] if stem_delta is None else [stem_delta]
    for delta in stems:
        shapes.append(delta.shape)
        scratch += [dma((2,)), dma((4,)), dma((4,))] + [pltpu.VMEM(delta.shape, bf16)] * 3
        scratch.append(pltpu.VMEM(delta.shape, f32))
    return pl.pallas_call(
        functools.partial(reduce_kernel, layer, bool(stems)),
        out_shape=[shape_of(shape, f32) for shape in shapes],
        in_specs=[anywhere] * (5 + len(states) + len(stems) + len(begun)),
        out_specs=[anywhere] * len(shapes),
        scratch_shapes=scratch,
        compiler_params=pltpu.CompilerParams(
            vmem_limit_bytes=62 * MIB, collective_id=1 + layer, has_side_effects=True
        ),
        name="reduce_layer",
    )(dex, dqkvo, dup, ddn, extra, *states, *begun, *stems)


def shard_part(kind, ref, quarter, half=None):
    if kind == "stem":
        begin, size = quarter * (STEM_LANES // 4), STEM_LANES // 4
        if half is not None:
            begin, size = begin + half * (size // 2), size // 2
        return ref.at[:, pl.ds(pl.multiple_of(begin, 128), size)]
    if kind == "lin":
        begin, size = lax.rem(quarter, 2) * 432, 432
        if half is not None:
            begin, size = begin + half * 208, (208, 224)[half]
        return ref.at[quarter // 2, pl.ds(pl.multiple_of(begin, 16), size)]
    begin, size = quarter * (D // 4), D // 4
    if half is not None:
        begin, size = begin + half * (size // 2), size // 2
    return ref.at[pl.ds(pl.multiple_of(begin, 16), size)]


class WeightGather:
    def __init__(self, kinds, sources, targets, sends, recvs, cores_send, cores_recv, own_sem):
        self.kinds, self.sources, self.targets = kinds, sources, targets
        self.sends, self.recvs = sends, recvs
        self.cores_send, self.cores_recv, self.own_sem = cores_send, cores_recv, own_sem
        self.at, self.core, self.group = lax.axis_index(LINE), lax.axis_index(CORE), lax.axis_index(GROUP)
        self.sibling = {CORE: 1 - self.core}
        self.side_x, self.side_y = plane_partners()
        self.group_x = self.group + 1 - 2 * lax.rem(self.group, 2)
        self.group_y = lax.rem(self.group + 2, 4)
        near = jnp.where(self.at == 3, 3, 1)
        far = jnp.where(self.at == 0, 3, jnp.where(self.at == 3, 1, 2))
        self.order = (near, 6 - near - far, far)

    def enter(self):
        barrier = pltpu.get_barrier_semaphore()
        others = [{LINE: lax.rem(self.at + step, 4)} for step in (1, 2, 3)]
        for partner in others + [self.sibling, self.side_x, self.side_y]:
            pl.semaphore_signal(barrier, inc=1, device_id=partner, device_id_type=MESH_ID)
        pl.semaphore_wait(barrier, 6)

    def whole_part(self, unit, owner, core):
        target = self.targets[unit]
        if self.kinds[unit] == "lin":
            return target.at[:, owner * 2 + core]
        return target.at[owner * 2 + core]

    def copy(self, unit, source, target, slot, kind, device):
        return pltpu.make_async_remote_copy(
            source, target, self.sends.at[unit, slot, kind], self.recvs.at[unit, slot, kind],
            device_id=device, device_id_type=MESH_ID,
        )

    def line_copy(self, unit, step):
        target = shard_part(self.kinds[unit], self.whole_part(unit, self.at, self.core), self.group)
        source = shard_part(self.kinds[unit], self.sources[unit], self.group)
        return pltpu.make_async_remote_copy(
            source, target, self.sends.at[unit, step - 1, 0], self.recvs.at[unit, 3 - step, 0],
            device_id={LINE: lax.rem(self.at + step, 4)}, device_id_type=MESH_ID,
        )

    def owner_of(self, slot):
        return lax.rem(self.at + slot, 4)

    def part(self, unit, slot, quarter, half=None):
        return shard_part(self.kinds[unit], self.whole_part(unit, self.owner_of(slot), self.core), quarter, half)

    def core_copy(self, unit, slot, own=False):
        source = self.sources[unit] if own else self.whole_part(unit, self.owner_of(slot), self.core)
        return pltpu.make_async_remote_copy(
            source, self.whole_part(unit, self.owner_of(slot), self.core),
            self.cores_send.at[unit, slot], self.cores_recv.at[unit, slot],
            device_id=self.sibling, device_id_type=MESH_ID,
        )

    def own_copy(self, unit):
        return pltpu.make_async_copy(
            self.sources[unit], self.whole_part(unit, self.at, self.core), self.own_sem.at[unit]
        )

    def begin(self, unit):
        for step in (2, 1, 3):
            self.line_copy(unit, step).start()
        self.core_copy(unit, 0, True).start()
        self.own_copy(unit).start()

    def plane_copies(self, unit, slot):
        mine = self.part(unit, slot, self.group)
        return [self.copy(unit, mine, mine, slot - 1, 1, self.side_x), self.copy(unit, mine, mine, slot - 1, 2, self.side_y)]

    def plane_arrivals(self, unit, slot):
        parts = [self.part(unit, slot, self.group_x), self.part(unit, slot, self.group_y)]
        return [self.copy(unit, parts[0], parts[0], slot - 1, 1, self.side_x), self.copy(unit, parts[1], parts[1], slot - 1, 2, self.side_y)]

    def corner_copies(self, unit, slot):
        parts = [self.part(unit, slot, self.group_x, 0), self.part(unit, slot, self.group_y, 1)]
        return [self.copy(unit, parts[0], parts[0], slot - 1, 3, self.side_y), self.copy(unit, parts[1], parts[1], slot - 1, 4, self.side_x)]

    def corner_arrivals(self, unit, slot):
        corner = 3 - self.group
        parts = [self.part(unit, slot, corner, 0), self.part(unit, slot, corner, 1)]
        return [self.copy(unit, parts[0], parts[0], slot - 1, 3, self.side_y), self.copy(unit, parts[1], parts[1], slot - 1, 4, self.side_x)]

    def along_line(self, unit):
        for slot in self.order:
            mine = self.part(unit, slot, self.group)
            self.copy(unit, mine, mine, slot - 1, 0, self.sibling).wait_recv()
            for copy in self.plane_copies(unit, slot):
                copy.start()

    def in_plane(self, unit):
        for slot in self.order:
            for copy in self.plane_arrivals(unit, slot):
                copy.wait_recv()
            for copy in self.corner_copies(unit, slot):
                copy.start()

    def to_sibling(self, unit):
        for slot in self.order:
            for copy in self.corner_arrivals(unit, slot):
                copy.wait_recv()
            self.core_copy(unit, slot).start()

    def end(self, unit):
        self.own_copy(unit).wait()
        for slot in range(4):
            self.core_copy(unit, slot, slot == 0).wait_send()
            other = self.whole_part(unit, self.owner_of(slot), 1 - self.core)
            pltpu.make_async_remote_copy(
                other, other, self.cores_send.at[unit, slot], self.cores_recv.at[unit, slot],
                device_id=self.sibling, device_id_type=MESH_ID,
            ).wait_recv()
        for slot in (1, 2, 3):
            self.line_copy(unit, slot).wait_send()
            for copy in self.plane_copies(unit, slot) + self.corner_copies(unit, slot):
                copy.wait_send()


def gather_semaphores(number):
    dma = pltpu.SemaphoreType.DMA
    return [dma((number, 3, 5)), dma((number, 3, 5)), dma((number, 4)), dma((number, 4)), dma((number,))]


def gather_kernel(kinds, split, *refs):
    count = len(split)
    arrays_in, arrays_out, sems = refs[:count], refs[count : 2 * count], refs[2 * count :]
    sources, targets = [], []
    for given, target, parts in zip(arrays_in, arrays_out, split):
        for part in parts:
            sources.append(given if part is None else given.at[part])
            targets.append(target if part is None else target.at[(slice(None),) + part])
    work = WeightGather(kinds, sources, targets, *sems)
    work.enter()
    number = len(kinds)
    work.begin(0)
    work.begin(1)
    for turn in range(number + 2):
        for lag, action in enumerate((work.along_line, work.in_plane, work.to_sibling)):
            if 0 <= turn - lag < number:
                action(turn - lag)
            if lag == 0 and turn + 2 < number:
                work.begin(turn + 2)
    for unit in range(number):
        work.end(unit)


def gather_beside(step, last, given, taken, sems):
    parts = [(matrix, slice(None), pl.ds(begin, D)) for matrix in range(2) for begin in (0, D)]
    sources = [given[0].at[part] for part in parts]
    targets = [taken[0].at[(slice(None),) + part] for part in parts]
    work = WeightGather(["rows"] * 4, sources, targets, *sems)
    line, plane, pair = work.along_line, work.in_plane, work.to_sibling
    schedule = {
        0: [(work.begin, 0), (work.begin, 1)],
        2: [(line, 0), (work.begin, 2)],
        3: [(line, 1), (work.begin, 3)],
        5: [(plane, 0), (line, 2)],
        6: [(plane, 1), (line, 3)],
        8: [(pair, 0), (plane, 2)],
        9: [(pair, 1), (plane, 3)],
        10: [(pair, 2)],
        11: [(pair, 3)] + [(work.end, unit) for unit in range(4)],
    }
    for when, actions in schedule.items():

        @pl.when(step == (last if when == 11 else when))
        def _(when=when, actions=actions):
            if when == 0:
                work.enter()
            for action, unit in actions:
                action(unit)


def gather_weights(stem, lin, louts, experts_in):
    lanes = [pl.ds(begin, 128) for begin in range(0, D, 128)]
    every = slice(None)
    arrays = [stem, lin] + list(louts) + list(experts_in)
    kinds = ["stem"] + ["lin"] * len(lanes) + ["rows"] * (len(louts) + 4 * len(experts_in))
    split = [[None], [(every, every, part) for part in lanes]] + [[None]] * len(louts)
    split += [[(matrix, every, pl.ds(begin, D)) for matrix in range(2) for begin in (0, D)]] * len(experts_in)
    shapes = [(8,) + stem.shape, (lin.shape[0], 8) + lin.shape[1:]]
    shapes += [(8,) + part.shape for part in arrays[2:]]
    anywhere = pl.BlockSpec(memory_space=pl.ANY)
    return pl.pallas_call(
        functools.partial(gather_kernel, kinds, split),
        out_shape=[shape_of(shape, bf16) for shape in shapes],
        in_specs=[anywhere] * len(arrays),
        out_specs=[anywhere] * len(arrays),
        scratch_shapes=gather_semaphores(len(kinds)),
        compiler_params=pltpu.CompilerParams(collective_id=5, has_side_effects=True),
        name="gather_weights",
    )(*arrays)


def exchange_kernel(packed, loss, all_packed, total, from_x, from_y, losses, held, send, recv, core_send, core_recv, plane_send, plane_recv, own_sem):
    at, core = lax.axis_index(LINE), lax.axis_index(CORE)
    side_x, side_y = plane_partners()
    sibling = {CORE: 1 - core}
    barrier = pltpu.get_barrier_semaphore()
    others = [{LINE: lax.rem(at + step, 4)} for step in (1, 2, 3)]
    for partner in others + [sibling, side_x, side_y]:
        pl.semaphore_signal(barrier, inc=1, device_id=partner, device_id_type=MESH_ID)
    pl.semaphore_wait(barrier, 6)

    def slots(owner, which):
        return all_packed.at[owner * 2 + which], losses.at[owner * 2 + which]

    own = [pltpu.make_async_copy(source, target, own_sem.at[place]) for place, (source, target) in enumerate(zip((packed, loss), slots(at, core)))]
    for copy in own:
        copy.start()

    def line(step, place):
        source, target = ((packed, loss)[place], slots(at, core)[place])
        return pltpu.make_async_remote_copy(
            source, target, send.at[step - 1, place], recv.at[step - 1, place],
            device_id=others[step - 1], device_id_type=MESH_ID,
        )

    def across(step, place):
        owner = lax.rem(at + 4 - step, 4)
        source = (packed, loss)[place] if step == 0 else slots(owner, core)[place]
        return pltpu.make_async_remote_copy(
            source, slots(owner, core)[place], core_send.at[step, place], core_recv.at[step, place],
            device_id=sibling, device_id_type=MESH_ID,
        )

    def arrival(step, place, which, sem):
        here = slots(lax.rem(at + 4 - step, 4), which)[place]
        return pltpu.make_async_remote_copy(
            here, here, core_send.at[step, place], sem, device_id=sibling, device_id_type=MESH_ID
        )

    for place in (1, 0):
        for step in (2, 3, 1):
            line(step, place).start()
        across(0, place).start()
    for place in (1, 0):
        for step in (1, 3, 2):
            arrival(step, place, core, recv.at[step - 1, place]).wait_recv()
            across(step, place).start()
        for step in range(4):
            arrival(step, place, 1 - core, core_recv.at[step, place]).wait_recv()
        if place == 1:
            own[1].wait()
            held[...] = jnp.sum(losses[...], axis=0)
            first = pltpu.make_async_remote_copy(held, from_x, plane_send.at[0], plane_recv.at[0], device_id=side_x, device_id_type=MESH_ID)
            first.start()
    first.wait()
    held[...] += from_x[...]
    second = pltpu.make_async_remote_copy(held, from_y, plane_send.at[1], plane_recv.at[1], device_id=side_y, device_id_type=MESH_ID)
    second.start()
    second.wait()
    total[...] = held[...] + from_y[...]
    own[0].wait()
    for place in range(2):
        for step in (1, 2, 3):
            line(step, place).wait_send()
        for step in range(4):
            across(step, place).wait_send()


def exchange_small(packed, loss):
    dma = pltpu.SemaphoreType.DMA
    vmem = pl.BlockSpec(memory_space=pltpu.VMEM)
    return pl.pallas_call(
        exchange_kernel,
        out_shape=[shape_of((8,) + packed.shape, packed.dtype), shape_of(loss.shape, f32)],
        in_specs=[vmem, vmem],
        out_specs=[vmem, vmem],
        scratch_shapes=[pltpu.VMEM(loss.shape, f32)] * 2
        + [pltpu.VMEM((8,) + loss.shape, f32), pltpu.VMEM(loss.shape, f32)]
        + [dma((3, 2)), dma((3, 2)), dma((4, 2)), dma((4, 2)), dma((2,)), dma((2,)), dma((2,))],
        compiler_params=pltpu.CompilerParams(collective_id=6, has_side_effects=True, vmem_limit_bytes=16 * MIB),
        name="exchange_small",
    )(packed, loss)


def few_experts(
    patches,
    target_noise,
    timesteps,
    labels,
    routes,
    route_gates,
    stem_weights,
    layer_in,
    layer_out,
    experts,
    stem_first,
    layer_in_first,
    layer_out_first,
    experts_first,
    stem_second,
    layer_in_second,
    layer_out_second,
    experts_second,
    stem_moment,
    layer_in_moment,
    layer_out_moment,
    experts_moment,
):
    count = patches.shape[0]
    items = timesteps.shape[0]
    halves = lax.axis_size(CORE)
    sharers = lax.axis_size(LINE) * halves
    expert_count = lax.axis_size(LINE) * experts.shape[1]
    place = lax.axis_index(LINE) * halves + lax.axis_index(CORE)

    stem_t = stem_weights.T
    lin_t = jnp.swapaxes(layer_in, 1, 2)
    louts = [to_half(layer_out[layer]) for layer in range(LAYERS)]
    pairs = [to_half(experts[layer, 0]) for layer in range(LAYERS)]
    gathered = gather_weights(stem_lanes(to_half(stem_t)), to_half(lin_t), louts, pairs[:1])
    stem_all = gathered[0].reshape(D, STEM_LANES)
    lin_all = gathered[1].reshape(LAYERS, -1, D)
    lout_all = [gathered[2 + layer].reshape(-1, D) for layer in range(LAYERS)]
    expert_all = [gathered[2 + LAYERS]]

    feat = time_features(timesteps)
    hot = label_table(labels)
    hot_pad = jnp.pad(hot, ((0, 32 - items), (0, STEM_PADDED[3] - hot.shape[1]))).astype(bf16)
    cond, hidden, pre_one, pre_two, mods, fin_mods = cond_forward(pad_rows(feat), hot_pad, stem_all, lin_all)
    tokens = product_nt(patches, stem_all[:, :PATCH_DIM])
    tokens = (tokens.reshape(items, -1, D) + positions_table()[None]).reshape(-1, D)
    expert_ids = jnp.arange(expert_count, dtype=jnp.int32)
    saved = []
    for layer in range(LAYERS):
        g4 = jnp.sum(
            jnp.where(routes[layer][:, :, None] == expert_ids, route_gates[layer][:, :, None], 0.0), axis=1
        )
        normed, qkv, attended, branch, middle, n2 = attn_forward(layer, tokens, mods[layer], lin_all)
        beside = (pairs[layer + 1],) if layer + 1 < LAYERS else ()
        active, slope, mixed, result, *arrived = ffn_forward(
            layer, n2, middle, mods[layer], g4, lin_all, lout_all[layer], expert_all[layer], halves, beside
        )
        if beside:
            expert_all.append(arrived[0])
        saved.append((tokens, g4, normed, qkv, attended, branch, middle, n2, active, slope, mixed))
        tokens = result
    fo_rows = stem_all[:, STEM_AT[5] : STEM_AT[5] + PATCH_DIM].T
    grad, grad_fin, grad_out_w, loss_rows = final_step(tokens, fin_mods, fo_rows, target_noise.T)

    stem_cols = stem_weights.shape[1]
    lin_cols = layer_in.shape[2]

    def outer(left_in, right_in):
        return lax.dot_general(left_in, right_in, (((0,), (0,)), ((), ())), preferred_element_type=f32)

    def flip(values):
        return jnp.swapaxes(values, -1, -2)

    states = (experts, experts_first, experts_second, lin_t, flip(layer_in_first[0]), flip(layer_in_second[0]))
    states = states + (layer_out, layer_out_first, layer_out_second)
    grad_mods, reduced, outgoing = [None] * LAYERS, [None] * LAYERS, [None] * LAYERS
    for layer in reversed(range(LAYERS)):
        tokens, g4, normed, qkv, attended, branch, middle, n2, active, slope, mixed = saved[layer]
        early = () if outgoing[1] is None else (outgoing[1][0].reshape((-1, halves) + pairs[0].shape),)
        dup, ddn, dex, gn2, grad_gate, *begun = ffn_backward(
            layer, grad, n2, mods[layer], g4, mixed, active, slope, lin_all, lout_all[layer], expert_all[layer], halves, early
        )
        grad, grad_mods[layer], dqkvo = attn_backward(
            layer, gn2, grad, middle, tokens, normed, qkv, attended, branch, mods[layer], grad_gate, lin_all,
            halves * lin_cols,
        )
        outgoing[layer] = (dex, dqkvo, dup, ddn)
    grad_patch = product_tn(patches, to_half(grad))
    dpre_one, dpre_two = cond_backward(grad_mods[0], grad_mods[1], grad_fin, pre_one, pre_two, stem_all, lin_all)

    names = jnp.stack([labels // 32, labels % 32], axis=1).astype(f32)
    factors = jnp.concatenate(
        [cond[:items], grad_mods[0][:items], grad_mods[1][:items], hidden[:items], dpre_one[:items], dpre_two[:items]]
        + [grad_fin[:items], feat, jnp.pad(names, ((0, 0), (0, 126)))],
        axis=1,
    ).astype(bf16)
    width = factors.shape[1]
    ends = jnp.concatenate([grad_patch, grad_out_w], axis=0).astype(bf16)
    packed = jnp.concatenate([factors.reshape(-1), ends.reshape(-1)])
    lanes = -(-packed.size // (16 * 128)) * 128
    packed = jnp.pad(packed, (0, 16 * lanes - packed.size)).reshape(16, lanes)
    loss = jnp.pad(loss_rows.reshape(1, PATCH_DIM), ((0, 7), (0, 128 - PATCH_DIM)))
    gathered, loss_all = exchange_small(packed, loss)
    loss_total = jnp.sum(loss_all)
    gathered = gathered.reshape(sharers, -1)
    factors = gathered[:, : items * width].reshape(sharers * items, width)
    ends = gathered[:, items * width : items * width + 2 * PATCH_DIM * D].reshape(sharers, 2, PATCH_DIM, D)
    ends = jnp.sum(ends.astype(f32), axis=0)
    cond_f, gm_a, gm_b, hidden_f, done_f, dtwo_f, fin_f, feat_f, names = jnp.split(
        factors, [D, 7 * D, 13 * D, 14 * D, 15 * D, 16 * D, 18 * D, 18 * D + FREQ], axis=1
    )
    hot_all = label_table((names[:, 0].astype(f32) * 32 + names[:, 1].astype(f32)).astype(jnp.int32)).astype(bf16)
    def own(values):
        return lax.dynamic_slice_in_dim(values, place * stem_cols, stem_cols, axis=1)

    stem_grad = jnp.concatenate(
        [
            own(ends[0]).T,
            outer(own(done_f), feat_f),
            outer(own(dtwo_f), hidden_f),
            outer(own(dtwo_f), hot_all),
            outer(own(cond_f), fin_f),
            own(ends[1]).T,
        ],
        axis=1,
    )
    stem_stepped = adam_step(stem_t, stem_grad, stem_first[0].T, stem_second[0].T)
    stem_delta = jnp.pad(to_half(stem_stepped[0]), ((0, 0), (0, -stem_t.shape[1] % 128)))
    for layer, gm in ((1, gm_b), (0, gm_a)):
        spread = jnp.pad(gm, ((0, 0), (4 * D, lin_cols * sharers - 10 * D)))
        window = lax.dynamic_slice_in_dim(spread, place * lin_cols, lin_cols, axis=1)
        dex, dqkvo, dup, ddn = outgoing[layer]
        reduced[layer] = reduce_layer(
            layer,
            dex.reshape((-1, halves) + dex.shape[1:]),
            dqkvo.reshape(halves, lin_cols, D),
            dup.reshape(-1, halves, lin_cols, D),
            ddn.reshape(-1, halves, layer_out.shape[1], D),
            outer(window, cond_f),
            states,
            stem_delta if layer == 1 else None,
            begun if layer == 1 else (),
        )
    stem_total = reduced[1][6]
    group_count = lax.axis_size(GROUP)

    mean_delta = stem_total[:, : stem_t.shape[1]] / group_count
    moment_new = outer_mom * stem_moment.T + mean_delta
    new_weight = stem_t - outer_rate * (mean_delta + outer_mom * moment_new)
    stem_out = [flip(v) for v in (new_weight, to_half(new_weight), stem_stepped[1][None], stem_stepped[2][None], moment_new)]

    def both(at, rows, tile, weight, first, second, moment):
        grads = [reduced[layer][at].reshape(rows, -1) for layer in range(LAYERS)]
        totals = [reduced[layer][3 + at].reshape(rows, -1) for layer in range(LAYERS)]
        shaped = [v.reshape(LAYERS, rows, -1) for v in (weight, first, second, moment)]
        return update_arrays(tile, grads, totals, *shaped)

    lin_out = both(1, lin_cols, 432, lin_t, flip(layer_in_first), flip(layer_in_second), flip(layer_in_moment))
    lin_out = [flip(v.reshape((1,) * (at in (2, 3)) + v.shape)) for at, v in enumerate(lin_out)]
    lout_rows = layer_out.shape[1]
    lout_out = both(2, lout_rows, lout_rows // 2, layer_out, layer_out_first, layer_out_second, layer_out_moment)
    lout_out = [v.reshape((1,) * (at in (2, 3)) + v.shape) for at, v in enumerate(lout_out)]
    expert_out = both(0, 2 * D, D // 2, experts, experts_first, experts_second, experts_moment)
    likes = (experts, experts, experts_first, experts_second, experts)
    expert_out = [v.reshape(like.shape) for v, like in zip(expert_out, likes)]
    results = []
    for at in range(5):
        results += [stem_out[at], lin_out[at], lout_out[at], expert_out[at]]
    return (loss_total, *results)


def solution(mesh):
    placed = (
        P((GROUP, LINE, CORE), None),
        P((GROUP, LINE, CORE), None),
        P((GROUP, LINE, CORE)),
        P((GROUP, LINE, CORE)),
        P(None, (GROUP, LINE, CORE), None),
        P(None, (GROUP, LINE, CORE), None),
        P(None, (LINE, CORE)),
        P(None, None, (LINE, CORE)),
        P(None, (LINE, CORE), None),
        P(None, LINE, None, None, CORE),
        P(GROUP, None, (LINE, CORE)),
        P(GROUP, None, None, (LINE, CORE)),
        P(GROUP, None, (LINE, CORE), None),
        P(GROUP, None, LINE, None, None, CORE),
        P(GROUP, None, (LINE, CORE)),
        P(GROUP, None, None, (LINE, CORE)),
        P(GROUP, None, (LINE, CORE), None),
        P(GROUP, None, LINE, None, None, CORE),
        P(None, (LINE, CORE)),
        P(None, None, (LINE, CORE)),
        P(None, (LINE, CORE), None),
        P(None, LINE, None, None, CORE),
    )
    step = few_experts if mesh.shape[LINE] <= 4 else per_device
    return jax.shard_map(
        step,
        mesh=mesh,
        in_specs=placed,
        out_specs=(
            P(),
            P(None, (LINE, CORE)),
            P(None, None, (LINE, CORE)),
            P(None, (LINE, CORE), None),
            P(None, LINE, None, None, CORE),
            P(None, (LINE, CORE)),
            P(None, None, (LINE, CORE)),
            P(None, (LINE, CORE), None),
            P(None, LINE, None, None, CORE),
            P(GROUP, None, (LINE, CORE)),
            P(GROUP, None, None, (LINE, CORE)),
            P(GROUP, None, (LINE, CORE), None),
            P(GROUP, None, LINE, None, None, CORE),
            P(GROUP, None, (LINE, CORE)),
            P(GROUP, None, None, (LINE, CORE)),
            P(GROUP, None, (LINE, CORE), None),
            P(GROUP, None, LINE, None, None, CORE),
            P(None, (LINE, CORE)),
            P(None, None, (LINE, CORE)),
            P(None, (LINE, CORE), None),
            P(None, LINE, None, None, CORE),
        ),
        check_vma=False,
    )
```

```python
import functools

import jax
import jax.numpy as jnp
from jax import lax
from jax.experimental import pallas as pl
from jax.experimental.pallas import tpu as pltpu
from jax.sharding import PartitionSpec as P

GROUP, LINE, CORE = "group", "expert", "dp"
D = 384
HEADS = 6
IMG = 32
FREQ = 256
CLASSES = 1000
LAYERS = 2
STEP = 10
PATCH_DIM = 16
PATCHES = 256


highest = lax.Precision.HIGHEST
beta_one = 0.9
beta_two = 0.95
eps_adam = 1e-08
inner_rate = 0.03
weight_decay = 0.05
outer_rate = 0.7
outer_mom = 0.9
ln_eps = 1e-06


def to_half(values):
    return values.astype(jnp.bfloat16)


def product(left_in, right_in):
    return jnp.dot(left_in, right_in, preferred_element_type=jnp.float32)


def product_tn(left_in, right_in):
    return lax.dot_general(
        left_in, right_in, (((0,), (0,)), ((), ())), preferred_element_type=jnp.float32
    )


def product_nt(left_in, right_in):
    return lax.dot_general(
        left_in, right_in, (((1,), (1,)), ((), ())), preferred_element_type=jnp.float32
    )


def gelu_tanh(values):
    return jax.nn.gelu(values, approximate=True)


def gelu_back(values, gradient):
    _, pull = jax.vjp(gelu_tanh, values)
    return pull(gradient)[0]


def norm_mod(values, shift_in, scale_in):
    centre = values - jnp.mean(values, axis=-1, keepdims=True)
    spread = jnp.mean(centre * centre, axis=-1, keepdims=True)
    return centre * lax.rsqrt(spread + ln_eps) * (1.0 + scale_in) + shift_in


def positions_table():
    grid_side = IMG // 2
    quarter = D // 4
    omegas = 1.0 / 10000.0 ** (jnp.arange(quarter, dtype=jnp.float32) / quarter)
    index_all = jnp.arange(PATCHES, dtype=jnp.int32)
    row_angle = (index_all // grid_side).astype(jnp.float32)[:, None] * omegas[None, :]
    col_angle = (index_all % grid_side).astype(jnp.float32)[:, None] * omegas[None, :]
    return jnp.concatenate(
        [jnp.sin(row_angle), jnp.cos(row_angle), jnp.sin(col_angle), jnp.cos(col_angle)], axis=1
    )


def time_features(step_ids):
    half_freq = FREQ // 2
    frequency = jnp.exp(-jnp.log(10000.0) * jnp.arange(half_freq, dtype=jnp.float32) / half_freq)
    angles = step_ids.astype(jnp.float32)[:, None] * frequency[None, :]
    return jnp.concatenate([jnp.cos(angles), jnp.sin(angles)], axis=1)


def label_table(label_ids):
    return (label_ids[:, None] == jnp.arange(CLASSES + 1, dtype=jnp.int32)[None, :]).astype(
        jnp.float32
    )


def split_stem(stem_all):
    end_patch = PATCH_DIM
    end_time = end_patch + FREQ
    end_second = end_time + D
    end_table = end_second + CLASSES + 1
    end_ada = end_table + 2 * D
    return (
        stem_all[:end_patch],
        stem_all[end_patch:end_time],
        stem_all[end_time:end_second],
        stem_all[end_second:end_table],
        stem_all[end_table:end_ada],
        stem_all[end_ada:],
    )


def slot_places(route_ids, expert_count, capacity):
    flat_ids = route_ids.reshape(-1)
    one_hot_ids = (flat_ids[:, None] == jnp.arange(expert_count, dtype=jnp.int32)[None, :]).astype(
        jnp.int32
    )
    rank_in = jnp.sum((jnp.cumsum(one_hot_ids, axis=0) - one_hot_ids) * one_hot_ids, axis=1)
    return flat_ids * capacity + rank_in


def expert_major(received, local_count):
    sources = received.shape[0] // local_count
    shaped = received.reshape(sources, local_count, received.shape[1], received.shape[2])
    return jnp.swapaxes(shaped, 0, 1).reshape(local_count, -1, received.shape[2])


def source_major(rows_in, sources):
    local_count = rows_in.shape[0]
    shaped = rows_in.reshape(local_count, sources, -1, rows_in.shape[2])
    return jnp.swapaxes(shaped, 0, 1).reshape(sources * local_count, -1, rows_in.shape[2])


def attention_split(qkv, item_count):
    head_dim = qkv.shape[1] // (3 * HEADS)
    shaped = qkv.reshape(item_count, -1, 3, HEADS, head_dim)
    return (shaped[:, :, 0], shaped[:, :, 1], shaped[:, :, 2], head_dim ** (-0.5))


def attention_forward(qkv, item_count):
    queries, keys_in, values_in, scale_att = attention_split(qkv, item_count)
    scores = (
        jnp.einsum("bqhd,bkhd->bhqk", queries, keys_in, preferred_element_type=jnp.float32)
        * scale_att
    )
    row_max = jnp.max(scores, axis=-1, keepdims=True)
    log_sums = row_max + jnp.log(jnp.sum(jnp.exp(scores - row_max), axis=-1, keepdims=True))
    attn_probs = to_half(jnp.exp(scores - log_sums))
    attended = jnp.einsum(
        "bhqk,bkhd->bqhd", attn_probs, values_in, preferred_element_type=jnp.float32
    )
    return (to_half(attended.reshape(qkv.shape[0], -1)), log_sums)


def attention_backward(qkv, log_sums, grad_attended, item_count):
    queries, keys_in, values_in, scale_att = attention_split(qkv, item_count)
    scores = (
        jnp.einsum("bqhd,bkhd->bhqk", queries, keys_in, preferred_element_type=jnp.float32)
        * scale_att
    )
    probs_full = jnp.exp(scores - log_sums)
    grad_out = grad_attended.reshape(queries.shape)
    grad_values = jnp.einsum(
        "bhqk,bqhd->bkhd", to_half(probs_full), grad_out, preferred_element_type=jnp.float32
    )
    grad_probs = jnp.einsum(
        "bqhd,bkhd->bhqk", grad_out, values_in, preferred_element_type=jnp.float32
    )
    grad_scores = probs_full * (
        grad_probs - jnp.sum(probs_full * grad_probs, axis=-1, keepdims=True)
    )
    grad_half = to_half(grad_scores)
    grad_queries = (
        jnp.einsum("bhqk,bkhd->bqhd", grad_half, keys_in, preferred_element_type=jnp.float32)
        * scale_att
    )
    grad_keys = (
        jnp.einsum("bhqk,bqhd->bkhd", grad_half, queries, preferred_element_type=jnp.float32)
        * scale_att
    )
    stacked = jnp.stack([grad_queries, grad_keys, grad_values], axis=2)
    return to_half(stacked.reshape(qkv.shape[0], -1))


def layer_forward(tokens, cond_act, lin, lout, expert_w, route_ids, gate_vals):
    item_count = cond_act.shape[0]
    model_width = tokens.shape[1]
    local_count = expert_w.shape[0]
    expert_count = lax.axis_size(LINE) * local_count
    capacity = 4 * tokens.shape[0] // expert_count
    mods = jnp.dot(
        cond_act, lin[:, 4 * model_width : 10 * model_width].astype(jnp.float32), precision=highest
    )
    mods = mods.reshape(item_count, 6, 1, model_width)
    shaped = tokens.reshape(item_count, -1, model_width)
    normed = to_half(norm_mod(shaped, mods[:, 0], mods[:, 1]).reshape(-1, model_width))
    qkv = to_half(product(normed, lin[:, : 3 * model_width]))
    attended, log_sums = attention_forward(qkv, item_count)
    branch = product(attended, lin[:, 3 * model_width : 4 * model_width])
    middle = shaped + mods[:, 2] * branch.reshape(item_count, -1, model_width)
    normed_two = to_half(norm_mod(middle, mods[:, 3], mods[:, 4]).reshape(-1, model_width))
    inner_pre = product(normed_two, lin[:, 10 * model_width :])
    active = to_half(gelu_tanh(inner_pre))
    shared = product(active, lout)
    slot_index = slot_places(route_ids, expert_count, capacity)
    send_rows = jnp.zeros((expert_count * capacity, model_width), jnp.bfloat16)
    send_rows = send_rows.at[slot_index].set(jnp.repeat(normed_two, 2, axis=0))
    received = lax.all_to_all(
        send_rows.reshape(expert_count, capacity, model_width),
        LINE,
        split_axis=0,
        concat_axis=0,
        tiled=True,
    )
    rows_exp = expert_major(received, local_count)
    inner_exp = jnp.einsum(
        "erd,edf->erf", rows_exp, expert_w[:, 0], preferred_element_type=jnp.float32
    )
    active_exp = to_half(gelu_tanh(inner_exp))
    out_exp = to_half(
        jnp.einsum("erf,edf->erd", active_exp, expert_w[:, 1], preferred_element_type=jnp.float32)
    )
    returned = lax.all_to_all(
        source_major(out_exp, lax.axis_size(LINE)),
        LINE,
        split_axis=0,
        concat_axis=0,
        tiled=True,
    )
    picked = (
        returned.reshape(-1, model_width)[slot_index]
        .astype(jnp.float32)
        .reshape(-1, 2, model_width)
    )
    mixed_out = shared + jnp.sum(gate_vals[:, :, None] * picked, axis=1)
    result = middle + mods[:, 5] * mixed_out.reshape(item_count, -1, model_width)
    saved = (
        tokens,
        mods,
        normed,
        qkv,
        attended,
        log_sums,
        branch,
        middle,
        normed_two,
        inner_pre,
        active,
        mixed_out,
        slot_index,
        rows_exp,
        inner_exp,
        active_exp,
    )
    return (result.reshape(-1, model_width), saved)


def layer_backward(grad_tokens, saved, cond_act, lin, lout, expert_w, gate_vals):
    (
        tokens,
        mods,
        normed,
        qkv,
        attended,
        log_sums,
        branch,
        middle,
        normed_two,
        inner_pre,
        active,
        mixed_out,
        slot_index,
        rows_exp,
        inner_exp,
        active_exp,
    ) = saved
    item_count = cond_act.shape[0]
    model_width = tokens.shape[1]
    local_count = expert_w.shape[0]
    expert_count = lax.axis_size(LINE) * local_count
    capacity = 4 * tokens.shape[0] // expert_count
    grad_shaped = grad_tokens.reshape(item_count, -1, model_width)
    grad_gate_two = jnp.sum(
        grad_shaped * mixed_out.reshape(item_count, -1, model_width), axis=1, keepdims=True
    )
    grad_mixed = (mods[:, 5] * grad_shaped).reshape(-1, model_width)
    grad_shared = to_half(grad_mixed)
    grad_lout = product_tn(active, grad_shared)
    grad_inner = to_half(gelu_back(inner_pre, product_nt(grad_shared, lout)))
    grad_w_up = product_tn(normed_two, grad_inner)
    grad_normed_two = product_nt(grad_inner, lin[:, 10 * model_width :])
    routed_grad = to_half(gate_vals[:, :, None] * grad_mixed[:, None, :]).reshape(-1, model_width)
    send_grad = (
        jnp.zeros((expert_count * capacity, model_width), jnp.bfloat16)
        .at[slot_index]
        .set(routed_grad)
    )
    received = lax.all_to_all(
        send_grad.reshape(expert_count, capacity, model_width),
        LINE,
        split_axis=0,
        concat_axis=0,
        tiled=True,
    )
    grad_rows = expert_major(received, local_count)
    grad_down_exp = jnp.einsum(
        "erd,erf->edf", grad_rows, active_exp, preferred_element_type=jnp.float32
    )
    grad_active_exp = jnp.einsum(
        "erd,edf->erf", grad_rows, expert_w[:, 1], preferred_element_type=jnp.float32
    )
    grad_inner_exp = to_half(gelu_back(inner_exp, grad_active_exp))
    grad_up_exp = jnp.einsum(
        "erd,erf->edf", rows_exp, grad_inner_exp, preferred_element_type=jnp.float32
    )
    grad_rows_in = to_half(
        jnp.einsum(
            "erf,edf->erd", grad_inner_exp, expert_w[:, 0], preferred_element_type=jnp.float32
        )
    )
    back_rows = lax.all_to_all(
        source_major(grad_rows_in, lax.axis_size(LINE)),
        LINE,
        split_axis=0,
        concat_axis=0,
        tiled=True,
    )
    picked = (
        back_rows.reshape(-1, model_width)[slot_index]
        .astype(jnp.float32)
        .reshape(-1, 2, model_width)
    )
    grad_normed_two = grad_normed_two + jnp.sum(picked, axis=1)
    _, second_back = jax.vjp(norm_mod, middle, mods[:, 3], mods[:, 4])
    grad_middle, grad_shift_two, grad_scale_two = second_back(
        grad_normed_two.reshape(item_count, -1, model_width)
    )
    grad_middle = grad_middle + grad_shaped
    grad_gate_one = jnp.sum(
        grad_middle * branch.reshape(item_count, -1, model_width), axis=1, keepdims=True
    )
    grad_branch = to_half((mods[:, 2] * grad_middle).reshape(-1, model_width))
    grad_w_out = product_tn(attended, grad_branch)
    grad_attended = to_half(product_nt(grad_branch, lin[:, 3 * model_width : 4 * model_width]))
    grad_qkv = attention_backward(qkv, log_sums, grad_attended, item_count)
    grad_w_qkv = product_tn(normed, grad_qkv)
    grad_normed = product_nt(grad_qkv, lin[:, : 3 * model_width])
    _, first_back = jax.vjp(
        norm_mod, tokens.reshape(item_count, -1, model_width), mods[:, 0], mods[:, 1]
    )
    grad_input, grad_shift_one, grad_scale_one = first_back(
        grad_normed.reshape(item_count, -1, model_width)
    )
    grad_input = grad_input + grad_middle
    grad_mods = jnp.stack(
        [
            grad_shift_one,
            grad_scale_one,
            grad_gate_one,
            grad_shift_two,
            grad_scale_two,
            grad_gate_two,
        ],
        axis=1,
    )
    grad_mods = grad_mods.reshape(item_count, 6 * model_width)
    grad_ada = jnp.dot(cond_act.T, grad_mods, precision=highest)
    grad_cond = jnp.dot(
        grad_mods,
        lin[:, 4 * model_width : 10 * model_width].astype(jnp.float32).T,
        precision=highest,
    )
    grad_lin = jnp.concatenate([grad_w_qkv, grad_w_out, grad_ada, grad_w_up], axis=1)
    grad_expert = jnp.stack([grad_up_exp, grad_down_exp], axis=1)
    return (grad_input.reshape(-1, model_width), grad_cond, grad_lin, grad_lout, grad_expert)


def adam_step(weight_in, gradient, first_in, second_in):
    first_new = beta_one * first_in + (1.0 - beta_one) * gradient
    second_new = beta_two * second_in + (1.0 - beta_two) * gradient * gradient
    first_hat = first_new / (1.0 - beta_one**STEP)
    second_hat = second_new / (1.0 - beta_two**STEP)
    stepped = weight_in - inner_rate * (
        first_hat / (jnp.sqrt(second_hat) + eps_adam) + weight_decay * weight_in
    )
    return (weight_in - stepped, first_new, second_new)


def per_device(
    patches,
    target_noise,
    timesteps,
    labels,
    routes,
    route_gates,
    stem_weights,
    layer_in,
    layer_out,
    experts,
    stem_first,
    layer_in_first,
    layer_out_first,
    experts_first,
    stem_second,
    layer_in_second,
    layer_out_second,
    experts_second,
    stem_moment,
    layer_in_moment,
    layer_out_moment,
    experts_moment,
):
    stem_all, lin_all, lout_all = (
        lax.all_gather(to_half(stem_weights), (LINE, CORE), axis=1, tiled=True),
        lax.all_gather(to_half(layer_in), (LINE, CORE), axis=2, tiled=True),
        lax.all_gather(to_half(layer_out), (LINE, CORE), axis=1, tiled=True),
    )
    expert_all = lax.all_gather(to_half(experts), CORE, axis=4, tiled=True)
    model_width = stem_all.shape[1]
    item_count = timesteps.shape[0]
    patch_w, time_one, time_two, table_w, final_ada, final_out = split_stem(stem_all)
    features = time_features(timesteps)
    hot_labels = label_table(labels)

    def condition(first_w, second_w, table_in):
        hidden_time = jax.nn.silu(jnp.dot(features, first_w, precision=highest))
        return jax.nn.silu(
            jnp.dot(hidden_time, second_w, precision=highest)
            + jnp.dot(hot_labels, table_in, precision=highest)
        )

    cond_act, cond_back = jax.vjp(
        condition,
        time_one.astype(jnp.float32),
        time_two.astype(jnp.float32),
        table_w.astype(jnp.float32),
    )
    tokens = product(patches, patch_w)
    tokens = (tokens.reshape(item_count, -1, model_width) + positions_table()[None]).reshape(
        -1, model_width
    )
    saved_all = []
    for layer_idx in range(LAYERS):
        tokens, saved = layer_forward(
            tokens,
            cond_act,
            lin_all[layer_idx],
            lout_all[layer_idx],
            expert_all[layer_idx],
            routes[layer_idx],
            route_gates[layer_idx],
        )
        saved_all.append(saved)
    final_ada_f = final_ada.astype(jnp.float32)
    final_mods = jnp.dot(cond_act, final_ada_f.T, precision=highest).reshape(
        item_count, 2, 1, model_width
    )
    final_pre, final_back = jax.vjp(
        norm_mod, tokens.reshape(item_count, -1, model_width), final_mods[:, 0], final_mods[:, 1]
    )
    final_normed = to_half(final_pre.reshape(-1, model_width))
    predicted = product_nt(final_normed, final_out)
    residual_err = predicted - target_noise
    loss_total = lax.psum(jnp.sum(residual_err * residual_err), (GROUP, LINE, CORE))
    grad_pred = to_half(2.0 * residual_err)
    grad_final_out = product_tn(grad_pred, final_normed)
    grad_final_normed = product(grad_pred, final_out)
    grad_tokens, grad_fshift, grad_fscale = final_back(
        grad_final_normed.reshape(item_count, -1, model_width)
    )
    grad_tokens = grad_tokens.reshape(-1, model_width)
    grad_final_mods = jnp.concatenate([grad_fshift, grad_fscale], axis=1).reshape(
        item_count, 2 * model_width
    )
    grad_final_ada = jnp.dot(grad_final_mods.T, cond_act, precision=highest)
    grad_cond = jnp.dot(grad_final_mods, final_ada_f, precision=highest)
    lin_grads = []
    lout_grads = []
    expert_grads = []
    for layer_idx in reversed(range(LAYERS)):
        grad_tokens, grad_cond_layer, grad_lin, grad_lout, grad_expert = layer_backward(
            grad_tokens,
            saved_all[layer_idx],
            cond_act,
            lin_all[layer_idx],
            lout_all[layer_idx],
            expert_all[layer_idx],
            route_gates[layer_idx],
        )
        grad_cond = grad_cond + grad_cond_layer
        lin_grads.append(grad_lin)
        lout_grads.append(grad_lout)
        expert_grads.append(grad_expert)
    lin_stack = jnp.stack(lin_grads[::-1])
    lout_stack = jnp.stack(lout_grads[::-1])
    expert_stack = jnp.stack(expert_grads[::-1])
    grad_patch = product_tn(patches, to_half(grad_tokens))
    grad_time_one, grad_time_two, grad_table = cond_back(grad_cond)
    grad_stem = jnp.concatenate(
        [grad_patch, grad_time_one, grad_time_two, grad_table, grad_final_ada, grad_final_out],
        axis=0,
    )
    stem_sum, lin_sum, lout_sum = (
        lax.psum_scatter(grad_stem, (LINE, CORE), scatter_dimension=1, tiled=True),
        lax.psum_scatter(lin_stack, (LINE, CORE), scatter_dimension=2, tiled=True),
        lax.psum_scatter(lout_stack, (LINE, CORE), scatter_dimension=1, tiled=True),
    )
    expert_sum = lax.psum_scatter(
        expert_stack.astype(jnp.bfloat16), CORE, scatter_dimension=4, tiled=True
    ).astype(jnp.float32)
    weights_all = (stem_weights, layer_in, layer_out, experts)
    gradients = (stem_sum, lin_sum, lout_sum, expert_sum)
    firsts = (stem_first, layer_in_first, layer_out_first, experts_first)
    seconds = (stem_second, layer_in_second, layer_out_second, experts_second)
    moments = (stem_moment, layer_in_moment, layer_out_moment, experts_moment)
    stepped = [
        adam_step(
            weights_all[array_idx],
            gradients[array_idx],
            firsts[array_idx][0],
            seconds[array_idx][0],
        )
        for array_idx in range(4)
    ]
    delta_all = (
        lax.psum(stepped[0][0].astype(jnp.bfloat16), GROUP).astype(jnp.float32),
        lax.psum(stepped[1][0].astype(jnp.bfloat16), GROUP).astype(jnp.float32),
        lax.psum(stepped[2][0].astype(jnp.bfloat16), GROUP).astype(jnp.float32),
        lax.psum(stepped[3][0].astype(jnp.bfloat16), GROUP).astype(jnp.float32),
    )
    group_count = lax.axis_size(GROUP)
    new_weights = []
    new_moments = []
    for array_idx in range(4):
        mean_delta = delta_all[array_idx] / group_count
        moment_new = outer_mom * moments[array_idx] + mean_delta
        new_weights.append(
            weights_all[array_idx] - outer_rate * (mean_delta + outer_mom * moment_new)
        )
        new_moments.append(moment_new)
    return (
        loss_total,
        new_weights[0],
        new_weights[1],
        new_weights[2],
        new_weights[3],
        to_half(new_weights[0]),
        to_half(new_weights[1]),
        to_half(new_weights[2]),
        to_half(new_weights[3]),
        stepped[0][1][None],
        stepped[1][1][None],
        stepped[2][1][None],
        stepped[3][1][None],
        stepped[0][2][None],
        stepped[1][2][None],
        stepped[2][2][None],
        stepped[3][2][None],
        new_moments[0],
        new_moments[1],
        new_moments[2],
        new_moments[3],
    )


bf16 = jnp.bfloat16
f32 = jnp.float32
MIB = 1024 * 1024
CHUNK = 768
FWD_ROWS = 256
BWD_ROWS = 256
STEM_SIZES = (PATCH_DIM, FREQ, D, CLASSES + 1, 2 * D, PATCH_DIM)
STEM_PADDED = tuple(-(-size // 128) * 128 for size in STEM_SIZES)
STEM_AT = tuple(sum(STEM_PADDED[:place]) for place in range(len(STEM_PADDED)))
STEM_LANES = -(-sum(STEM_PADDED) // 1024) * 1024


def dot_nn(left_in, right_in):
    return lax.dot_general(left_in, right_in, (((1,), (0,)), ((), ())), preferred_element_type=f32)


def dot_nt(left_in, right_in):
    return lax.dot_general(left_in, right_in, (((1,), (1,)), ((), ())), preferred_element_type=f32)


def dot_tn(left_in, right_in):
    return lax.dot_general(left_in, right_in, (((0,), (0,)), ((), ())), preferred_element_type=f32)


def three_parts(rows):
    high = rows.astype(bf16).astype(f32)
    rest = rows - high
    mid = rest.astype(bf16).astype(f32)
    low = rest - mid
    return jnp.concatenate([high, mid, low, jnp.zeros_like(low)], axis=0).astype(bf16)


def three_sum(stacked):
    return stacked[0:8] + stacked[8:16] + stacked[16:24]


def full_nt(rows, weight):
    return three_sum(dot_nt(three_parts(rows), weight))


def full_nn(rows, weight):
    return three_sum(dot_nn(three_parts(rows), weight))


def silu_slope(values):
    gate = 1.0 / (1.0 + jnp.exp(-values))
    return gate * (1.0 + values * (1.0 - gate))


def silu_of(values):
    return values / (1.0 + jnp.exp(-values))


def stem_piece(stem_ref, place):
    return stem_ref[:, STEM_AT[place] : STEM_AT[place] + STEM_PADDED[place]]


def cond_kernel(feat_ref, hot_ref, stem_ref, ada_ref, cond_ref, hid_ref, one_ref, two_ref, mods_ref, fin_ref):
    @pl.when(pl.program_id(0) == 0)
    def _():
        pre_one = full_nt(feat_ref[...], stem_piece(stem_ref, 1))
        hidden = silu_of(pre_one)
        pre_two = full_nt(hidden, stem_piece(stem_ref, 2)) + dot_nt(hot_ref[...], stem_piece(stem_ref, 3))[0:8]
        cond = silu_of(pre_two)
        one_ref[...] = pre_one
        two_ref[...] = pre_two
        hid_ref[...] = hidden
        cond_ref[...] = cond
        fin_ref[...] = full_nn(cond, stem_piece(stem_ref, 4))

    for layer in range(LAYERS):
        mods_ref[layer] = full_nt(cond_ref[...], ada_ref[layer])


def cond_back_kernel(gm_a, gm_b, gf_ref, one_ref, two_ref, stem_ref, ada_ref, done_ref, dtwo_ref):
    @pl.when(pl.program_id(0) == 0)
    def _():
        dtwo_ref[...] = full_nt(gf_ref[...], stem_piece(stem_ref, 4))

    dtwo_ref[...] += full_nn(gm_a[...], ada_ref[0]) + full_nn(gm_b[...], ada_ref[1])

    @pl.when(pl.program_id(0) == pl.num_programs(0) - 1)
    def _():
        dtwo = dtwo_ref[...] * silu_slope(two_ref[...])
        dtwo_ref[...] = dtwo
        done_ref[...] = full_nn(dtwo, stem_piece(stem_ref, 2)) * silu_slope(one_ref[...])


def norm_parts(values):
    centre = values - jnp.mean(values, axis=-1, keepdims=True)
    spread = jnp.mean(centre * centre, axis=-1, keepdims=True)
    root = lax.rsqrt(spread + ln_eps)
    return centre * root, root


def norm_back(values, scale_in, gradient):
    unit, root = norm_parts(values)
    grad_unit = gradient * (1.0 + scale_in)
    inner = jnp.mean(grad_unit * unit, axis=-1, keepdims=True)
    grad_in = root * (grad_unit - jnp.mean(grad_unit, axis=-1, keepdims=True) - unit * inner)
    return (
        grad_in,
        jnp.sum(gradient, axis=0, keepdims=True),
        jnp.sum(gradient * unit, axis=0, keepdims=True),
    )


def mod_row(mods_ref, item, place):
    return mods_ref[pl.ds(item, 1), place * D : (place + 1) * D]


def head_masks():
    lane = lax.broadcasted_iota(jnp.int32, (1, 128), 1)
    return lane, [(lane // 64 == half).astype(f32).astype(bf16) for half in range(2)]


def attn_fwd_kernel(x_ref, mods_ref, w_ref, normed_ref, qkv_ref, att_ref, branch_ref, mid_ref, n2_ref):
    item = pl.program_id(0)
    tokens = x_ref[...]
    unit, _ = norm_parts(tokens)
    normed = (unit * (1.0 + mod_row(mods_ref, item, 1)) + mod_row(mods_ref, item, 0)).astype(bf16)
    normed_ref[...] = normed
    qkv_ref[...] = dot_nt(normed, w_ref[0 : 3 * D, :]).astype(bf16)
    lane, masks = head_masks()
    heads = [(pair, half) for pair in range(HEADS // 2) for half in range(2)]

    def part(place, pair):
        return qkv_ref[:, place * D + pair * 128 : place * D + pair * 128 + 128]

    all_scores = [dot_nt(part(0, pair) * (masks[half] * jnp.asarray(0.125, bf16)), part(1, pair)) for pair, half in heads]
    powers = [jnp.exp(scores - jnp.max(scores, axis=-1, keepdims=True)) for scores in all_scores]
    probs = [(power * (1.0 / jnp.sum(power, axis=-1, keepdims=True))).astype(bf16) for power in powers]
    outs = [dot_nn(prob, part(2, pair)) for prob, (pair, _) in zip(probs, heads)]
    for pair in range(HEADS // 2):
        att_ref[:, pair * 128 : pair * 128 + 128] = jnp.where(lane < 64, outs[2 * pair], outs[2 * pair + 1]).astype(bf16)
    branch = dot_nt(att_ref[...], w_ref[3 * D : 4 * D, :])
    branch_ref[...] = branch
    middle = tokens + mod_row(mods_ref, item, 2) * branch
    mid_ref[...] = middle
    unit, _ = norm_parts(middle)
    n2_ref[...] = (unit * (1.0 + mod_row(mods_ref, item, 4)) + mod_row(mods_ref, item, 3)).astype(bf16)


def attn_bwd_kernel(
    gn2_ref, g_ref, mid_ref, x_ref, normed_ref, qkv_ref, att_ref, branch_ref, mods_ref, gg_ref, w_ref,
    gx_ref, gmods_ref, dw_ref, dqkv, acc,
):
    item = pl.program_id(0)

    @pl.when(item == 0)
    def _():
        acc[...] = jnp.zeros_like(acc)
        gmods_ref[...] = jnp.zeros_like(gmods_ref)

    grad_mid, dshift, dscale = norm_back(mid_ref[...], mod_row(mods_ref, item, 4), gn2_ref[...])
    grad_mid = grad_mid + g_ref[...]
    dgate = jnp.sum(grad_mid * branch_ref[...], axis=0, keepdims=True)
    gmods_ref[pl.ds(item, 1), 2 * D : 3 * D] = dgate
    gmods_ref[pl.ds(item, 1), 3 * D : 4 * D] = dshift
    gmods_ref[pl.ds(item, 1), 4 * D : 5 * D] = dscale
    gmods_ref[pl.ds(item, 1), 5 * D : 6 * D] = gg_ref[pl.ds(item, 1), :]
    grad_branch = (mod_row(mods_ref, item, 2) * grad_mid).astype(bf16)
    acc[3 * D : 4 * D, :] += dot_tn(grad_branch, att_ref[...])
    grad_att = dot_nn(grad_branch, w_ref[3 * D : 4 * D, :]).astype(bf16)
    lane, masks = head_masks()
    heads = [(pair, half) for pair in range(HEADS // 2) for half in range(2)]

    def part(place, pair):
        return qkv_ref[:, place * D + pair * 128 : place * D + pair * 128 + 128]

    outs = [grad_att[:, pair * 128 : pair * 128 + 128] for pair in range(HEADS // 2)]
    all_scores = [dot_nt(part(0, pair) * (masks[half] * jnp.asarray(0.125, bf16)), part(1, pair)) for pair, half in heads]
    all_grads = [dot_nt(outs[pair] * masks[half], part(2, pair)) for pair, half in heads]
    powers = [jnp.exp(scores - jnp.max(scores, axis=-1, keepdims=True)) for scores in all_scores]
    probs = [power * (1.0 / jnp.sum(power, axis=-1, keepdims=True)) for power in powers]
    halved = [prob.astype(bf16) for prob in probs]
    grad_scores = [
        (prob * (grads - jnp.sum(prob * grads, axis=-1, keepdims=True))).astype(bf16)
        for prob, grads in zip(probs, all_grads)
    ]
    for pair in range(HEADS // 2):
        at = pair * 128
        two = (2 * pair, 2 * pair + 1)
        results = (
            [dot_nn(grad_scores[head], part(1, pair)) * 0.125 for head in two],
            [dot_tn(grad_scores[head], part(0, pair)) * 0.125 for head in two],
            [dot_tn(halved[head], outs[pair]) for head in two],
        )
        for place, (low, high) in enumerate(results):
            dqkv[:, place * D + at : place * D + at + 128] = jnp.where(lane < 64, low, high).astype(bf16)
    acc[0 : 3 * D, :] += dot_tn(dqkv[...], normed_ref[...])
    grad_normed = dot_nn(dqkv[...], w_ref[0 : 3 * D, :])
    grad_in, dshift, dscale = norm_back(x_ref[...], mod_row(mods_ref, item, 1), grad_normed)
    gx_ref[...] = grad_in + grad_mid
    gmods_ref[pl.ds(item, 1), 0:D] = dshift
    gmods_ref[pl.ds(item, 1), D : 2 * D] = dscale

    @pl.when(item == pl.num_programs(0) - 1)
    def _():
        dw_ref[0 : 4 * D, :] = acc[...].astype(bf16)
        dw_ref[4 * D :, :] = jnp.zeros_like(dw_ref[4 * D :, :])


def gelu_both(values):
    outer = 0.7978845608028654
    cubic = outer * 0.044715
    square = values * values
    angle = jnp.tanh(values * (square * cubic + outer))
    half = 0.5 * values
    above = 1.0 + angle
    slope = above * (half * (square * (3.0 * cubic) + outer) * (1.0 - angle) + 0.5)
    return (half * above).astype(bf16), slope.astype(bf16)


def gate_column(g4_ref, rows, expert):
    gates = g4_ref[rows, :]
    lane = lax.broadcasted_iota(jnp.int32, gates.shape, 1)
    return jnp.sum(jnp.where(lane == expert, gates, 0.0), axis=1, keepdims=True)


def ffn_fwd_kernel(shared_steps, halves, gathers, n2_ref, mid_ref, mods_ref, g4_ref, up_ref, dn_ref, ex_ref, *rest):
    step = pl.program_id(0)
    given, (act_ref, dg_ref, mixed_ref, x_ref) = rest[:gathers], rest[gathers : gathers + 4]
    taken, (acc, racc), sems = rest[gathers + 4 : 2 * gathers + 4], rest[2 * gathers + 4 : 2 * gathers + 6], rest[2 * gathers + 6 :]
    if gathers:
        gather_beside(step, pl.num_programs(0) - 1, given, taken, sems)
    items = n2_ref.shape[0] // PATCHES

    @pl.when(step == 0)
    def _():
        acc[...] = jnp.zeros_like(acc)
        racc[...] = jnp.zeros_like(racc)

    @pl.when(step < shared_steps)
    def _():
        for block in range(n2_ref.shape[0] // FWD_ROWS):
            rows = pl.ds(block * FWD_ROWS, FWD_ROWS)
            active, slope = gelu_both(dot_nt(n2_ref[rows, :], up_ref[...]))
            act_ref[0, rows, :] = active
            dg_ref[0, rows, :] = slope
            acc[rows, :] += dot_nn(active, dn_ref[...])

    @pl.when(step >= shared_steps)
    def _():
        for block in range(n2_ref.shape[0] // FWD_ROWS):
            rows = pl.ds(block * FWD_ROWS, FWD_ROWS)
            active, slope = gelu_both(dot_nn(n2_ref[rows, :], ex_ref[0, 0]))
            act_ref[0, rows, :] = active
            dg_ref[0, rows, :] = slope
            racc[rows, :] += dot_nt(active, ex_ref[0, 1])

    expert, half = (step - shared_steps) // halves, (step - shared_steps) % halves

    @pl.when((step >= shared_steps) & (half == halves - 1))
    def _():
        for item in range(items):
            rows = pl.ds(item * PATCHES, PATCHES)
            acc[rows, :] += gate_column(g4_ref, rows, expert) * racc[rows, :].astype(bf16).astype(f32)
            racc[rows, :] = jnp.zeros((PATCHES, D), f32)

    @pl.when(step == pl.num_programs(0) - 1)
    def _():
        mixed_ref[...] = acc[...]
        for item in range(items):
            rows = pl.ds(item * PATCHES, PATCHES)
            x_ref[rows, :] = mid_ref[rows, :] + mod_row(mods_ref, item, 5) * acc[rows, :]


EARLY = 2
END_ROUTES = {0: [(3, 1), (2, 1), (1, 1)], 3: [(0, -1), (1, -1), (2, -1)]}


def early_slot(owner, step, place):
    return 4 if step == -1 and owner == place - 1 else owner


def early_beside(step, last, dex, chip_out, came_out, chip, local, core_send, core_recv, load_sem, line_send, line_recv, out_sem):
    at, core = lax.axis_index(LINE), lax.axis_index(CORE)
    units = reduce_units()[:EARLY]
    sibling = {CORE: 1 - core}

    def source(unit, which):
        _, matrix, row, rows, _, _ = units[unit]
        return dex.at[:, which, matrix, pl.ds(row, rows)]

    def given(unit):
        return pltpu.make_async_remote_copy(
            source(unit, 1 - core), chip.at[unit], core_send.at[unit], core_recv.at[unit],
            device_id=sibling, device_id_type=MESH_ID,
        )

    def loaded(unit):
        return pltpu.make_async_copy(source(unit, core), local.at[unit], load_sem.at[unit])

    def stored(unit):
        return pltpu.make_async_copy(chip.at[unit], chip_out.at[unit], out_sem.at[unit])

    def sent(unit, place, owner, direction):
        slot = early_slot(owner, direction, place)
        return pltpu.make_async_remote_copy(
            chip.at[unit, owner], came_out.at[unit, slot], line_send.at[unit, owner], line_recv.at[unit, slot],
            device_id={LINE: at + direction}, device_id_type=MESH_ID,
        )

    @pl.when(step == 0)
    def _():
        greet([sibling], at, 4)
        for unit in range(EARLY):
            given(unit).start()
            loaded(unit).start()

    for unit in range(EARLY):

        @pl.when(step == 1 + unit)
        def _(unit=unit):
            given(unit).wait_recv()
            loaded(unit).wait()
            for owner in range(4):

                def add(tile, owner=owner):
                    total = chip[unit, owner, tile, :].astype(f32) + local[unit, owner, tile, :].astype(f32)
                    chip[unit, owner, tile, :] = total.astype(bf16)

                row_tiles(units[unit][3], add)
            stored(unit).start()
            for place, routes in END_ROUTES.items():

                @pl.when(at == place)
                def _(place=place, routes=routes):
                    for owner, direction in routes:
                        sent(unit, place, owner, direction).start()

    @pl.when(step == last)
    def _():
        for unit in range(EARLY):
            given(unit).wait_send()
            stored(unit).wait()
            for place, routes in END_ROUTES.items():

                @pl.when(at == place)
                def _(unit=unit, place=place, routes=routes):
                    for owner, direction in routes:
                        sent(unit, place, owner, direction).wait_send()

                @pl.when(at == place + routes[0][1])
                def _(unit=unit, place=place, routes=routes):
                    for owner, direction in routes:
                        slot = early_slot(owner, direction, place)
                        pltpu.make_async_remote_copy(
                            came_out.at[unit, slot], came_out.at[unit, slot], line_send.at[unit, owner],
                            line_recv.at[unit, slot], device_id=sibling, device_id_type=MESH_ID,
                        ).wait_recv()


def ffn_bwd_kernel(
    shared_steps, halves, early, g_ref, n2_ref, mods_ref, g4_ref, mixed_ref, act_ref, dg_ref, up_ref, dn_ref, ex_ref, *rest
):
    step = pl.program_id(0)
    if early:
        other_dex, *rest = rest
        early_refs = [other_dex] + rest[5:7] + rest[14:]
        rest = rest[:5] + rest[7:14]
        early_beside(step, pl.num_programs(0) - 1, *early_refs)
    dup_ref, ddn_ref, dex_ref, gn2_ref, gg_ref, gmix, gs, gst, n2t, din, acc, racc = rest
    items = n2_ref.shape[0] // PATCHES

    @pl.when(step == 0)
    def _():
        gg_ref[...] = jnp.zeros_like(gg_ref)
        dup_ref[0:D, :] = jnp.zeros((D, D), bf16)
        for item in range(items):
            rows = pl.ds(item * PATCHES, PATCHES)
            grad = g_ref[rows, :]
            gg_ref[pl.ds(item, 1), :] = jnp.sum(grad * mixed_ref[rows, :], axis=0, keepdims=True)
            grad = mod_row(mods_ref, item, 5) * grad
            gmix[rows, :] = grad
            gs[rows, :] = grad.astype(bf16)
            gst[:, rows] = grad.astype(bf16).T
            n2t[:, rows] = n2_ref[rows, :].T
        acc[...] = jnp.zeros_like(acc)
        racc[...] = jnp.zeros_like(racc)

    @pl.when(step < shared_steps)
    def _():
        for block in range(n2_ref.shape[0] // BWD_ROWS):
            rows = pl.ds(block * BWD_ROWS, BWD_ROWS)
            inner = (dot_nt(gs[rows, :], dn_ref[...]) * dg_ref[0, rows, :].astype(f32)).astype(bf16)
            din[rows, :] = inner
            acc[rows, :] += dot_nn(inner, up_ref[...])
        at = dup_ref.shape[0] - shared_steps * CHUNK + step * CHUNK
        dup_ref[pl.ds(pl.multiple_of(at, D), CHUNK), :] = dot_nn(n2t[...], din[...]).astype(bf16).T
        ddn_ref[...] = dot_nn(gst[...], act_ref[0]).astype(bf16).T

    @pl.when(step >= shared_steps)
    def _():
        expert, half = (step - shared_steps) // halves, (step - shared_steps) % halves

        @pl.when(half == 0)
        def _():
            for item in range(items):
                rows = pl.ds(item * PATCHES, PATCHES)
                grad = (gate_column(g4_ref, rows, expert) * gmix[rows, :]).astype(bf16)
                gs[rows, :] = grad
                gst[:, rows] = grad.T

        for block in range(n2_ref.shape[0] // BWD_ROWS):
            rows = pl.ds(block * BWD_ROWS, BWD_ROWS)
            inner = (dot_nn(gs[rows, :], ex_ref[0, 1]) * dg_ref[0, rows, :].astype(f32)).astype(bf16)
            din[rows, :] = inner
            racc[rows, :] += dot_nt(inner, ex_ref[0, 0])

        dex_ref[0, 0] = dot_nn(n2t[...], din[...]).astype(bf16)
        dex_ref[0, 1] = dot_nn(gst[...], act_ref[0]).astype(bf16)

        @pl.when(half == halves - 1)
        def _():
            acc[...] += racc[...].astype(bf16).astype(f32)
            racc[...] = jnp.zeros_like(racc)

    @pl.when(step == pl.num_programs(0) - 1)
    def _():
        gn2_ref[...] = acc[...]


def final_kernel(x_ref, mods_ref, fo_ref, tgt_ref, gx_ref, gfm_ref, dfo_ref, loss_ref):
    item = pl.program_id(0)

    @pl.when(item == 0)
    def _():
        gfm_ref[...] = jnp.zeros_like(gfm_ref)
        dfo_ref[...] = jnp.zeros_like(dfo_ref)
        loss_ref[...] = jnp.zeros_like(loss_ref)

    tokens = x_ref[...]
    unit, _ = norm_parts(tokens)
    scale = mod_row(mods_ref, item, 1)
    normed = (unit * (1.0 + scale) + mod_row(mods_ref, item, 0)).astype(bf16)
    err = dot_nt(fo_ref[...], normed) - tgt_ref[...]
    loss_ref[...] += jnp.sum(err * err, axis=1, keepdims=True)
    grad_pred = (2.0 * err).astype(bf16)
    dfo_ref[...] += dot_nn(grad_pred, normed)
    grad_in, dshift, dscale = norm_back(tokens, scale, dot_tn(grad_pred, fo_ref[...]))
    gx_ref[...] = grad_in
    gfm_ref[pl.ds(item, 1), 0:D] = dshift
    gfm_ref[pl.ds(item, 1), D : 2 * D] = dscale


def params(limit):
    return pltpu.CompilerParams(vmem_limit_bytes=limit * MIB)


def cost(multiplies, moved):
    return pl.CostEstimate(flops=2 * multiplies, bytes_accessed=moved, transcendentals=0)


def whole(shape):
    return pl.BlockSpec(shape, lambda step: (0,) * len(shape))


def rows_of(width):
    return pl.BlockSpec((PATCHES, width), lambda step: (step, 0))


def shape_of(shape, kind):
    return jax.ShapeDtypeStruct(shape, kind)


ADA_STEPS = 6 * D // CHUNK
ADA_AT = 4 * D // CHUNK


def cond_forward(feat, hot, stem_t, lin):
    shapes = [(8, D)] * 4 + [(LAYERS, 8, 6 * D), (8, 2 * D)]
    return pl.pallas_call(
        cond_kernel,
        grid=(ADA_STEPS,),
        in_specs=[
            whole(feat.shape),
            whole(hot.shape),
            whole(stem_t.shape),
            pl.BlockSpec((LAYERS, CHUNK, D), lambda step: (0, ADA_AT + step, 0)),
        ],
        out_specs=[whole((8, D))] * 4 + [pl.BlockSpec((LAYERS, 8, CHUNK), lambda step: (0, 0, step)), whole((8, 2 * D))],
        out_shape=[shape_of(shape, f32) for shape in shapes],
        compiler_params=params(60),
        name="cond_forward",
    )(feat, hot, stem_t, lin)


def cond_backward(gm_a, gm_b, gfm, pre_one, pre_two, stem_t, lin):
    columns = pl.BlockSpec((8, CHUNK), lambda step: (0, step))
    return pl.pallas_call(
        cond_back_kernel,
        grid=(ADA_STEPS,),
        in_specs=[columns, columns, whole(gfm.shape), whole((8, D)), whole((8, D)), whole(stem_t.shape)]
        + [pl.BlockSpec((LAYERS, CHUNK, D), lambda step: (0, ADA_AT + step, 0))],
        out_specs=[whole((8, D))] * 2,
        out_shape=[shape_of((8, D), f32)] * 2,
        compiler_params=params(60),
        name="cond_backward",
    )(gm_a, gm_b, gfm, pre_one, pre_two, stem_t, lin)


def attn_forward(layer, tokens, mods, lin):
    count = tokens.shape[0]
    return pl.pallas_call(
        attn_fwd_kernel,
        grid=(count // PATCHES,),
        in_specs=[rows_of(D), whole(mods.shape), attn_weights(layer)],
        out_specs=[rows_of(D), rows_of(3 * D), rows_of(D), rows_of(D), rows_of(D), rows_of(D)],
        out_shape=[
            shape_of((count, D), bf16),
            shape_of((count, 3 * D), bf16),
            shape_of((count, D), bf16),
            shape_of((count, D), f32),
            shape_of((count, D), f32),
            shape_of((count, D), bf16),
        ],
        compiler_params=params(60),
        cost_estimate=cost(count * D * 4 * D * 9, 16 * count * D),
        name="attention_forward",
    )(tokens, mods, lin)


def attn_weights(layer):
    return pl.BlockSpec((None, 4 * D, D), lambda step: (layer, 0, 0))


def attn_backward(layer, gn2, grad, middle, tokens, normed, qkv, attended, branch, mods, grad_gate, lin, out_rows):
    count = tokens.shape[0]
    return pl.pallas_call(
        attn_bwd_kernel,
        grid=(count // PATCHES,),
        in_specs=[rows_of(D)] * 5
        + [rows_of(3 * D), rows_of(D), rows_of(D), whole(mods.shape), whole(grad_gate.shape), attn_weights(layer)],
        out_specs=[rows_of(D), whole((8, 6 * D)), whole((out_rows, D))],
        out_shape=[shape_of((count, D), f32), shape_of((8, 6 * D), f32), shape_of((out_rows, D), bf16)],
        scratch_shapes=[pltpu.VMEM((PATCHES, 3 * D), bf16), pltpu.VMEM((4 * D, D), f32)],
        compiler_params=params(60),
        cost_estimate=cost(count * D * 4 * D * 22, 16 * count * D),
        name="attention_backward",
    )(gn2, grad, middle, tokens, normed, qkv, attended, branch, mods, grad_gate, lin)


def weight_specs(layer, shared_steps, lin_rows):
    up_at = lin_rows // CHUNK - shared_steps
    return [
        pl.BlockSpec((None, CHUNK, D), lambda step: (layer, up_at + jnp.minimum(step, shared_steps - 1), 0)),
        pl.BlockSpec((CHUNK, D), lambda step: (jnp.minimum(step, shared_steps - 1), 0)),
        pl.BlockSpec((1, 2, D, CHUNK), lambda step: (jnp.maximum(step - shared_steps, 0), 0, 0, 0)),
    ]


def ffn_forward(layer, n2, middle, mods, g4, lin, lout, experts_w, halves, beside=()):
    count = n2.shape[0]
    shared_steps = lout.shape[0] // CHUNK
    steps = shared_steps + experts_w.shape[0]
    wide = pl.BlockSpec((1, count, CHUNK), lambda step: (step, 0, 0))
    anywhere = [pl.BlockSpec(memory_space=pl.ANY)] * len(beside)
    remote = pltpu.CompilerParams(vmem_limit_bytes=60 * MIB, collective_id=7, has_side_effects=True)
    return pl.pallas_call(
        functools.partial(ffn_fwd_kernel, shared_steps, halves, len(beside)),
        grid=(steps,),
        in_specs=[whole(n2.shape), whole(middle.shape), whole(mods.shape), whole(g4.shape)]
        + weight_specs(layer, shared_steps, lin.shape[1])
        + anywhere,
        out_specs=[wide, wide, whole((count, D)), whole((count, D))] + anywhere,
        out_shape=[
            shape_of((steps, count, CHUNK), bf16),
            shape_of((steps, count, CHUNK), bf16),
            shape_of((count, D), f32),
            shape_of((count, D), f32),
        ]
        + [shape_of((8,) + part.shape, bf16) for part in beside],
        scratch_shapes=[pltpu.VMEM((count, D), f32)] * 2 + (gather_semaphores(4) if beside else []),
        compiler_params=remote if beside else params(60),
        cost_estimate=cost(4 * steps * count * D * CHUNK * 2, 8 * steps * count * CHUNK),
        name="ffn_forward",
    )(n2, middle, mods, g4, lin, lout, experts_w, *beside)


def ffn_backward(layer, grad, n2, mods, g4, mixed, active, slope, lin, lout, experts_w, halves, early=()):
    count = n2.shape[0]
    shared_steps = lout.shape[0] // CHUNK
    steps = shared_steps + experts_w.shape[0]
    wide = pl.BlockSpec((1, count, CHUNK), lambda step: (step, 0, 0))
    specs = weight_specs(layer, shared_steps, lin.shape[1])
    anywhere = [pl.BlockSpec(memory_space=pl.ANY)] * len(early)
    remote = pltpu.CompilerParams(vmem_limit_bytes=62 * MIB, collective_id=8, has_side_effects=True)
    dma = pltpu.SemaphoreType.DMA
    early_scratch = [pltpu.VMEM((EARLY, 4, D // 2, CHUNK), bf16)] * 2
    early_scratch += [dma((EARLY,)), dma((EARLY,)), dma((EARLY,)), dma((EARLY, 4)), dma((EARLY, 5)), dma((EARLY,))]
    return pl.pallas_call(
        functools.partial(ffn_bwd_kernel, shared_steps, halves, len(early)),
        grid=(steps,),
        in_specs=[whole(grad.shape), whole(n2.shape), whole(mods.shape), whole(g4.shape), whole(mixed.shape), wide, wide]
        + specs
        + anywhere,
        out_specs=[whole((lout.shape[0] + D, D)), specs[1], specs[2], whole((count, D)), whole((8, D))] + anywhere * 2,
        out_shape=[
            shape_of((lout.shape[0] + D, D), bf16),
            shape_of(lout.shape, bf16),
            shape_of(experts_w.shape, bf16),
            shape_of((count, D), f32),
            shape_of((8, D), f32),
        ]
        + [shape_of((EARLY, lead, D // 2, CHUNK), bf16) for lead in (4, 5) if early],
        scratch_shapes=[
            pltpu.VMEM((count, D), f32),
            pltpu.VMEM((count, D), bf16),
            pltpu.VMEM((D, count), bf16),
            pltpu.VMEM((D, count), bf16),
            pltpu.VMEM((count, CHUNK), bf16),
            pltpu.VMEM((count, D), f32),
            pltpu.VMEM((count, D), f32),
        ]
        + (early_scratch if early else []),
        compiler_params=remote if early else params(60),
        cost_estimate=cost(4 * steps * count * D * CHUNK * 4 // 2, 8 * steps * count * CHUNK),
        name="ffn_backward",
    )(grad, n2, mods, g4, mixed, active, slope, lin, lout, experts_w, *early)


def final_step(tokens, mods, fo_rows, target_t):
    count = tokens.shape[0]
    return pl.pallas_call(
        final_kernel,
        grid=(count // PATCHES,),
        in_specs=[
            rows_of(D),
            whole(mods.shape),
            whole(fo_rows.shape),
            pl.BlockSpec((PATCH_DIM, PATCHES), lambda step: (0, step)),
        ],
        out_specs=[rows_of(D), whole((8, 2 * D)), whole((PATCH_DIM, D)), whole((PATCH_DIM, 1))],
        out_shape=[
            shape_of((count, D), f32),
            shape_of((8, 2 * D), f32),
            shape_of((PATCH_DIM, D), f32),
            shape_of((PATCH_DIM, 1), f32),
        ],
        compiler_params=params(60),
        name="final_step",
    )(tokens, mods, fo_rows, target_t)


def update_kernel(groups, grad_a, grad_b, total_a, total_b, w_ref, f_ref, s_ref, m_ref, new_ref, half_ref, fn_ref, sn_ref, mn_ref):
    for layer, (grad_ref, total_ref) in enumerate(((grad_a, total_a), (grad_b, total_b))):

        @pl.when(pl.program_id(0) == layer)
        def _(grad_ref=grad_ref, total_ref=total_ref):
            gradient = grad_ref[...]
            fn_ref[0] = beta_one * f_ref[0] + (1.0 - beta_one) * gradient
            sn_ref[0] = beta_two * s_ref[0] + (1.0 - beta_two) * gradient * gradient
            mean_delta = total_ref[...] / groups
            moment_new = outer_mom * m_ref[0] + mean_delta
            weight = w_ref[0] - outer_rate * (mean_delta + outer_mom * moment_new)
            mn_ref[0] = moment_new
            new_ref[0] = weight
            half_ref[0] = weight.astype(bf16)


def update_arrays(tile, grads, totals, weight, first, second, moment):
    layers, rows, width = weight.shape
    tiles = rows // tile
    state = pl.BlockSpec((1, tile, width), lambda layer, step: (layer, step, 0))
    early = pl.BlockSpec((tile, width), lambda layer, step: (jnp.where(layer == 0, step, tiles - 1), 0))
    late = pl.BlockSpec((tile, width), lambda layer, step: (jnp.where(layer == 0, 0, step), 0))
    return pl.pallas_call(
        functools.partial(update_kernel, lax.axis_size(GROUP)),
        grid=(layers, tiles),
        in_specs=[early, late, early, late] + [state] * 4,
        out_specs=[state] * 5,
        out_shape=[shape_of(weight.shape, kind) for kind in (f32, bf16, f32, f32, f32)],
        compiler_params=params(60),
        name="update_arrays",
    )(*grads, *totals, weight, first, second, moment)


def pad_rows(values):
    return jnp.pad(values, ((0, 8 - values.shape[0]), (0, 0)))


def stem_lanes(stem_t):
    pieces, at = [], 0
    for size, padded in zip(STEM_SIZES, STEM_PADDED):
        pieces.append(jnp.pad(stem_t[:, at : at + size], ((0, 0), (0, padded - size))))
        at = at + size
    pieces.append(jnp.zeros((stem_t.shape[0], STEM_LANES - sum(STEM_PADDED)), stem_t.dtype))
    return jnp.concatenate(pieces, axis=1)


MESH_ID = pl.DeviceIdType.MESH
TILE = 48


def plane_partners():
    group = lax.axis_index(GROUP)
    return {GROUP: group + 1 - 2 * lax.rem(group, 2)}, {GROUP: lax.rem(group + 2, 4)}


def greet(partners, line_at, line_size):
    barrier = pltpu.get_barrier_semaphore()
    for partner in partners:
        pl.semaphore_signal(barrier, inc=1, device_id=partner, device_id_type=MESH_ID)

    @pl.when(line_at > 0)
    def _():
        pl.semaphore_signal(barrier, inc=1, device_id={LINE: line_at - 1}, device_id_type=MESH_ID)

    @pl.when(line_at < line_size - 1)
    def _():
        pl.semaphore_signal(barrier, inc=1, device_id={LINE: line_at + 1}, device_id_type=MESH_ID)

    ends = jnp.where(line_at == 0, 1, 0) + jnp.where(line_at == line_size - 1, 1, 0)
    pl.semaphore_wait(barrier, len(partners) + 2 - ends)


def row_tiles(rows, body):
    def step(index, carry):
        body(pl.ds(pl.multiple_of(index * TILE, TILE), TILE))
        return carry

    lax.fori_loop(0, rows // TILE, step, 0)


def adam_delta(weight, gradient, first, second):
    return adam_step(weight, gradient, first, second)[0]


def reduce_units():
    units = []
    for matrix in range(2):
        for half in range(2):
            units.append((0, matrix, half * D // 2, D // 2, CHUNK, ()))
    for half in range(2):
        units.append((1, 0, half * 432, 432, D, (1,)))
    units.append((2, 0, 0, D, D, ()))
    return units


def reduce_kernel(
    layer, with_stem, dex, dqkvo, dup, ddn, extra, ex_w, ex_f, ex_s, li_w, li_f, li_s, lo_w, lo_f, lo_s, *rest
):
    early = EARLY if with_stem else 0
    if early:
        chip_in, came_in, *rest = rest
    if with_stem:
        stem_in, *rest, stem_sem, stem_send, stem_recv, stem_a, stem_b, stem_c, stem_d = rest
        stem_out = rest.pop(6)
    g_ex, g_li, g_lo, m_ex, m_li, m_lo, *scratch = rest
    units = reduce_units()
    number = len(units)
    banks = [scratch[at * number : (at + 1) * number] for at in range(9)]
    chip, local, came, delta, swapped, swapped_two, weight, first, second = banks
    extra_buf = scratch[9 * number]
    core_send, core_recv, line_send, line_recv, load_sem, plane_send, plane_recv, out_sem = scratch[9 * number + 1 :]
    at = lax.axis_index(LINE)
    core = lax.axis_index(CORE)
    sibling = {CORE: 1 - core}
    side_x, side_y = plane_partners()
    greet([sibling, side_x, side_y], at, 4)

    def pieces(unit, which):
        kind, matrix, row, rows, _, _ = units[unit]
        if kind == 0:
            return [(dex.at[:, which, matrix, pl.ds(row, rows)], slice(0, 4))]
        if kind == 2:
            return [(ddn.at[:, which, pl.ds(row, rows)], slice(0, 4))]
        return [
            (dqkvo.at[which, pl.ds(row, rows)], 0),
            (dup.at[0, which, pl.ds(row, rows)], 2),
            (dup.at[1, which, pl.ds(row, rows)], 3),
        ]

    def dest(bank, unit, where):
        return bank[unit].at[pl.ds(0, 4)] if isinstance(where, slice) else bank[unit].at[where]

    if with_stem:
        load = pltpu.make_async_copy(stem_in, stem_a, stem_sem.at[0])
        load.start()
        load.wait()

    def stem_copies(second_step):
        landing, sides = ((stem_b, (side_x, side_y)), (stem_c, (side_y, side_x)))[second_step]
        return [
            pltpu.make_async_remote_copy(
                stem_a.at[pl.ds(begin, size)], landing.at[pl.ds(begin, size)], stem_send.at[2 * second_step + half],
                stem_recv.at[2 * second_step + half], device_id=sides[half], device_id_type=MESH_ID,
            )
            for half, (begin, size) in enumerate(((0, 16), (16, 32)))
        ]

    def stem_turn(turn):
        if not with_stem or turn > 2:
            return
        if turn == 0:
            for copy in stem_copies(0):
                copy.start()
        elif turn == 1:
            for copy in stem_copies(0):
                copy.wait()
            stem_a[...] = (stem_a[...].astype(f32) + stem_b[...].astype(f32)).astype(bf16)
            for copy in stem_copies(1):
                copy.start()
        else:
            for copy in stem_copies(1):
                copy.wait()
            stem_d[...] = stem_a[...].astype(f32) + stem_c[...].astype(f32)
            pltpu.make_async_copy(stem_d, stem_out, stem_sem.at[1]).start()

    early_slots = {1: [3, 2, 1], 2: [0, 1, 4]}

    def early_load(unit, slot, index):
        sem = (load_sem.at[unit, 1], load_sem.at[unit, 2], load_sem.at[number, 1 + unit])[index]
        return pltpu.make_async_copy(came_in.at[unit, slot], came[unit].at[slot], sem)

    given, loads = [], []
    for unit in range(number):
        given.append([])
        loads.append([])
        if unit < early:
            copy = pltpu.make_async_copy(chip_in.at[unit], chip[unit], load_sem.at[unit, 0])
            copy.start()
            loads[unit].append(copy)
            for place, slots in early_slots.items():

                @pl.when(at == place)
                def _(unit=unit, slots=slots):
                    for index, slot in enumerate(slots):
                        early_load(unit, slot, index).start()

            continue
        for place, (source, where) in enumerate(pieces(unit, 1 - core)):
            copy = pltpu.make_async_remote_copy(
                source, dest(chip, unit, where), core_send.at[unit, place], core_recv.at[unit, place],
                device_id=sibling, device_id_type=MESH_ID,
            )
            copy.start()
            given[unit].append(copy)
        for place, (source, where) in enumerate(pieces(unit, core)):
            copy = pltpu.make_async_copy(source, dest(local, unit, where), load_sem.at[unit, place])
            copy.start()
            loads[unit].append(copy)
    state_loads = []
    for unit, (kind, matrix, row, rows, _, _) in enumerate(units):
        if kind == 0:
            sources = [ex_w.at[layer, 0, matrix], ex_f.at[0, layer, 0, matrix], ex_s.at[0, layer, 0, matrix]]
        elif kind == 1:
            sources = [li_w.at[layer], li_f.at[layer], li_s.at[layer]]
        else:
            sources = [lo_w.at[layer], lo_f.at[0, layer], lo_s.at[0, layer]]
        state_loads.append([])
        for place, (source, bank) in enumerate(zip(sources, (weight, first, second))):
            copy = pltpu.make_async_copy(source.at[pl.ds(row, rows)], bank[unit], load_sem.at[unit, 3 + place])
            copy.start()
            state_loads[unit].append(copy)
    extra_load = pltpu.make_async_copy(extra, extra_buf, load_sem.at[number, 0])
    extra_load.start()

    def line_copy(unit, owner, step, place):
        slot = 4 if step == -1 and owner == place - 1 else owner
        return pltpu.make_async_remote_copy(
            chip[unit].at[owner], came[unit].at[slot], line_send.at[unit, owner], line_recv.at[unit, slot],
            device_id={LINE: at + step}, device_id_type=MESH_ID,
        )

    def arrived(unit, slot, place):
        if unit < early and slot in early_slots.get(place, ()):
            early_load(unit, slot, early_slots[place].index(slot)).wait()
            return
        pltpu.make_async_remote_copy(
            came[unit].at[slot], came[unit].at[slot], line_send.at[unit, 0], line_recv.at[unit, slot],
            device_id=sibling, device_id_type=MESH_ID,
        ).wait_recv()

    routes_of = {0: [(3, 1), (2, 1), (1, 1)], 1: [(3, 1), (2, 1), (0, -1)], 2: [(0, -1), (1, -1), (3, 1)], 3: [(0, -1), (1, -1), (2, -1)]}
    finals = {0: [4], 1: [1, 4], 2: [2, 4], 3: [3]}

    def forward(unit):
        rows, absent = units[unit][3], units[unit][5]
        for middle in (1, 2):

            @pl.when(at == middle)
            def _(middle=middle):
                for owner, step in routes_of[middle]:
                    if owner in absent:
                        continue
                    arrived(unit, owner, middle)

                    def add(tile, owner=owner):
                        total = chip[unit][owner, tile, :].astype(f32) + came[unit][owner, tile, :].astype(f32)
                        chip[unit][owner, tile, :] = total.astype(bf16)

                    row_tiles(rows, add)
                    line_copy(unit, owner, step, middle).start()

    for unit, (kind, matrix, row, rows, _, absent) in enumerate(units):
        for copy in given[unit]:
            copy.wait_recv()
        for copy in loads[unit]:
            copy.wait()
        for owner in range(0 if unit < early else 4):
            if owner in absent:
                chip[unit][owner] = jnp.zeros(chip[unit].shape[1:], bf16)
                continue

            def add(tile, owner=owner, unit=unit):
                total = chip[unit][owner, tile, :].astype(f32) + local[unit][owner, tile, :].astype(f32)
                chip[unit][owner, tile, :] = total.astype(bf16)

            row_tiles(rows, add)
        for end in (0, 3):

            @pl.when(at == end)
            def _(unit=unit, end=end, absent=absent):
                for owner, step in routes_of[end]:
                    if owner not in absent and unit >= early:
                        line_copy(unit, owner, step, end).start()
                came[unit][0 if end == 0 else 4] = jnp.zeros(chip[unit].shape[1:], bf16)

        for owner in absent:

            @pl.when(at == owner)
            def _(unit=unit, owner=owner):
                came[unit][owner] = jnp.zeros(chip[unit].shape[1:], bf16)
                came[unit][4] = jnp.zeros(chip[unit].shape[1:], bf16)
        if unit < early:
            forward(unit)

    def plane_copies(unit, second_step):
        rows = units[unit][3]
        middle = rows // 32 * 16
        sides = (side_y, side_x) if second_step else (side_x, side_y)
        landing = swapped_two if second_step else swapped
        copies = []
        for half, (begin, size) in enumerate(((0, middle), (middle, rows - middle))):
            part = pl.ds(begin, size)
            copies.append(
                pltpu.make_async_remote_copy(
                    delta[unit].at[part], landing[unit].at[part], plane_send.at[unit, 2 * second_step + half],
                    plane_recv.at[unit, 2 * second_step + half], device_id=sides[half], device_id_type=MESH_ID,
                )
            )
        return copies

    def out_copy(unit, means):
        kind, matrix, row, rows, _, _ = units[unit]
        target = ((g_ex.at[matrix], g_li, g_lo), (m_ex.at[matrix], m_li, m_lo))[means][kind]
        source = first[unit] if means else weight[unit]
        return pltpu.make_async_copy(source, target.at[pl.ds(row, rows)], out_sem.at[unit, means])

    firsts, seconds = {}, {}

    def finish(unit):
        kind, matrix, row, rows, _, absent = units[unit]
        for place in range(4):

            @pl.when(at == place)
            def _(place=place):
                if place not in absent:
                    for slot in finals[place]:
                        arrived(unit, slot, place)

        for copy in state_loads[unit]:
            copy.wait()
        if kind == 1 and row == 0:
            extra_load.wait()

        def body(tile):
            grad = chip[unit][at, tile, :].astype(f32) + came[unit][at, tile, :].astype(f32)
            grad = grad + came[unit][4, tile, :].astype(f32)
            if kind == 1:
                grad = grad + extra_buf[pl.ds(row + tile.start, TILE), :]
            change = adam_delta(weight[unit][tile, :], grad, first[unit][tile, :], second[unit][tile, :])
            delta[unit][tile, :] = change.astype(bf16)
            weight[unit][tile, :] = grad

        row_tiles(rows, body)
        out_copy(unit, 0).start()
        firsts[unit] = plane_copies(unit, 0)
        for copy in firsts[unit]:
            copy.start()

    def exchange(unit):
        for copy in firsts[unit]:
            copy.wait()

        def body(tile):
            total = delta[unit][tile, :].astype(f32) + swapped[unit][tile, :].astype(f32)
            delta[unit][tile, :] = total.astype(bf16)

        row_tiles(units[unit][3], body)
        seconds[unit] = plane_copies(unit, 1)
        for copy in seconds[unit]:
            copy.start()

    def close(unit):
        for copy in seconds[unit]:
            copy.wait_recv()

        def body(tile):
            first[unit][tile, :] = delta[unit][tile, :].astype(f32) + swapped_two[unit][tile, :].astype(f32)

        row_tiles(units[unit][3], body)
        out_copy(unit, 1).start()

    for turn in range(number + 3):
        stem_turn(turn)
        for lag, action in enumerate((forward, finish, exchange, close)):
            if 0 <= turn - lag < number and (lag or turn >= early):
                action(turn - lag)

    if with_stem:
        pltpu.make_async_copy(stem_d, stem_out, stem_sem.at[1]).wait()
    for unit in range(number):
        for copy in given[unit]:
            copy.wait_send()
        for copy in seconds[unit]:
            copy.wait_send()
        out_copy(unit, 0).wait()
        out_copy(unit, 1).wait()
        for place in range(4):

            @pl.when(at == place)
            def _(place=place, unit=unit):
                for owner, step in routes_of[place]:
                    if owner not in units[unit][5] and (unit >= early or place in (1, 2)):
                        line_copy(unit, owner, step, place).wait_send()


def reduce_layer(layer, dex, dqkvo, dup, ddn, extra, states, stem_delta=None, begun=()):
    units = reduce_units()
    scratch = []
    for lead, kind in (((4,), bf16), ((4,), bf16), ((5,), bf16), ((), bf16), ((), bf16), ((), bf16), ((), f32), ((), f32), ((), f32)):
        scratch += [pltpu.VMEM(lead + (unit[3], unit[4]), kind) for unit in units]
    number = len(units)
    scratch.append(pltpu.VMEM(extra.shape, f32))
    dma = pltpu.SemaphoreType.DMA
    scratch += [dma((number, 3)), dma((number, 3)), dma((number, 4)), dma((number, 5)), dma((number + 1, 6))]
    scratch += [dma((number, 4)), dma((number, 4)), dma((number, 2))]
    anywhere = pl.BlockSpec(memory_space=pl.ANY)
    shapes = [(2, D, CHUNK), extra.shape, (D, D)] * 2
    stems = [] if stem_delta is None else [stem_delta]
    for delta in stems:
        shapes.append(delta.shape)
        scratch += [dma((2,)), dma((4,)), dma((4,))] + [pltpu.VMEM(delta.shape, bf16)] * 3
        scratch.append(pltpu.VMEM(delta.shape, f32))
    return pl.pallas_call(
        functools.partial(reduce_kernel, layer, bool(stems)),
        out_shape=[shape_of(shape, f32) for shape in shapes],
        in_specs=[anywhere] * (5 + len(states) + len(stems) + len(begun)),
        out_specs=[anywhere] * len(shapes),
        scratch_shapes=scratch,
        compiler_params=pltpu.CompilerParams(
            vmem_limit_bytes=62 * MIB, collective_id=1 + layer, has_side_effects=True
        ),
        name="reduce_layer",
    )(dex, dqkvo, dup, ddn, extra, *states, *begun, *stems)


def shard_part(kind, ref, quarter, half=None):
    if kind == "stem":
        begin, size = quarter * (STEM_LANES // 4), STEM_LANES // 4
        if half is not None:
            begin, size = begin + half * (size // 2), size // 2
        return ref.at[:, pl.ds(pl.multiple_of(begin, 128), size)]
    if kind == "lin":
        begin, size = lax.rem(quarter, 2) * 432, 432
        if half is not None:
            begin, size = begin + half * 208, (208, 224)[half]
        return ref.at[quarter // 2, pl.ds(pl.multiple_of(begin, 16), size)]
    begin, size = quarter * (D // 4), D // 4
    if half is not None:
        begin, size = begin + half * (size // 2), size // 2
    return ref.at[pl.ds(pl.multiple_of(begin, 16), size)]


class WeightGather:
    def __init__(self, kinds, sources, targets, sends, recvs, cores_send, cores_recv, own_sem):
        self.kinds, self.sources, self.targets = kinds, sources, targets
        self.sends, self.recvs = sends, recvs
        self.cores_send, self.cores_recv, self.own_sem = cores_send, cores_recv, own_sem
        self.at, self.core, self.group = lax.axis_index(LINE), lax.axis_index(CORE), lax.axis_index(GROUP)
        self.sibling = {CORE: 1 - self.core}
        self.side_x, self.side_y = plane_partners()
        self.group_x = self.group + 1 - 2 * lax.rem(self.group, 2)
        self.group_y = lax.rem(self.group + 2, 4)
        near = jnp.where(self.at == 3, 3, 1)
        far = jnp.where(self.at == 0, 3, jnp.where(self.at == 3, 1, 2))
        self.order = (near, 6 - near - far, far)

    def enter(self):
        barrier = pltpu.get_barrier_semaphore()
        others = [{LINE: lax.rem(self.at + step, 4)} for step in (1, 2, 3)]
        for partner in others + [self.sibling, self.side_x, self.side_y]:
            pl.semaphore_signal(barrier, inc=1, device_id=partner, device_id_type=MESH_ID)
        pl.semaphore_wait(barrier, 6)

    def whole_part(self, unit, owner, core):
        target = self.targets[unit]
        if self.kinds[unit] == "lin":
            return target.at[:, owner * 2 + core]
        return target.at[owner * 2 + core]

    def copy(self, unit, source, target, slot, kind, device):
        return pltpu.make_async_remote_copy(
            source, target, self.sends.at[unit, slot, kind], self.recvs.at[unit, slot, kind],
            device_id=device, device_id_type=MESH_ID,
        )

    def line_copy(self, unit, step):
        target = shard_part(self.kinds[unit], self.whole_part(unit, self.at, self.core), self.group)
        source = shard_part(self.kinds[unit], self.sources[unit], self.group)
        return pltpu.make_async_remote_copy(
            source, target, self.sends.at[unit, step - 1, 0], self.recvs.at[unit, 3 - step, 0],
            device_id={LINE: lax.rem(self.at + step, 4)}, device_id_type=MESH_ID,
        )

    def owner_of(self, slot):
        return lax.rem(self.at + slot, 4)

    def part(self, unit, slot, quarter, half=None):
        return shard_part(self.kinds[unit], self.whole_part(unit, self.owner_of(slot), self.core), quarter, half)

    def core_copy(self, unit, slot, own=False):
        source = self.sources[unit] if own else self.whole_part(unit, self.owner_of(slot), self.core)
        return pltpu.make_async_remote_copy(
            source, self.whole_part(unit, self.owner_of(slot), self.core),
            self.cores_send.at[unit, slot], self.cores_recv.at[unit, slot],
            device_id=self.sibling, device_id_type=MESH_ID,
        )

    def own_copy(self, unit):
        return pltpu.make_async_copy(
            self.sources[unit], self.whole_part(unit, self.at, self.core), self.own_sem.at[unit]
        )

    def begin(self, unit):
        for step in (2, 1, 3):
            self.line_copy(unit, step).start()
        self.core_copy(unit, 0, True).start()
        self.own_copy(unit).start()

    def plane_copies(self, unit, slot):
        mine = self.part(unit, slot, self.group)
        return [self.copy(unit, mine, mine, slot - 1, 1, self.side_x), self.copy(unit, mine, mine, slot - 1, 2, self.side_y)]

    def plane_arrivals(self, unit, slot):
        parts = [self.part(unit, slot, self.group_x), self.part(unit, slot, self.group_y)]
        return [self.copy(unit, parts[0], parts[0], slot - 1, 1, self.side_x), self.copy(unit, parts[1], parts[1], slot - 1, 2, self.side_y)]

    def corner_copies(self, unit, slot):
        parts = [self.part(unit, slot, self.group_x, 0), self.part(unit, slot, self.group_y, 1)]
        return [self.copy(unit, parts[0], parts[0], slot - 1, 3, self.side_y), self.copy(unit, parts[1], parts[1], slot - 1, 4, self.side_x)]

    def corner_arrivals(self, unit, slot):
        corner = 3 - self.group
        parts = [self.part(unit, slot, corner, 0), self.part(unit, slot, corner, 1)]
        return [self.copy(unit, parts[0], parts[0], slot - 1, 3, self.side_y), self.copy(unit, parts[1], parts[1], slot - 1, 4, self.side_x)]

    def along_line(self, unit):
        for slot in self.order:
            mine = self.part(unit, slot, self.group)
            self.copy(unit, mine, mine, slot - 1, 0, self.sibling).wait_recv()
            for copy in self.plane_copies(unit, slot):
                copy.start()

    def in_plane(self, unit):
        for slot in self.order:
            for copy in self.plane_arrivals(unit, slot):
                copy.wait_recv()
            for copy in self.corner_copies(unit, slot):
                copy.start()

    def to_sibling(self, unit):
        for slot in self.order:
            for copy in self.corner_arrivals(unit, slot):
                copy.wait_recv()
            self.core_copy(unit, slot).start()

    def end(self, unit):
        self.own_copy(unit).wait()
        for slot in range(4):
            self.core_copy(unit, slot, slot == 0).wait_send()
            other = self.whole_part(unit, self.owner_of(slot), 1 - self.core)
            pltpu.make_async_remote_copy(
                other, other, self.cores_send.at[unit, slot], self.cores_recv.at[unit, slot],
                device_id=self.sibling, device_id_type=MESH_ID,
            ).wait_recv()
        for slot in (1, 2, 3):
            self.line_copy(unit, slot).wait_send()
            for copy in self.plane_copies(unit, slot) + self.corner_copies(unit, slot):
                copy.wait_send()


def gather_semaphores(number):
    dma = pltpu.SemaphoreType.DMA
    return [dma((number, 3, 5)), dma((number, 3, 5)), dma((number, 4)), dma((number, 4)), dma((number,))]


def gather_kernel(kinds, split, *refs):
    count = len(split)
    arrays_in, arrays_out, sems = refs[:count], refs[count : 2 * count], refs[2 * count :]
    sources, targets = [], []
    for given, target, parts in zip(arrays_in, arrays_out, split):
        for part in parts:
            sources.append(given if part is None else given.at[part])
            targets.append(target if part is None else target.at[(slice(None),) + part])
    work = WeightGather(kinds, sources, targets, *sems)
    work.enter()
    number = len(kinds)
    work.begin(0)
    work.begin(1)
    for turn in range(number + 2):
        for lag, action in enumerate((work.along_line, work.in_plane, work.to_sibling)):
            if 0 <= turn - lag < number:
                action(turn - lag)
            if lag == 0 and turn + 2 < number:
                work.begin(turn + 2)
    for unit in range(number):
        work.end(unit)


def gather_beside(step, last, given, taken, sems):
    parts = [(matrix, slice(None), pl.ds(begin, D)) for matrix in range(2) for begin in (0, D)]
    sources = [given[0].at[part] for part in parts]
    targets = [taken[0].at[(slice(None),) + part] for part in parts]
    work = WeightGather(["rows"] * 4, sources, targets, *sems)
    line, plane, pair = work.along_line, work.in_plane, work.to_sibling
    schedule = {
        0: [(work.begin, 0), (work.begin, 1)],
        1: [(work.begin, 2)],
        2: [(work.begin, 3)],
        3: [(line, 0)],
        4: [(line, 1)],
        5: [(plane, 0)],
        6: [(line, 2), (plane, 1)],
        7: [(line, 3), (pair, 0)],
        8: [(plane, 2)],
        9: [(plane, 3), (pair, 1)],
        10: [(pair, 2)],
        11: [(pair, 3)] + [(work.end, unit) for unit in range(4)],
    }
    for when, actions in schedule.items():

        @pl.when(step == (last if when == 11 else when))
        def _(when=when, actions=actions):
            if when == 0:
                work.enter()
            for action, unit in actions:
                action(unit)


def gather_weights(stem, lin, louts, experts_in):
    lanes = [pl.ds(begin, 128) for begin in range(0, D, 128)]
    every = slice(None)
    arrays = [stem, lin] + list(louts) + list(experts_in)
    kinds = ["stem"] + ["lin"] * len(lanes) + ["rows"] * (len(louts) + 4 * len(experts_in))
    split = [[None], [(every, every, part) for part in lanes]] + [[None]] * len(louts)
    split += [[(matrix, every, pl.ds(begin, D)) for matrix in range(2) for begin in (0, D)]] * len(experts_in)
    shapes = [(8,) + stem.shape, (lin.shape[0], 8) + lin.shape[1:]]
    shapes += [(8,) + part.shape for part in arrays[2:]]
    anywhere = pl.BlockSpec(memory_space=pl.ANY)
    return pl.pallas_call(
        functools.partial(gather_kernel, kinds, split),
        out_shape=[shape_of(shape, bf16) for shape in shapes],
        in_specs=[anywhere] * len(arrays),
        out_specs=[anywhere] * len(arrays),
        scratch_shapes=gather_semaphores(len(kinds)),
        compiler_params=pltpu.CompilerParams(collective_id=5, has_side_effects=True),
        name="gather_weights",
    )(*arrays)


def exchange_kernel(packed, loss, all_packed, total, from_x, from_y, losses, held, send, recv, core_send, core_recv, plane_send, plane_recv, own_sem):
    at, core = lax.axis_index(LINE), lax.axis_index(CORE)
    side_x, side_y = plane_partners()
    sibling = {CORE: 1 - core}
    barrier = pltpu.get_barrier_semaphore()
    others = [{LINE: lax.rem(at + step, 4)} for step in (1, 2, 3)]
    for partner in others + [sibling, side_x, side_y]:
        pl.semaphore_signal(barrier, inc=1, device_id=partner, device_id_type=MESH_ID)
    pl.semaphore_wait(barrier, 6)

    def slots(owner, which):
        return all_packed.at[owner * 2 + which], losses.at[owner * 2 + which]

    own = [pltpu.make_async_copy(source, target, own_sem.at[place]) for place, (source, target) in enumerate(zip((packed, loss), slots(at, core)))]
    for copy in own:
        copy.start()

    def line(step, place):
        source, target = ((packed, loss)[place], slots(at, core)[place])
        return pltpu.make_async_remote_copy(
            source, target, send.at[step - 1, place], recv.at[step - 1, place],
            device_id=others[step - 1], device_id_type=MESH_ID,
        )

    def across(step, place):
        owner = lax.rem(at + 4 - step, 4)
        source = (packed, loss)[place] if step == 0 else slots(owner, core)[place]
        return pltpu.make_async_remote_copy(
            source, slots(owner, core)[place], core_send.at[step, place], core_recv.at[step, place],
            device_id=sibling, device_id_type=MESH_ID,
        )

    def arrival(step, place, which, sem):
        here = slots(lax.rem(at + 4 - step, 4), which)[place]
        return pltpu.make_async_remote_copy(
            here, here, core_send.at[step, place], sem, device_id=sibling, device_id_type=MESH_ID
        )

    for place in (1, 0):
        for step in (2, 3, 1):
            line(step, place).start()
        across(0, place).start()
    for place in (1, 0):
        for step in (1, 3, 2):
            arrival(step, place, core, recv.at[step - 1, place]).wait_recv()
            across(step, place).start()
        for step in range(4):
            arrival(step, place, 1 - core, core_recv.at[step, place]).wait_recv()
        if place == 1:
            own[1].wait()
            held[...] = jnp.sum(losses[...], axis=0)
            first = pltpu.make_async_remote_copy(held, from_x, plane_send.at[0], plane_recv.at[0], device_id=side_x, device_id_type=MESH_ID)
            first.start()
    first.wait()
    held[...] += from_x[...]
    second = pltpu.make_async_remote_copy(held, from_y, plane_send.at[1], plane_recv.at[1], device_id=side_y, device_id_type=MESH_ID)
    second.start()
    second.wait()
    total[...] = held[...] + from_y[...]
    own[0].wait()
    for place in range(2):
        for step in (1, 2, 3):
            line(step, place).wait_send()
        for step in range(4):
            across(step, place).wait_send()


def exchange_small(packed, loss):
    dma = pltpu.SemaphoreType.DMA
    vmem = pl.BlockSpec(memory_space=pltpu.VMEM)
    return pl.pallas_call(
        exchange_kernel,
        out_shape=[shape_of((8,) + packed.shape, packed.dtype), shape_of(loss.shape, f32)],
        in_specs=[vmem, vmem],
        out_specs=[vmem, vmem],
        scratch_shapes=[pltpu.VMEM(loss.shape, f32)] * 2
        + [pltpu.VMEM((8,) + loss.shape, f32), pltpu.VMEM(loss.shape, f32)]
        + [dma((3, 2)), dma((3, 2)), dma((4, 2)), dma((4, 2)), dma((2,)), dma((2,)), dma((2,))],
        compiler_params=pltpu.CompilerParams(collective_id=6, has_side_effects=True, vmem_limit_bytes=16 * MIB),
        name="exchange_small",
    )(packed, loss)


def few_experts(
    patches,
    target_noise,
    timesteps,
    labels,
    routes,
    route_gates,
    stem_weights,
    layer_in,
    layer_out,
    experts,
    stem_first,
    layer_in_first,
    layer_out_first,
    experts_first,
    stem_second,
    layer_in_second,
    layer_out_second,
    experts_second,
    stem_moment,
    layer_in_moment,
    layer_out_moment,
    experts_moment,
):
    count = patches.shape[0]
    items = timesteps.shape[0]
    halves = lax.axis_size(CORE)
    sharers = lax.axis_size(LINE) * halves
    expert_count = lax.axis_size(LINE) * experts.shape[1]
    place = lax.axis_index(LINE) * halves + lax.axis_index(CORE)

    stem_t = stem_weights.T
    lin_t = jnp.swapaxes(layer_in, 1, 2)
    louts = [to_half(layer_out[layer]) for layer in range(LAYERS)]
    pairs = [to_half(experts[layer, 0]) for layer in range(LAYERS)]
    gathered = gather_weights(stem_lanes(to_half(stem_t)), to_half(lin_t), louts, pairs[:1])
    stem_all = gathered[0].reshape(D, STEM_LANES)
    lin_all = gathered[1].reshape(LAYERS, -1, D)
    lout_all = [gathered[2 + layer].reshape(-1, D) for layer in range(LAYERS)]
    expert_all = [gathered[2 + LAYERS]]

    feat = time_features(timesteps)
    hot = label_table(labels)
    hot_pad = jnp.pad(hot, ((0, 32 - items), (0, STEM_PADDED[3] - hot.shape[1]))).astype(bf16)
    cond, hidden, pre_one, pre_two, mods, fin_mods = cond_forward(pad_rows(feat), hot_pad, stem_all, lin_all)
    tokens = product_nt(patches, stem_all[:, :PATCH_DIM])
    tokens = (tokens.reshape(items, -1, D) + positions_table()[None]).reshape(-1, D)
    expert_ids = jnp.arange(expert_count, dtype=jnp.int32)
    saved = []
    for layer in range(LAYERS):
        g4 = jnp.sum(
            jnp.where(routes[layer][:, :, None] == expert_ids, route_gates[layer][:, :, None], 0.0), axis=1
        )
        normed, qkv, attended, branch, middle, n2 = attn_forward(layer, tokens, mods[layer], lin_all)
        beside = (pairs[layer + 1],) if layer + 1 < LAYERS else ()
        active, slope, mixed, result, *arrived = ffn_forward(
            layer, n2, middle, mods[layer], g4, lin_all, lout_all[layer], expert_all[layer], halves, beside
        )
        if beside:
            expert_all.append(arrived[0])
        saved.append((tokens, g4, normed, qkv, attended, branch, middle, n2, active, slope, mixed))
        tokens = result
    fo_rows = stem_all[:, STEM_AT[5] : STEM_AT[5] + PATCH_DIM].T
    grad, grad_fin, grad_out_w, loss_rows = final_step(tokens, fin_mods, fo_rows, target_noise.T)

    stem_cols = stem_weights.shape[1]
    lin_cols = layer_in.shape[2]

    def outer(left_in, right_in):
        return lax.dot_general(left_in, right_in, (((0,), (0,)), ((), ())), preferred_element_type=f32)

    def flip(values):
        return jnp.swapaxes(values, -1, -2)

    states = (experts, experts_first, experts_second, lin_t, flip(layer_in_first[0]), flip(layer_in_second[0]))
    states = states + (layer_out, layer_out_first, layer_out_second)
    grad_mods, reduced, outgoing = [None] * LAYERS, [None] * LAYERS, [None] * LAYERS
    for layer in reversed(range(LAYERS)):
        tokens, g4, normed, qkv, attended, branch, middle, n2, active, slope, mixed = saved[layer]
        early = () if outgoing[1] is None else (outgoing[1][0].reshape((-1, halves) + pairs[0].shape),)
        dup, ddn, dex, gn2, grad_gate, *begun = ffn_backward(
            layer, grad, n2, mods[layer], g4, mixed, active, slope, lin_all, lout_all[layer], expert_all[layer], halves, early
        )
        grad, grad_mods[layer], dqkvo = attn_backward(
            layer, gn2, grad, middle, tokens, normed, qkv, attended, branch, mods[layer], grad_gate, lin_all,
            halves * lin_cols,
        )
        outgoing[layer] = (dex, dqkvo, dup, ddn)
    grad_patch = product_tn(patches, to_half(grad))
    dpre_one, dpre_two = cond_backward(grad_mods[0], grad_mods[1], grad_fin, pre_one, pre_two, stem_all, lin_all)

    names = jnp.stack([labels // 32, labels % 32], axis=1).astype(f32)
    factors = jnp.concatenate(
        [cond[:items], grad_mods[0][:items], grad_mods[1][:items], hidden[:items], dpre_one[:items], dpre_two[:items]]
        + [grad_fin[:items], feat, jnp.pad(names, ((0, 0), (0, 126)))],
        axis=1,
    ).astype(bf16)
    width = factors.shape[1]
    ends = jnp.concatenate([grad_patch, grad_out_w], axis=0).astype(bf16)
    packed = jnp.concatenate([factors.reshape(-1), ends.reshape(-1)])
    lanes = -(-packed.size // (16 * 128)) * 128
    packed = jnp.pad(packed, (0, 16 * lanes - packed.size)).reshape(16, lanes)
    loss = jnp.pad(loss_rows.reshape(1, PATCH_DIM), ((0, 7), (0, 128 - PATCH_DIM)))
    gathered, loss_all = exchange_small(packed, loss)
    loss_total = jnp.sum(loss_all)
    gathered = gathered.reshape(sharers, -1)
    factors = gathered[:, : items * width].reshape(sharers * items, width)
    ends = gathered[:, items * width : items * width + 2 * PATCH_DIM * D].reshape(sharers, 2, PATCH_DIM, D)
    ends = jnp.sum(ends.astype(f32), axis=0)
    cond_f, gm_a, gm_b, hidden_f, done_f, dtwo_f, fin_f, feat_f, names = jnp.split(
        factors, [D, 7 * D, 13 * D, 14 * D, 15 * D, 16 * D, 18 * D, 18 * D + FREQ], axis=1
    )
    hot_all = label_table((names[:, 0].astype(f32) * 32 + names[:, 1].astype(f32)).astype(jnp.int32)).astype(bf16)
    def own(values):
        return lax.dynamic_slice_in_dim(values, place * stem_cols, stem_cols, axis=1)

    stem_grad = jnp.concatenate(
        [
            own(ends[0]).T,
            outer(own(done_f), feat_f),
            outer(own(dtwo_f), hidden_f),
            outer(own(dtwo_f), hot_all),
            outer(own(cond_f), fin_f),
            own(ends[1]).T,
        ],
        axis=1,
    )
    stem_stepped = adam_step(stem_t, stem_grad, stem_first[0].T, stem_second[0].T)
    stem_delta = jnp.pad(to_half(stem_stepped[0]), ((0, 0), (0, -stem_t.shape[1] % 128)))
    for layer, gm in ((1, gm_b), (0, gm_a)):
        spread = jnp.pad(gm, ((0, 0), (4 * D, lin_cols * sharers - 10 * D)))
        window = lax.dynamic_slice_in_dim(spread, place * lin_cols, lin_cols, axis=1)
        dex, dqkvo, dup, ddn = outgoing[layer]
        reduced[layer] = reduce_layer(
            layer,
            dex.reshape((-1, halves) + dex.shape[1:]),
            dqkvo.reshape(halves, lin_cols, D),
            dup.reshape(-1, halves, lin_cols, D),
            ddn.reshape(-1, halves, layer_out.shape[1], D),
            outer(window, cond_f),
            states,
            stem_delta if layer == 1 else None,
            begun if layer == 1 else (),
        )
    stem_total = reduced[1][6]
    group_count = lax.axis_size(GROUP)

    mean_delta = stem_total[:, : stem_t.shape[1]] / group_count
    moment_new = outer_mom * stem_moment.T + mean_delta
    new_weight = stem_t - outer_rate * (mean_delta + outer_mom * moment_new)
    stem_out = [flip(v) for v in (new_weight, to_half(new_weight), stem_stepped[1][None], stem_stepped[2][None], moment_new)]

    def both(at, rows, tile, weight, first, second, moment):
        grads = [reduced[layer][at].reshape(rows, -1) for layer in range(LAYERS)]
        totals = [reduced[layer][3 + at].reshape(rows, -1) for layer in range(LAYERS)]
        shaped = [v.reshape(LAYERS, rows, -1) for v in (weight, first, second, moment)]
        return update_arrays(tile, grads, totals, *shaped)

    lin_out = both(1, lin_cols, 432, lin_t, flip(layer_in_first), flip(layer_in_second), flip(layer_in_moment))
    lin_out = [flip(v.reshape((1,) * (at in (2, 3)) + v.shape)) for at, v in enumerate(lin_out)]
    lout_rows = layer_out.shape[1]
    lout_out = both(2, lout_rows, lout_rows // 2, layer_out, layer_out_first, layer_out_second, layer_out_moment)
    lout_out = [v.reshape((1,) * (at in (2, 3)) + v.shape) for at, v in enumerate(lout_out)]
    expert_out = both(0, 2 * D, D // 2, experts, experts_first, experts_second, experts_moment)
    likes = (experts, experts, experts_first, experts_second, experts)
    expert_out = [v.reshape(like.shape) for v, like in zip(expert_out, likes)]
    results = []
    for at in range(5):
        results += [stem_out[at], lin_out[at], lout_out[at], expert_out[at]]
    return (loss_total, *results)


def solution(mesh):
    placed = (
        P((GROUP, LINE, CORE), None),
        P((GROUP, LINE, CORE), None),
        P((GROUP, LINE, CORE)),
        P((GROUP, LINE, CORE)),
        P(None, (GROUP, LINE, CORE), None),
        P(None, (GROUP, LINE, CORE), None),
        P(None, (LINE, CORE)),
        P(None, None, (LINE, CORE)),
        P(None, (LINE, CORE), None),
        P(None, LINE, None, None, CORE),
        P(GROUP, None, (LINE, CORE)),
        P(GROUP, None, None, (LINE, CORE)),
        P(GROUP, None, (LINE, CORE), None),
        P(GROUP, None, LINE, None, None, CORE),
        P(GROUP, None, (LINE, CORE)),
        P(GROUP, None, None, (LINE, CORE)),
        P(GROUP, None, (LINE, CORE), None),
        P(GROUP, None, LINE, None, None, CORE),
        P(None, (LINE, CORE)),
        P(None, None, (LINE, CORE)),
        P(None, (LINE, CORE), None),
        P(None, LINE, None, None, CORE),
    )
    step = few_experts if mesh.shape[LINE] <= 4 else per_device
    return jax.shard_map(
        step,
        mesh=mesh,
        in_specs=placed,
        out_specs=(
            P(),
            P(None, (LINE, CORE)),
            P(None, None, (LINE, CORE)),
            P(None, (LINE, CORE), None),
            P(None, LINE, None, None, CORE),
            P(None, (LINE, CORE)),
            P(None, None, (LINE, CORE)),
            P(None, (LINE, CORE), None),
            P(None, LINE, None, None, CORE),
            P(GROUP, None, (LINE, CORE)),
            P(GROUP, None, None, (LINE, CORE)),
            P(GROUP, None, (LINE, CORE), None),
            P(GROUP, None, LINE, None, None, CORE),
            P(GROUP, None, (LINE, CORE)),
            P(GROUP, None, None, (LINE, CORE)),
            P(GROUP, None, (LINE, CORE), None),
            P(GROUP, None, LINE, None, None, CORE),
            P(None, (LINE, CORE)),
            P(None, None, (LINE, CORE)),
            P(None, (LINE, CORE), None),
            P(None, LINE, None, None, CORE),
        ),
        check_vma=False,
    )
```

```python
import functools

import jax
import jax.numpy as jnp
from jax import lax
from jax.experimental import pallas as pl
from jax.experimental.pallas import tpu as pltpu
from jax.sharding import PartitionSpec as P

GROUP, LINE, CORE = "group", "expert", "dp"
D = 384
HEADS = 6
IMG = 32
FREQ = 256
CLASSES = 1000
LAYERS = 2
STEP = 10
PATCH_DIM = 16
PATCHES = 256


highest = lax.Precision.HIGHEST
beta_one = 0.9
beta_two = 0.95
eps_adam = 1e-08
inner_rate = 0.03
weight_decay = 0.05
outer_rate = 0.7
outer_mom = 0.9
ln_eps = 1e-06


def to_half(values):
    return values.astype(jnp.bfloat16)


def product(left_in, right_in):
    return jnp.dot(left_in, right_in, preferred_element_type=jnp.float32)


def product_tn(left_in, right_in):
    return lax.dot_general(
        left_in, right_in, (((0,), (0,)), ((), ())), preferred_element_type=jnp.float32
    )


def product_nt(left_in, right_in):
    return lax.dot_general(
        left_in, right_in, (((1,), (1,)), ((), ())), preferred_element_type=jnp.float32
    )


def gelu_tanh(values):
    return jax.nn.gelu(values, approximate=True)


def gelu_back(values, gradient):
    _, pull = jax.vjp(gelu_tanh, values)
    return pull(gradient)[0]


def norm_mod(values, shift_in, scale_in):
    centre = values - jnp.mean(values, axis=-1, keepdims=True)
    spread = jnp.mean(centre * centre, axis=-1, keepdims=True)
    return centre * lax.rsqrt(spread + ln_eps) * (1.0 + scale_in) + shift_in


def positions_table():
    grid_side = IMG // 2
    quarter = D // 4
    omegas = 1.0 / 10000.0 ** (jnp.arange(quarter, dtype=jnp.float32) / quarter)
    index_all = jnp.arange(PATCHES, dtype=jnp.int32)
    row_angle = (index_all // grid_side).astype(jnp.float32)[:, None] * omegas[None, :]
    col_angle = (index_all % grid_side).astype(jnp.float32)[:, None] * omegas[None, :]
    return jnp.concatenate(
        [jnp.sin(row_angle), jnp.cos(row_angle), jnp.sin(col_angle), jnp.cos(col_angle)], axis=1
    )


def time_features(step_ids):
    half_freq = FREQ // 2
    frequency = jnp.exp(-jnp.log(10000.0) * jnp.arange(half_freq, dtype=jnp.float32) / half_freq)
    angles = step_ids.astype(jnp.float32)[:, None] * frequency[None, :]
    return jnp.concatenate([jnp.cos(angles), jnp.sin(angles)], axis=1)


def label_table(label_ids):
    return (label_ids[:, None] == jnp.arange(CLASSES + 1, dtype=jnp.int32)[None, :]).astype(
        jnp.float32
    )


def split_stem(stem_all):
    end_patch = PATCH_DIM
    end_time = end_patch + FREQ
    end_second = end_time + D
    end_table = end_second + CLASSES + 1
    end_ada = end_table + 2 * D
    return (
        stem_all[:end_patch],
        stem_all[end_patch:end_time],
        stem_all[end_time:end_second],
        stem_all[end_second:end_table],
        stem_all[end_table:end_ada],
        stem_all[end_ada:],
    )


def slot_places(route_ids, expert_count, capacity):
    flat_ids = route_ids.reshape(-1)
    one_hot_ids = (flat_ids[:, None] == jnp.arange(expert_count, dtype=jnp.int32)[None, :]).astype(
        jnp.int32
    )
    rank_in = jnp.sum((jnp.cumsum(one_hot_ids, axis=0) - one_hot_ids) * one_hot_ids, axis=1)
    return flat_ids * capacity + rank_in


def expert_major(received, local_count):
    sources = received.shape[0] // local_count
    shaped = received.reshape(sources, local_count, received.shape[1], received.shape[2])
    return jnp.swapaxes(shaped, 0, 1).reshape(local_count, -1, received.shape[2])


def source_major(rows_in, sources):
    local_count = rows_in.shape[0]
    shaped = rows_in.reshape(local_count, sources, -1, rows_in.shape[2])
    return jnp.swapaxes(shaped, 0, 1).reshape(sources * local_count, -1, rows_in.shape[2])


def attention_split(qkv, item_count):
    head_dim = qkv.shape[1] // (3 * HEADS)
    shaped = qkv.reshape(item_count, -1, 3, HEADS, head_dim)
    return (shaped[:, :, 0], shaped[:, :, 1], shaped[:, :, 2], head_dim ** (-0.5))


def attention_forward(qkv, item_count):
    queries, keys_in, values_in, scale_att = attention_split(qkv, item_count)
    scores = (
        jnp.einsum("bqhd,bkhd->bhqk", queries, keys_in, preferred_element_type=jnp.float32)
        * scale_att
    )
    row_max = jnp.max(scores, axis=-1, keepdims=True)
    log_sums = row_max + jnp.log(jnp.sum(jnp.exp(scores - row_max), axis=-1, keepdims=True))
    attn_probs = to_half(jnp.exp(scores - log_sums))
    attended = jnp.einsum(
        "bhqk,bkhd->bqhd", attn_probs, values_in, preferred_element_type=jnp.float32
    )
    return (to_half(attended.reshape(qkv.shape[0], -1)), log_sums)


def attention_backward(qkv, log_sums, grad_attended, item_count):
    queries, keys_in, values_in, scale_att = attention_split(qkv, item_count)
    scores = (
        jnp.einsum("bqhd,bkhd->bhqk", queries, keys_in, preferred_element_type=jnp.float32)
        * scale_att
    )
    probs_full = jnp.exp(scores - log_sums)
    grad_out = grad_attended.reshape(queries.shape)
    grad_values = jnp.einsum(
        "bhqk,bqhd->bkhd", to_half(probs_full), grad_out, preferred_element_type=jnp.float32
    )
    grad_probs = jnp.einsum(
        "bqhd,bkhd->bhqk", grad_out, values_in, preferred_element_type=jnp.float32
    )
    grad_scores = probs_full * (
        grad_probs - jnp.sum(probs_full * grad_probs, axis=-1, keepdims=True)
    )
    grad_half = to_half(grad_scores)
    grad_queries = (
        jnp.einsum("bhqk,bkhd->bqhd", grad_half, keys_in, preferred_element_type=jnp.float32)
        * scale_att
    )
    grad_keys = (
        jnp.einsum("bhqk,bqhd->bkhd", grad_half, queries, preferred_element_type=jnp.float32)
        * scale_att
    )
    stacked = jnp.stack([grad_queries, grad_keys, grad_values], axis=2)
    return to_half(stacked.reshape(qkv.shape[0], -1))


def layer_forward(tokens, cond_act, lin, lout, expert_w, route_ids, gate_vals):
    item_count = cond_act.shape[0]
    model_width = tokens.shape[1]
    local_count = expert_w.shape[0]
    expert_count = lax.axis_size(LINE) * local_count
    capacity = 4 * tokens.shape[0] // expert_count
    mods = jnp.dot(
        cond_act, lin[:, 4 * model_width : 10 * model_width].astype(jnp.float32), precision=highest
    )
    mods = mods.reshape(item_count, 6, 1, model_width)
    shaped = tokens.reshape(item_count, -1, model_width)
    normed = to_half(norm_mod(shaped, mods[:, 0], mods[:, 1]).reshape(-1, model_width))
    qkv = to_half(product(normed, lin[:, : 3 * model_width]))
    attended, log_sums = attention_forward(qkv, item_count)
    branch = product(attended, lin[:, 3 * model_width : 4 * model_width])
    middle = shaped + mods[:, 2] * branch.reshape(item_count, -1, model_width)
    normed_two = to_half(norm_mod(middle, mods[:, 3], mods[:, 4]).reshape(-1, model_width))
    inner_pre = product(normed_two, lin[:, 10 * model_width :])
    active = to_half(gelu_tanh(inner_pre))
    shared = product(active, lout)
    slot_index = slot_places(route_ids, expert_count, capacity)
    send_rows = jnp.zeros((expert_count * capacity, model_width), jnp.bfloat16)
    send_rows = send_rows.at[slot_index].set(jnp.repeat(normed_two, 2, axis=0))
    received = lax.all_to_all(
        send_rows.reshape(expert_count, capacity, model_width),
        LINE,
        split_axis=0,
        concat_axis=0,
        tiled=True,
    )
    rows_exp = expert_major(received, local_count)
    inner_exp = jnp.einsum(
        "erd,edf->erf", rows_exp, expert_w[:, 0], preferred_element_type=jnp.float32
    )
    active_exp = to_half(gelu_tanh(inner_exp))
    out_exp = to_half(
        jnp.einsum("erf,edf->erd", active_exp, expert_w[:, 1], preferred_element_type=jnp.float32)
    )
    returned = lax.all_to_all(
        source_major(out_exp, lax.axis_size(LINE)),
        LINE,
        split_axis=0,
        concat_axis=0,
        tiled=True,
    )
    picked = (
        returned.reshape(-1, model_width)[slot_index]
        .astype(jnp.float32)
        .reshape(-1, 2, model_width)
    )
    mixed_out = shared + jnp.sum(gate_vals[:, :, None] * picked, axis=1)
    result = middle + mods[:, 5] * mixed_out.reshape(item_count, -1, model_width)
    saved = (
        tokens,
        mods,
        normed,
        qkv,
        attended,
        log_sums,
        branch,
        middle,
        normed_two,
        inner_pre,
        active,
        mixed_out,
        slot_index,
        rows_exp,
        inner_exp,
        active_exp,
    )
    return (result.reshape(-1, model_width), saved)


def layer_backward(grad_tokens, saved, cond_act, lin, lout, expert_w, gate_vals):
    (
        tokens,
        mods,
        normed,
        qkv,
        attended,
        log_sums,
        branch,
        middle,
        normed_two,
        inner_pre,
        active,
        mixed_out,
        slot_index,
        rows_exp,
        inner_exp,
        active_exp,
    ) = saved
    item_count = cond_act.shape[0]
    model_width = tokens.shape[1]
    local_count = expert_w.shape[0]
    expert_count = lax.axis_size(LINE) * local_count
    capacity = 4 * tokens.shape[0] // expert_count
    grad_shaped = grad_tokens.reshape(item_count, -1, model_width)
    grad_gate_two = jnp.sum(
        grad_shaped * mixed_out.reshape(item_count, -1, model_width), axis=1, keepdims=True
    )
    grad_mixed = (mods[:, 5] * grad_shaped).reshape(-1, model_width)
    grad_shared = to_half(grad_mixed)
    grad_lout = product_tn(active, grad_shared)
    grad_inner = to_half(gelu_back(inner_pre, product_nt(grad_shared, lout)))
    grad_w_up = product_tn(normed_two, grad_inner)
    grad_normed_two = product_nt(grad_inner, lin[:, 10 * model_width :])
    routed_grad = to_half(gate_vals[:, :, None] * grad_mixed[:, None, :]).reshape(-1, model_width)
    send_grad = (
        jnp.zeros((expert_count * capacity, model_width), jnp.bfloat16)
        .at[slot_index]
        .set(routed_grad)
    )
    received = lax.all_to_all(
        send_grad.reshape(expert_count, capacity, model_width),
        LINE,
        split_axis=0,
        concat_axis=0,
        tiled=True,
    )
    grad_rows = expert_major(received, local_count)
    grad_down_exp = jnp.einsum(
        "erd,erf->edf", grad_rows, active_exp, preferred_element_type=jnp.float32
    )
    grad_active_exp = jnp.einsum(
        "erd,edf->erf", grad_rows, expert_w[:, 1], preferred_element_type=jnp.float32
    )
    grad_inner_exp = to_half(gelu_back(inner_exp, grad_active_exp))
    grad_up_exp = jnp.einsum(
        "erd,erf->edf", rows_exp, grad_inner_exp, preferred_element_type=jnp.float32
    )
    grad_rows_in = to_half(
        jnp.einsum(
            "erf,edf->erd", grad_inner_exp, expert_w[:, 0], preferred_element_type=jnp.float32
        )
    )
    back_rows = lax.all_to_all(
        source_major(grad_rows_in, lax.axis_size(LINE)),
        LINE,
        split_axis=0,
        concat_axis=0,
        tiled=True,
    )
    picked = (
        back_rows.reshape(-1, model_width)[slot_index]
        .astype(jnp.float32)
        .reshape(-1, 2, model_width)
    )
    grad_normed_two = grad_normed_two + jnp.sum(picked, axis=1)
    _, second_back = jax.vjp(norm_mod, middle, mods[:, 3], mods[:, 4])
    grad_middle, grad_shift_two, grad_scale_two = second_back(
        grad_normed_two.reshape(item_count, -1, model_width)
    )
    grad_middle = grad_middle + grad_shaped
    grad_gate_one = jnp.sum(
        grad_middle * branch.reshape(item_count, -1, model_width), axis=1, keepdims=True
    )
    grad_branch = to_half((mods[:, 2] * grad_middle).reshape(-1, model_width))
    grad_w_out = product_tn(attended, grad_branch)
    grad_attended = to_half(product_nt(grad_branch, lin[:, 3 * model_width : 4 * model_width]))
    grad_qkv = attention_backward(qkv, log_sums, grad_attended, item_count)
    grad_w_qkv = product_tn(normed, grad_qkv)
    grad_normed = product_nt(grad_qkv, lin[:, : 3 * model_width])
    _, first_back = jax.vjp(
        norm_mod, tokens.reshape(item_count, -1, model_width), mods[:, 0], mods[:, 1]
    )
    grad_input, grad_shift_one, grad_scale_one = first_back(
        grad_normed.reshape(item_count, -1, model_width)
    )
    grad_input = grad_input + grad_middle
    grad_mods = jnp.stack(
        [
            grad_shift_one,
            grad_scale_one,
            grad_gate_one,
            grad_shift_two,
            grad_scale_two,
            grad_gate_two,
        ],
        axis=1,
    )
    grad_mods = grad_mods.reshape(item_count, 6 * model_width)
    grad_ada = jnp.dot(cond_act.T, grad_mods, precision=highest)
    grad_cond = jnp.dot(
        grad_mods,
        lin[:, 4 * model_width : 10 * model_width].astype(jnp.float32).T,
        precision=highest,
    )
    grad_lin = jnp.concatenate([grad_w_qkv, grad_w_out, grad_ada, grad_w_up], axis=1)
    grad_expert = jnp.stack([grad_up_exp, grad_down_exp], axis=1)
    return (grad_input.reshape(-1, model_width), grad_cond, grad_lin, grad_lout, grad_expert)


def adam_step(weight_in, gradient, first_in, second_in):
    first_new = beta_one * first_in + (1.0 - beta_one) * gradient
    second_new = beta_two * second_in + (1.0 - beta_two) * gradient * gradient
    first_hat = first_new / (1.0 - beta_one**STEP)
    second_hat = second_new / (1.0 - beta_two**STEP)
    stepped = weight_in - inner_rate * (
        first_hat / (jnp.sqrt(second_hat) + eps_adam) + weight_decay * weight_in
    )
    return (weight_in - stepped, first_new, second_new)


def per_device(
    patches,
    target_noise,
    timesteps,
    labels,
    routes,
    route_gates,
    stem_weights,
    layer_in,
    layer_out,
    experts,
    stem_first,
    layer_in_first,
    layer_out_first,
    experts_first,
    stem_second,
    layer_in_second,
    layer_out_second,
    experts_second,
    stem_moment,
    layer_in_moment,
    layer_out_moment,
    experts_moment,
):
    stem_all, lin_all, lout_all = (
        lax.all_gather(to_half(stem_weights), (LINE, CORE), axis=1, tiled=True),
        lax.all_gather(to_half(layer_in), (LINE, CORE), axis=2, tiled=True),
        lax.all_gather(to_half(layer_out), (LINE, CORE), axis=1, tiled=True),
    )
    expert_all = lax.all_gather(to_half(experts), CORE, axis=4, tiled=True)
    model_width = stem_all.shape[1]
    item_count = timesteps.shape[0]
    patch_w, time_one, time_two, table_w, final_ada, final_out = split_stem(stem_all)
    features = time_features(timesteps)
    hot_labels = label_table(labels)

    def condition(first_w, second_w, table_in):
        hidden_time = jax.nn.silu(jnp.dot(features, first_w, precision=highest))
        return jax.nn.silu(
            jnp.dot(hidden_time, second_w, precision=highest)
            + jnp.dot(hot_labels, table_in, precision=highest)
        )

    cond_act, cond_back = jax.vjp(
        condition,
        time_one.astype(jnp.float32),
        time_two.astype(jnp.float32),
        table_w.astype(jnp.float32),
    )
    tokens = product(patches, patch_w)
    tokens = (tokens.reshape(item_count, -1, model_width) + positions_table()[None]).reshape(
        -1, model_width
    )
    saved_all = []
    for layer_idx in range(LAYERS):
        tokens, saved = layer_forward(
            tokens,
            cond_act,
            lin_all[layer_idx],
            lout_all[layer_idx],
            expert_all[layer_idx],
            routes[layer_idx],
            route_gates[layer_idx],
        )
        saved_all.append(saved)
    final_ada_f = final_ada.astype(jnp.float32)
    final_mods = jnp.dot(cond_act, final_ada_f.T, precision=highest).reshape(
        item_count, 2, 1, model_width
    )
    final_pre, final_back = jax.vjp(
        norm_mod, tokens.reshape(item_count, -1, model_width), final_mods[:, 0], final_mods[:, 1]
    )
    final_normed = to_half(final_pre.reshape(-1, model_width))
    predicted = product_nt(final_normed, final_out)
    residual_err = predicted - target_noise
    loss_total = lax.psum(jnp.sum(residual_err * residual_err), (GROUP, LINE, CORE))
    grad_pred = to_half(2.0 * residual_err)
    grad_final_out = product_tn(grad_pred, final_normed)
    grad_final_normed = product(grad_pred, final_out)
    grad_tokens, grad_fshift, grad_fscale = final_back(
        grad_final_normed.reshape(item_count, -1, model_width)
    )
    grad_tokens = grad_tokens.reshape(-1, model_width)
    grad_final_mods = jnp.concatenate([grad_fshift, grad_fscale], axis=1).reshape(
        item_count, 2 * model_width
    )
    grad_final_ada = jnp.dot(grad_final_mods.T, cond_act, precision=highest)
    grad_cond = jnp.dot(grad_final_mods, final_ada_f, precision=highest)
    lin_grads = []
    lout_grads = []
    expert_grads = []
    for layer_idx in reversed(range(LAYERS)):
        grad_tokens, grad_cond_layer, grad_lin, grad_lout, grad_expert = layer_backward(
            grad_tokens,
            saved_all[layer_idx],
            cond_act,
            lin_all[layer_idx],
            lout_all[layer_idx],
            expert_all[layer_idx],
            route_gates[layer_idx],
        )
        grad_cond = grad_cond + grad_cond_layer
        lin_grads.append(grad_lin)
        lout_grads.append(grad_lout)
        expert_grads.append(grad_expert)
    lin_stack = jnp.stack(lin_grads[::-1])
    lout_stack = jnp.stack(lout_grads[::-1])
    expert_stack = jnp.stack(expert_grads[::-1])
    grad_patch = product_tn(patches, to_half(grad_tokens))
    grad_time_one, grad_time_two, grad_table = cond_back(grad_cond)
    grad_stem = jnp.concatenate(
        [grad_patch, grad_time_one, grad_time_two, grad_table, grad_final_ada, grad_final_out],
        axis=0,
    )
    stem_sum, lin_sum, lout_sum = (
        lax.psum_scatter(grad_stem, (LINE, CORE), scatter_dimension=1, tiled=True),
        lax.psum_scatter(lin_stack, (LINE, CORE), scatter_dimension=2, tiled=True),
        lax.psum_scatter(lout_stack, (LINE, CORE), scatter_dimension=1, tiled=True),
    )
    expert_sum = lax.psum_scatter(
        expert_stack.astype(jnp.bfloat16), CORE, scatter_dimension=4, tiled=True
    ).astype(jnp.float32)
    weights_all = (stem_weights, layer_in, layer_out, experts)
    gradients = (stem_sum, lin_sum, lout_sum, expert_sum)
    firsts = (stem_first, layer_in_first, layer_out_first, experts_first)
    seconds = (stem_second, layer_in_second, layer_out_second, experts_second)
    moments = (stem_moment, layer_in_moment, layer_out_moment, experts_moment)
    stepped = [
        adam_step(
            weights_all[array_idx],
            gradients[array_idx],
            firsts[array_idx][0],
            seconds[array_idx][0],
        )
        for array_idx in range(4)
    ]
    delta_all = (
        lax.psum(stepped[0][0].astype(jnp.bfloat16), GROUP).astype(jnp.float32),
        lax.psum(stepped[1][0].astype(jnp.bfloat16), GROUP).astype(jnp.float32),
        lax.psum(stepped[2][0].astype(jnp.bfloat16), GROUP).astype(jnp.float32),
        lax.psum(stepped[3][0].astype(jnp.bfloat16), GROUP).astype(jnp.float32),
    )
    group_count = lax.axis_size(GROUP)
    new_weights = []
    new_moments = []
    for array_idx in range(4):
        mean_delta = delta_all[array_idx] / group_count
        moment_new = outer_mom * moments[array_idx] + mean_delta
        new_weights.append(
            weights_all[array_idx] - outer_rate * (mean_delta + outer_mom * moment_new)
        )
        new_moments.append(moment_new)
    return (
        loss_total,
        new_weights[0],
        new_weights[1],
        new_weights[2],
        new_weights[3],
        to_half(new_weights[0]),
        to_half(new_weights[1]),
        to_half(new_weights[2]),
        to_half(new_weights[3]),
        stepped[0][1][None],
        stepped[1][1][None],
        stepped[2][1][None],
        stepped[3][1][None],
        stepped[0][2][None],
        stepped[1][2][None],
        stepped[2][2][None],
        stepped[3][2][None],
        new_moments[0],
        new_moments[1],
        new_moments[2],
        new_moments[3],
    )


bf16 = jnp.bfloat16
f32 = jnp.float32
MIB = 1024 * 1024
CHUNK = 768
FWD_ROWS = 256
BWD_ROWS = 256
STEM_SIZES = (PATCH_DIM, FREQ, D, CLASSES + 1, 2 * D, PATCH_DIM)
STEM_PADDED = tuple(-(-size // 128) * 128 for size in STEM_SIZES)
STEM_AT = tuple(sum(STEM_PADDED[:place]) for place in range(len(STEM_PADDED)))
STEM_LANES = -(-sum(STEM_PADDED) // 1024) * 1024


def dot_nn(left_in, right_in):
    return lax.dot_general(left_in, right_in, (((1,), (0,)), ((), ())), preferred_element_type=f32)


def dot_nt(left_in, right_in):
    return lax.dot_general(left_in, right_in, (((1,), (1,)), ((), ())), preferred_element_type=f32)


def dot_tn(left_in, right_in):
    return lax.dot_general(left_in, right_in, (((0,), (0,)), ((), ())), preferred_element_type=f32)


def three_parts(rows):
    high = rows.astype(bf16).astype(f32)
    rest = rows - high
    mid = rest.astype(bf16).astype(f32)
    low = rest - mid
    return jnp.concatenate([high, mid, low, jnp.zeros_like(low)], axis=0).astype(bf16)


def three_sum(stacked):
    return stacked[0:8] + stacked[8:16] + stacked[16:24]


def full_nt(rows, weight):
    return three_sum(dot_nt(three_parts(rows), weight))


def full_nn(rows, weight):
    return three_sum(dot_nn(three_parts(rows), weight))


def silu_slope(values):
    gate = 1.0 / (1.0 + jnp.exp(-values))
    return gate * (1.0 + values * (1.0 - gate))


def silu_of(values):
    return values / (1.0 + jnp.exp(-values))


def stem_piece(stem_ref, place):
    return stem_ref[:, STEM_AT[place] : STEM_AT[place] + STEM_PADDED[place]]


def cond_kernel(feat_ref, hot_ref, stem_ref, ada_ref, cond_ref, hid_ref, one_ref, two_ref, mods_ref, fin_ref):
    @pl.when(pl.program_id(0) == 0)
    def _():
        pre_one = full_nt(feat_ref[...], stem_piece(stem_ref, 1))
        hidden = silu_of(pre_one)
        pre_two = full_nt(hidden, stem_piece(stem_ref, 2)) + dot_nt(hot_ref[...], stem_piece(stem_ref, 3))[0:8]
        cond = silu_of(pre_two)
        one_ref[...] = pre_one
        two_ref[...] = pre_two
        hid_ref[...] = hidden
        cond_ref[...] = cond
        fin_ref[...] = full_nn(cond, stem_piece(stem_ref, 4))

    for layer in range(LAYERS):
        mods_ref[layer] = full_nt(cond_ref[...], ada_ref[layer])


def cond_back_kernel(gm_a, gm_b, gf_ref, one_ref, two_ref, stem_ref, ada_ref, done_ref, dtwo_ref):
    @pl.when(pl.program_id(0) == 0)
    def _():
        dtwo_ref[...] = full_nt(gf_ref[...], stem_piece(stem_ref, 4))

    dtwo_ref[...] += full_nn(gm_a[...], ada_ref[0]) + full_nn(gm_b[...], ada_ref[1])

    @pl.when(pl.program_id(0) == pl.num_programs(0) - 1)
    def _():
        dtwo = dtwo_ref[...] * silu_slope(two_ref[...])
        dtwo_ref[...] = dtwo
        done_ref[...] = full_nn(dtwo, stem_piece(stem_ref, 2)) * silu_slope(one_ref[...])


def norm_parts(values):
    centre = values - jnp.mean(values, axis=-1, keepdims=True)
    spread = jnp.mean(centre * centre, axis=-1, keepdims=True)
    root = lax.rsqrt(spread + ln_eps)
    return centre * root, root


def norm_back(values, scale_in, gradient):
    unit, root = norm_parts(values)
    grad_unit = gradient * (1.0 + scale_in)
    inner = jnp.mean(grad_unit * unit, axis=-1, keepdims=True)
    grad_in = root * (grad_unit - jnp.mean(grad_unit, axis=-1, keepdims=True) - unit * inner)
    return (
        grad_in,
        jnp.sum(gradient, axis=0, keepdims=True),
        jnp.sum(gradient * unit, axis=0, keepdims=True),
    )


def mod_row(mods_ref, item, place):
    return mods_ref[pl.ds(item, 1), place * D : (place + 1) * D]


def head_masks():
    lane = lax.broadcasted_iota(jnp.int32, (1, 128), 1)
    return lane, [(lane // 64 == half).astype(f32).astype(bf16) for half in range(2)]


def attn_fwd_kernel(x_ref, mods_ref, w_ref, normed_ref, qkv_ref, att_ref, branch_ref, mid_ref, n2_ref):
    item = pl.program_id(0)
    tokens = x_ref[...]
    unit, _ = norm_parts(tokens)
    normed = (unit * (1.0 + mod_row(mods_ref, item, 1)) + mod_row(mods_ref, item, 0)).astype(bf16)
    normed_ref[...] = normed
    qkv_ref[...] = dot_nt(normed, w_ref[0 : 3 * D, :]).astype(bf16)
    lane, masks = head_masks()
    heads = [(pair, half) for pair in range(HEADS // 2) for half in range(2)]

    def part(place, pair):
        return qkv_ref[:, place * D + pair * 128 : place * D + pair * 128 + 128]

    all_scores = [dot_nt(part(0, pair) * (masks[half] * jnp.asarray(0.125, bf16)), part(1, pair)) for pair, half in heads]
    powers = [jnp.exp(scores - jnp.max(scores, axis=-1, keepdims=True)) for scores in all_scores]
    probs = [(power * (1.0 / jnp.sum(power, axis=-1, keepdims=True))).astype(bf16) for power in powers]
    outs = [dot_nn(prob, part(2, pair)) for prob, (pair, _) in zip(probs, heads)]
    for pair in range(HEADS // 2):
        att_ref[:, pair * 128 : pair * 128 + 128] = jnp.where(lane < 64, outs[2 * pair], outs[2 * pair + 1]).astype(bf16)
    branch = dot_nt(att_ref[...], w_ref[3 * D : 4 * D, :])
    branch_ref[...] = branch
    middle = tokens + mod_row(mods_ref, item, 2) * branch
    mid_ref[...] = middle
    unit, _ = norm_parts(middle)
    n2_ref[...] = (unit * (1.0 + mod_row(mods_ref, item, 4)) + mod_row(mods_ref, item, 3)).astype(bf16)


def attn_bwd_kernel(
    gn2_ref, g_ref, mid_ref, x_ref, normed_ref, qkv_ref, att_ref, branch_ref, mods_ref, gg_ref, w_ref,
    gx_ref, gmods_ref, dw_ref, dqkv, acc,
):
    item = pl.program_id(0)

    @pl.when(item == 0)
    def _():
        acc[...] = jnp.zeros_like(acc)
        gmods_ref[...] = jnp.zeros_like(gmods_ref)

    grad_mid, dshift, dscale = norm_back(mid_ref[...], mod_row(mods_ref, item, 4), gn2_ref[...])
    grad_mid = grad_mid + g_ref[...]
    dgate = jnp.sum(grad_mid * branch_ref[...], axis=0, keepdims=True)
    gmods_ref[pl.ds(item, 1), 2 * D : 3 * D] = dgate
    gmods_ref[pl.ds(item, 1), 3 * D : 4 * D] = dshift
    gmods_ref[pl.ds(item, 1), 4 * D : 5 * D] = dscale
    gmods_ref[pl.ds(item, 1), 5 * D : 6 * D] = gg_ref[pl.ds(item, 1), :]
    grad_branch = (mod_row(mods_ref, item, 2) * grad_mid).astype(bf16)
    acc[3 * D : 4 * D, :] += dot_tn(grad_branch, att_ref[...])
    grad_att = dot_nn(grad_branch, w_ref[3 * D : 4 * D, :]).astype(bf16)
    lane, masks = head_masks()
    heads = [(pair, half) for pair in range(HEADS // 2) for half in range(2)]

    def part(place, pair):
        return qkv_ref[:, place * D + pair * 128 : place * D + pair * 128 + 128]

    outs = [grad_att[:, pair * 128 : pair * 128 + 128] for pair in range(HEADS // 2)]
    all_scores = [dot_nt(part(0, pair) * (masks[half] * jnp.asarray(0.125, bf16)), part(1, pair)) for pair, half in heads]
    all_grads = [dot_nt(outs[pair] * masks[half], part(2, pair)) for pair, half in heads]
    powers = [jnp.exp(scores - jnp.max(scores, axis=-1, keepdims=True)) for scores in all_scores]
    probs = [power * (1.0 / jnp.sum(power, axis=-1, keepdims=True)) for power in powers]
    halved = [prob.astype(bf16) for prob in probs]
    grad_scores = [
        (prob * (grads - jnp.sum(prob * grads, axis=-1, keepdims=True))).astype(bf16)
        for prob, grads in zip(probs, all_grads)
    ]
    for pair in range(HEADS // 2):
        at = pair * 128
        two = (2 * pair, 2 * pair + 1)
        results = (
            [dot_nn(grad_scores[head], part(1, pair)) * 0.125 for head in two],
            [dot_tn(grad_scores[head], part(0, pair)) * 0.125 for head in two],
            [dot_tn(halved[head], outs[pair]) for head in two],
        )
        for place, (low, high) in enumerate(results):
            dqkv[:, place * D + at : place * D + at + 128] = jnp.where(lane < 64, low, high).astype(bf16)
    acc[0 : 3 * D, :] += dot_tn(dqkv[...], normed_ref[...])
    grad_normed = dot_nn(dqkv[...], w_ref[0 : 3 * D, :])
    grad_in, dshift, dscale = norm_back(x_ref[...], mod_row(mods_ref, item, 1), grad_normed)
    gx_ref[...] = grad_in + grad_mid
    gmods_ref[pl.ds(item, 1), 0:D] = dshift
    gmods_ref[pl.ds(item, 1), D : 2 * D] = dscale

    @pl.when(item == pl.num_programs(0) - 1)
    def _():
        dw_ref[0 : 4 * D, :] = acc[...].astype(bf16)
        dw_ref[4 * D :, :] = jnp.zeros_like(dw_ref[4 * D :, :])


def gelu_both(values):
    outer = 0.7978845608028654
    cubic = outer * 0.044715
    square = values * values
    angle = jnp.tanh(values * (square * cubic + outer))
    half = 0.5 * values
    above = 1.0 + angle
    slope = above * (half * (square * (3.0 * cubic) + outer) * (1.0 - angle) + 0.5)
    return (half * above).astype(bf16), slope.astype(bf16)


def gate_column(g4_ref, rows, expert):
    gates = g4_ref[rows, :]
    lane = lax.broadcasted_iota(jnp.int32, gates.shape, 1)
    return jnp.sum(jnp.where(lane == expert, gates, 0.0), axis=1, keepdims=True)


def ffn_fwd_kernel(shared_steps, halves, gathers, n2_ref, mid_ref, mods_ref, g4_ref, up_ref, dn_ref, ex_ref, *rest):
    step = pl.program_id(0)
    given, (act_ref, dg_ref, mixed_ref, x_ref) = rest[:gathers], rest[gathers : gathers + 4]
    taken, (acc, racc), sems = rest[gathers + 4 : 2 * gathers + 4], rest[2 * gathers + 4 : 2 * gathers + 6], rest[2 * gathers + 6 :]
    if gathers:
        gather_beside(step, pl.num_programs(0) - 1, given, taken, sems)
    items = n2_ref.shape[0] // PATCHES

    @pl.when(step == 0)
    def _():
        acc[...] = jnp.zeros_like(acc)
        racc[...] = jnp.zeros_like(racc)

    @pl.when(step < shared_steps)
    def _():
        blocks = [pl.ds(block * FWD_ROWS, FWD_ROWS) for block in range(n2_ref.shape[0] // FWD_ROWS)]
        inners = [dot_nt(n2_ref[rows, :], up_ref[...]) for rows in blocks]
        for inner, rows in zip(inners, blocks):
            active, slope = gelu_both(inner)
            act_ref[0, rows, :] = active
            dg_ref[0, rows, :] = slope
            acc[rows, :] += dot_nn(active, dn_ref[...])

    @pl.when(step >= shared_steps)
    def _():
        blocks = [pl.ds(block * FWD_ROWS, FWD_ROWS) for block in range(n2_ref.shape[0] // FWD_ROWS)]
        inners = [dot_nn(n2_ref[rows, :], ex_ref[0, 0]) for rows in blocks]
        for inner, rows in zip(inners, blocks):
            active, slope = gelu_both(inner)
            act_ref[0, rows, :] = active
            dg_ref[0, rows, :] = slope
            racc[rows, :] += dot_nt(active, ex_ref[0, 1])

    expert, half = (step - shared_steps) // halves, (step - shared_steps) % halves

    @pl.when((step >= shared_steps) & (half == halves - 1))
    def _():
        for item in range(items):
            rows = pl.ds(item * PATCHES, PATCHES)
            acc[rows, :] += gate_column(g4_ref, rows, expert) * racc[rows, :].astype(bf16).astype(f32)
            racc[rows, :] = jnp.zeros((PATCHES, D), f32)

    @pl.when(step == pl.num_programs(0) - 1)
    def _():
        mixed_ref[...] = acc[...]
        for item in range(items):
            rows = pl.ds(item * PATCHES, PATCHES)
            x_ref[rows, :] = mid_ref[rows, :] + mod_row(mods_ref, item, 5) * acc[rows, :]


EARLY = 2
END_ROUTES = {0: [(3, 1), (2, 1), (1, 1)], 3: [(0, -1), (1, -1), (2, -1)]}


def early_slot(owner, step, place):
    return 4 if step == -1 and owner == place - 1 else owner


def early_beside(step, last, dex, chip_out, came_out, chip, local, core_send, core_recv, load_sem, line_send, line_recv, out_sem):
    at, core = lax.axis_index(LINE), lax.axis_index(CORE)
    units = reduce_units()[:EARLY]
    sibling = {CORE: 1 - core}

    def source(unit, which):
        _, matrix, row, rows, _, _ = units[unit]
        return dex.at[:, which, matrix, pl.ds(row, rows)]

    def given(unit):
        return pltpu.make_async_remote_copy(
            source(unit, 1 - core), chip.at[unit], core_send.at[unit], core_recv.at[unit],
            device_id=sibling, device_id_type=MESH_ID,
        )

    def loaded(unit):
        return pltpu.make_async_copy(source(unit, core), local.at[unit], load_sem.at[unit])

    def stored(unit):
        return pltpu.make_async_copy(chip.at[unit], chip_out.at[unit], out_sem.at[unit])

    def sent(unit, place, owner, direction):
        slot = early_slot(owner, direction, place)
        return pltpu.make_async_remote_copy(
            chip.at[unit, owner], came_out.at[unit, slot], line_send.at[unit, owner], line_recv.at[unit, slot],
            device_id={LINE: at + direction}, device_id_type=MESH_ID,
        )

    @pl.when(step == 0)
    def _():
        greet([sibling], at, 4)
        for unit in range(EARLY):
            given(unit).start()
            loaded(unit).start()

    for unit in range(EARLY):

        @pl.when(step == 1 + unit)
        def _(unit=unit):
            given(unit).wait_recv()
            loaded(unit).wait()
            for owner in range(4):

                def add(tile, owner=owner):
                    total = chip[unit, owner, tile, :].astype(f32) + local[unit, owner, tile, :].astype(f32)
                    chip[unit, owner, tile, :] = total.astype(bf16)

                row_tiles(units[unit][3], add)
            stored(unit).start()
            for place, routes in END_ROUTES.items():

                @pl.when(at == place)
                def _(place=place, routes=routes):
                    for owner, direction in routes:
                        sent(unit, place, owner, direction).start()

    @pl.when(step == last)
    def _():
        for unit in range(EARLY):
            given(unit).wait_send()
            stored(unit).wait()
            for place, routes in END_ROUTES.items():

                @pl.when(at == place)
                def _(unit=unit, place=place, routes=routes):
                    for owner, direction in routes:
                        sent(unit, place, owner, direction).wait_send()

                @pl.when(at == place + routes[0][1])
                def _(unit=unit, place=place, routes=routes):
                    for owner, direction in routes:
                        slot = early_slot(owner, direction, place)
                        pltpu.make_async_remote_copy(
                            came_out.at[unit, slot], came_out.at[unit, slot], line_send.at[unit, owner],
                            line_recv.at[unit, slot], device_id=sibling, device_id_type=MESH_ID,
                        ).wait_recv()


def ffn_bwd_kernel(
    shared_steps, halves, early, g_ref, n2_ref, mods_ref, g4_ref, mixed_ref, act_ref, dg_ref, up_ref, dn_ref, ex_ref, *rest
):
    step = pl.program_id(0)
    if early:
        other_dex, *rest = rest
        early_refs = [other_dex] + rest[5:7] + rest[14:]
        rest = rest[:5] + rest[7:14]
        early_beside(step, pl.num_programs(0) - 1, *early_refs)
    dup_ref, ddn_ref, dex_ref, gn2_ref, gg_ref, gmix, gs, gst, n2t, din, acc, racc = rest
    items = n2_ref.shape[0] // PATCHES

    @pl.when(step == 0)
    def _():
        gg_ref[...] = jnp.zeros_like(gg_ref)
        dup_ref[0:D, :] = jnp.zeros((D, D), bf16)
        for item in range(items):
            rows = pl.ds(item * PATCHES, PATCHES)
            grad = g_ref[rows, :]
            gg_ref[pl.ds(item, 1), :] = jnp.sum(grad * mixed_ref[rows, :], axis=0, keepdims=True)
            grad = mod_row(mods_ref, item, 5) * grad
            gmix[rows, :] = grad
            gs[rows, :] = grad.astype(bf16)
            gst[:, rows] = grad.astype(bf16).T
            n2t[:, rows] = n2_ref[rows, :].T
        acc[...] = jnp.zeros_like(acc)
        racc[...] = jnp.zeros_like(racc)

    @pl.when(step < shared_steps)
    def _():
        ddn_ref[...] = dot_nn(gst[...], act_ref[0]).astype(bf16).T
        blocks = [pl.ds(block * BWD_ROWS, BWD_ROWS) for block in range(n2_ref.shape[0] // BWD_ROWS)]
        grads = [dot_nt(gs[rows, :], dn_ref[...]) for rows in blocks]
        inners = [(grad * dg_ref[0, rows, :].astype(f32)).astype(bf16) for grad, rows in zip(grads, blocks)]
        for inner, rows in zip(inners, blocks):
            din[rows, :] = inner
        for inner, rows in zip(inners, blocks):
            acc[rows, :] += dot_nn(inner, up_ref[...])
        at = dup_ref.shape[0] - shared_steps * CHUNK + step * CHUNK
        dup_ref[pl.ds(pl.multiple_of(at, D), CHUNK), :] = dot_nn(n2t[...], din[...]).astype(bf16).T

    @pl.when(step >= shared_steps)
    def _():
        expert, half = (step - shared_steps) // halves, (step - shared_steps) % halves

        @pl.when(half == 0)
        def _():
            for item in range(items):
                rows = pl.ds(item * PATCHES, PATCHES)
                grad = (gate_column(g4_ref, rows, expert) * gmix[rows, :]).astype(bf16)
                gs[rows, :] = grad
                gst[:, rows] = grad.T

        dex_ref[0, 1] = dot_nn(gst[...], act_ref[0]).astype(bf16)
        blocks = [pl.ds(block * BWD_ROWS, BWD_ROWS) for block in range(n2_ref.shape[0] // BWD_ROWS)]
        grads = [dot_nn(gs[rows, :], ex_ref[0, 1]) for rows in blocks]
        inners = [(grad * dg_ref[0, rows, :].astype(f32)).astype(bf16) for grad, rows in zip(grads, blocks)]
        for inner, rows in zip(inners, blocks):
            din[rows, :] = inner
        for inner, rows in zip(inners, blocks):
            racc[rows, :] += dot_nt(inner, ex_ref[0, 0])

        dex_ref[0, 0] = dot_nn(n2t[...], din[...]).astype(bf16)

        @pl.when(half == halves - 1)
        def _():
            acc[...] += racc[...].astype(bf16).astype(f32)
            racc[...] = jnp.zeros_like(racc)

    @pl.when(step == pl.num_programs(0) - 1)
    def _():
        gn2_ref[...] = acc[...]


def final_kernel(x_ref, mods_ref, fo_ref, tgt_ref, gx_ref, gfm_ref, dfo_ref, loss_ref):
    item = pl.program_id(0)

    @pl.when(item == 0)
    def _():
        gfm_ref[...] = jnp.zeros_like(gfm_ref)
        dfo_ref[...] = jnp.zeros_like(dfo_ref)
        loss_ref[...] = jnp.zeros_like(loss_ref)

    tokens = x_ref[...]
    unit, _ = norm_parts(tokens)
    scale = mod_row(mods_ref, item, 1)
    normed = (unit * (1.0 + scale) + mod_row(mods_ref, item, 0)).astype(bf16)
    err = dot_nt(fo_ref[...], normed) - tgt_ref[...]
    loss_ref[...] += jnp.sum(err * err, axis=1, keepdims=True)
    grad_pred = (2.0 * err).astype(bf16)
    dfo_ref[...] += dot_nn(grad_pred, normed)
    grad_in, dshift, dscale = norm_back(tokens, scale, dot_tn(grad_pred, fo_ref[...]))
    gx_ref[...] = grad_in
    gfm_ref[pl.ds(item, 1), 0:D] = dshift
    gfm_ref[pl.ds(item, 1), D : 2 * D] = dscale


def params(limit):
    return pltpu.CompilerParams(vmem_limit_bytes=limit * MIB)


def cost(multiplies, moved):
    return pl.CostEstimate(flops=2 * multiplies, bytes_accessed=moved, transcendentals=0)


def whole(shape):
    return pl.BlockSpec(shape, lambda step: (0,) * len(shape))


def rows_of(width):
    return pl.BlockSpec((PATCHES, width), lambda step: (step, 0))


def shape_of(shape, kind):
    return jax.ShapeDtypeStruct(shape, kind)


ADA_STEPS = 6 * D // CHUNK
ADA_AT = 4 * D // CHUNK


def cond_forward(feat, hot, stem_t, lin):
    shapes = [(8, D)] * 4 + [(LAYERS, 8, 6 * D), (8, 2 * D)]
    return pl.pallas_call(
        cond_kernel,
        grid=(ADA_STEPS,),
        in_specs=[
            whole(feat.shape),
            whole(hot.shape),
            whole(stem_t.shape),
            pl.BlockSpec((LAYERS, CHUNK, D), lambda step: (0, ADA_AT + step, 0)),
        ],
        out_specs=[whole((8, D))] * 4 + [pl.BlockSpec((LAYERS, 8, CHUNK), lambda step: (0, 0, step)), whole((8, 2 * D))],
        out_shape=[shape_of(shape, f32) for shape in shapes],
        compiler_params=params(60),
        name="cond_forward",
    )(feat, hot, stem_t, lin)


def cond_backward(gm_a, gm_b, gfm, pre_one, pre_two, stem_t, lin):
    columns = pl.BlockSpec((8, CHUNK), lambda step: (0, step))
    return pl.pallas_call(
        cond_back_kernel,
        grid=(ADA_STEPS,),
        in_specs=[columns, columns, whole(gfm.shape), whole((8, D)), whole((8, D)), whole(stem_t.shape)]
        + [pl.BlockSpec((LAYERS, CHUNK, D), lambda step: (0, ADA_AT + step, 0))],
        out_specs=[whole((8, D))] * 2,
        out_shape=[shape_of((8, D), f32)] * 2,
        compiler_params=params(60),
        name="cond_backward",
    )(gm_a, gm_b, gfm, pre_one, pre_two, stem_t, lin)


def attn_forward(layer, tokens, mods, lin):
    count = tokens.shape[0]
    return pl.pallas_call(
        attn_fwd_kernel,
        grid=(count // PATCHES,),
        in_specs=[rows_of(D), whole(mods.shape), attn_weights(layer)],
        out_specs=[rows_of(D), rows_of(3 * D), rows_of(D), rows_of(D), rows_of(D), rows_of(D)],
        out_shape=[
            shape_of((count, D), bf16),
            shape_of((count, 3 * D), bf16),
            shape_of((count, D), bf16),
            shape_of((count, D), f32),
            shape_of((count, D), f32),
            shape_of((count, D), bf16),
        ],
        compiler_params=params(60),
        cost_estimate=cost(count * D * 4 * D * 9, 16 * count * D),
        name="attention_forward",
    )(tokens, mods, lin)


def attn_weights(layer):
    return pl.BlockSpec((None, 4 * D, D), lambda step: (layer, 0, 0))


def attn_backward(layer, gn2, grad, middle, tokens, normed, qkv, attended, branch, mods, grad_gate, lin, out_rows):
    count = tokens.shape[0]
    return pl.pallas_call(
        attn_bwd_kernel,
        grid=(count // PATCHES,),
        in_specs=[rows_of(D)] * 5
        + [rows_of(3 * D), rows_of(D), rows_of(D), whole(mods.shape), whole(grad_gate.shape), attn_weights(layer)],
        out_specs=[rows_of(D), whole((8, 6 * D)), whole((out_rows, D))],
        out_shape=[shape_of((count, D), f32), shape_of((8, 6 * D), f32), shape_of((out_rows, D), bf16)],
        scratch_shapes=[pltpu.VMEM((PATCHES, 3 * D), bf16), pltpu.VMEM((4 * D, D), f32)],
        compiler_params=params(60),
        cost_estimate=cost(count * D * 4 * D * 22, 16 * count * D),
        name="attention_backward",
    )(gn2, grad, middle, tokens, normed, qkv, attended, branch, mods, grad_gate, lin)


def weight_specs(layer, shared_steps, lin_rows):
    up_at = lin_rows // CHUNK - shared_steps
    return [
        pl.BlockSpec((None, CHUNK, D), lambda step: (layer, up_at + jnp.minimum(step, shared_steps - 1), 0)),
        pl.BlockSpec((CHUNK, D), lambda step: (jnp.minimum(step, shared_steps - 1), 0)),
        pl.BlockSpec((1, 2, D, CHUNK), lambda step: (jnp.maximum(step - shared_steps, 0), 0, 0, 0)),
    ]


def ffn_forward(layer, n2, middle, mods, g4, lin, lout, experts_w, halves, beside=()):
    count = n2.shape[0]
    shared_steps = lout.shape[0] // CHUNK
    steps = shared_steps + experts_w.shape[0]
    wide = pl.BlockSpec((1, count, CHUNK), lambda step: (step, 0, 0))
    anywhere = [pl.BlockSpec(memory_space=pl.ANY)] * len(beside)
    remote = pltpu.CompilerParams(vmem_limit_bytes=60 * MIB, collective_id=7, has_side_effects=True)
    return pl.pallas_call(
        functools.partial(ffn_fwd_kernel, shared_steps, halves, len(beside)),
        grid=(steps,),
        in_specs=[whole(n2.shape), whole(middle.shape), whole(mods.shape), whole(g4.shape)]
        + weight_specs(layer, shared_steps, lin.shape[1])
        + anywhere,
        out_specs=[wide, wide, whole((count, D)), whole((count, D))] + anywhere,
        out_shape=[
            shape_of((steps, count, CHUNK), bf16),
            shape_of((steps, count, CHUNK), bf16),
            shape_of((count, D), f32),
            shape_of((count, D), f32),
        ]
        + [shape_of((8,) + part.shape, bf16) for part in beside],
        scratch_shapes=[pltpu.VMEM((count, D), f32)] * 2 + (gather_semaphores(4) if beside else []),
        compiler_params=remote if beside else params(60),
        cost_estimate=cost(4 * steps * count * D * CHUNK * 2, 8 * steps * count * CHUNK),
        name="ffn_forward",
    )(n2, middle, mods, g4, lin, lout, experts_w, *beside)


def ffn_backward(layer, grad, n2, mods, g4, mixed, active, slope, lin, lout, experts_w, halves, early=()):
    count = n2.shape[0]
    shared_steps = lout.shape[0] // CHUNK
    steps = shared_steps + experts_w.shape[0]
    wide = pl.BlockSpec((1, count, CHUNK), lambda step: (step, 0, 0))
    specs = weight_specs(layer, shared_steps, lin.shape[1])
    anywhere = [pl.BlockSpec(memory_space=pl.ANY)] * len(early)
    remote = pltpu.CompilerParams(vmem_limit_bytes=62 * MIB, collective_id=8, has_side_effects=True)
    dma = pltpu.SemaphoreType.DMA
    early_scratch = [pltpu.VMEM((EARLY, 4, D // 2, CHUNK), bf16)] * 2
    early_scratch += [dma((EARLY,)), dma((EARLY,)), dma((EARLY,)), dma((EARLY, 4)), dma((EARLY, 5)), dma((EARLY,))]
    return pl.pallas_call(
        functools.partial(ffn_bwd_kernel, shared_steps, halves, len(early)),
        grid=(steps,),
        in_specs=[whole(grad.shape), whole(n2.shape), whole(mods.shape), whole(g4.shape), whole(mixed.shape), wide, wide]
        + specs
        + anywhere,
        out_specs=[whole((lout.shape[0] + D, D)), specs[1], specs[2], whole((count, D)), whole((8, D))] + anywhere * 2,
        out_shape=[
            shape_of((lout.shape[0] + D, D), bf16),
            shape_of(lout.shape, bf16),
            shape_of(experts_w.shape, bf16),
            shape_of((count, D), f32),
            shape_of((8, D), f32),
        ]
        + [shape_of((EARLY, lead, D // 2, CHUNK), bf16) for lead in (4, 5) if early],
        scratch_shapes=[
            pltpu.VMEM((count, D), f32),
            pltpu.VMEM((count, D), bf16),
            pltpu.VMEM((D, count), bf16),
            pltpu.VMEM((D, count), bf16),
            pltpu.VMEM((count, CHUNK), bf16),
            pltpu.VMEM((count, D), f32),
            pltpu.VMEM((count, D), f32),
        ]
        + (early_scratch if early else []),
        compiler_params=remote if early else params(60),
        cost_estimate=cost(4 * steps * count * D * CHUNK * 4 // 2, 8 * steps * count * CHUNK),
        name="ffn_backward",
    )(grad, n2, mods, g4, mixed, active, slope, lin, lout, experts_w, *early)


def final_step(tokens, mods, fo_rows, target_t):
    count = tokens.shape[0]
    return pl.pallas_call(
        final_kernel,
        grid=(count // PATCHES,),
        in_specs=[
            rows_of(D),
            whole(mods.shape),
            whole(fo_rows.shape),
            pl.BlockSpec((PATCH_DIM, PATCHES), lambda step: (0, step)),
        ],
        out_specs=[rows_of(D), whole((8, 2 * D)), whole((PATCH_DIM, D)), whole((PATCH_DIM, 1))],
        out_shape=[
            shape_of((count, D), f32),
            shape_of((8, 2 * D), f32),
            shape_of((PATCH_DIM, D), f32),
            shape_of((PATCH_DIM, 1), f32),
        ],
        compiler_params=params(60),
        name="final_step",
    )(tokens, mods, fo_rows, target_t)


def update_kernel(groups, grad_a, grad_b, total_a, total_b, w_ref, f_ref, s_ref, m_ref, new_ref, half_ref, fn_ref, sn_ref, mn_ref):
    for layer, (grad_ref, total_ref) in enumerate(((grad_a, total_a), (grad_b, total_b))):

        @pl.when(pl.program_id(0) == layer)
        def _(grad_ref=grad_ref, total_ref=total_ref):
            gradient = grad_ref[...]
            fn_ref[0] = beta_one * f_ref[0] + (1.0 - beta_one) * gradient
            sn_ref[0] = beta_two * s_ref[0] + (1.0 - beta_two) * gradient * gradient
            mean_delta = total_ref[...] / groups
            moment_new = outer_mom * m_ref[0] + mean_delta
            weight = w_ref[0] - outer_rate * (mean_delta + outer_mom * moment_new)
            mn_ref[0] = moment_new
            new_ref[0] = weight
            half_ref[0] = weight.astype(bf16)


def update_arrays(tile, grads, totals, weight, first, second, moment):
    layers, rows, width = weight.shape
    tiles = rows // tile
    state = pl.BlockSpec((1, tile, width), lambda layer, step: (layer, step, 0))
    early = pl.BlockSpec((tile, width), lambda layer, step: (jnp.where(layer == 0, step, tiles - 1), 0))
    late = pl.BlockSpec((tile, width), lambda layer, step: (jnp.where(layer == 0, 0, step), 0))
    return pl.pallas_call(
        functools.partial(update_kernel, lax.axis_size(GROUP)),
        grid=(layers, tiles),
        in_specs=[early, late, early, late] + [state] * 4,
        out_specs=[state] * 5,
        out_shape=[shape_of(weight.shape, kind) for kind in (f32, bf16, f32, f32, f32)],
        compiler_params=params(60),
        name="update_arrays",
    )(*grads, *totals, weight, first, second, moment)


def pad_rows(values):
    return jnp.pad(values, ((0, 8 - values.shape[0]), (0, 0)))


def stem_lanes(stem_t):
    pieces, at = [], 0
    for size, padded in zip(STEM_SIZES, STEM_PADDED):
        pieces.append(jnp.pad(stem_t[:, at : at + size], ((0, 0), (0, padded - size))))
        at = at + size
    pieces.append(jnp.zeros((stem_t.shape[0], STEM_LANES - sum(STEM_PADDED)), stem_t.dtype))
    return jnp.concatenate(pieces, axis=1)


MESH_ID = pl.DeviceIdType.MESH
TILE = 48


def plane_partners():
    group = lax.axis_index(GROUP)
    return {GROUP: group + 1 - 2 * lax.rem(group, 2)}, {GROUP: lax.rem(group + 2, 4)}


def greet(partners, line_at, line_size):
    barrier = pltpu.get_barrier_semaphore()
    for partner in partners:
        pl.semaphore_signal(barrier, inc=1, device_id=partner, device_id_type=MESH_ID)

    @pl.when(line_at > 0)
    def _():
        pl.semaphore_signal(barrier, inc=1, device_id={LINE: line_at - 1}, device_id_type=MESH_ID)

    @pl.when(line_at < line_size - 1)
    def _():
        pl.semaphore_signal(barrier, inc=1, device_id={LINE: line_at + 1}, device_id_type=MESH_ID)

    ends = jnp.where(line_at == 0, 1, 0) + jnp.where(line_at == line_size - 1, 1, 0)
    pl.semaphore_wait(barrier, len(partners) + 2 - ends)


def row_tiles(rows, body):
    def step(index, carry):
        body(pl.ds(pl.multiple_of(index * TILE, TILE), TILE))
        return carry

    lax.fori_loop(0, rows // TILE, step, 0)


def adam_delta(weight, gradient, first, second):
    return adam_step(weight, gradient, first, second)[0]


def reduce_units():
    units = []
    for matrix in range(2):
        for half in range(2):
            units.append((0, matrix, half * D // 2, D // 2, CHUNK, ()))
    for half in range(2):
        units.append((1, 0, half * 432, 432, D, (1,)))
    units.append((2, 0, 0, D, D, ()))
    return units


def reduce_kernel(
    layer, with_stem, dex, dqkvo, dup, ddn, extra, ex_w, ex_f, ex_s, li_w, li_f, li_s, lo_w, lo_f, lo_s, *rest
):
    early = EARLY if with_stem else 0
    if early:
        chip_in, came_in, *rest = rest
    if with_stem:
        stem_in, *rest, stem_sem, stem_send, stem_recv, stem_a, stem_b, stem_c, stem_d = rest
        stem_out = rest.pop(6)
    g_ex, g_li, g_lo, m_ex, m_li, m_lo, *scratch = rest
    units = reduce_units()
    number = len(units)
    banks = [scratch[at * number : (at + 1) * number] for at in range(9)]
    chip, local, came, delta, swapped, swapped_two, weight, first, second = banks
    extra_buf = scratch[9 * number]
    core_send, core_recv, line_send, line_recv, load_sem, plane_send, plane_recv, out_sem = scratch[9 * number + 1 :]
    at = lax.axis_index(LINE)
    core = lax.axis_index(CORE)
    sibling = {CORE: 1 - core}
    side_x, side_y = plane_partners()
    greet([sibling, side_x, side_y], at, 4)

    def pieces(unit, which):
        kind, matrix, row, rows, _, _ = units[unit]
        if kind == 0:
            return [(dex.at[:, which, matrix, pl.ds(row, rows)], slice(0, 4))]
        if kind == 2:
            return [(ddn.at[:, which, pl.ds(row, rows)], slice(0, 4))]
        return [
            (dqkvo.at[which, pl.ds(row, rows)], 0),
            (dup.at[0, which, pl.ds(row, rows)], 2),
            (dup.at[1, which, pl.ds(row, rows)], 3),
        ]

    def dest(bank, unit, where):
        return bank[unit].at[pl.ds(0, 4)] if isinstance(where, slice) else bank[unit].at[where]

    if with_stem:
        load = pltpu.make_async_copy(stem_in, stem_a, stem_sem.at[0])
        load.start()
        load.wait()

    def stem_copies(second_step):
        landing, sides = ((stem_b, (side_x, side_y)), (stem_c, (side_y, side_x)))[second_step]
        return [
            pltpu.make_async_remote_copy(
                stem_a.at[pl.ds(begin, size)], landing.at[pl.ds(begin, size)], stem_send.at[2 * second_step + half],
                stem_recv.at[2 * second_step + half], device_id=sides[half], device_id_type=MESH_ID,
            )
            for half, (begin, size) in enumerate(((0, 16), (16, 32)))
        ]

    def stem_turn(turn):
        if not with_stem or turn > 2:
            return
        if turn == 0:
            for copy in stem_copies(0):
                copy.start()
        elif turn == 1:
            for copy in stem_copies(0):
                copy.wait()
            stem_a[...] = (stem_a[...].astype(f32) + stem_b[...].astype(f32)).astype(bf16)
            for copy in stem_copies(1):
                copy.start()
        else:
            for copy in stem_copies(1):
                copy.wait()
            stem_d[...] = stem_a[...].astype(f32) + stem_c[...].astype(f32)
            pltpu.make_async_copy(stem_d, stem_out, stem_sem.at[1]).start()

    early_slots = {1: [3, 2, 1], 2: [0, 1, 4]}

    def early_load(unit, slot, index):
        sem = (load_sem.at[unit, 1], load_sem.at[unit, 2], load_sem.at[number, 1 + unit])[index]
        return pltpu.make_async_copy(came_in.at[unit, slot], came[unit].at[slot], sem)

    given, loads = [], []
    for unit in range(number):
        given.append([])
        loads.append([])
        if unit < early:
            copy = pltpu.make_async_copy(chip_in.at[unit], chip[unit], load_sem.at[unit, 0])
            copy.start()
            loads[unit].append(copy)
            for place, slots in early_slots.items():

                @pl.when(at == place)
                def _(unit=unit, slots=slots):
                    for index, slot in enumerate(slots):
                        early_load(unit, slot, index).start()

            continue
        for place, (source, where) in enumerate(pieces(unit, 1 - core)):
            copy = pltpu.make_async_remote_copy(
                source, dest(chip, unit, where), core_send.at[unit, place], core_recv.at[unit, place],
                device_id=sibling, device_id_type=MESH_ID,
            )
            copy.start()
            given[unit].append(copy)
        for place, (source, where) in enumerate(pieces(unit, core)):
            copy = pltpu.make_async_copy(source, dest(local, unit, where), load_sem.at[unit, place])
            copy.start()
            loads[unit].append(copy)
    state_loads = []
    for unit, (kind, matrix, row, rows, _, _) in enumerate(units):
        if kind == 0:
            sources = [ex_w.at[layer, 0, matrix], ex_f.at[0, layer, 0, matrix], ex_s.at[0, layer, 0, matrix]]
        elif kind == 1:
            sources = [li_w.at[layer], li_f.at[layer], li_s.at[layer]]
        else:
            sources = [lo_w.at[layer], lo_f.at[0, layer], lo_s.at[0, layer]]
        state_loads.append([])
        for place, (source, bank) in enumerate(zip(sources, (weight, first, second))):
            copy = pltpu.make_async_copy(source.at[pl.ds(row, rows)], bank[unit], load_sem.at[unit, 3 + place])
            copy.start()
            state_loads[unit].append(copy)
    extra_load = pltpu.make_async_copy(extra, extra_buf, load_sem.at[number, 0])
    extra_load.start()

    def line_copy(unit, owner, step, place):
        slot = 4 if step == -1 and owner == place - 1 else owner
        return pltpu.make_async_remote_copy(
            chip[unit].at[owner], came[unit].at[slot], line_send.at[unit, owner], line_recv.at[unit, slot],
            device_id={LINE: at + step}, device_id_type=MESH_ID,
        )

    def arrived(unit, slot, place):
        if unit < early and slot in early_slots.get(place, ()):
            early_load(unit, slot, early_slots[place].index(slot)).wait()
            return
        pltpu.make_async_remote_copy(
            came[unit].at[slot], came[unit].at[slot], line_send.at[unit, 0], line_recv.at[unit, slot],
            device_id=sibling, device_id_type=MESH_ID,
        ).wait_recv()

    routes_of = {0: [(3, 1), (2, 1), (1, 1)], 1: [(3, 1), (2, 1), (0, -1)], 2: [(0, -1), (1, -1), (3, 1)], 3: [(0, -1), (1, -1), (2, -1)]}
    finals = {0: [4], 1: [1, 4], 2: [2, 4], 3: [3]}

    def forward(unit):
        rows, absent = units[unit][3], units[unit][5]
        for middle in (1, 2):

            @pl.when(at == middle)
            def _(middle=middle):
                for owner, step in routes_of[middle]:
                    if owner in absent:
                        continue
                    arrived(unit, owner, middle)

                    def add(tile, owner=owner):
                        total = chip[unit][owner, tile, :].astype(f32) + came[unit][owner, tile, :].astype(f32)
                        chip[unit][owner, tile, :] = total.astype(bf16)

                    row_tiles(rows, add)
                    line_copy(unit, owner, step, middle).start()

    for unit, (kind, matrix, row, rows, _, absent) in enumerate(units):
        for copy in given[unit]:
            copy.wait_recv()
        for copy in loads[unit]:
            copy.wait()
        for owner in range(0 if unit < early else 4):
            if owner in absent:
                chip[unit][owner] = jnp.zeros(chip[unit].shape[1:], bf16)
                continue

            def add(tile, owner=owner, unit=unit):
                total = chip[unit][owner, tile, :].astype(f32) + local[unit][owner, tile, :].astype(f32)
                chip[unit][owner, tile, :] = total.astype(bf16)

            row_tiles(rows, add)
        for end in (0, 3):

            @pl.when(at == end)
            def _(unit=unit, end=end, absent=absent):
                for owner, step in routes_of[end]:
                    if owner not in absent and unit >= early:
                        line_copy(unit, owner, step, end).start()
                came[unit][0 if end == 0 else 4] = jnp.zeros(chip[unit].shape[1:], bf16)

        for owner in absent:

            @pl.when(at == owner)
            def _(unit=unit, owner=owner):
                came[unit][owner] = jnp.zeros(chip[unit].shape[1:], bf16)
                came[unit][4] = jnp.zeros(chip[unit].shape[1:], bf16)
        if unit < early:
            forward(unit)

    def plane_copies(unit, second_step):
        rows = units[unit][3]
        middle = rows // 32 * 16
        sides = (side_y, side_x) if second_step else (side_x, side_y)
        landing = swapped_two if second_step else swapped
        copies = []
        for half, (begin, size) in enumerate(((0, middle), (middle, rows - middle))):
            part = pl.ds(begin, size)
            copies.append(
                pltpu.make_async_remote_copy(
                    delta[unit].at[part], landing[unit].at[part], plane_send.at[unit, 2 * second_step + half],
                    plane_recv.at[unit, 2 * second_step + half], device_id=sides[half], device_id_type=MESH_ID,
                )
            )
        return copies

    def out_copy(unit, means):
        kind, matrix, row, rows, _, _ = units[unit]
        target = ((g_ex.at[matrix], g_li, g_lo), (m_ex.at[matrix], m_li, m_lo))[means][kind]
        source = first[unit] if means else weight[unit]
        return pltpu.make_async_copy(source, target.at[pl.ds(row, rows)], out_sem.at[unit, means])

    firsts, seconds = {}, {}

    def finish(unit):
        kind, matrix, row, rows, _, absent = units[unit]
        for place in range(4):

            @pl.when(at == place)
            def _(place=place):
                if place not in absent:
                    for slot in finals[place]:
                        arrived(unit, slot, place)

        for copy in state_loads[unit]:
            copy.wait()
        if kind == 1 and row == 0:
            extra_load.wait()

        def body(tile):
            grad = chip[unit][at, tile, :].astype(f32) + came[unit][at, tile, :].astype(f32)
            grad = grad + came[unit][4, tile, :].astype(f32)
            if kind == 1:
                grad = grad + extra_buf[pl.ds(row + tile.start, TILE), :]
            change = adam_delta(weight[unit][tile, :], grad, first[unit][tile, :], second[unit][tile, :])
            delta[unit][tile, :] = change.astype(bf16)
            weight[unit][tile, :] = grad

        row_tiles(rows, body)
        out_copy(unit, 0).start()
        firsts[unit] = plane_copies(unit, 0)
        for copy in firsts[unit]:
            copy.start()

    def exchange(unit):
        for copy in firsts[unit]:
            copy.wait()

        def body(tile):
            total = delta[unit][tile, :].astype(f32) + swapped[unit][tile, :].astype(f32)
            delta[unit][tile, :] = total.astype(bf16)

        row_tiles(units[unit][3], body)
        seconds[unit] = plane_copies(unit, 1)
        for copy in seconds[unit]:
            copy.start()

    def close(unit):
        for copy in seconds[unit]:
            copy.wait_recv()

        def body(tile):
            first[unit][tile, :] = delta[unit][tile, :].astype(f32) + swapped_two[unit][tile, :].astype(f32)

        row_tiles(units[unit][3], body)
        out_copy(unit, 1).start()

    for turn in range(number + 3):
        stem_turn(turn)
        for lag, action in enumerate((forward, finish, exchange, close)):
            if 0 <= turn - lag < number and (lag or turn >= early):
                action(turn - lag)

    if with_stem:
        pltpu.make_async_copy(stem_d, stem_out, stem_sem.at[1]).wait()
    for unit in range(number):
        for copy in given[unit]:
            copy.wait_send()
        for copy in seconds[unit]:
            copy.wait_send()
        out_copy(unit, 0).wait()
        out_copy(unit, 1).wait()
        for place in range(4):

            @pl.when(at == place)
            def _(place=place, unit=unit):
                for owner, step in routes_of[place]:
                    if owner not in units[unit][5] and (unit >= early or place in (1, 2)):
                        line_copy(unit, owner, step, place).wait_send()


def reduce_layer(layer, dex, dqkvo, dup, ddn, extra, states, stem_delta=None, begun=()):
    units = reduce_units()
    scratch = []
    for lead, kind in (((4,), bf16), ((4,), bf16), ((5,), bf16), ((), bf16), ((), bf16), ((), bf16), ((), f32), ((), f32), ((), f32)):
        scratch += [pltpu.VMEM(lead + (unit[3], unit[4]), kind) for unit in units]
    number = len(units)
    scratch.append(pltpu.VMEM(extra.shape, f32))
    dma = pltpu.SemaphoreType.DMA
    scratch += [dma((number, 3)), dma((number, 3)), dma((number, 4)), dma((number, 5)), dma((number + 1, 6))]
    scratch += [dma((number, 4)), dma((number, 4)), dma((number, 2))]
    anywhere = pl.BlockSpec(memory_space=pl.ANY)
    shapes = [(2, D, CHUNK), extra.shape, (D, D)] * 2
    stems = [] if stem_delta is None else [stem_delta]
    for delta in stems:
        shapes.append(delta.shape)
        scratch += [dma((2,)), dma((4,)), dma((4,))] + [pltpu.VMEM(delta.shape, bf16)] * 3
        scratch.append(pltpu.VMEM(delta.shape, f32))
    return pl.pallas_call(
        functools.partial(reduce_kernel, layer, bool(stems)),
        out_shape=[shape_of(shape, f32) for shape in shapes],
        in_specs=[anywhere] * (5 + len(states) + len(stems) + len(begun)),
        out_specs=[anywhere] * len(shapes),
        scratch_shapes=scratch,
        compiler_params=pltpu.CompilerParams(
            vmem_limit_bytes=62 * MIB, collective_id=1 + layer, has_side_effects=True
        ),
        name="reduce_layer",
    )(dex, dqkvo, dup, ddn, extra, *states, *begun, *stems)


def shard_part(kind, ref, quarter, half=None):
    if kind == "stem":
        begin, size = quarter * (STEM_LANES // 4), STEM_LANES // 4
        if half is not None:
            begin, size = begin + half * (size // 2), size // 2
        return ref.at[:, pl.ds(pl.multiple_of(begin, 128), size)]
    if kind == "lin":
        begin, size = lax.rem(quarter, 2) * 432, 432
        if half is not None:
            begin, size = begin + half * 208, (208, 224)[half]
        return ref.at[quarter // 2, pl.ds(pl.multiple_of(begin, 16), size)]
    begin, size = quarter * (D // 4), D // 4
    if half is not None:
        begin, size = begin + half * (size // 2), size // 2
    return ref.at[pl.ds(pl.multiple_of(begin, 16), size)]


class WeightGather:
    def __init__(self, kinds, sources, targets, sends, recvs, cores_send, cores_recv, own_sem):
        self.kinds, self.sources, self.targets = kinds, sources, targets
        self.sends, self.recvs = sends, recvs
        self.cores_send, self.cores_recv, self.own_sem = cores_send, cores_recv, own_sem
        self.at, self.core, self.group = lax.axis_index(LINE), lax.axis_index(CORE), lax.axis_index(GROUP)
        self.sibling = {CORE: 1 - self.core}
        self.side_x, self.side_y = plane_partners()
        self.group_x = self.group + 1 - 2 * lax.rem(self.group, 2)
        self.group_y = lax.rem(self.group + 2, 4)
        near = jnp.where(self.at == 3, 3, 1)
        far = jnp.where(self.at == 0, 3, jnp.where(self.at == 3, 1, 2))
        self.order = (near, 6 - near - far, far)

    def enter(self):
        barrier = pltpu.get_barrier_semaphore()
        others = [{LINE: lax.rem(self.at + step, 4)} for step in (1, 2, 3)]
        for partner in others + [self.sibling, self.side_x, self.side_y]:
            pl.semaphore_signal(barrier, inc=1, device_id=partner, device_id_type=MESH_ID)
        pl.semaphore_wait(barrier, 6)

    def whole_part(self, unit, owner, core):
        target = self.targets[unit]
        if self.kinds[unit] == "lin":
            return target.at[:, owner * 2 + core]
        return target.at[owner * 2 + core]

    def copy(self, unit, source, target, slot, kind, device):
        return pltpu.make_async_remote_copy(
            source, target, self.sends.at[unit, slot, kind], self.recvs.at[unit, slot, kind],
            device_id=device, device_id_type=MESH_ID,
        )

    def line_copy(self, unit, step):
        target = shard_part(self.kinds[unit], self.whole_part(unit, self.at, self.core), self.group)
        source = shard_part(self.kinds[unit], self.sources[unit], self.group)
        return pltpu.make_async_remote_copy(
            source, target, self.sends.at[unit, step - 1, 0], self.recvs.at[unit, 3 - step, 0],
            device_id={LINE: lax.rem(self.at + step, 4)}, device_id_type=MESH_ID,
        )

    def owner_of(self, slot):
        return lax.rem(self.at + slot, 4)

    def part(self, unit, slot, quarter, half=None):
        return shard_part(self.kinds[unit], self.whole_part(unit, self.owner_of(slot), self.core), quarter, half)

    def core_copy(self, unit, slot, own=False):
        source = self.sources[unit] if own else self.whole_part(unit, self.owner_of(slot), self.core)
        return pltpu.make_async_remote_copy(
            source, self.whole_part(unit, self.owner_of(slot), self.core),
            self.cores_send.at[unit, slot], self.cores_recv.at[unit, slot],
            device_id=self.sibling, device_id_type=MESH_ID,
        )

    def own_copy(self, unit):
        return pltpu.make_async_copy(
            self.sources[unit], self.whole_part(unit, self.at, self.core), self.own_sem.at[unit]
        )

    def begin(self, unit):
        for step in (2, 1, 3):
            self.line_copy(unit, step).start()
        self.core_copy(unit, 0, True).start()
        self.own_copy(unit).start()

    def plane_copies(self, unit, slot):
        mine = self.part(unit, slot, self.group)
        return [self.copy(unit, mine, mine, slot - 1, 1, self.side_x), self.copy(unit, mine, mine, slot - 1, 2, self.side_y)]

    def plane_arrivals(self, unit, slot):
        parts = [self.part(unit, slot, self.group_x), self.part(unit, slot, self.group_y)]
        return [self.copy(unit, parts[0], parts[0], slot - 1, 1, self.side_x), self.copy(unit, parts[1], parts[1], slot - 1, 2, self.side_y)]

    def corner_copies(self, unit, slot):
        parts = [self.part(unit, slot, self.group_x, 0), self.part(unit, slot, self.group_y, 1)]
        return [self.copy(unit, parts[0], parts[0], slot - 1, 3, self.side_y), self.copy(unit, parts[1], parts[1], slot - 1, 4, self.side_x)]

    def corner_arrivals(self, unit, slot):
        corner = 3 - self.group
        parts = [self.part(unit, slot, corner, 0), self.part(unit, slot, corner, 1)]
        return [self.copy(unit, parts[0], parts[0], slot - 1, 3, self.side_y), self.copy(unit, parts[1], parts[1], slot - 1, 4, self.side_x)]

    def along_line(self, unit):
        for slot in self.order:
            mine = self.part(unit, slot, self.group)
            self.copy(unit, mine, mine, slot - 1, 0, self.sibling).wait_recv()
            for copy in self.plane_copies(unit, slot):
                copy.start()

    def in_plane(self, unit):
        for slot in self.order:
            for copy in self.plane_arrivals(unit, slot):
                copy.wait_recv()
            for copy in self.corner_copies(unit, slot):
                copy.start()

    def to_sibling(self, unit):
        for slot in self.order:
            for copy in self.corner_arrivals(unit, slot):
                copy.wait_recv()
            self.core_copy(unit, slot).start()

    def end(self, unit):
        self.own_copy(unit).wait()
        for slot in range(4):
            self.core_copy(unit, slot, slot == 0).wait_send()
            other = self.whole_part(unit, self.owner_of(slot), 1 - self.core)
            pltpu.make_async_remote_copy(
                other, other, self.cores_send.at[unit, slot], self.cores_recv.at[unit, slot],
                device_id=self.sibling, device_id_type=MESH_ID,
            ).wait_recv()
        for slot in (1, 2, 3):
            self.line_copy(unit, slot).wait_send()
            for copy in self.plane_copies(unit, slot) + self.corner_copies(unit, slot):
                copy.wait_send()


def gather_semaphores(number):
    dma = pltpu.SemaphoreType.DMA
    return [dma((number, 3, 5)), dma((number, 3, 5)), dma((number, 4)), dma((number, 4)), dma((number,))]


def gather_kernel(kinds, split, *refs):
    count = len(split)
    arrays_in, arrays_out, sems = refs[:count], refs[count : 2 * count], refs[2 * count :]
    sources, targets = [], []
    for given, target, parts in zip(arrays_in, arrays_out, split):
        for part in parts:
            sources.append(given if part is None else given.at[part])
            targets.append(target if part is None else target.at[(slice(None),) + part])
    work = WeightGather(kinds, sources, targets, *sems)
    work.enter()
    number = len(kinds)
    work.begin(0)
    work.begin(1)
    for turn in range(number + 2):
        for lag, action in enumerate((work.along_line, work.in_plane, work.to_sibling)):
            if 0 <= turn - lag < number:
                action(turn - lag)
            if lag == 0 and turn + 2 < number:
                work.begin(turn + 2)
    for unit in range(number):
        work.end(unit)


def gather_beside(step, last, given, taken, sems):
    parts = [(matrix, slice(None), pl.ds(begin, D)) for matrix in range(2) for begin in (0, D)]
    sources = [given[0].at[part] for part in parts]
    targets = [taken[0].at[(slice(None),) + part] for part in parts]
    work = WeightGather(["rows"] * 4, sources, targets, *sems)
    line, plane, pair = work.along_line, work.in_plane, work.to_sibling
    schedule = {
        0: [(work.begin, 0), (work.begin, 1)],
        1: [(work.begin, 2)],
        2: [(work.begin, 3)],
        3: [(line, 0)],
        4: [(line, 1)],
        5: [(plane, 0)],
        6: [(line, 2), (plane, 1)],
        7: [(line, 3), (pair, 0)],
        8: [(plane, 2)],
        9: [(plane, 3), (pair, 1)],
        10: [(pair, 2)],
        11: [(pair, 3)] + [(work.end, unit) for unit in range(4)],
    }
    for when, actions in schedule.items():

        @pl.when(step == (last if when == 11 else when))
        def _(when=when, actions=actions):
            if when == 0:
                work.enter()
            for action, unit in actions:
                action(unit)


def gather_weights(stem, lin, louts, experts_in):
    lanes = [pl.ds(begin, 128) for begin in range(0, D, 128)]
    every = slice(None)
    arrays = [stem, lin] + list(louts) + list(experts_in)
    kinds = ["stem"] + ["lin"] * len(lanes) + ["rows"] * (len(louts) + 4 * len(experts_in))
    split = [[None], [(every, every, part) for part in lanes]] + [[None]] * len(louts)
    split += [[(matrix, every, pl.ds(begin, D)) for matrix in range(2) for begin in (0, D)]] * len(experts_in)
    shapes = [(8,) + stem.shape, (lin.shape[0], 8) + lin.shape[1:]]
    shapes += [(8,) + part.shape for part in arrays[2:]]
    anywhere = pl.BlockSpec(memory_space=pl.ANY)
    return pl.pallas_call(
        functools.partial(gather_kernel, kinds, split),
        out_shape=[shape_of(shape, bf16) for shape in shapes],
        in_specs=[anywhere] * len(arrays),
        out_specs=[anywhere] * len(arrays),
        scratch_shapes=gather_semaphores(len(kinds)),
        compiler_params=pltpu.CompilerParams(collective_id=5, has_side_effects=True),
        name="gather_weights",
    )(*arrays)


def exchange_kernel(packed, loss, all_packed, total, from_x, from_y, losses, held, send, recv, core_send, core_recv, plane_send, plane_recv, own_sem):
    at, core = lax.axis_index(LINE), lax.axis_index(CORE)
    side_x, side_y = plane_partners()
    sibling = {CORE: 1 - core}
    barrier = pltpu.get_barrier_semaphore()
    others = [{LINE: lax.rem(at + step, 4)} for step in (1, 2, 3)]
    for partner in others + [sibling, side_x, side_y]:
        pl.semaphore_signal(barrier, inc=1, device_id=partner, device_id_type=MESH_ID)
    pl.semaphore_wait(barrier, 6)

    def slots(owner, which):
        return all_packed.at[owner * 2 + which], losses.at[owner * 2 + which]

    own = [pltpu.make_async_copy(source, target, own_sem.at[place]) for place, (source, target) in enumerate(zip((packed, loss), slots(at, core)))]
    for copy in own:
        copy.start()

    def line(step, place):
        source, target = ((packed, loss)[place], slots(at, core)[place])
        return pltpu.make_async_remote_copy(
            source, target, send.at[step - 1, place], recv.at[step - 1, place],
            device_id=others[step - 1], device_id_type=MESH_ID,
        )

    def across(step, place):
        owner = lax.rem(at + 4 - step, 4)
        source = (packed, loss)[place] if step == 0 else slots(owner, core)[place]
        return pltpu.make_async_remote_copy(
            source, slots(owner, core)[place], core_send.at[step, place], core_recv.at[step, place],
            device_id=sibling, device_id_type=MESH_ID,
        )

    def arrival(step, place, which, sem):
        here = slots(lax.rem(at + 4 - step, 4), which)[place]
        return pltpu.make_async_remote_copy(
            here, here, core_send.at[step, place], sem, device_id=sibling, device_id_type=MESH_ID
        )

    for place in (1, 0):
        for step in (2, 3, 1):
            line(step, place).start()
        across(0, place).start()
    for place in (1, 0):
        for step in (1, 3, 2):
            arrival(step, place, core, recv.at[step - 1, place]).wait_recv()
            across(step, place).start()
        for step in range(4):
            arrival(step, place, 1 - core, core_recv.at[step, place]).wait_recv()
        if place == 1:
            own[1].wait()
            held[...] = jnp.sum(losses[...], axis=0)
            first = pltpu.make_async_remote_copy(held, from_x, plane_send.at[0], plane_recv.at[0], device_id=side_x, device_id_type=MESH_ID)
            first.start()
    first.wait()
    held[...] += from_x[...]
    second = pltpu.make_async_remote_copy(held, from_y, plane_send.at[1], plane_recv.at[1], device_id=side_y, device_id_type=MESH_ID)
    second.start()
    second.wait()
    total[...] = held[...] + from_y[...]
    own[0].wait()
    for place in range(2):
        for step in (1, 2, 3):
            line(step, place).wait_send()
        for step in range(4):
            across(step, place).wait_send()


def exchange_small(packed, loss):
    dma = pltpu.SemaphoreType.DMA
    vmem = pl.BlockSpec(memory_space=pltpu.VMEM)
    return pl.pallas_call(
        exchange_kernel,
        out_shape=[shape_of((8,) + packed.shape, packed.dtype), shape_of(loss.shape, f32)],
        in_specs=[vmem, vmem],
        out_specs=[vmem, vmem],
        scratch_shapes=[pltpu.VMEM(loss.shape, f32)] * 2
        + [pltpu.VMEM((8,) + loss.shape, f32), pltpu.VMEM(loss.shape, f32)]
        + [dma((3, 2)), dma((3, 2)), dma((4, 2)), dma((4, 2)), dma((2,)), dma((2,)), dma((2,))],
        compiler_params=pltpu.CompilerParams(collective_id=6, has_side_effects=True, vmem_limit_bytes=16 * MIB),
        name="exchange_small",
    )(packed, loss)


def few_experts(
    patches,
    target_noise,
    timesteps,
    labels,
    routes,
    route_gates,
    stem_weights,
    layer_in,
    layer_out,
    experts,
    stem_first,
    layer_in_first,
    layer_out_first,
    experts_first,
    stem_second,
    layer_in_second,
    layer_out_second,
    experts_second,
    stem_moment,
    layer_in_moment,
    layer_out_moment,
    experts_moment,
):
    count = patches.shape[0]
    items = timesteps.shape[0]
    halves = lax.axis_size(CORE)
    sharers = lax.axis_size(LINE) * halves
    expert_count = lax.axis_size(LINE) * experts.shape[1]
    place = lax.axis_index(LINE) * halves + lax.axis_index(CORE)

    stem_t = stem_weights.T
    lin_t = jnp.swapaxes(layer_in, 1, 2)
    louts = [to_half(layer_out[layer]) for layer in range(LAYERS)]
    pairs = [to_half(experts[layer, 0]) for layer in range(LAYERS)]
    gathered = gather_weights(stem_lanes(to_half(stem_t)), to_half(lin_t), louts, pairs[:1])
    stem_all = gathered[0].reshape(D, STEM_LANES)
    lin_all = gathered[1].reshape(LAYERS, -1, D)
    lout_all = [gathered[2 + layer].reshape(-1, D) for layer in range(LAYERS)]
    expert_all = [gathered[2 + LAYERS]]

    feat = time_features(timesteps)
    hot = label_table(labels)
    hot_pad = jnp.pad(hot, ((0, 32 - items), (0, STEM_PADDED[3] - hot.shape[1]))).astype(bf16)
    cond, hidden, pre_one, pre_two, mods, fin_mods = cond_forward(pad_rows(feat), hot_pad, stem_all, lin_all)
    tokens = product_nt(patches, stem_all[:, :PATCH_DIM])
    tokens = (tokens.reshape(items, -1, D) + positions_table()[None]).reshape(-1, D)
    expert_ids = jnp.arange(expert_count, dtype=jnp.int32)
    saved = []
    for layer in range(LAYERS):
        g4 = jnp.sum(
            jnp.where(routes[layer][:, :, None] == expert_ids, route_gates[layer][:, :, None], 0.0), axis=1
        )
        normed, qkv, attended, branch, middle, n2 = attn_forward(layer, tokens, mods[layer], lin_all)
        beside = (pairs[layer + 1],) if layer + 1 < LAYERS else ()
        active, slope, mixed, result, *arrived = ffn_forward(
            layer, n2, middle, mods[layer], g4, lin_all, lout_all[layer], expert_all[layer], halves, beside
        )
        if beside:
            expert_all.append(arrived[0])
        saved.append((tokens, g4, normed, qkv, attended, branch, middle, n2, active, slope, mixed))
        tokens = result
    fo_rows = stem_all[:, STEM_AT[5] : STEM_AT[5] + PATCH_DIM].T
    grad, grad_fin, grad_out_w, loss_rows = final_step(tokens, fin_mods, fo_rows, target_noise.T)

    stem_cols = stem_weights.shape[1]
    lin_cols = layer_in.shape[2]

    def outer(left_in, right_in):
        return lax.dot_general(left_in, right_in, (((0,), (0,)), ((), ())), preferred_element_type=f32)

    def flip(values):
        return jnp.swapaxes(values, -1, -2)

    states = (experts, experts_first, experts_second, lin_t, flip(layer_in_first[0]), flip(layer_in_second[0]))
    states = states + (layer_out, layer_out_first, layer_out_second)
    grad_mods, reduced, outgoing = [None] * LAYERS, [None] * LAYERS, [None] * LAYERS
    for layer in reversed(range(LAYERS)):
        tokens, g4, normed, qkv, attended, branch, middle, n2, active, slope, mixed = saved[layer]
        early = () if outgoing[1] is None else (outgoing[1][0].reshape((-1, halves) + pairs[0].shape),)
        dup, ddn, dex, gn2, grad_gate, *begun = ffn_backward(
            layer, grad, n2, mods[layer], g4, mixed, active, slope, lin_all, lout_all[layer], expert_all[layer], halves, early
        )
        grad, grad_mods[layer], dqkvo = attn_backward(
            layer, gn2, grad, middle, tokens, normed, qkv, attended, branch, mods[layer], grad_gate, lin_all,
            halves * lin_cols,
        )
        outgoing[layer] = (dex, dqkvo, dup, ddn)
    grad_patch = product_tn(patches, to_half(grad))
    dpre_one, dpre_two = cond_backward(grad_mods[0], grad_mods[1], grad_fin, pre_one, pre_two, stem_all, lin_all)

    names = jnp.stack([labels // 32, labels % 32], axis=1).astype(f32)
    factors = jnp.concatenate(
        [cond[:items], grad_mods[0][:items], grad_mods[1][:items], hidden[:items], dpre_one[:items], dpre_two[:items]]
        + [grad_fin[:items], feat, jnp.pad(names, ((0, 0), (0, 126)))],
        axis=1,
    ).astype(bf16)
    width = factors.shape[1]
    ends = jnp.concatenate([grad_patch, grad_out_w], axis=0).astype(bf16)
    packed = jnp.concatenate([factors.reshape(-1), ends.reshape(-1)])
    lanes = -(-packed.size // (16 * 128)) * 128
    packed = jnp.pad(packed, (0, 16 * lanes - packed.size)).reshape(16, lanes)
    loss = jnp.pad(loss_rows.reshape(1, PATCH_DIM), ((0, 7), (0, 128 - PATCH_DIM)))
    gathered, loss_all = exchange_small(packed, loss)
    loss_total = jnp.sum(loss_all)
    gathered = gathered.reshape(sharers, -1)
    factors = gathered[:, : items * width].reshape(sharers * items, width)
    ends = gathered[:, items * width : items * width + 2 * PATCH_DIM * D].reshape(sharers, 2, PATCH_DIM, D)
    ends = jnp.sum(ends.astype(f32), axis=0)
    cond_f, gm_a, gm_b, hidden_f, done_f, dtwo_f, fin_f, feat_f, names = jnp.split(
        factors, [D, 7 * D, 13 * D, 14 * D, 15 * D, 16 * D, 18 * D, 18 * D + FREQ], axis=1
    )
    hot_all = label_table((names[:, 0].astype(f32) * 32 + names[:, 1].astype(f32)).astype(jnp.int32)).astype(bf16)
    def own(values):
        return lax.dynamic_slice_in_dim(values, place * stem_cols, stem_cols, axis=1)

    stem_grad = jnp.concatenate(
        [
            own(ends[0]).T,
            outer(own(done_f), feat_f),
            outer(own(dtwo_f), hidden_f),
            outer(own(dtwo_f), hot_all),
            outer(own(cond_f), fin_f),
            own(ends[1]).T,
        ],
        axis=1,
    )
    stem_stepped = adam_step(stem_t, stem_grad, stem_first[0].T, stem_second[0].T)
    stem_delta = jnp.pad(to_half(stem_stepped[0]), ((0, 0), (0, -stem_t.shape[1] % 128)))
    for layer, gm in ((1, gm_b), (0, gm_a)):
        spread = jnp.pad(gm, ((0, 0), (4 * D, lin_cols * sharers - 10 * D)))
        window = lax.dynamic_slice_in_dim(spread, place * lin_cols, lin_cols, axis=1)
        dex, dqkvo, dup, ddn = outgoing[layer]
        reduced[layer] = reduce_layer(
            layer,
            dex.reshape((-1, halves) + dex.shape[1:]),
            dqkvo.reshape(halves, lin_cols, D),
            dup.reshape(-1, halves, lin_cols, D),
            ddn.reshape(-1, halves, layer_out.shape[1], D),
            outer(window, cond_f),
            states,
            stem_delta if layer == 1 else None,
            begun if layer == 1 else (),
        )
    stem_total = reduced[1][6]
    group_count = lax.axis_size(GROUP)

    mean_delta = stem_total[:, : stem_t.shape[1]] / group_count
    moment_new = outer_mom * stem_moment.T + mean_delta
    new_weight = stem_t - outer_rate * (mean_delta + outer_mom * moment_new)
    stem_out = [flip(v) for v in (new_weight, to_half(new_weight), stem_stepped[1][None], stem_stepped[2][None], moment_new)]

    def both(at, rows, tile, weight, first, second, moment):
        grads = [reduced[layer][at].reshape(rows, -1) for layer in range(LAYERS)]
        totals = [reduced[layer][3 + at].reshape(rows, -1) for layer in range(LAYERS)]
        shaped = [v.reshape(LAYERS, rows, -1) for v in (weight, first, second, moment)]
        return update_arrays(tile, grads, totals, *shaped)

    lin_out = both(1, lin_cols, 432, lin_t, flip(layer_in_first), flip(layer_in_second), flip(layer_in_moment))
    lin_out = [flip(v.reshape((1,) * (at in (2, 3)) + v.shape)) for at, v in enumerate(lin_out)]
    lout_rows = layer_out.shape[1]
    lout_out = both(2, lout_rows, lout_rows // 2, layer_out, layer_out_first, layer_out_second, layer_out_moment)
    lout_out = [v.reshape((1,) * (at in (2, 3)) + v.shape) for at, v in enumerate(lout_out)]
    expert_out = both(0, 2 * D, D // 2, experts, experts_first, experts_second, experts_moment)
    likes = (experts, experts, experts_first, experts_second, experts)
    expert_out = [v.reshape(like.shape) for v, like in zip(expert_out, likes)]
    results = []
    for at in range(5):
        results += [stem_out[at], lin_out[at], lout_out[at], expert_out[at]]
    return (loss_total, *results)


def solution(mesh):
    placed = (
        P((GROUP, LINE, CORE), None),
        P((GROUP, LINE, CORE), None),
        P((GROUP, LINE, CORE)),
        P((GROUP, LINE, CORE)),
        P(None, (GROUP, LINE, CORE), None),
        P(None, (GROUP, LINE, CORE), None),
        P(None, (LINE, CORE)),
        P(None, None, (LINE, CORE)),
        P(None, (LINE, CORE), None),
        P(None, LINE, None, None, CORE),
        P(GROUP, None, (LINE, CORE)),
        P(GROUP, None, None, (LINE, CORE)),
        P(GROUP, None, (LINE, CORE), None),
        P(GROUP, None, LINE, None, None, CORE),
        P(GROUP, None, (LINE, CORE)),
        P(GROUP, None, None, (LINE, CORE)),
        P(GROUP, None, (LINE, CORE), None),
        P(GROUP, None, LINE, None, None, CORE),
        P(None, (LINE, CORE)),
        P(None, None, (LINE, CORE)),
        P(None, (LINE, CORE), None),
        P(None, LINE, None, None, CORE),
    )
    step = few_experts if mesh.shape[LINE] <= 4 else per_device
    return jax.shard_map(
        step,
        mesh=mesh,
        in_specs=placed,
        out_specs=(
            P(),
            P(None, (LINE, CORE)),
            P(None, None, (LINE, CORE)),
            P(None, (LINE, CORE), None),
            P(None, LINE, None, None, CORE),
            P(None, (LINE, CORE)),
            P(None, None, (LINE, CORE)),
            P(None, (LINE, CORE), None),
            P(None, LINE, None, None, CORE),
            P(GROUP, None, (LINE, CORE)),
            P(GROUP, None, None, (LINE, CORE)),
            P(GROUP, None, (LINE, CORE), None),
            P(GROUP, None, LINE, None, None, CORE),
            P(GROUP, None, (LINE, CORE)),
            P(GROUP, None, None, (LINE, CORE)),
            P(GROUP, None, (LINE, CORE), None),
            P(GROUP, None, LINE, None, None, CORE),
            P(None, (LINE, CORE)),
            P(None, None, (LINE, CORE)),
            P(None, (LINE, CORE), None),
            P(None, LINE, None, None, CORE),
        ),
        check_vma=False,
    )
```
